32 devices in a mesh: seq: 4 (over y, x), fsdp: 8 (over z, core).
Axes of the slice: x: 2, y: 2, z: 4, core: 2. Of those that a mesh axis runs over, the one named last changes fastest.
Arguments:
- inputs: bfloat16 [8, 1024, 1536], P('fsdp', 'seq'), may hold values from -6 to 6
- cotangent: bfloat16 [8, 1024, 1536], P('fsdp', 'seq'), may hold values from -6 to 6
- qkv_weight: float32 [1536, 3072], P('fsdp'), may hold values from -0.15625 to 0.15625
- out_weight: float32 [1536, 1536], P('fsdp'), may hold values from -1.75 to 1.75
- gate_up_weight: float32 [1536, 8192], P('fsdp'), may hold values from -0.15625 to 0.15625
- down_weight: float32 [4096, 1536], P('fsdp'), may hold values from -0.09375 to 0.09375
- norm_gains: float32 [2, 1536], P(None, 'fsdp'), may hold values from 0.5 to 1.5
- qkv_first: float32 [1536, 3072], P('fsdp'), may hold values from -40 to 40
- qkv_second: float32 [1536, 3072], P('fsdp'), may hold values from 212.992 to 860.16
- out_first: float32 [1536, 1536], P('fsdp'), may hold values from -3.5 to 3.5
- out_second: float32 [1536, 1536], P('fsdp'), may hold values from 1.55648 to 6.22592
- gate_up_first: float32 [1536, 8192], P('fsdp'), may hold values from -24 to 24
- gate_up_second: float32 [1536, 8192], P('fsdp'), may hold values from 68.8128 to 278.528
- down_first: float32 [4096, 1536], P('fsdp'), may hold values from -32 to 32
- down_second: float32 [4096, 1536], P('fsdp'), may hold values from 155.648 to 622.592
- gain_first: float32 [2, 1536], P(None, 'fsdp'), may hold values from -64 to 64
- gain_second: float32 [2, 1536], P(None, 'fsdp'), may hold values from 434.176 to 1720.32
Outputs:
- block_out: bfloat16 [8, 1024, 1536], P('fsdp', 'seq')
- input_grad: float32 [8, 1024, 1536], P('fsdp', 'seq')
- qkv_weight_new: float32 [1536, 3072], P('fsdp')
- qkv_first_new: float32 [1536, 3072], P('fsdp')
- qkv_second_new: float32 [1536, 3072], P('fsdp')
- out_weight_new: float32 [1536, 1536], P('fsdp')
- out_first_new: float32 [1536, 1536], P('fsdp')
- out_second_new: float32 [1536, 1536], P('fsdp')
- gate_up_weight_new: float32 [1536, 8192], P('fsdp')
- gate_up_first_new: float32 [1536, 8192], P('fsdp')
- gate_up_second_new: float32 [1536, 8192], P('fsdp')
- down_weight_new: float32 [4096, 1536], P('fsdp')
- down_first_new: float32 [4096, 1536], P('fsdp')
- down_second_new: float32 [4096, 1536], P('fsdp')
- norm_gains_new: float32 [2, 1536], P(None, 'fsdp')
- gain_first_new: float32 [2, 1536], P(None, 'fsdp')
- gain_second_new: float32 [2, 1536], P(None, 'fsdp')
The draws below stay inside these ranges and needn't reach their ends.
All inputs are finite; a program needn't handle non-finite values.
Results may differ from the reference program's by a relative error of at most 0.03.
Values may be sent and summed in bfloat16 or wider, within the bound.
A program may use at most 384 MiB of HBM per device.

```python
import math
import jax
import jax.numpy as jnp
from jax import lax

D = 1536
KV_HEADS = 8
HEAD_DIM = 96
FF = 4096
SEQ_LEN = 1024
ADAM_STEP = 10
GROUP = 2
QKV_COLS = 3072
SEQS = 8
TOKENS = 8192


def shard_levels(own_key, shape, cuts, least, largest):
    def one(position, parts):
        steps = jax.random.uniform(jax.random.fold_in(jax.random.fold_in(own_key, 6), position), (parts,), jnp.float32, least / len(cuts), largest / len(cuts))
        return jnp.repeat(jnp.exp(steps), shape[position] // parts).reshape((-1,) + (1,) * (len(shape) - position - 1))

    gain = one(*cuts[0])
    for cut in cuts[1:]:
        gain = gain * one(*cut)
    return gain


def gaussian(rng, dims, width, most, split=(), kind=jnp.bfloat16):
    gain = shard_levels(rng, dims, split, -0.22, 0.18) if split else 1.0
    values = jax.random.normal(rng, dims, jnp.float32) * width * gain
    return jnp.minimum(jnp.maximum(values, -most), most).astype(kind)


def setup_inputs(seed: int = 0) -> dict:
    key_list = jax.random.split(jax.random.key(seed), 18)
    inputs = gaussian(key_list[0], (SEQS, SEQ_LEN, D), 1.0, 6.0, ((0, 8), (1, 4)))
    cotangent = gaussian(key_list[1], (SEQS, SEQ_LEN, D), 1.0, 6.0, ((0, 8), (1, 4)))
    qkv_weight = gaussian(key_list[2], (D, QKV_COLS), D ** -0.5, 0.15625, ((0, 8),), jnp.float32)
    out_weight = gaussian(key_list[3], (D, D), (D * 8 // SEQ_LEN) ** -0.5, 1.75, ((0, 8),), jnp.float32)
    gate_up_weight = gaussian(key_list[4], (D, 2 * FF), D ** -0.5, 0.15625, ((0, 8),), jnp.float32)
    down_weight = gaussian(key_list[5], (FF, D), FF ** -0.5, 0.09375, ((0, 8),), jnp.float32)
    norm_gains = jnp.clip(1.0 + 0.1 * jax.random.normal(key_list[6], (2, D), jnp.float32), 0.5, 1.5)
    qkv_first = gaussian(key_list[7], (D, QKV_COLS), (0.079 * TOKENS ** 0.5), 40.0, ((0, 8),), jnp.float32)
    qkv_second = jnp.clip(jnp.exp(math.log(860.16) - 1.3958638 * jax.random.uniform(key_list[8], (D, QKV_COLS), jnp.float32) ** shard_levels(key_list[8], (D, QKV_COLS), ((0, 8),), -0.2, 0.2)), 212.992, 860.16)
    out_first = gaussian(key_list[9], (D, D), (0.0067 * TOKENS ** 0.5), 3.5, ((0, 8),), jnp.float32)
    out_second = jnp.clip(jnp.exp(math.log(6.22592) - 1.3862944 * jax.random.uniform(key_list[10], (D, D), jnp.float32) ** shard_levels(key_list[10], (D, D), ((0, 8),), -0.2, 0.2)), 1.55648, 6.22592)
    gate_up_first = gaussian(key_list[11], (D, 2 * FF), (0.044 * TOKENS ** 0.5), 24.0, ((0, 8),), jnp.float32)
    gate_up_second = jnp.clip(jnp.exp(math.log(278.528) - 1.3981289 * jax.random.uniform(key_list[12], (D, 2 * FF), jnp.float32) ** shard_levels(key_list[12], (D, 2 * FF), ((0, 8),), -0.2, 0.2)), 68.8128, 278.528)
    down_first = gaussian(key_list[13], (FF, D), (0.067 * TOKENS ** 0.5), 32.0, ((0, 8),), jnp.float32)
    down_second = jnp.clip(jnp.exp(math.log(622.592) - 1.3862944 * jax.random.uniform(key_list[14], (FF, D), jnp.float32) ** shard_levels(key_list[14], (FF, D), ((0, 8),), -0.2, 0.2)), 155.648, 622.592)
    gain_first = gaussian(key_list[15], (2, D), (0.11 * TOKENS ** 0.5), 64.0, ((1, 8),), jnp.float32)
    gain_second = jnp.clip(jnp.exp(math.log(1720.32) - 1.3768156 * jax.random.uniform(key_list[16], (2, D), jnp.float32) ** shard_levels(key_list[16], (2, D), ((1, 8),), -0.2, 0.2)), 434.176, 1720.32)
    return dict(inputs=inputs, cotangent=cotangent, qkv_weight=qkv_weight, out_weight=out_weight, gate_up_weight=gate_up_weight, down_weight=down_weight, norm_gains=norm_gains, qkv_first=qkv_first, qkv_second=qkv_second, out_first=out_first, out_second=out_second, gate_up_first=gate_up_first, gate_up_second=gate_up_second, down_first=down_first, down_second=down_second, gain_first=gain_first, gain_second=gain_second)


@jax.custom_vjp
def low(v):
    return lax.optimization_barrier(v.astype(jnp.bfloat16)).astype(jnp.float32)

@jax.custom_vjp
def low_back(v):
    return v

def low_keep(v):
    return (low(v), None)

def low_pass(kept, grad):
    return (grad,)

def back_keep(v):
    return (v, None)

def back_low(kept, grad):
    return (low(grad),)
low.defvjp(low_keep, low_pass)
low_back.defvjp(back_keep, back_low)
NORM_EPS = 1e-05
ROPE_BASE = 100000.0
BETA_ONE = 0.9
BETA_TWO = 0.95
ADAM_EPS = 1e-08
WEIGHT_DECAY = 0.1
RATE_QKV = 0.07
RATE_OUT = 0.8
RATE_GATE_UP = 0.07
RATE_DOWN = 0.045
RATE_GAINS = 0.6
HIGHEST = lax.Precision.HIGHEST

def rms_scale(array_in, gain_row):
    inverse = lax.rsqrt(lax.optimization_barrier(jnp.mean(array_in * array_in, axis=-1, keepdims=True)) + NORM_EPS)
    return array_in * inverse * gain_row

def rope_tables(seq_length, head_width):
    half_width = head_width // 2
    frequencies = ROPE_BASE ** (-(2.0 * jnp.arange(half_width, dtype=jnp.float32)) / head_width)
    angles = jnp.arange(seq_length, dtype=jnp.float32)[:, None] * frequencies[None, :]
    return (jnp.cos(angles), jnp.sin(angles))

def rotate(array_in, cos_table, sin_table):
    half_width = array_in.shape[-1] // 2
    front_half = array_in[..., :half_width]
    back_half = array_in[..., half_width:]
    return jnp.concatenate([front_half * cos_table - back_half * sin_table, back_half * cos_table + front_half * sin_table], axis=-1)

def attend_block(query_rows, key_heads, value_heads, row_start):
    block_rows = query_rows.shape[0]
    scores = low_back(jnp.einsum('qghe,kge->ghqk', query_rows, key_heads, precision=HIGHEST)) * HEAD_DIM ** (-0.5)
    query_pos = row_start + jnp.arange(block_rows, dtype=jnp.int32)
    key_pos = jnp.arange(SEQ_LEN, dtype=jnp.int32)
    allowed = key_pos[None, :] <= query_pos[:, None]
    scores = jnp.where(allowed, scores, -1e+30)
    row_max = lax.optimization_barrier(jnp.max(scores, axis=-1, keepdims=True))
    exp_terms = jnp.exp(scores - row_max)
    attn_probs = exp_terms / lax.optimization_barrier(jnp.sum(exp_terms, axis=-1, keepdims=True))
    return jnp.einsum('ghqk,kge->qghe', low(attn_probs), value_heads, precision=HIGHEST)

def attend_sequence(packed):
    query_heads, key_heads, value_heads = packed
    block_rows = min(512, SEQ_LEN)
    starts = (jnp.arange(SEQ_LEN // block_rows, dtype=jnp.int32) * block_rows).astype(jnp.int32)

    def one_block(row_start):
        query_rows = lax.dynamic_slice_in_dim(query_heads, row_start.astype(jnp.int32), block_rows, 0)
        return attend_block(query_rows, key_heads, value_heads, row_start)
    blocks_out = lax.map(jax.checkpoint(one_block), starts)
    return blocks_out.reshape(SEQ_LEN, D)

def layer_group(seq_group, weights):
    qkv_low, out_low, gate_up_low, down_low, gains_low = weights
    seq_count = seq_group.shape[0]
    normed_in = low(rms_scale(seq_group, gains_low[0]))
    projected = low(low_back(jnp.einsum('tsd,dc->tsc', normed_in, qkv_low, precision=HIGHEST)))
    head_parts = projected.reshape(seq_count, SEQ_LEN, KV_HEADS, GROUP + 2, HEAD_DIM)
    cos_table, sin_table = rope_tables(SEQ_LEN, HEAD_DIM)
    query_heads = low(rotate(head_parts[:, :, :, :GROUP], cos_table[:, None, None, :], sin_table[:, None, None, :]))
    key_heads = low(rotate(head_parts[:, :, :, GROUP], cos_table[:, None, :], sin_table[:, None, :]))
    value_heads = head_parts[:, :, :, GROUP + 1]
    attended = lax.map(attend_sequence, (query_heads, key_heads, value_heads))
    attended = low(low_back(attended))
    branch = low_back(jnp.einsum('tsc,cd->tsd', attended, out_low, precision=HIGHEST))
    hidden = seq_group + branch
    normed_mid = low(rms_scale(hidden, gains_low[1]))
    gate_up = low_back(jnp.einsum('tsd,dc->tsc', normed_mid, gate_up_low, precision=HIGHEST))
    gate_part = gate_up[..., :FF]
    up_part = gate_up[..., FF:]
    activated = low(gate_part * jax.nn.sigmoid(gate_part) * up_part)
    return hidden + jnp.einsum('tsf,fd->tsd', activated, down_low, precision=HIGHEST)

def forward(inputs, qkv_weight, out_weight, gate_up_weight, down_weight, norm_gains):
    weights = (low(qkv_weight), low(out_weight), low(gate_up_weight), low(down_weight), low(norm_gains))
    per_step = math.gcd(SEQS, max(1, 4096 // SEQ_LEN))
    grouped = inputs.reshape(SEQS // per_step, per_step, SEQ_LEN, D)

    def run_group(seq_group):
        return layer_group(seq_group, weights)
    results = lax.map(jax.checkpoint(run_group), grouped)
    return results.reshape(SEQS, SEQ_LEN, D)

def adamw(weight, first, second, grad, rate, decay):
    first_new = BETA_ONE * first + (1.0 - BETA_ONE) * grad
    second_new = BETA_TWO * second + (1.0 - BETA_TWO) * grad * grad
    first_hat = first_new / (1.0 - BETA_ONE ** ADAM_STEP)
    second_hat = second_new / (1.0 - BETA_TWO ** ADAM_STEP)
    weight_new = weight - rate * (first_hat / (jnp.sqrt(second_hat) + ADAM_EPS) + decay * weight)
    return (weight_new, first_new, second_new)

def reference(inputs, cotangent, qkv_weight, out_weight, gate_up_weight, down_weight, norm_gains, qkv_first, qkv_second, out_first, out_second, gate_up_first, gate_up_second, down_first, down_second, gain_first, gain_second):
    primals = (inputs.astype(jnp.float32), qkv_weight, out_weight, gate_up_weight, down_weight, norm_gains)
    result, pullback = jax.vjp(forward, *primals)
    grads = pullback(cotangent.astype(jnp.float32))
    qkv_new = adamw(qkv_weight, qkv_first, qkv_second, grads[1], RATE_QKV, WEIGHT_DECAY)
    out_new = adamw(out_weight, out_first, out_second, grads[2], RATE_OUT, WEIGHT_DECAY)
    gate_up_new = adamw(gate_up_weight, gate_up_first, gate_up_second, grads[3], RATE_GATE_UP, WEIGHT_DECAY)
    down_new = adamw(down_weight, down_first, down_second, grads[4], RATE_DOWN, WEIGHT_DECAY)
    gains_new = adamw(norm_gains, gain_first, gain_second, grads[5], RATE_GAINS, 0.0)
    return (result.astype(jnp.bfloat16), grads[0], qkv_new[0], qkv_new[1], qkv_new[2], out_new[0], out_new[1], out_new[2], gate_up_new[0], gate_up_new[1], gate_up_new[2], down_new[0], down_new[1], down_new[2], gains_new[0], gains_new[1], gains_new[2])
```

```python
import jax
import jax.numpy as jnp
from jax import lax
from jax.sharding import PartitionSpec as P

HEAD_DIM = 96
KV_HEADS = 8
ADAM_STEP = 10
GROUP = 2

NORM_EPS = 1e-05
ROPE_BASE = 100000.0
BETA_ONE = 0.9
BETA_TWO = 0.95
ADAM_EPS = 1e-08
WEIGHT_DECAY = 0.1
RATE_QKV = 0.07
RATE_OUT = 0.8
RATE_GATE_UP = 0.07
RATE_DOWN = 0.045
RATE_GAINS = 0.6
BF = jnp.bfloat16
F32 = jnp.float32


def rope_tables(seq_length, head_width):
    half_width = head_width // 2
    frequencies = ROPE_BASE ** (-(2.0 * jnp.arange(half_width, dtype=jnp.float32)) / head_width)
    angles = jnp.arange(seq_length, dtype=jnp.float32)[:, None] * frequencies[None, :]
    return (jnp.cos(angles), jnp.sin(angles))


def rotate(array_in, cos_table, sin_table):
    half_width = array_in.shape[-1] // 2
    front_half = array_in[..., :half_width]
    back_half = array_in[..., half_width:]
    return jnp.concatenate(
        [
            front_half * cos_table - back_half * sin_table,
            back_half * cos_table + front_half * sin_table,
        ],
        axis=-1,
    )


def causal_mask(row_start, block_rows, seq_length):
    query_pos = row_start + jnp.arange(block_rows, dtype=jnp.int32)
    key_pos = jnp.arange(seq_length, dtype=jnp.int32)
    return key_pos[None, :] <= query_pos[:, None]


def split_heads(block_seq):
    seq_length = block_seq.shape[0]
    local_groups = block_seq.shape[1] // ((GROUP + 2) * HEAD_DIM)
    head_parts = block_seq.reshape(seq_length, local_groups, GROUP + 2, HEAD_DIM)
    cos_table, sin_table = rope_tables(seq_length, HEAD_DIM)
    query_heads = rotate(
        head_parts[:, :, :GROUP].astype(jnp.float32),
        cos_table[:, None, None, :],
        sin_table[:, None, None, :],
    ).astype(jnp.bfloat16)
    key_heads = rotate(
        head_parts[:, :, GROUP].astype(jnp.float32), cos_table[:, None, :], sin_table[:, None, :]
    ).astype(jnp.bfloat16)
    value_heads = head_parts[:, :, GROUP + 1]
    return (query_heads, key_heads, value_heads, cos_table, sin_table)


def attend_one(block_seq):
    query_heads, key_heads, value_heads, cos_table, sin_table = split_heads(block_seq)
    seq_length = block_seq.shape[0]
    block_rows = min(512, seq_length)
    scale_factor = HEAD_DIM ** (-0.5)

    def one_block(block_index):
        row_start = block_index * block_rows
        query_rows = lax.dynamic_slice_in_dim(query_heads, row_start, block_rows, 0)
        scores = (
            jnp.einsum("qghe,kge->ghqk", query_rows, key_heads, preferred_element_type=jnp.float32)
            * scale_factor
        )
        scores = jnp.where(causal_mask(row_start, block_rows, seq_length), scores, -1e30)
        row_max = jnp.max(scores, axis=-1, keepdims=True)
        exp_terms = jnp.exp(scores - row_max)
        row_sum = jnp.sum(exp_terms, axis=-1, keepdims=True)
        attn_probs = (exp_terms / row_sum).astype(jnp.bfloat16)
        attended = jnp.einsum(
            "ghqk,kge->qghe", attn_probs, value_heads, preferred_element_type=jnp.float32
        )
        return (
            attended.astype(jnp.bfloat16).reshape(block_rows, -1),
            (row_max + jnp.log(row_sum))[..., 0],
        )

    blocks_out, log_sums = lax.map(one_block, jnp.arange(seq_length // block_rows, dtype=jnp.int32))
    return (blocks_out.reshape(seq_length, -1), log_sums)


def attend_back(packed):
    block_seq, log_sums, grad_attended = packed
    query_heads, key_heads, value_heads, cos_table, sin_table = split_heads(block_seq)
    seq_length = block_seq.shape[0]
    local_groups = key_heads.shape[1]
    block_rows = min(512, seq_length)
    scale_factor = HEAD_DIM ** (-0.5)
    grad_heads = grad_attended.reshape(seq_length, local_groups, GROUP, HEAD_DIM)

    def one_block(running, inputs_here):
        grad_keys, grad_values = running
        block_index, block_sums = inputs_here
        row_start = block_index * block_rows
        query_rows = lax.dynamic_slice_in_dim(query_heads, row_start, block_rows, 0)
        grad_rows = lax.dynamic_slice_in_dim(grad_heads, row_start, block_rows, 0)
        scores = (
            jnp.einsum("qghe,kge->ghqk", query_rows, key_heads, preferred_element_type=jnp.float32)
            * scale_factor
        )
        scores = jnp.where(causal_mask(row_start, block_rows, seq_length), scores, -1e30)
        attn_probs = jnp.exp(scores - block_sums[..., None])
        grad_probs = jnp.einsum(
            "qghe,kge->ghqk", grad_rows, value_heads, preferred_element_type=jnp.float32
        )
        grad_scores = attn_probs * (
            grad_probs - jnp.sum(attn_probs * grad_probs, axis=-1, keepdims=True)
        )
        grad_dot = (grad_scores * scale_factor).astype(jnp.bfloat16)
        grad_query = jnp.einsum(
            "ghqk,kge->qghe", grad_dot, key_heads, preferred_element_type=jnp.float32
        )
        grad_keys = grad_keys + jnp.einsum(
            "ghqk,qghe->kge", grad_dot, query_rows, preferred_element_type=jnp.float32
        )
        grad_values = grad_values + jnp.einsum(
            "ghqk,qghe->kge",
            attn_probs.astype(jnp.bfloat16),
            grad_rows,
            preferred_element_type=jnp.float32,
        )
        return ((grad_keys, grad_values), grad_query)

    zeros_kv = jnp.zeros((seq_length, local_groups, HEAD_DIM), jnp.float32)
    block_ids = jnp.arange(seq_length // block_rows, dtype=jnp.int32)
    (grad_keys, grad_values), grad_queries = lax.scan(
        one_block, (zeros_kv, zeros_kv), (block_ids, log_sums)
    )
    grad_queries = grad_queries.reshape(seq_length, local_groups, GROUP, HEAD_DIM)
    grad_queries = rotate(grad_queries, cos_table[:, None, None, :], -sin_table[:, None, None, :])
    grad_keys = rotate(grad_keys, cos_table[:, None, :], -sin_table[:, None, :])
    stacked = jnp.concatenate(
        [grad_queries, grad_keys[:, :, None, :], grad_values[:, :, None, :]], axis=2
    )
    return stacked.reshape(seq_length, -1).astype(jnp.bfloat16)


def adamw(weight, first, second, grad, rate, decay):
    first_new = BETA_ONE * first + (1.0 - BETA_ONE) * grad
    second_new = BETA_TWO * second + (1.0 - BETA_TWO) * grad * grad
    first_hat = first_new / (1.0 - BETA_ONE**ADAM_STEP)
    second_hat = second_new / (1.0 - BETA_TWO**ADAM_STEP)
    weight_new = weight - rate * (first_hat / (jnp.sqrt(second_hat) + ADAM_EPS) + decay * weight)
    return (weight_new, first_new, second_new)


def dot(a, b, dims):
    return lax.dot_general(a, b, (dims, ((), ())), preferred_element_type=F32)


def make(n_seq, n_fsdp):
    sib = KV_HEADS // n_seq
    planes = n_fsdp // sib
    sib_groups = [[p * sib + c for c in range(sib)] for p in range(planes)]
    col_groups = [[p * sib + c for p in range(planes)] for c in range(sib)]

    def plane_gather(x):
        x = lax.all_gather(x, "seq", axis=1, tiled=True)
        return lax.all_gather(x, "fsdp", axis=0, tiled=True, axis_index_groups=sib_groups)

    def plane_scatter(x):
        x = lax.psum_scatter(
            x, "fsdp", scatter_dimension=0, tiled=True, axis_index_groups=sib_groups
        )
        return lax.psum_scatter(x, "seq", scatter_dimension=1, tiled=True)

    def on_device(
        inputs, cotangent, qkv_weight, out_weight, gate_up_weight, down_weight, norm_gains,
        qkv_first, qkv_second, out_first, out_second, gate_up_first, gate_up_second,
        down_first, down_second, gain_first, gain_second,
    ):
        s_idx = lax.axis_index("seq")
        c_idx = lax.rem(lax.axis_index("fsdp"), sib)
        width = inputs.shape[-1]
        rows = qkv_weight.shape[0]
        head_cols = (GROUP + 2) * HEAD_DIM
        ff_rows = down_weight.shape[0]
        units = ff_rows // n_seq
        hidden_units = ff_rows * n_fsdp
        local_units = hidden_units // KV_HEADS
        gains = norm_gains.astype(BF).astype(F32)

        w_qkv = lax.dynamic_slice_in_dim(qkv_weight, s_idx * sib * head_cols, sib * head_cols, 1)
        w_qkv = (w_qkv * gains[0][:, None]).astype(BF)
        w_qkv = lax.all_gather(w_qkv, "fsdp", axis=0, tiled=True)
        w_qkv = lax.dynamic_slice_in_dim(w_qkv, c_idx * head_cols, head_cols, 1)
        w_out = lax.all_gather(out_weight.astype(BF), "fsdp", axis=0, tiled=True)
        w_gu = gate_up_weight.reshape(rows, 2, planes, sib, n_seq, units)
        w_gu = lax.dynamic_index_in_dim(w_gu, s_idx, 4, keepdims=False)
        w_gu = (w_gu * gains[1][:, None, None, None, None]).astype(BF)
        w_gu = w_gu.transpose(0, 3, 1, 2, 4).reshape(rows, sib * 2 * local_units)
        w_gu = lax.all_gather(w_gu, "fsdp", axis=0, tiled=True)
        w_gu = lax.dynamic_slice_in_dim(w_gu, c_idx * 2 * local_units, 2 * local_units, 1)
        w_down = lax.dynamic_slice_in_dim(down_weight, s_idx * units, units, 0).astype(BF)
        w_down = lax.all_gather(w_down, "fsdp", axis=0, tiled=True, axis_index_groups=col_groups)

        x_own = inputs.astype(F32)
        inv_one = lax.rsqrt(jnp.mean(x_own * x_own, axis=-1, keepdims=True) + NORM_EPS)
        norm_one = x_own * inv_one
        n_one = plane_gather(norm_one.astype(BF))
        cot_all = plane_gather(cotangent)
        seq_len = n_one.shape[1]
        tokens = sib * seq_len
        n_one_flat = n_one.reshape(tokens, width)

        projected = dot(n_one_flat, w_qkv, ((1,), (0,))).astype(BF).reshape(sib, seq_len, head_cols)
        attended, log_sums = lax.map(attend_one, projected)
        att = lax.all_to_all(attended, "seq", split_axis=1, concat_axis=2, tiled=True)
        length = att.shape[1]
        att = att.reshape(sib, length, n_seq, 1, GROUP * HEAD_DIM)
        att = lax.all_to_all(
            att, "fsdp", split_axis=0, concat_axis=3, tiled=True, axis_index_groups=sib_groups
        )
        att = att.reshape(length, width)
        hidden = x_own[0] + dot(att, w_out, ((1,), (0,)))
        inv_mid = lax.rsqrt(jnp.mean(hidden * hidden, axis=-1, keepdims=True) + NORM_EPS)
        norm_mid = hidden * inv_mid
        n_mid = plane_gather(norm_mid.astype(BF)[None]).reshape(tokens, width)
        gate_up = dot(n_mid, w_gu, ((1,), (0,)))
        gate = gate_up[:, :local_units]
        up = gate_up[:, local_units:]
        sig = jax.nn.sigmoid(gate)
        silu = gate * sig
        activated = (silu * up).astype(BF)
        down_part = dot(activated, w_down, ((1,), (0,))).astype(BF)
        down_sum = plane_scatter(down_part.reshape(sib, seq_len, width))
        block_out = (hidden + down_sum[0].astype(F32)).astype(BF)[None]
        cot_flat = cot_all.reshape(tokens, width)
        grad_act = dot(cot_flat, w_down, ((1,), (1,)))
        s_down = dot(activated, cot_flat, ((0,), (0,))).astype(BF)
        grad_gu = jnp.concatenate(
            [grad_act * up * sig * (1.0 + gate * (1.0 - sig)), grad_act * silu], axis=-1
        ).astype(BF)
        s_gu = dot(n_mid, grad_gu, ((0,), (0,))).astype(BF)
        e_mid = dot(grad_gu, w_gu, ((1,), (1,))).astype(BF)
        e_mid = plane_scatter(e_mid.reshape(sib, seq_len, width))[0].astype(F32)
        grad_hidden = cotangent[0].astype(F32) + inv_mid * (
            e_mid - norm_mid * jnp.mean(e_mid * norm_mid, axis=-1, keepdims=True)
        )
        grad_branch = grad_hidden.astype(BF)
        s_out = dot(att, grad_branch, ((0,), (0,))).astype(BF)
        grad_att = dot(grad_branch, w_out, ((1,), (1,))).astype(BF)
        grad_att = grad_att.reshape(1, length, n_seq, sib, GROUP * HEAD_DIM)
        grad_att = lax.all_to_all(
            grad_att, "fsdp", split_axis=3, concat_axis=0, tiled=True, axis_index_groups=sib_groups
        ).reshape(sib, length, n_seq * GROUP * HEAD_DIM)
        grad_heads = lax.all_to_all(grad_att, "seq", split_axis=2, concat_axis=1, tiled=True)
        grad_qkv = lax.map(attend_back, (projected, log_sums, grad_heads)).reshape(tokens, head_cols)
        s_qkv = dot(n_one_flat, grad_qkv, ((0,), (0,))).astype(BF)
        e_in = dot(grad_qkv, w_qkv, ((1,), (1,))).astype(BF)
        e_in = plane_scatter(e_in.reshape(sib, seq_len, width)).astype(F32)
        input_grad = grad_hidden[None] + inv_one * (
            e_in - norm_one * jnp.mean(e_in * norm_one, axis=-1, keepdims=True)
        )

        def column_sum(part):
            cols = part.shape[-1]
            part = part.reshape(planes, 1, sib, rows, cols)
            part = lax.all_to_all(
                part, "fsdp", split_axis=2, concat_axis=1, tiled=True, axis_index_groups=sib_groups
            ).reshape(planes, sib, rows, cols)
            part = lax.psum_scatter(
                part, "fsdp", scatter_dimension=0, tiled=True, axis_index_groups=col_groups
            )
            return part.reshape(sib, rows, cols)

        g_qkv = column_sum(s_qkv).transpose(1, 0, 2).reshape(rows, sib * head_cols)
        g_qkv = lax.all_gather(g_qkv, "seq", axis=1, tiled=True).astype(F32)
        g_gu = column_sum(s_gu)
        g_gu = lax.all_gather(g_gu, "seq", axis=0, tiled=False)
        g_gu = g_gu.reshape(n_seq, sib, rows, 2, planes, units).transpose(2, 3, 4, 1, 0, 5)
        g_gu = g_gu.reshape(rows, 2 * hidden_units).astype(F32)
        g_down = lax.psum_scatter(
            s_down, "fsdp", scatter_dimension=0, tiled=True, axis_index_groups=col_groups
        )
        g_down = lax.all_gather(g_down, "seq", axis=0, tiled=True).astype(F32)
        g_out = lax.psum_scatter(s_out, "seq", scatter_dimension=1, tiled=True)
        g_out = lax.psum_scatter(g_out, "fsdp", scatter_dimension=0, tiled=True)
        g_out = lax.all_gather(g_out, "seq", axis=1, tiled=True).astype(F32)
        gain_grad = jnp.stack(
            [
                jnp.sum(g_qkv * qkv_weight.astype(BF).astype(F32), axis=1),
                jnp.sum(g_gu * gate_up_weight.astype(BF).astype(F32), axis=1),
            ]
        )
        g_qkv = g_qkv * gains[0][:, None]
        g_gu = g_gu * gains[1][:, None]
        qkv_new = adamw(qkv_weight, qkv_first, qkv_second, g_qkv, RATE_QKV, WEIGHT_DECAY)
        out_new = adamw(out_weight, out_first, out_second, g_out, RATE_OUT, WEIGHT_DECAY)
        gu_new = adamw(
            gate_up_weight, gate_up_first, gate_up_second, g_gu, RATE_GATE_UP, WEIGHT_DECAY
        )
        down_new = adamw(down_weight, down_first, down_second, g_down, RATE_DOWN, WEIGHT_DECAY)
        gains_new = adamw(norm_gains, gain_first, gain_second, gain_grad, RATE_GAINS, 0.0)
        return (block_out, input_grad, *qkv_new, *out_new, *gu_new, *down_new, *gains_new)

    return on_device


def solution(mesh):
    tokens = P("fsdp", "seq", None)
    weight = P("fsdp", None)
    gain = P(None, "fsdp")
    in_specs = (tokens, tokens, weight, weight, weight, weight, gain) + (weight,) * 8 + (gain,) * 2
    out_specs = (tokens, tokens) + (weight,) * 12 + (gain,) * 3
    return jax.shard_map(
        make(mesh.shape["seq"], mesh.shape["fsdp"]),
        mesh=mesh, in_specs=in_specs, out_specs=out_specs, check_vma=False,
    )
```

```python
import functools

import jax
import jax.numpy as jnp
from jax import lax
from jax.experimental import pallas as pl
from jax.experimental.pallas import tpu as pltpu
from jax.sharding import PartitionSpec as P

HEAD_DIM = 96
KV_HEADS = 8
ADAM_STEP = 10
GROUP = 2

NORM_EPS = 1e-05
ROPE_BASE = 100000.0
BETA_ONE = 0.9
BETA_TWO = 0.95
ADAM_EPS = 1e-08
WEIGHT_DECAY = 0.1
RATE_QKV = 0.07
RATE_OUT = 0.8
RATE_GATE_UP = 0.07
RATE_DOWN = 0.045
RATE_GAINS = 0.6
BF = jnp.bfloat16
F32 = jnp.float32
VMEM_LIMIT = 62 * 1024 * 1024


MESH = pl.DeviceIdType.MESH


def rdma(src, dst, ssem, rsem, dev):
    return pltpu.make_async_remote_copy(
        src_ref=src, dst_ref=dst, send_sem=ssem, recv_sem=rsem, device_id=dev, device_id_type=MESH
    )


class Place:
    def __init__(self, n, sib, planes):
        self.n, self.sib, self.planes = n, sib, planes
        self.s = lax.axis_index("seq")
        self.f = lax.axis_index("fsdp")
        self.c = lax.rem(self.f, sib)
        self.p = lax.div(self.f, sib)
        a, b = lax.div(self.s, 2), lax.rem(self.s, 2)
        self.r = a * (1 - b) + (n - 1 - a) * b

    def seq_at(self, j):
        if j == 0:
            return self.s
        n = self.n
        q = lax.rem(self.r + (j + n), n)
        t = lax.div(q, n // 2)
        return (1 - t) * 2 * q + t * (2 * (n - 1 - q) + 1)

    def dev(self, s, c):
        return (s, self.p * self.sib + c)

    def col(self, dp, dc):
        return lax.rem(self.p + dp, self.planes) * self.sib + lax.rem(self.c + dc, self.sib)

    def barrier(self):
        sem = pltpu.get_barrier_semaphore()
        group = self.n * self.sib
        tau = self.s * self.sib + self.c
        for j in range(1, group):
            t = lax.rem(tau + j, group)
            pl.semaphore_signal(
                sem, inc=1, device_id=self.dev(lax.div(t, self.sib), lax.rem(t, self.sib)),
                device_id_type=MESH,
            )
        for dp in range(1, self.planes):
            for dc in range(self.sib):
                pl.semaphore_signal(
                    sem, inc=1, device_id=(self.s, self.col(dp, dc)), device_id_type=MESH
                )
        pl.semaphore_wait(sem, group - 1 + (self.planes - 1) * self.sib)


class Gather:
    def __init__(self, at, part, sems):
        self.at, self.part = at, part
        self.ring_s, self.ring_r, self.sib_s, self.sib_r = sems
        self.sent = []

    @staticmethod
    def scratch(n):
        d = pltpu.SemaphoreType.DMA
        return [d((2, n // 2, 2)), d((2, n // 2, 2)), d((n, 2)), d((n, 2))]

    def _send(self, copy):
        copy.start()
        self.sent.append(copy)

    def _ring(self, way, hop, half):
        at = self.at
        src = self.part(at.c, at.seq_at(-(hop - 1) if way == 0 else hop - 1), half)
        to = at.dev(at.seq_at(1 if way == 0 else -1), at.c)
        self._send(
            rdma(src, src, self.ring_s.at[way, hop - 1, half], self.ring_r.at[way, hop - 1, half], to)
        )

    def _sib(self, j, half):
        at = self.at
        if at.sib > 1:
            src = self.part(at.c, at.seq_at(j), half)
            slot = j % at.n
            self._send(
                rdma(src, src, self.sib_s.at[slot, half], self.sib_r.at[slot, half],
                     at.dev(at.s, 1 - at.c))
            )

    def start(self):
        self._ring(0, 1, 0)
        self._ring(1, 1, 1)
        self._ring(0, 1, 1)
        self._ring(1, 1, 0)
        self._sib(0, 0)
        self._sib(0, 1)

    def _arrive(self, way, hop, half):
        at = self.at
        j = -hop if way == 0 else hop
        ref = self.part(at.c, at.seq_at(j), half)
        rdma(ref, ref, self.ring_s.at[way, hop - 1, half], self.ring_r.at[way, hop - 1, half],
             at.dev(at.s, at.c)).wait_recv()
        last = at.n // 2
        if hop + 1 < last or (hop + 1 == last and half == way):
            self._ring(way, hop + 1, half)
        if hop == last:
            j = last
        self._sib(j, half)

    def hop(self, hop):
        self._arrive(0, hop, 0)
        self._arrive(1, hop, 1)
        if hop < self.at.n // 2:
            self._arrive(0, hop, 1)
            self._arrive(1, hop, 0)

    def sib_wait(self, j):
        at = self.at
        if at.sib > 1:
            for half in range(2):
                ref = self.part(1 - at.c, at.seq_at(j), half)
                slot = j % at.n
                rdma(ref, ref, self.sib_s.at[slot, half], self.sib_r.at[slot, half],
                     at.dev(at.s, at.c)).wait_recv()

    def stages(self):
        last = self.at.n // 2
        yield 0, [0]
        for h in range(1, last):
            yield h, [-h, h]
        yield last, [last]

    def wait_stage(self, h, offsets):
        if h:
            self.hop(h)
        for j in offsets:
            self.sib_wait(j)

    def drain(self):
        for copy in self.sent:
            copy.wait_send()


class Scatter:
    def __init__(self, at, bufs, sems):
        self.at = at
        self.stage, self.sib_in, self.out, self.inn = bufs
        self.sib_s, self.sib_r, self.ring_s, self.ring_r = sems
        self.sent = []

    @staticmethod
    def scratch(n, shape):
        d = pltpu.SemaphoreType.DMA
        bufs = [
            pltpu.VMEM((2, *shape), BF), pltpu.VMEM((n, *shape), BF),
            pltpu.VMEM((2, n // 2, *shape), BF), pltpu.VMEM((2, n // 2, *shape), BF),
        ]
        return bufs, [d((n,)), d((n,)), d((2, n // 2)), d((2, n // 2))]

    def offsets(self):
        last = self.at.n // 2
        order = [last]
        for h in range(last - 1, 0, -1):
            order += [h, -h]
        return order + [0]

    def to_sibling(self, produce):
        at = self.at
        if at.sib == 1:
            return
        copies = []
        for k, j in enumerate(self.offsets()):
            if k >= 2:
                copies[k - 2].wait_send()
            produce(1 - at.c, at.seq_at(j), self.stage.at[k % 2])
            copy = rdma(self.stage.at[k % 2], self.sib_in.at[k], self.sib_s.at[k], self.sib_r.at[k],
                        at.dev(at.s, 1 - at.c))
            copy.start()
            copies.append(copy)
        self.sent += copies[-2:]

    def _send(self, way, k, rows):
        at = self.at
        src = self.out.at[way, k, rows]
        copy = rdma(src, self.inn.at[way, k, rows], self.ring_s.at[way, k], self.ring_r.at[way, k],
                    at.dev(at.seq_at(1 if way == 0 else -1), at.c))
        copy.start()
        self.sent.append(copy)

    def _wait(self, way, k, rows):
        ref = self.inn.at[way, k, rows]
        at = self.at
        rdma(ref, ref, self.ring_s.at[way, k], self.ring_r.at[way, k],
             at.dev(at.s, at.c)).wait_recv()

    def round(self, produce, between, finish):
        at = self.at
        last = at.n // 2
        length = self.stage.shape[1]
        half = length // 2
        halves = (pl.ds(0, half), pl.ds(half, half))
        whole = pl.ds(0, length)
        for k, j in enumerate(self.offsets()):
            if at.sib > 1:
                ref = self.sib_in.at[k]
                rdma(ref, ref, self.sib_s.at[k], self.sib_r.at[k], at.dev(at.s, at.c)).wait_recv()
            h = abs(j)
            if h == last:
                got = []
            else:
                ways = (0, 1) if h == 0 else ((0,) if j > 0 else (1,))
                rows_in = [halves[w] if h + 1 == last else whole for w in ways]
                got = [(w, rw) for w, rw in zip(ways, rows_in)]
            pending = [True]

            def store(cols, value, k=k, h=h, j=j, got=got, pending=pending):
                if pending[0]:
                    for w, rw in got:
                        self._wait(w, h, rw)
                    pending[0] = False
                if at.sib > 1:
                    value = value + self.sib_in[k, :, cols].astype(F32)
                for w, rw in got:
                    if h + 1 == last:
                        add = self.inn[w, h, pl.ds(w * half, half), cols].astype(F32)
                        if w == 0:
                            value = jnp.concatenate([value[:half] + add, value[half:]], axis=0)
                        else:
                            value = jnp.concatenate([value[:half], value[half:] + add], axis=0)
                    else:
                        value = value + self.inn[w, h, :, cols].astype(F32)
                if h == last:
                    low = value.astype(BF)
                    self.out[0, h - 1, pl.ds(0, half), cols] = low[:half]
                    self.out[1, h - 1, pl.ds(half, half), cols] = low[half:]
                elif h:
                    self.out[0 if j > 0 else 1, h - 1, :, cols] = value.astype(BF)
                else:
                    finish(cols, value)

            produce(at.c, at.seq_at(j), store)
            if h == last:
                self._send(0, h - 1, halves[0])
                self._send(1, h - 1, halves[1])
            elif h:
                self._send(0 if j > 0 else 1, h - 1, whole)
            between(k)

    def drain(self):
        for copy in self.sent:
            copy.wait_send()


def nt(a, b):
    return lax.dot_general(a, b, (((1,), (1,)), ((), ())), preferred_element_type=F32)


def tn(a, b):
    return lax.dot_general(a, b, (((0,), (0,)), ((), ())), preferred_element_type=F32)


def nn(a, b):
    return lax.dot_general(a, b, (((1,), (0,)), ((), ())), preferred_element_type=F32)


def rope(value, cos, front, back):
    return value * cos + pltpu.roll(value, 80, 1) * front + pltpu.roll(value, 48, 1) * back


def forward_kernel(
    dims,
    x, cot, cos, front, back, widen, widen_att, wq_s, gu_s, dn_s, wo_s,
    o_n1, o_qkv, o_lse, o_gh, o_att, o_hidden, o_ghid, o_act, o_dn, o_wq, o_sgu, o_sdn,
    nbuf, cbuf, qkv, wq, wqp, wo, gu, dn, act, ggu, att_out, att_in, ga_out, gh_in, stg, sgu_t,
    sc_stage, sc_in, sc_out, sc_inn,
    z_ws, z_wr, z_os, z_or, z_gs, z_gr, z_ds, z_dr, z_ss, z_sr, local,
    n1_a, n1_b, n1_c, n1_d, ct_a, ct_b, ct_c, ct_d, n2_a, n2_b, n2_c, n2_d, wo_a, wo_b, wo_c, wo_d,
    rs_a, rs_b, rs_c, rs_d, at_s, at_r, gh_s, gh_r,
):
    n, sib, planes = dims
    at = Place(n, sib, planes)
    length, width = x.shape
    seq_len = n * length
    rows = wq_s.shape[1]
    owners = planes * sib
    chunks = GROUP * HEAD_DIM // rows
    units = dn_s.shape[0]
    local_units = planes * units
    part_cols = wo_s.shape[1]
    heads_per = rows // HEAD_DIM
    half_len = length // 2
    tau = at.s * sib + at.c
    scale = HEAD_DIM ** (-0.5)
    log2e = 1.4426950408889634
    sent = []

    def token_part(ref):
        return lambda c, s, h: ref.at[c, s, pl.ds(h * half_len, half_len)]

    def z_pairs():
        for dp in range(planes):
            for dc in range(sib):
                yield dp, dc

    def z_source(dp, dc):
        return (
            lax.rem(at.p - dp + planes, planes) * sib + lax.rem(at.c - dc + sib, sib)
        )

    def z_send_all(src, dst, ssem, rsem, lsem, cols=False):
        mine = pl.ds(pl.multiple_of(at.f * rows, rows), rows)
        own = pltpu.make_async_copy(src.at[at.c], dst.at[mine], lsem)
        own.start()
        for dp, dc in z_pairs():
            if dp or dc:
                to = (at.s, at.col(dp, dc))
                copy = rdma(src.at[lax.rem(at.c + dc, sib)], dst.at[mine],
                            ssem.at[dp, dc], rsem.at[dp, dc], to)
                copy.start()
                sent.append(copy)
        return own

    def z_wait_all(dst, ssem, rsem, own):
        own.wait()
        for dp, dc in z_pairs():
            if dp or dc:
                ref = dst.at[pl.ds(pl.multiple_of(z_source(dp, dc) * rows, rows), rows)]
                rdma(ref, ref, ssem.at[dp, dc], rsem.at[dp, dc], (at.s, at.f)).wait_recv()

    def col_send_all(src, place, ssem, rsem, lsem):
        own = pltpu.make_async_copy(src, place(at.p), lsem)
        own.start()
        for dp in range(1, planes):
            copy = rdma(src, place(at.p), ssem.at[dp], rsem.at[dp], (at.s, at.col(dp, 0)))
            copy.start()
            sent.append(copy)
        return own

    def col_wait_all(place, ssem, rsem, own):
        own.wait()
        for dp in range(1, planes):
            ref = place(lax.rem(at.p - dp + planes, planes))
            rdma(ref, ref, ssem.at[dp], rsem.at[dp], (at.s, at.f)).wait_recv()

    at.barrier()
    wq_own = z_send_all(wq_s, wq, z_ws, z_wr, local.at[0])

    x_f = x[...].astype(F32)
    inv_one = lax.rsqrt(jnp.mean(x_f * x_f, axis=-1, keepdims=True) + NORM_EPS)
    nbuf[at.c, at.s] = (x_f * inv_one).astype(BF)
    cbuf[at.c, at.s] = cot[...]
    n_one = Gather(at, token_part(nbuf), (n1_a, n1_b, n1_c, n1_d))
    n_one.start()
    z_wait_all(wq, z_ws, z_wr, wq_own)
    wo_mine = lambda p: wo.at[at.c, at.s, p]
    wo_own = col_send_all(wo_s, wo_mine, z_os, z_or, local.at[1])

    @pl.loop(0, width // 256)
    def _(t):
        here = pl.ds(pl.multiple_of(t * 256, 256), 256)
        wqp[here] = nn(wq[here], widen[...]).astype(BF)

    save_wq = pltpu.make_async_copy(wqp, o_wq, local.at[2])
    save_wq.start()

    def project(c, s):
        y = nn(nbuf[c, s], wqp[...]).astype(BF)
        here = pl.ds(pl.multiple_of(s * length, length), length)
        cs, fr, bk = cos[here], front[here], back[here]
        for k in range(3):
            lanes = slice(128 * k, 128 * k + 128)
            qkv[c, here, lanes] = rope(y[:, lanes].astype(F32), cs, fr, bk).astype(BF)
        qkv[c, here, 384:512] = y[:, 384:512]

    for h, offsets in n_one.stages():
        n_one.wait_stage(h, offsets)
        for j in offsets:
            s_j = at.seq_at(j)

            @pl.loop(0, sib)
            def _(c):
                project(c, s_j)

    save_n1 = pltpu.make_async_copy(nbuf, o_n1, local.at[3])
    save_n1.start()
    save_qkv = pltpu.make_async_copy(qkv, o_qkv, local.at[4])
    save_qkv.start()

    tri = lax.broadcasted_iota(jnp.int32, (length, length), 0) >= lax.broadcasted_iota(
        jnp.int32, (length, length), 1
    )

    def attend(i):
        @pl.loop(0, sib)
        def _(b):
            past = i * length
            here = slice(past, past + length)
            outs = []
            for h in range(GROUP):
                q = qkv[b, here, 128 * h : 128 * h + 128]
                d = jnp.where(tri, nt(q, qkv[b, here, 256:384]) * (scale * log2e), -1e30)
                m = jnp.max(d, axis=1, keepdims=True)
                if i:
                    e = nt(q, qkv[b, 0:past, 256:384]) * (scale * log2e)
                    m = jnp.maximum(m, jnp.max(e, axis=1, keepdims=True))
                d = jnp.exp2(d - m)
                total = jnp.sum(d, axis=1, keepdims=True)
                o = nn(d.astype(BF), qkv[b, here, 384:512])
                if i:
                    e = jnp.exp2(e - m)
                    total = total + jnp.sum(e, axis=1, keepdims=True)
                    o = o + nn(e.astype(BF), qkv[b, 0:past, 384:512])
                outs.append((o / total).astype(BF))
                lse = jnp.broadcast_to(m + jnp.log2(total), (length, 128))
                o_lse[b, h, i] = lse.T[0:8]
            for k in range(chunks):
                pair = jnp.concatenate(outs[k * heads_per : (k + 1) * heads_per], axis=1)
                att_out[k, b, i] = nt(pair, widen_att[...]).astype(BF)

    def send_attended(i):
        for k in range(chunks):
            for b in range(sib):
                mine = jnp.logical_and(at.s == i, at.c == b)

                @pl.when(mine)
                def _():
                    att_in[tau * chunks + k] = att_out[k, b, i]

                @pl.when(jnp.logical_not(mine))
                def _():
                    rdma(att_out.at[k, b, i], att_in.at[tau * chunks + k], at_s.at[k, b, i],
                         at_r.at[tau * chunks + k], at.dev(i, b)).start()

    wo_gather = Gather(
        at, lambda c, s, h: wo.at[c, s, pl.ds(h * (planes // 2), planes // 2)],
        (wo_a, wo_b, wo_c, wo_d),
    )
    cot_gather = Gather(at, token_part(cbuf), (ct_a, ct_b, ct_c, ct_d))
    attend(n - 1)
    save_n1.wait()
    n_one.drain()
    send_attended(n - 1)
    col_wait_all(wo_mine, z_os, z_or, wo_own)
    wo_gather.start()
    gu_own = z_send_all(gu_s, gu, z_gs, z_gr, local.at[5])
    dn_place = lambda p: dn.at[pl.ds(pl.multiple_of(p * units, units), units)]
    dn_own = col_send_all(dn_s, dn_place, z_ds, z_dr, local.at[6])
    for i in range(n - 2, 0, -1):
        attend(i)
        send_attended(i)
    wo_hops = list(wo_gather.stages())
    for h, offsets in wo_hops[:-1]:
        wo_gather.wait_stage(h, offsets)
    attend(0)
    send_attended(0)
    cot_gather.start()
    wo_gather.wait_stage(*wo_hops[-1])
    wo_gather.drain()
    save_qkv.wait()
    save_wq.wait()

    group = n * sib
    for j in range(1, group):
        t = lax.rem(tau + j, group)
        for k in range(chunks):
            ref = att_in.at[t * chunks + k]
            rdma(ref, ref, at_s.at[0, 0, 0], at_r.at[t * chunks + k], at.dev(at.s, at.c)).wait_recv()
    for k in range(chunks):
        for i in range(n):
            for b in range(sib):
                @pl.when(jnp.logical_not(jnp.logical_and(at.s == i, at.c == b)))
                def _():
                    rdma(att_out.at[k, b, i], att_out.at[k, b, i], at_s.at[k, b, i],
                         at_r.at[0], at.dev(at.s, at.c)).wait_send()
    save_att = pltpu.make_async_copy(att_in, o_att, local.at[3])
    save_att.start()

    x_f = x[...].astype(F32)
    for s in range(n):
        cols = slice(s * part_cols, (s + 1) * part_cols)
        acc = x_f[:, cols]
        for p in range(planes):
            for c in range(sib):
                acc = acc + nn(att_in[p * sib + c], wo[c, s, p])
        o_hidden[:, cols] = acc
    hidden = o_hidden[...]
    inv_mid = lax.rsqrt(jnp.mean(hidden * hidden, axis=-1, keepdims=True) + NORM_EPS)
    nbuf[at.c, at.s] = (hidden * inv_mid).astype(BF)
    n_two = Gather(at, token_part(nbuf), (n2_a, n2_b, n2_c, n2_d))
    n_two.start()

    z_wait_all(gu, z_gs, z_gr, gu_own)
    col_wait_all(dn_place, z_ds, z_dr, dn_own)
    save_dn = pltpu.make_async_copy(dn, o_dn, local.at[4])
    save_dn.start()

    def feed_forward(c, s):
        n_here = nbuf[c, s]
        gate = nn(n_here, gu[:, :local_units])
        up = nn(n_here, gu[:, local_units:])
        sig = 1.0 / (1.0 + jnp.exp(-gate))
        silu = gate * sig
        act[c, s] = (silu * up).astype(BF)
        grad_act = nt(cbuf[c, s], dn[...])
        ggu[c, s, :, :local_units] = (grad_act * up * sig * (1.0 + gate * (1.0 - sig))).astype(BF)
        ggu[c, s, :, local_units:] = (grad_act * silu).astype(BF)

    for h, offsets in n_two.stages():
        cot_gather.wait_stage(h, offsets)
        n_two.wait_stage(h, offsets)
        for j in offsets:
            s_j = at.seq_at(j)

            @pl.loop(0, sib)
            def _(c):
                feed_forward(c, s_j)

    save_act = pltpu.make_async_copy(act, o_act, local.at[5])
    save_act.start()

    scatter = Scatter(at, (sc_stage, sc_in, sc_out, sc_inn), (rs_a, rs_b, rs_c, rs_d))
    tile = 512

    def to_stage(c, s, ref):
        for t in range(width // tile):
            cols = slice(t * tile, (t + 1) * tile)
            ref[:, cols] = nt(ggu[c, s], gu[cols, :]).astype(BF)

    def to_ring(c, s, store):
        for t in range(width // tile):
            cols = slice(t * tile, (t + 1) * tile)
            store(cols, nt(ggu[c, s], gu[cols, :]))

    tokens = sib * seq_len
    down_copies = []

    def grad_down():
        cot_all = cbuf[...].reshape(tokens, width)
        down_rows = local_units // 2
        for t in range(2):
            rows_here = slice(t * down_rows, (t + 1) * down_rows)
            lhs = act[:, :, :, rows_here].reshape(tokens, down_rows)
            stg[rows_here] = tn(lhs, cot_all).astype(BF)
        own = pltpu.make_async_copy(
            stg.at[pl.ds(pl.multiple_of(at.p * units, units), units)], o_sdn.at[at.p], local.at[6]
        )
        own.start()
        down_copies.append(own)
        for dp in range(1, planes):
            to = lax.rem(at.p + dp, planes)
            copy = rdma(stg.at[pl.ds(pl.multiple_of(to * units, units), units)], o_sdn.at[at.p],
                        z_ss.at[dp], z_sr.at[dp], (at.s, at.col(dp, 0)))
            copy.start()
            sent.append(copy)

    gu_tile = sgu_t.shape[1]
    gu_steps = width // gu_tile

    def gu_copy(m, slot):
        return pltpu.make_async_copy(
            sgu_t.at[slot], o_sgu.at[pl.ds(m * gu_tile, gu_tile)], local.at[7 + slot]
        )

    def grad_gu(lo, hi):
        for m in range(lo, hi):
            slot = m % 2
            if m >= 2:
                gu_copy(m - 2, slot).wait()
            lhs = nbuf[:, :, :, m * gu_tile : (m + 1) * gu_tile].reshape(tokens, gu_tile)
            sgu_t[slot] = tn(lhs, ggu[...].reshape(tokens, 2 * local_units)).astype(BF)
            gu_copy(m, slot).start()

    def finish(cols, value):
        o_ghid[:, cols] = value

    n_sends = len(scatter.offsets())

    def between(k):
        if k == 0:
            grad_down()
            grad_gu(0, gu_steps // 3)
        if k == n_sends - 2:
            grad_gu(gu_steps // 3, gu_steps)

    scatter.to_sibling(to_stage)
    scatter.round(to_ring, between, finish)
    e_mid = o_ghid[...]
    hidden = o_hidden[...]
    inv_mid = lax.rsqrt(jnp.mean(hidden * hidden, axis=-1, keepdims=True) + NORM_EPS)
    norm_mid = hidden * inv_mid
    o_ghid[...] = cot[...].astype(F32) + inv_mid * (
        e_mid - norm_mid * jnp.mean(e_mid * norm_mid, axis=-1, keepdims=True)
    )
    branch = o_ghid[...].astype(BF)
    for f in range(owners):
        p, c = f // sib, f % sib
        acc = nt(branch[:, :part_cols], wo[c, 0, p])
        for s in range(1, n):
            acc = acc + nt(branch[:, s * part_cols : (s + 1) * part_cols], wo[c, s, p])
        ga_out[f] = acc.astype(BF)
        t, k = f // chunks, f % chunks
        mine = tau == t

        @pl.when(mine)
        def _():
            gh_in[k, at.c, at.s] = ga_out[f]

        @pl.when(jnp.logical_not(mine))
        def _():
            rdma(ga_out.at[f], gh_in.at[k, at.c, at.s], gh_s.at[f], gh_r.at[k, tau],
                 at.dev(t // sib, t % sib)).start()

    for j in range(1, group):
        t = lax.rem(tau + j, group)
        for k in range(chunks):
            ref = gh_in.at[k, lax.rem(t, sib), lax.div(t, sib)]
            rdma(ref, ref, gh_s.at[0], gh_r.at[k, t], at.dev(at.s, at.c)).wait_recv()
    save_gh = pltpu.make_async_copy(gh_in, o_gh, local.at[0])
    save_gh.start()
    for f in range(owners):
        @pl.when(jnp.logical_not(tau == f // chunks))
        def _():
            rdma(ga_out.at[f], ga_out.at[f], gh_s.at[f], gh_r.at[0, 0],
                 at.dev(at.s, at.c)).wait_send()

    for dp in range(1, planes):
        ref = o_sdn.at[lax.rem(at.p - dp + planes, planes)]
        rdma(ref, ref, z_ss.at[dp], z_sr.at[dp], (at.s, at.f)).wait_recv()
    for copy in down_copies:
        copy.wait()
    for m in range(max(0, gu_steps - 2), gu_steps):
        gu_copy(m, m % 2).wait()
    cot_gather.drain()
    n_two.drain()
    scatter.drain()
    for copy in sent:
        copy.wait_send()
    save_att.wait()
    save_act.wait()
    save_dn.wait()
    save_gh.wait()


def forward_call(dims, x, cot, tables, widen, widen_att, wq_s, gu_s, dn_s, wo_s):
    n, sib, planes = dims
    length, width = x.shape
    rows, units, part_cols = wq_s.shape[1], dn_s.shape[0], wo_s.shape[1]
    owners = planes * sib
    chunks = GROUP * HEAD_DIM // rows
    ffl = planes * units
    seq_len = n * length
    vm, hb = pl.BlockSpec(memory_space=pltpu.VMEM), pl.BlockSpec(memory_space=pl.ANY)
    blocks = (sib, n, length, width)
    sds = jax.ShapeDtypeStruct
    outs = [
        (sds(blocks, BF), hb),
        (sds((sib, seq_len, 512), BF), hb),
        (sds((sib, GROUP, n, 8, length), F32), vm),
        (sds((chunks, sib, n, length, rows), BF), hb),
        (sds((owners, length, rows), BF), hb),
        (sds((length, width), F32), vm),
        (sds((length, width), F32), vm),
        (sds((sib, n, length, ffl), BF), hb),
        (sds((ffl, width), BF), hb),
        (sds((width, 512), BF), hb),
        (sds((width, 2 * ffl), BF), hb),
        (sds((planes, units, width), BF), hb),
    ]
    sc_bufs, sc_sems = Scatter.scratch(n, (length, width))
    dma = pltpu.SemaphoreType.DMA
    scratch = [
        pltpu.VMEM(blocks, BF), pltpu.VMEM(blocks, BF), pltpu.VMEM((sib, seq_len, 512), BF),
        pltpu.VMEM((width, wq_s.shape[2]), BF), pltpu.VMEM((width, 512), BF),
        pltpu.VMEM((sib, n, planes, rows, part_cols), BF),
        pltpu.VMEM((width, 2 * ffl), BF), pltpu.VMEM((ffl, width), BF),
        pltpu.VMEM((sib, n, length, ffl), BF), pltpu.VMEM((sib, n, length, 2 * ffl), BF),
        pltpu.VMEM((chunks, sib, n, length, rows), BF), pltpu.VMEM((owners, length, rows), BF),
        pltpu.VMEM((owners, length, rows), BF), pltpu.VMEM((chunks, sib, n, length, rows), BF),
        pltpu.VMEM((ffl, width), BF), pltpu.VMEM((2, 256, 2 * ffl), BF),
        *sc_bufs,
        dma((planes, sib)), dma((planes, sib)), dma((planes,)), dma((planes,)),
        dma((planes, sib)), dma((planes, sib)), dma((planes,)), dma((planes,)),
        dma((planes,)), dma((planes,)), dma((9,)),
        *Gather.scratch(n), *Gather.scratch(n), *Gather.scratch(n), *Gather.scratch(n),
        *sc_sems,
        dma((chunks, sib, n)), dma((owners,)), dma((owners,)), dma((chunks, n * sib)),
    ]
    return pl.pallas_call(
        functools.partial(forward_kernel, dims),
        out_shape=[o[0] for o in outs],
        out_specs=[o[1] for o in outs],
        in_specs=[vm] * 7 + [hb] * 4,
        scratch_shapes=scratch,
        compiler_params=pltpu.CompilerParams(
            collective_id=0, has_side_effects=True, vmem_limit_bytes=VMEM_LIMIT
        ),
    )(x, cot, *tables, widen, widen_att, wq_s, gu_s, dn_s, wo_s)


def attend_back_kernel(dims, qkv, gh, lse, cos, front, back, widen_att, out, gk, gv):
    n, sib = dims
    chunks, _, _, length, rows = gh.shape
    heads_per = rows // HEAD_DIM
    scale = HEAD_DIM ** (-0.5)
    log2e = 1.4426950408889634
    tri = lax.broadcasted_iota(jnp.int32, (length, length), 0) <= lax.broadcasted_iota(
        jnp.int32, (length, length), 1
    )

    @pl.loop(0, sib)
    def _(b):
        gk[...] = jnp.zeros_like(gk)
        gv[...] = jnp.zeros_like(gv)
        for i in range(n):
            past = i * length
            here = slice(past, past + length)
            for h in range(GROUP):
                k, slot = h // heads_per, h % heads_per
                q = qkv[b, here, 128 * h : 128 * h + 128]
                do = nn(
                    gh[k, b, i], widen_att[:, 128 * slot : 128 * slot + 128]
                ).astype(BF)
                row = lse[b, h, i, 0:1]
                parts = [(here, True)] + ([(slice(0, past), False)] if i else [])
                probs, grads = [], []
                delta = 0.0
                for part, diagonal in parts:
                    sc = nt(qkv[b, part, 256:384], q) * (scale * log2e)
                    if diagonal:
                        sc = jnp.where(tri, sc, -1e30)
                    pr = jnp.exp2(sc - row)
                    dp = nt(qkv[b, part, 384:512], do)
                    delta = delta + jnp.sum(pr * dp, axis=0, keepdims=True)
                    probs.append(pr)
                    grads.append(dp)
                dq = jnp.zeros((length, 128), F32)
                for (part, _), pr, dp in zip(parts, probs, grads):
                    ds = (pr * (dp - delta) * scale).astype(BF)
                    gv[part] += nn(pr.astype(BF), do)
                    gk[part] += nn(ds, q)
                    dq = dq + tn(ds, qkv[b, part, 256:384])
                out[b, here, 128 * h : 128 * h + 128] = rope(
                    dq, cos[here], -front[here], -back[here]
                ).astype(BF)
        for i in range(n):
            here = slice(i * length, (i + 1) * length)
            out[b, here, 256:384] = rope(gk[here], cos[here], -front[here], -back[here]).astype(BF)
            out[b, here, 384:512] = gv[here].astype(BF)


def attend_back_call(dims, qkv, gh, lse, tables, widen_att):
    n, sib = dims
    seq_len = qkv.shape[1]
    vm = pl.BlockSpec(memory_space=pltpu.VMEM)
    return pl.pallas_call(
        functools.partial(attend_back_kernel, dims),
        out_shape=jax.ShapeDtypeStruct(qkv.shape, BF),
        in_specs=[vm] * 7,
        out_specs=vm,
        scratch_shapes=[pltpu.VMEM((seq_len, 128), F32), pltpu.VMEM((seq_len, 128), F32)],
        compiler_params=pltpu.CompilerParams(vmem_limit_bytes=VMEM_LIMIT),
    )(qkv, gh, lse, *tables, widen_att)


def adamw(weight, first, second, grad, rate, decay):
    first_new = BETA_ONE * first + (1.0 - BETA_ONE) * grad
    second_new = BETA_TWO * second + (1.0 - BETA_TWO) * grad * grad
    first_hat = first_new / (1.0 - BETA_ONE**ADAM_STEP)
    second_hat = second_new / (1.0 - BETA_TWO**ADAM_STEP)
    weight_new = weight - rate * (first_hat / (jnp.sqrt(second_hat) + ADAM_EPS) + decay * weight)
    return (weight_new, first_new, second_new)


def dot(a, b, dims):
    return lax.dot_general(a, b, (dims, ((), ())), preferred_element_type=F32)


def rope_arrays(seq_len):
    half = HEAD_DIM // 2
    frequencies = ROPE_BASE ** (-(2.0 * jnp.arange(half, dtype=F32)) / HEAD_DIM)
    angles = jnp.arange(seq_len, dtype=F32)[:, None] * frequencies[None, :]
    cos, sin = jnp.cos(angles), jnp.sin(angles)
    pad = jnp.zeros((seq_len, 128 - HEAD_DIM), F32)
    none = jnp.zeros_like(sin)
    return (
        jnp.concatenate([cos, cos, pad], axis=1),
        jnp.concatenate([-sin, none, pad], axis=1),
        jnp.concatenate([none, sin, pad], axis=1),
    )


def widening(heads):
    row = jnp.arange(heads * HEAD_DIM)[:, None]
    col = jnp.arange(heads * 128)[None, :]
    return (col == row // HEAD_DIM * 128 + row % HEAD_DIM).astype(BF)


def make(n_seq, n_fsdp):
    sib = KV_HEADS // n_seq
    planes = n_fsdp // sib
    sib_groups = [[p * sib + c for c in range(sib)] for p in range(planes)]
    col_groups = [[p * sib + c for p in range(planes)] for c in range(sib)]

    def plane_scatter(x):
        x = lax.psum_scatter(
            x, "fsdp", scatter_dimension=0, tiled=True, axis_index_groups=sib_groups
        )
        return lax.psum_scatter(x, "seq", scatter_dimension=1, tiled=True)

    def on_device(
        inputs, cotangent, qkv_weight, out_weight, gate_up_weight, down_weight, norm_gains,
        qkv_first, qkv_second, out_first, out_second, gate_up_first, gate_up_second,
        down_first, down_second, gain_first, gain_second,
    ):
        s_idx = lax.axis_index("seq")
        _, length, width = inputs.shape
        seq_len = length * n_seq
        tokens = sib * seq_len
        rows = qkv_weight.shape[0]
        head_cols = (GROUP + 2) * HEAD_DIM
        ff_rows = down_weight.shape[0]
        units = ff_rows // n_seq
        hidden_units = ff_rows * n_fsdp
        local_units = hidden_units // KV_HEADS
        gains = norm_gains.astype(BF).astype(F32)

        wq_s = lax.dynamic_slice_in_dim(qkv_weight, s_idx * sib * head_cols, sib * head_cols, 1)
        wq_s = (wq_s * gains[0][:, None]).astype(BF).reshape(rows, sib, head_cols).transpose(1, 0, 2)
        gu_s = gate_up_weight.reshape(rows, 2, planes, sib, n_seq, units)
        gu_s = lax.dynamic_index_in_dim(gu_s, s_idx, 4, keepdims=False)
        gu_s = (gu_s * gains[1][:, None, None, None, None]).astype(BF)
        gu_s = gu_s.transpose(3, 0, 1, 2, 4).reshape(sib, rows, 2 * local_units)
        dn_s = lax.dynamic_slice_in_dim(down_weight, s_idx * units, units, 0).astype(BF)
        part_cols = width // n_seq
        wo_s = lax.dynamic_slice_in_dim(out_weight, s_idx * part_cols, part_cols, 1).astype(BF)
        tables = rope_arrays(seq_len)
        widen = widening(GROUP + 2)
        widen_att = widening(rows // HEAD_DIM)

        (n_one, qkv, lse, gh, att, hidden, grad_hidden, act, w_down, w_qkv, s_gu, s_down) = forward_call(
            (n_seq, sib, planes), inputs[0], cotangent[0], tables, widen, widen_att,
            wq_s, gu_s, dn_s, wo_s,
        )
        x_own = inputs.astype(F32)
        inv_one = lax.rsqrt(jnp.mean(x_own * x_own, axis=-1, keepdims=True) + NORM_EPS)
        norm_one = x_own * inv_one
        n_one_flat = n_one.reshape(tokens, width)
        act = act.reshape(tokens, local_units)
        down_part = dot(act, w_down, ((1,), (0,))).astype(BF)
        down_sum = plane_scatter(down_part.reshape(sib, seq_len, width))
        block_out = (hidden + down_sum[0].astype(F32)).astype(BF)[None]
        att = att.transpose(1, 0, 2).reshape(length, width)
        s_out = dot(att, grad_hidden.astype(BF), ((0,), (0,))).astype(BF)
        grad_qkv = attend_back_call((n_seq, sib), qkv, gh, lse, tables, widen_att)
        grad_qkv = grad_qkv.reshape(tokens, (GROUP + 2) * 128)
        s_qkv = dot(n_one_flat, grad_qkv, ((0,), (0,))).astype(BF)
        s_qkv = s_qkv.reshape(width, GROUP + 2, 128)[:, :, :HEAD_DIM].reshape(width, head_cols)
        e_in = dot(grad_qkv, w_qkv, ((1,), (1,))).astype(BF)
        e_in = plane_scatter(e_in.reshape(sib, seq_len, width)).astype(F32)
        input_grad = grad_hidden[None] + inv_one * (
            e_in - norm_one * jnp.mean(e_in * norm_one, axis=-1, keepdims=True)
        )

        def column_sum(part):
            cols = part.shape[-1]
            part = part.reshape(planes, 1, sib, rows, cols)
            part = lax.all_to_all(
                part, "fsdp", split_axis=2, concat_axis=1, tiled=True, axis_index_groups=sib_groups
            ).reshape(planes, sib, rows, cols)
            part = lax.psum_scatter(
                part, "fsdp", scatter_dimension=0, tiled=True, axis_index_groups=col_groups
            )
            return part.reshape(sib, rows, cols)

        g_qkv = column_sum(s_qkv).transpose(1, 0, 2).reshape(rows, sib * head_cols)
        g_qkv = lax.all_gather(g_qkv, "seq", axis=1, tiled=True).astype(F32)
        g_gu = column_sum(s_gu)
        g_gu = lax.all_gather(g_gu, "seq", axis=0, tiled=False)
        g_gu = g_gu.reshape(n_seq, sib, rows, 2, planes, units).transpose(2, 3, 4, 1, 0, 5)
        g_gu = g_gu.reshape(rows, 2 * hidden_units).astype(F32)
        g_down = jnp.sum(s_down.astype(F32), axis=0).astype(BF)
        g_down = lax.all_gather(g_down, "seq", axis=0, tiled=True).astype(F32)
        g_out = lax.psum_scatter(s_out, "seq", scatter_dimension=1, tiled=True)
        g_out = lax.psum_scatter(g_out, "fsdp", scatter_dimension=0, tiled=True)
        g_out = lax.all_gather(g_out, "seq", axis=1, tiled=True).astype(F32)
        gain_grad = jnp.stack(
            [
                jnp.sum(g_qkv * qkv_weight.astype(BF).astype(F32), axis=1),
                jnp.sum(g_gu * gate_up_weight.astype(BF).astype(F32), axis=1),
            ]
        )
        g_qkv = g_qkv * gains[0][:, None]
        g_gu = g_gu * gains[1][:, None]
        qkv_new = adamw(qkv_weight, qkv_first, qkv_second, g_qkv, RATE_QKV, WEIGHT_DECAY)
        out_new = adamw(out_weight, out_first, out_second, g_out, RATE_OUT, WEIGHT_DECAY)
        gu_new = adamw(
            gate_up_weight, gate_up_first, gate_up_second, g_gu, RATE_GATE_UP, WEIGHT_DECAY
        )
        down_new = adamw(down_weight, down_first, down_second, g_down, RATE_DOWN, WEIGHT_DECAY)
        gains_new = adamw(norm_gains, gain_first, gain_second, gain_grad, RATE_GAINS, 0.0)
        return (block_out, input_grad, *qkv_new, *out_new, *gu_new, *down_new, *gains_new)

    return on_device


def solution(mesh):
    tokens = P("fsdp", "seq", None)
    weight = P("fsdp", None)
    gain = P(None, "fsdp")
    in_specs = (tokens, tokens, weight, weight, weight, weight, gain) + (weight,) * 8 + (gain,) * 2
    out_specs = (tokens, tokens) + (weight,) * 12 + (gain,) * 3
    return jax.shard_map(
        make(mesh.shape["seq"], mesh.shape["fsdp"]),
        mesh=mesh, in_specs=in_specs, out_specs=out_specs, check_vma=False,
    )
```

```python
import functools

import jax
import jax.numpy as jnp
from jax import lax
from jax.experimental import pallas as pl
from jax.experimental.pallas import tpu as pltpu
from jax.sharding import PartitionSpec as P

HEAD_DIM = 96
KV_HEADS = 8
ADAM_STEP = 10
GROUP = 2

NORM_EPS = 1e-05
ROPE_BASE = 100000.0
BETA_ONE = 0.9
BETA_TWO = 0.95
ADAM_EPS = 1e-08
WEIGHT_DECAY = 0.1
RATE_QKV = 0.07
RATE_OUT = 0.8
RATE_GATE_UP = 0.07
RATE_DOWN = 0.045
RATE_GAINS = 0.6
BF = jnp.bfloat16
F32 = jnp.float32
VMEM_LIMIT = 62 * 1024 * 1024


MESH = pl.DeviceIdType.MESH


def rdma(src, dst, ssem, rsem, dev):
    return pltpu.make_async_remote_copy(
        src_ref=src, dst_ref=dst, send_sem=ssem, recv_sem=rsem, device_id=dev, device_id_type=MESH
    )


class Place:
    def __init__(self, n, sib, planes):
        self.n, self.sib, self.planes = n, sib, planes
        self.s = lax.axis_index("seq")
        self.f = lax.axis_index("fsdp")
        self.c = lax.rem(self.f, sib)
        self.p = lax.div(self.f, sib)
        a, b = lax.div(self.s, 2), lax.rem(self.s, 2)
        self.r = a * (1 - b) + (n - 1 - a) * b

    def seq_at(self, j):
        if j == 0:
            return self.s
        n = self.n
        q = lax.rem(self.r + (j + n), n)
        t = lax.div(q, n // 2)
        return (1 - t) * 2 * q + t * (2 * (n - 1 - q) + 1)

    def dev(self, s, c):
        return (s, self.p * self.sib + c)

    def col(self, dp, dc):
        return lax.rem(self.p + dp, self.planes) * self.sib + lax.rem(self.c + dc, self.sib)

    def barrier(self):
        sem = pltpu.get_barrier_semaphore()
        group = self.n * self.sib
        tau = self.s * self.sib + self.c
        for j in range(1, group):
            t = lax.rem(tau + j, group)
            pl.semaphore_signal(
                sem, inc=1, device_id=self.dev(lax.div(t, self.sib), lax.rem(t, self.sib)),
                device_id_type=MESH,
            )
        for dp in range(1, self.planes):
            for dc in range(self.sib):
                pl.semaphore_signal(
                    sem, inc=1, device_id=(self.s, self.col(dp, dc)), device_id_type=MESH
                )
        pl.semaphore_wait(sem, group - 1 + (self.planes - 1) * self.sib)


class Gather:
    def __init__(self, at, part, sems):
        self.at, self.part = at, part
        self.ring_s, self.ring_r = sems[:2]
        self.share = at.sib > 1 and len(sems) > 2
        if self.share:
            self.sib_s, self.sib_r = sems[2:]
        self.sent = []

    @staticmethod
    def scratch(n, share=True):
        d = pltpu.SemaphoreType.DMA
        ring = [d((2, n // 2, 2)), d((2, n // 2, 2))]
        return ring + [d((n, 2)), d((n, 2))] if share else ring

    def _send(self, copy):
        copy.start()
        self.sent.append(copy)

    def _ring(self, way, hop, half):
        at = self.at
        src = self.part(at.c, at.seq_at(-(hop - 1) if way == 0 else hop - 1), half)
        to = at.dev(at.seq_at(1 if way == 0 else -1), at.c)
        self._send(
            rdma(src, src, self.ring_s.at[way, hop - 1, half], self.ring_r.at[way, hop - 1, half], to)
        )

    def _sib(self, j, half):
        at = self.at
        if self.share:
            src = self.part(at.c, at.seq_at(j), half)
            slot = j % at.n
            self._send(
                rdma(src, src, self.sib_s.at[slot, half], self.sib_r.at[slot, half],
                     at.dev(at.s, 1 - at.c))
            )

    def start(self):
        self._ring(0, 1, 0)
        self._ring(1, 1, 1)
        self._ring(0, 1, 1)
        self._ring(1, 1, 0)
        self._sib(0, 0)
        self._sib(0, 1)

    def _arrive(self, way, hop, half):
        at = self.at
        j = -hop if way == 0 else hop
        ref = self.part(at.c, at.seq_at(j), half)
        rdma(ref, ref, self.ring_s.at[way, hop - 1, half], self.ring_r.at[way, hop - 1, half],
             at.dev(at.s, at.c)).wait_recv()
        last = at.n // 2
        if hop + 1 < last or (hop + 1 == last and half == way):
            self._ring(way, hop + 1, half)
        if hop == last:
            j = last
        self._sib(j, half)

    def hop(self, hop):
        self._arrive(0, hop, 0)
        self._arrive(1, hop, 1)
        if hop < self.at.n // 2:
            self._arrive(0, hop, 1)
            self._arrive(1, hop, 0)

    def sib_wait(self, j):
        at = self.at
        if self.share:
            for half in range(2):
                ref = self.part(1 - at.c, at.seq_at(j), half)
                slot = j % at.n
                rdma(ref, ref, self.sib_s.at[slot, half], self.sib_r.at[slot, half],
                     at.dev(at.s, at.c)).wait_recv()

    def stages(self):
        last = self.at.n // 2
        yield 0, [0]
        for h in range(1, last):
            yield h, [-h, h]
        yield last, [last]

    def wait_stage(self, h, offsets):
        if h:
            self.hop(h)
        for j in offsets:
            self.sib_wait(j)

    def drain(self):
        for copy in self.sent:
            copy.wait_send()


class Scatter:
    def __init__(self, at, bufs, sems, rows, cols):
        self.at, self.rows, self.cols = at, rows, pl.ds(0, cols)
        self.stage, self.sib_in, self.out, self.inn = bufs
        self.sib_s, self.sib_r, self.ring_s, self.ring_r = sems
        self.sent = []

    @staticmethod
    def scratch(n, shape):
        return [
            pltpu.VMEM((2, *shape), BF), pltpu.VMEM((n, *shape), BF),
            pltpu.VMEM((2, n // 2, *shape), BF), pltpu.VMEM((2, n // 2, *shape), BF),
        ]

    @staticmethod
    def sems(n):
        d = pltpu.SemaphoreType.DMA
        return [d((n,)), d((n,)), d((2, n // 2)), d((2, n // 2))]

    def offsets(self):
        last = self.at.n // 2
        order = [last]
        for h in range(last - 1, 0, -1):
            order += [h, -h]
        return order + [0]

    def to_sibling(self, produce):
        at = self.at
        if at.sib == 1:
            return
        copies = []
        for k, j in enumerate(self.offsets()):
            if k >= 2:
                copies[k - 2].wait_send()
            view = self.stage.at[k % 2, pl.ds(0, self.rows), self.cols]
            produce(1 - at.c, at.seq_at(j), view)
            copy = rdma(view, self.sib_in.at[k, pl.ds(0, self.rows), self.cols],
                        self.sib_s.at[k], self.sib_r.at[k], at.dev(at.s, 1 - at.c))
            copy.start()
            copies.append(copy)
        self.sent += copies[-2:]

    def _send(self, way, k, rows):
        at = self.at
        src = self.out.at[way, k, rows, self.cols]
        copy = rdma(src, self.inn.at[way, k, rows, self.cols], self.ring_s.at[way, k], self.ring_r.at[way, k],
                    at.dev(at.seq_at(1 if way == 0 else -1), at.c))
        copy.start()
        self.sent.append(copy)

    def _wait(self, way, k, rows):
        ref = self.inn.at[way, k, rows, self.cols]
        at = self.at
        rdma(ref, ref, self.ring_s.at[way, k], self.ring_r.at[way, k],
             at.dev(at.s, at.c)).wait_recv()

    def round(self, produce, between, finish):
        at = self.at
        last = at.n // 2
        length = self.rows
        half = length // 2
        halves = (pl.ds(0, half), pl.ds(half, half))
        whole = pl.ds(0, length)
        for k, j in enumerate(self.offsets()):
            if at.sib > 1:
                ref = self.sib_in.at[k, pl.ds(0, length), self.cols]
                rdma(ref, ref, self.sib_s.at[k], self.sib_r.at[k], at.dev(at.s, at.c)).wait_recv()
            h = abs(j)
            if h == last:
                got = []
            else:
                ways = (0, 1) if h == 0 else ((0,) if j > 0 else (1,))
                rows_in = [halves[w] if h + 1 == last else whole for w in ways]
                got = [(w, rw) for w, rw in zip(ways, rows_in)]
            pending = [True]

            def store(cols, value, k=k, h=h, j=j, got=got, pending=pending):
                if pending[0]:
                    for w, rw in got:
                        self._wait(w, h, rw)
                    pending[0] = False
                if at.sib > 1:
                    value = value + self.sib_in[k, pl.ds(0, length), cols].astype(F32)
                for w, rw in got:
                    if h + 1 == last:
                        add = self.inn[w, h, pl.ds(w * half, half), cols].astype(F32)
                        if w == 0:
                            value = jnp.concatenate([value[:half] + add, value[half:]], axis=0)
                        else:
                            value = jnp.concatenate([value[:half], value[half:] + add], axis=0)
                    else:
                        value = value + self.inn[w, h, pl.ds(0, length), cols].astype(F32)
                if h == last:
                    low = value.astype(BF)
                    self.out[0, h - 1, pl.ds(0, half), cols] = low[:half]
                    self.out[1, h - 1, pl.ds(half, half), cols] = low[half:]
                elif h:
                    self.out[0 if j > 0 else 1, h - 1, pl.ds(0, length), cols] = value.astype(BF)
                else:
                    finish(cols, value)

            produce(at.c, at.seq_at(j), store)
            if h == last:
                self._send(0, h - 1, halves[0])
                self._send(1, h - 1, halves[1])
            elif h:
                self._send(0 if j > 0 else 1, h - 1, whole)
            between(k)

    def drain(self):
        for copy in self.sent:
            copy.wait_send()


def nt(a, b):
    return lax.dot_general(a, b, (((1,), (1,)), ((), ())), preferred_element_type=F32)


def tn(a, b):
    return lax.dot_general(a, b, (((0,), (0,)), ((), ())), preferred_element_type=F32)


def nn(a, b):
    return lax.dot_general(a, b, (((1,), (0,)), ((), ())), preferred_element_type=F32)


def rope(value, cos, front, back):
    return value * cos + pltpu.roll(value, 80, 1) * front + pltpu.roll(value, 48, 1) * back


def forward_kernel(
    dims,
    x, cot, cos, front, back, widen, widen_att, wq_s, gu_s, dn_s, wo_s,
    o_n1, o_qkv, o_lse, o_gh, o_att, o_hidden, o_ghid, o_act, o_dn, o_wq, o_sgu, o_sdn,
    nbuf, cbuf, qkv, wq, wqp, wo, gu, dn, act, ggu, att_out, att_in, ga_out, gh_in, stg, sgu_t,
    sc_stage, sc_in, sc_out, sc_inn,
    z_ws, z_wr, z_os, z_or, z_gs, z_gr, z_ds, z_dr, z_ss, z_sr, local,
    n1_a, n1_b, n1_c, n1_d, ct_a, ct_b, ct_c, ct_d, n2_a, n2_b, n2_c, n2_d, wo_a, wo_b, wo_c, wo_d,
    rs_a, rs_b, rs_c, rs_d, at_s, at_r, gh_s, gh_r,
):
    n, sib, planes = dims
    at = Place(n, sib, planes)
    length, width = x.shape
    seq_len = n * length
    rows = wq_s.shape[1]
    owners = planes * sib
    chunks = GROUP * HEAD_DIM // rows
    units = dn_s.shape[0]
    local_units = planes * units
    part_cols = wo_s.shape[1]
    heads_per = rows // HEAD_DIM
    half_len = length // 2
    tau = at.s * sib + at.c
    scale = HEAD_DIM ** (-0.5)
    log2e = 1.4426950408889634
    sent = []

    def token_part(ref):
        return lambda c, s, h: ref.at[c, s, pl.ds(h * half_len, half_len)]

    def z_pairs():
        for dp in range(planes):
            for dc in range(sib):
                yield dp, dc

    def z_source(dp, dc):
        return (
            lax.rem(at.p - dp + planes, planes) * sib + lax.rem(at.c - dc + sib, sib)
        )

    def z_send_all(src, dst, ssem, rsem, lsem, cols=False):
        mine = pl.ds(pl.multiple_of(at.f * rows, rows), rows)
        own = pltpu.make_async_copy(src.at[at.c], dst.at[mine], lsem)
        own.start()
        for dp, dc in z_pairs():
            if dp or dc:
                to = (at.s, at.col(dp, dc))
                copy = rdma(src.at[lax.rem(at.c + dc, sib)], dst.at[mine],
                            ssem.at[dp, dc], rsem.at[dp, dc], to)
                copy.start()
                sent.append(copy)
        return own

    def z_wait_all(dst, ssem, rsem, own):
        own.wait()
        for dp, dc in z_pairs():
            if dp or dc:
                ref = dst.at[pl.ds(pl.multiple_of(z_source(dp, dc) * rows, rows), rows)]
                rdma(ref, ref, ssem.at[dp, dc], rsem.at[dp, dc], (at.s, at.f)).wait_recv()

    def col_send_all(src, place, ssem, rsem, lsem):
        own = pltpu.make_async_copy(src, place(at.p), lsem)
        own.start()
        for dp in range(1, planes):
            copy = rdma(src, place(at.p), ssem.at[dp], rsem.at[dp], (at.s, at.col(dp, 0)))
            copy.start()
            sent.append(copy)
        return own

    def col_wait_all(place, ssem, rsem, own):
        own.wait()
        for dp in range(1, planes):
            ref = place(lax.rem(at.p - dp + planes, planes))
            rdma(ref, ref, ssem.at[dp], rsem.at[dp], (at.s, at.f)).wait_recv()

    at.barrier()
    wq_own = z_send_all(wq_s, wq, z_ws, z_wr, local.at[0])

    x_f = x[...].astype(F32)
    inv_one = lax.rsqrt(jnp.mean(x_f * x_f, axis=-1, keepdims=True) + NORM_EPS)
    nbuf[at.c, at.s] = (x_f * inv_one).astype(BF)
    cbuf[at.c, at.s] = cot[...]
    n_one = Gather(at, token_part(nbuf), (n1_a, n1_b, n1_c, n1_d))
    n_one.start()
    z_wait_all(wq, z_ws, z_wr, wq_own)
    wo_mine = lambda p: wo.at[at.c, at.s, p]
    wo_own = col_send_all(wo_s, wo_mine, z_os, z_or, local.at[1])

    @pl.loop(0, width // 256)
    def _(t):
        here = pl.ds(pl.multiple_of(t * 256, 256), 256)
        wqp[here] = nn(wq[here], widen[...]).astype(BF)

    save_wq = pltpu.make_async_copy(wqp, o_wq, local.at[2])
    save_wq.start()

    def project(c, s):
        y = nn(nbuf[c, s], wqp[...]).astype(BF)
        here = pl.ds(pl.multiple_of(s * length, length), length)
        cs, fr, bk = cos[here], front[here], back[here]
        for k in range(3):
            lanes = slice(128 * k, 128 * k + 128)
            qkv[c, here, lanes] = rope(y[:, lanes].astype(F32), cs, fr, bk).astype(BF)
        qkv[c, here, 384:512] = y[:, 384:512]

    for h, offsets in n_one.stages():
        n_one.wait_stage(h, offsets)
        for j in offsets:
            s_j = at.seq_at(j)

            @pl.loop(0, sib)
            def _(c):
                project(c, s_j)

    save_n1 = pltpu.make_async_copy(nbuf, o_n1, local.at[3])
    save_n1.start()
    save_qkv = pltpu.make_async_copy(qkv, o_qkv, local.at[4])
    save_qkv.start()

    tri = lax.broadcasted_iota(jnp.int32, (length, length), 0) >= lax.broadcasted_iota(
        jnp.int32, (length, length), 1
    )

    def attend(i):
        @pl.loop(0, sib)
        def _(b):
            past = i * length
            here = slice(past, past + length)
            outs = []
            for h in range(GROUP):
                q = qkv[b, here, 128 * h : 128 * h + 128]
                d = jnp.where(tri, nt(q, qkv[b, here, 256:384]) * (scale * log2e), -1e30)
                m = jnp.max(d, axis=1, keepdims=True)
                if i:
                    e = nt(q, qkv[b, 0:past, 256:384]) * (scale * log2e)
                    m = jnp.maximum(m, jnp.max(e, axis=1, keepdims=True))
                d = jnp.exp2(d - m)
                total = jnp.sum(d, axis=1, keepdims=True)
                o = nn(d.astype(BF), qkv[b, here, 384:512])
                if i:
                    e = jnp.exp2(e - m)
                    total = total + jnp.sum(e, axis=1, keepdims=True)
                    o = o + nn(e.astype(BF), qkv[b, 0:past, 384:512])
                outs.append((o / total).astype(BF))
                lse = jnp.broadcast_to(m + jnp.log2(total), (length, 128))
                o_lse[b, h, i] = lse.T[0:8]
            for k in range(chunks):
                pair = jnp.concatenate(outs[k * heads_per : (k + 1) * heads_per], axis=1)
                att_out[k, b, i] = nt(pair, widen_att[...]).astype(BF)

    def send_attended(i):
        for k in range(chunks):
            for b in range(sib):
                mine = jnp.logical_and(at.s == i, at.c == b)

                @pl.when(mine)
                def _():
                    att_in[tau * chunks + k] = att_out[k, b, i]

                @pl.when(jnp.logical_not(mine))
                def _():
                    rdma(att_out.at[k, b, i], att_in.at[tau * chunks + k], at_s.at[k, b, i],
                         at_r.at[tau * chunks + k], at.dev(i, b)).start()

    wo_gather = Gather(
        at, lambda c, s, h: wo.at[c, s, pl.ds(h * (planes // 2), planes // 2)],
        (wo_a, wo_b, wo_c, wo_d),
    )
    cot_gather = Gather(at, token_part(cbuf), (ct_a, ct_b, ct_c, ct_d))
    attend(n - 1)
    save_n1.wait()
    n_one.drain()
    send_attended(n - 1)
    col_wait_all(wo_mine, z_os, z_or, wo_own)
    wo_gather.start()
    gu_own = z_send_all(gu_s, gu, z_gs, z_gr, local.at[5])
    dn_place = lambda p: dn.at[pl.ds(pl.multiple_of(p * units, units), units)]
    dn_own = col_send_all(dn_s, dn_place, z_ds, z_dr, local.at[6])
    for i in range(n - 2, 0, -1):
        attend(i)
        send_attended(i)
    wo_hops = list(wo_gather.stages())
    for h, offsets in wo_hops[:-1]:
        wo_gather.wait_stage(h, offsets)
    attend(0)
    send_attended(0)
    cot_gather.start()
    wo_gather.wait_stage(*wo_hops[-1])
    wo_gather.drain()
    save_qkv.wait()
    save_wq.wait()

    group = n * sib
    for j in range(1, group):
        t = lax.rem(tau + j, group)
        for k in range(chunks):
            ref = att_in.at[t * chunks + k]
            rdma(ref, ref, at_s.at[0, 0, 0], at_r.at[t * chunks + k], at.dev(at.s, at.c)).wait_recv()
    for k in range(chunks):
        for i in range(n):
            for b in range(sib):
                @pl.when(jnp.logical_not(jnp.logical_and(at.s == i, at.c == b)))
                def _():
                    rdma(att_out.at[k, b, i], att_out.at[k, b, i], at_s.at[k, b, i],
                         at_r.at[0], at.dev(at.s, at.c)).wait_send()
    save_att = pltpu.make_async_copy(att_in, o_att, local.at[3])
    save_att.start()

    x_f = x[...].astype(F32)
    for s in range(n):
        cols = slice(s * part_cols, (s + 1) * part_cols)
        acc = x_f[:, cols]
        for p in range(planes):
            for c in range(sib):
                acc = acc + nn(att_in[p * sib + c], wo[c, s, p])
        o_hidden[:, cols] = acc
    hidden = o_hidden[...]
    inv_mid = lax.rsqrt(jnp.mean(hidden * hidden, axis=-1, keepdims=True) + NORM_EPS)
    nbuf[at.c, at.s] = (hidden * inv_mid).astype(BF)
    n_two = Gather(at, token_part(nbuf), (n2_a, n2_b, n2_c, n2_d))
    n_two.start()

    z_wait_all(gu, z_gs, z_gr, gu_own)
    col_wait_all(dn_place, z_ds, z_dr, dn_own)
    save_dn = pltpu.make_async_copy(dn, o_dn, local.at[4])
    save_dn.start()

    def feed_forward(c, s):
        n_here = nbuf[c, s]
        gate = nn(n_here, gu[:, :local_units])
        up = nn(n_here, gu[:, local_units:])
        sig = 1.0 / (1.0 + jnp.exp(-gate))
        silu = gate * sig
        act[c, s] = (silu * up).astype(BF)
        grad_act = nt(cbuf[c, s], dn[...])
        ggu[c, s, :, :local_units] = (grad_act * up * sig * (1.0 + gate * (1.0 - sig))).astype(BF)
        ggu[c, s, :, local_units:] = (grad_act * silu).astype(BF)

    for h, offsets in n_two.stages():
        cot_gather.wait_stage(h, offsets)
        n_two.wait_stage(h, offsets)
        for j in offsets:
            s_j = at.seq_at(j)

            @pl.loop(0, sib)
            def _(c):
                feed_forward(c, s_j)

    save_act = pltpu.make_async_copy(act, o_act, local.at[5])
    save_act.start()

    scatter = Scatter(at, (sc_stage, sc_in, sc_out, sc_inn), (rs_a, rs_b, rs_c, rs_d), length, width)
    tile = 512

    def to_stage(c, s, ref):
        for t in range(width // tile):
            cols = slice(t * tile, (t + 1) * tile)
            ref[:, cols] = nt(ggu[c, s], gu[cols, :]).astype(BF)

    def to_ring(c, s, store):
        for t in range(width // tile):
            cols = slice(t * tile, (t + 1) * tile)
            store(cols, nt(ggu[c, s], gu[cols, :]))

    tokens = sib * seq_len
    down_copies = []

    def grad_down():
        cot_all = cbuf[...].reshape(tokens, width)
        down_rows = local_units // 2
        for t in range(2):
            rows_here = slice(t * down_rows, (t + 1) * down_rows)
            lhs = act[:, :, :, rows_here].reshape(tokens, down_rows)
            stg[rows_here] = tn(lhs, cot_all).astype(BF)
        own = pltpu.make_async_copy(
            stg.at[pl.ds(pl.multiple_of(at.p * units, units), units)], o_sdn.at[at.p], local.at[6]
        )
        own.start()
        down_copies.append(own)
        for dp in range(1, planes):
            to = lax.rem(at.p + dp, planes)
            copy = rdma(stg.at[pl.ds(pl.multiple_of(to * units, units), units)], o_sdn.at[at.p],
                        z_ss.at[dp], z_sr.at[dp], (at.s, at.col(dp, 0)))
            copy.start()
            sent.append(copy)

    gu_tile = sgu_t.shape[1]
    gu_steps = width // gu_tile

    def gu_copy(m, slot):
        return pltpu.make_async_copy(
            sgu_t.at[slot], o_sgu.at[pl.ds(m * gu_tile, gu_tile)], local.at[7 + slot]
        )

    def grad_gu(lo, hi):
        for m in range(lo, hi):
            slot = m % 2
            if m >= 2:
                gu_copy(m - 2, slot).wait()
            lhs = nbuf[:, :, :, m * gu_tile : (m + 1) * gu_tile].reshape(tokens, gu_tile)
            sgu_t[slot] = tn(lhs, ggu[...].reshape(tokens, 2 * local_units)).astype(BF)
            gu_copy(m, slot).start()

    def finish(cols, value):
        o_ghid[:, cols] = value

    n_sends = len(scatter.offsets())

    def between(k):
        if k == 0:
            grad_down()
            grad_gu(0, gu_steps // 3)
        if k == n_sends - 2:
            grad_gu(gu_steps // 3, gu_steps)

    scatter.to_sibling(to_stage)
    scatter.round(to_ring, between, finish)
    e_mid = o_ghid[...]
    hidden = o_hidden[...]
    inv_mid = lax.rsqrt(jnp.mean(hidden * hidden, axis=-1, keepdims=True) + NORM_EPS)
    norm_mid = hidden * inv_mid
    o_ghid[...] = cot[...].astype(F32) + inv_mid * (
        e_mid - norm_mid * jnp.mean(e_mid * norm_mid, axis=-1, keepdims=True)
    )
    branch = o_ghid[...].astype(BF)
    for f in range(owners):
        p, c = f // sib, f % sib
        acc = nt(branch[:, :part_cols], wo[c, 0, p])
        for s in range(1, n):
            acc = acc + nt(branch[:, s * part_cols : (s + 1) * part_cols], wo[c, s, p])
        ga_out[f] = acc.astype(BF)
        t, k = f // chunks, f % chunks
        mine = tau == t

        @pl.when(mine)
        def _():
            gh_in[k, at.c, at.s] = ga_out[f]

        @pl.when(jnp.logical_not(mine))
        def _():
            rdma(ga_out.at[f], gh_in.at[k, at.c, at.s], gh_s.at[f], gh_r.at[k, tau],
                 at.dev(t // sib, t % sib)).start()

    for j in range(1, group):
        t = lax.rem(tau + j, group)
        for k in range(chunks):
            ref = gh_in.at[k, lax.rem(t, sib), lax.div(t, sib)]
            rdma(ref, ref, gh_s.at[0], gh_r.at[k, t], at.dev(at.s, at.c)).wait_recv()
    save_gh = pltpu.make_async_copy(gh_in, o_gh, local.at[0])
    save_gh.start()
    for f in range(owners):
        @pl.when(jnp.logical_not(tau == f // chunks))
        def _():
            rdma(ga_out.at[f], ga_out.at[f], gh_s.at[f], gh_r.at[0, 0],
                 at.dev(at.s, at.c)).wait_send()

    for dp in range(1, planes):
        ref = o_sdn.at[lax.rem(at.p - dp + planes, planes)]
        rdma(ref, ref, z_ss.at[dp], z_sr.at[dp], (at.s, at.f)).wait_recv()
    for copy in down_copies:
        copy.wait()
    for m in range(max(0, gu_steps - 2), gu_steps):
        gu_copy(m, m % 2).wait()
    cot_gather.drain()
    n_two.drain()
    scatter.drain()
    for copy in sent:
        copy.wait_send()
    save_att.wait()
    save_act.wait()
    save_dn.wait()
    save_gh.wait()


def forward_call(dims, x, cot, tables, widen, widen_att, wq_s, gu_s, dn_s, wo_s):
    n, sib, planes = dims
    length, width = x.shape
    rows, units, part_cols = wq_s.shape[1], dn_s.shape[0], wo_s.shape[1]
    owners = planes * sib
    chunks = GROUP * HEAD_DIM // rows
    ffl = planes * units
    seq_len = n * length
    vm, hb = pl.BlockSpec(memory_space=pltpu.VMEM), pl.BlockSpec(memory_space=pl.ANY)
    blocks = (sib, n, length, width)
    sds = jax.ShapeDtypeStruct
    outs = [
        (sds(blocks, BF), hb),
        (sds((sib, seq_len, 512), BF), hb),
        (sds((sib, GROUP, n, 8, length), F32), vm),
        (sds((chunks, sib, n, length, rows), BF), hb),
        (sds((owners, length, rows), BF), hb),
        (sds((length, width), F32), vm),
        (sds((length, width), F32), vm),
        (sds((sib, n, length, ffl), BF), hb),
        (sds((ffl, width), BF), hb),
        (sds((width, 512), BF), hb),
        (sds((width, 2 * ffl), BF), hb),
        (sds((planes, units, width), BF), hb),
    ]
    dma = pltpu.SemaphoreType.DMA
    scratch = [
        pltpu.VMEM(blocks, BF), pltpu.VMEM(blocks, BF), pltpu.VMEM((sib, seq_len, 512), BF),
        pltpu.VMEM((width, wq_s.shape[2]), BF), pltpu.VMEM((width, 512), BF),
        pltpu.VMEM((sib, n, planes, rows, part_cols), BF),
        pltpu.VMEM((width, 2 * ffl), BF), pltpu.VMEM((ffl, width), BF),
        pltpu.VMEM((sib, n, length, ffl), BF), pltpu.VMEM((sib, n, length, 2 * ffl), BF),
        pltpu.VMEM((chunks, sib, n, length, rows), BF), pltpu.VMEM((owners, length, rows), BF),
        pltpu.VMEM((owners, length, rows), BF), pltpu.VMEM((chunks, sib, n, length, rows), BF),
        pltpu.VMEM((ffl, width), BF), pltpu.VMEM((2, 256, 2 * ffl), BF),
        *Scatter.scratch(n, (length, width)),
        dma((planes, sib)), dma((planes, sib)), dma((planes,)), dma((planes,)),
        dma((planes, sib)), dma((planes, sib)), dma((planes,)), dma((planes,)),
        dma((planes,)), dma((planes,)), dma((9,)),
        *Gather.scratch(n), *Gather.scratch(n), *Gather.scratch(n), *Gather.scratch(n),
        *Scatter.sems(n),
        dma((chunks, sib, n)), dma((owners,)), dma((owners,)), dma((chunks, n * sib)),
    ]
    return pl.pallas_call(
        functools.partial(forward_kernel, dims),
        out_shape=[o[0] for o in outs],
        out_specs=[o[1] for o in outs],
        in_specs=[vm] * 7 + [hb] * 4,
        scratch_shapes=scratch,
        compiler_params=pltpu.CompilerParams(
            collective_id=0, has_side_effects=True, vmem_limit_bytes=VMEM_LIMIT
        ),
    )(x, cot, *tables, widen, widen_att, wq_s, gu_s, dn_s, wo_s)


def backward_kernel(
    dims,
    x, cos, front, back, widen, widen_att, lse,
    n1, qkv_h, gh_h, att_h, hidden, ghid, act_h, dn_h, wqp_h, sgu, sdn_h,
    o_block, o_input, o_gq, o_ggu, o_gdn, o_gout,
    qkv, gh, att, act, dn, wqp, sdn, gq, gk, gv, n1_t, sq, so, branch,
    r_gu, r_qkv, r_out, g_gu, g_qkv, g_dn, g_out,
    sc_stage, sc_in, sc_out, sc_inn, free,
    loads, z_gs, z_gr, z_qs, z_qr, z_os, z_or,
    d_a, d_b, d_c, d_d, e_a, e_b, e_c, e_d, s_a, s_b, s_c, s_d,
    a_dn_s, a_dn_r, a_gu_s, a_gu_r, a_qk_s, a_qk_r, a_ou_s, a_ou_r,
):
    n, sib, planes = dims
    at = Place(n, sib, planes)
    length, width = x.shape
    owners = planes * sib
    chunks, _, _, _, rows = gh.shape
    heads_per = rows // HEAD_DIM
    part_cols = r_out.shape[2]
    scale = HEAD_DIM ** (-0.5)
    log2e = 1.4426950408889634
    tokens = sib * n * length
    sent = []
    bufs = (sc_stage, sc_in, sc_out, sc_inn)

    def load(src, dst, k):
        copy = pltpu.make_async_copy(src, dst, loads.at[k])
        copy.start()
        return copy

    def owner_rows(f):
        return pl.ds(pl.multiple_of(f * rows, rows), rows)

    def z_source(dp, dc):
        return (
            lax.rem(at.p - dp + planes, planes) * sib + lax.rem(at.c - dc + sib, sib)
        )

    def z_scatter(src, dst, ssem, rsem, k):
        own = load(src.at[owner_rows(at.f)], dst.at[at.f], k)
        for dp in range(planes):
            for dc in range(sib):
                if dp or dc:
                    to = at.col(dp, dc)
                    copy = rdma(src.at[owner_rows(to)], dst.at[at.f],
                                ssem.at[dp, dc], rsem.at[dp, dc], (at.s, to))
                    copy.start()
                    sent.append(copy)
        return own

    def z_collect(dst, ssem, rsem, own):
        own.wait()
        for dp in range(planes):
            for dc in range(sib):
                if dp or dc:
                    ref = dst.at[z_source(dp, dc)]
                    rdma(ref, ref, ssem.at[dp, dc], rsem.at[dp, dc], (at.s, at.f)).wait_recv()

    def plane_total(dst, c):
        acc = dst[c].astype(F32)
        for p in range(1, planes):
            acc = acc + dst[p * sib + c].astype(F32)
        return acc.astype(BF)

    def release():
        if sib > 1:
            pl.semaphore_signal(free, inc=1, device_id=at.dev(at.s, 1 - at.c), device_id_type=MESH)
        for way in (1, -1):
            pl.semaphore_signal(
                free, inc=1, device_id=at.dev(at.seq_at(way), at.c), device_id_type=MESH
            )

    def acquire():
        pl.semaphore_wait(free, 3 if sib > 1 else 2)

    at.barrier()
    in_qkv, in_gh = load(qkv_h, qkv, 0), load(gh_h, gh, 1)
    in_act, in_dn, in_sdn = load(act_h, act, 2), load(dn_h, dn, 3), load(sdn_h, sdn, 4)
    gu_own = z_scatter(sgu, r_gu, z_gs, z_gr, 5)
    in_att, in_wqp = load(att_h, att, 6), load(wqp_h, wqp, 7)
    n1_cols = n1_t.shape[4]
    n1_steps = width // n1_cols

    def n1_load(m):
        return pltpu.make_async_copy(
            n1.at[:, :, :, pl.ds(m * n1_cols, n1_cols)], n1_t.at[m % 2], loads.at[8 + m % 2]
        )

    n1_load(0).start()
    n1_load(1).start()

    def row_half(ref):
        size = ref.shape[-2] // 2
        if len(ref.shape) == 4:
            return lambda c, s, h: ref.at[s, :, pl.ds(h * size, size)]
        return lambda c, s, h: ref.at[s, pl.ds(h * size, size)]

    in_sdn.wait()
    acc = sdn[0].astype(F32)
    for p in range(1, planes):
        acc = acc + sdn[p].astype(F32)
    g_dn[at.s] = acc.astype(BF)
    ag_dn = Gather(at, row_half(g_dn), (a_dn_s, a_dn_r))
    ag_dn.start()

    tri = lax.broadcasted_iota(jnp.int32, (length, length), 0) <= lax.broadcasted_iota(
        jnp.int32, (length, length), 1
    )

    def attend_back(b):
        gk[...] = jnp.zeros_like(gk)
        gv[...] = jnp.zeros_like(gv)
        for i in range(n):
            past = i * length
            here = slice(past, past + length)
            for h in range(GROUP):
                k, slot = h // heads_per, h % heads_per
                q = qkv[b, here, 128 * h : 128 * h + 128]
                do = nn(gh[k, b, i], widen_att[:, 128 * slot : 128 * slot + 128]).astype(BF)
                row = lse[b, h, i, 0:1]
                parts = [(here, True)] + ([(slice(0, past), False)] if i else [])
                probs, grads = [], []
                delta = 0.0
                for part, diagonal in parts:
                    sc = nt(qkv[b, part, 256:384], q) * (scale * log2e)
                    if diagonal:
                        sc = jnp.where(tri, sc, -1e30)
                    pr = jnp.exp2(sc - row)
                    dp = nt(qkv[b, part, 384:512], do)
                    delta = delta + jnp.sum(pr * dp, axis=0, keepdims=True)
                    probs.append(pr)
                    grads.append(dp)
                dq = jnp.zeros((length, 128), F32)
                for (part, _), pr, dp in zip(parts, probs, grads):
                    ds = (pr * (dp - delta) * scale).astype(BF)
                    gv[part] += nn(pr.astype(BF), do)
                    gk[part] += nn(ds, q)
                    dq = dq + tn(ds, qkv[b, part, 256:384])
                gq[b, here, 128 * h : 128 * h + 128] = rope(
                    dq, cos[here], -front[here], -back[here]
                ).astype(BF)
        for i in range(n):
            here = slice(i * length, (i + 1) * length)
            gq[b, here, 256:384] = rope(gk[here], cos[here], -front[here], -back[here]).astype(BF)
            gq[b, here, 384:512] = gv[here].astype(BF)

    tile = 512

    def tiles():
        return [slice(t * tile, (t + 1) * tile) for t in range(width // tile)]

    in_act.wait()
    in_dn.wait()
    down = Scatter(at, bufs, (d_a, d_b, d_c, d_d), length, width)

    def down_stage(c, s, ref):
        for cols in tiles():
            ref[:, cols] = nn(act[c, s], dn[:, cols]).astype(BF)

    def down_ring(c, s, store):
        for cols in tiles():
            store(cols, nn(act[c, s], dn[:, cols]))

    def down_finish(cols, value):
        o_block[:, cols] = (hidden[:, cols] + value).astype(BF)

    n_sends = len(down.offsets())

    def down_between(k):
        if k == 0:
            in_qkv.wait()
            in_gh.wait()
            attend_back(0)
        if k == n_sends - 2 and sib > 1:
            attend_back(1)

    down.to_sibling(down_stage)
    down.round(down_ring, down_between, down_finish)
    down.drain()
    release()
    ag_dn.hop(1)

    gq_all = lambda: gq[...].reshape(tokens, 512)
    for m in range(n1_steps):
        n1_load(m).wait()
        part = tn(n1_t[m % 2].reshape(tokens, n1_cols), gq_all()).astype(BF)
        sq[m * n1_cols : (m + 1) * n1_cols] = nt(part, widen[...]).astype(BF)
        if m + 2 < n1_steps:
            n1_load(m + 2).start()
    qkv_own = z_scatter(sq, r_qkv, z_qs, z_qr, 10)

    in_wqp.wait()
    in_att.wait()
    acquire()
    e_in = Scatter(at, bufs, (e_a, e_b, e_c, e_d), length, width)

    def gq_block(c, s):
        return gq[c, pl.ds(pl.multiple_of(s * length, length), length)]

    def e_stage(c, s, ref):
        for cols in tiles():
            ref[:, cols] = nt(gq_block(c, s), wqp[cols, :]).astype(BF)

    def e_ring(c, s, store):
        for cols in tiles():
            store(cols, nt(gq_block(c, s), wqp[cols, :]))

    def e_finish(cols, value):
        o_input[:, cols] = value

    def nothing(k):
        pass

    e_in.to_sibling(e_stage)
    for h in range(2, n // 2 + 1):
        ag_dn.hop(h)
    e_in.round(e_ring, nothing, e_finish)
    e_in.drain()
    release()
    x_f = x[...].astype(F32)
    inv_one = lax.rsqrt(jnp.mean(x_f * x_f, axis=-1, keepdims=True) + NORM_EPS)
    norm_one = x_f * inv_one
    e_val = o_input[...]
    o_input[...] = ghid[...] + inv_one * (
        e_val - norm_one * jnp.mean(e_val * norm_one, axis=-1, keepdims=True)
    )

    acquire()
    s_out = Scatter(at, bufs, (s_a, s_b, s_c, s_d), rows, planes * part_cols)

    for s in range(n):
        branch[s] = ghid[:, s * part_cols : (s + 1) * part_cols].astype(BF)

    def out_pieces(c, s):
        low = branch[s]
        for p in range(planes):
            yield slice(p * part_cols, (p + 1) * part_cols), tn(att[p * sib + c], low)

    def out_stage(c, s, ref):
        for cols, value in out_pieces(c, s):
            ref[:, cols] = value.astype(BF)

    def out_ring(c, s, store):
        for cols, value in out_pieces(c, s):
            store(cols, value)

    def out_finish(cols, value):
        so[cols.start // part_cols] = value.astype(BF)

    s_out.to_sibling(out_stage)
    s_out.round(out_ring, nothing, out_finish)
    s_out.drain()
    out_own = load(so.at[at.p], r_out.at[at.p], 11)
    for dp in range(1, planes):
        to = lax.rem(at.p + dp, planes)
        copy = rdma(so.at[to], r_out.at[at.p], z_os.at[dp], z_or.at[dp], (at.s, at.col(dp, 0)))
        copy.start()
        sent.append(copy)

    z_collect(r_gu, z_gs, z_gr, gu_own)
    for c in range(sib):
        g_gu[at.s, c] = plane_total(r_gu, c)
    ag_gu = Gather(at, row_half(g_gu), (a_gu_s, a_gu_r))
    ag_gu.start()
    z_collect(r_qkv, z_qs, z_qr, qkv_own)
    for c in range(sib):
        g_qkv[at.s, c] = plane_total(r_qkv, c)
    ag_qkv = Gather(at, row_half(g_qkv), (a_qk_s, a_qk_r))
    ag_qkv.start()
    out_own.wait()
    for dp in range(1, planes):
        ref = r_out.at[lax.rem(at.p - dp + planes, planes)]
        rdma(ref, ref, z_os.at[dp], z_or.at[dp], (at.s, at.f)).wait_recv()
    acc = r_out[0].astype(F32)
    for p in range(1, planes):
        acc = acc + r_out[p].astype(F32)
    g_out[at.s] = acc.astype(BF)
    ag_out = Gather(at, row_half(g_out), (a_ou_s, a_ou_r))
    ag_out.start()
    save_dn = load(g_dn, o_gdn, 0)
    for h in range(1, n // 2 + 1):
        for ag in (ag_gu, ag_qkv, ag_out):
            ag.hop(h)
    saves = [load(g_gu, o_ggu, 1), load(g_qkv, o_gq, 2), load(g_out, o_gout, 3), save_dn]
    for ag in (ag_dn, ag_gu, ag_qkv, ag_out):
        ag.drain()
    for copy in sent:
        copy.wait_send()
    for copy in saves:
        copy.wait()


def backward_call(dims, x, tables, widen, widen_att, lse, n1, qkv, gh, att, hidden, ghid, act, dn, wqp, sgu, sdn):
    n, sib, planes = dims
    length, width = x.shape
    chunks, _, _, _, rows = gh.shape
    owners = planes * sib
    units = sdn.shape[1]
    part_cols = width // n
    seq_len = n * length
    head_cols = (GROUP + 2) * HEAD_DIM
    vm, hb = pl.BlockSpec(memory_space=pltpu.VMEM), pl.BlockSpec(memory_space=pl.ANY)
    sds = jax.ShapeDtypeStruct
    g_shapes = [
        (n, sib, rows, head_cols), (n, sib, rows, sgu.shape[1]), (n, units, width),
        (n, rows, part_cols),
    ]
    outs = [(sds((length, width), BF), vm), (sds((length, width), F32), vm)] + [
        (sds(shape, BF), hb) for shape in g_shapes
    ]
    dma = pltpu.SemaphoreType.DMA
    scratch = [
        pltpu.VMEM(qkv.shape, BF), pltpu.VMEM(gh.shape, BF), pltpu.VMEM(att.shape, BF),
        pltpu.VMEM(act.shape, BF), pltpu.VMEM(dn.shape, BF), pltpu.VMEM(wqp.shape, BF),
        pltpu.VMEM(sdn.shape, BF), pltpu.VMEM(qkv.shape, BF),
        pltpu.VMEM((seq_len, 128), F32), pltpu.VMEM((seq_len, 128), F32),
        pltpu.VMEM((2, *n1.shape[:3], 384), BF), pltpu.VMEM((width, head_cols), BF),
        pltpu.VMEM((planes, rows, part_cols), BF), pltpu.VMEM((n, length, part_cols), BF),
        pltpu.VMEM((owners, rows, sgu.shape[1]), BF), pltpu.VMEM((owners, rows, head_cols), BF),
        pltpu.VMEM((planes, rows, part_cols), BF),
        pltpu.VMEM(g_shapes[1], BF), pltpu.VMEM(g_shapes[0], BF), pltpu.VMEM(g_shapes[2], BF),
        pltpu.VMEM(g_shapes[3], BF),
        *Scatter.scratch(n, (length, max(width, planes * part_cols))),
        pltpu.SemaphoreType.REGULAR,
        dma((12,)), dma((planes, sib)), dma((planes, sib)), dma((planes, sib)),
        dma((planes, sib)), dma((planes,)), dma((planes,)),
        *Scatter.sems(n), *Scatter.sems(n), *Scatter.sems(n),
        *Gather.scratch(n, False), *Gather.scratch(n, False), *Gather.scratch(n, False),
        *Gather.scratch(n, False),
    ]
    return pl.pallas_call(
        functools.partial(backward_kernel, dims),
        out_shape=[o[0] for o in outs],
        out_specs=[o[1] for o in outs],
        in_specs=[vm] * 7 + [hb] * 4 + [vm] * 2 + [hb] * 5,
        scratch_shapes=scratch,
        compiler_params=pltpu.CompilerParams(
            collective_id=1, has_side_effects=True, vmem_limit_bytes=VMEM_LIMIT
        ),
    )(x, *tables, widen, widen_att, lse, n1, qkv, gh, att, hidden, ghid, act, dn, wqp, sgu, sdn)


def adamw(weight, first, second, grad, rate, decay):
    first_new = BETA_ONE * first + (1.0 - BETA_ONE) * grad
    second_new = BETA_TWO * second + (1.0 - BETA_TWO) * grad * grad
    first_hat = first_new / (1.0 - BETA_ONE**ADAM_STEP)
    second_hat = second_new / (1.0 - BETA_TWO**ADAM_STEP)
    weight_new = weight - rate * (first_hat / (jnp.sqrt(second_hat) + ADAM_EPS) + decay * weight)
    return (weight_new, first_new, second_new)


def rope_arrays(seq_len):
    half = HEAD_DIM // 2
    frequencies = ROPE_BASE ** (-(2.0 * jnp.arange(half, dtype=F32)) / HEAD_DIM)
    angles = jnp.arange(seq_len, dtype=F32)[:, None] * frequencies[None, :]
    cos, sin = jnp.cos(angles), jnp.sin(angles)
    pad = jnp.zeros((seq_len, 128 - HEAD_DIM), F32)
    none = jnp.zeros_like(sin)
    return (
        jnp.concatenate([cos, cos, pad], axis=1),
        jnp.concatenate([-sin, none, pad], axis=1),
        jnp.concatenate([none, sin, pad], axis=1),
    )


def widening(heads):
    row = jnp.arange(heads * HEAD_DIM)[:, None]
    col = jnp.arange(heads * 128)[None, :]
    return (col == row // HEAD_DIM * 128 + row % HEAD_DIM).astype(BF)


def make(n_seq, n_fsdp):
    sib = KV_HEADS // n_seq
    planes = n_fsdp // sib

    def on_device(
        inputs, cotangent, qkv_weight, out_weight, gate_up_weight, down_weight, norm_gains,
        qkv_first, qkv_second, out_first, out_second, gate_up_first, gate_up_second,
        down_first, down_second, gain_first, gain_second,
    ):
        s_idx = lax.axis_index("seq")
        _, length, width = inputs.shape
        seq_len = length * n_seq
        rows = qkv_weight.shape[0]
        head_cols = (GROUP + 2) * HEAD_DIM
        ff_rows = down_weight.shape[0]
        units = ff_rows // n_seq
        hidden_units = ff_rows * n_fsdp
        local_units = hidden_units // KV_HEADS
        gains = norm_gains.astype(BF).astype(F32)

        wq_s = lax.dynamic_slice_in_dim(qkv_weight, s_idx * sib * head_cols, sib * head_cols, 1)
        wq_s = (wq_s * gains[0][:, None]).astype(BF).reshape(rows, sib, head_cols).transpose(1, 0, 2)
        gu_s = gate_up_weight.reshape(rows, 2, planes, sib, n_seq, units)
        gu_s = lax.dynamic_index_in_dim(gu_s, s_idx, 4, keepdims=False)
        gu_s = (gu_s * gains[1][:, None, None, None, None]).astype(BF)
        gu_s = gu_s.transpose(3, 0, 1, 2, 4).reshape(sib, rows, 2 * local_units)
        dn_s = lax.dynamic_slice_in_dim(down_weight, s_idx * units, units, 0).astype(BF)
        part_cols = width // n_seq
        wo_s = lax.dynamic_slice_in_dim(out_weight, s_idx * part_cols, part_cols, 1).astype(BF)
        tables = rope_arrays(seq_len)
        widen = widening(GROUP + 2)
        widen_att = widening(rows // HEAD_DIM)

        (n_one, qkv, lse, gh, att, hidden, grad_hidden, act, w_down, w_qkv, s_gu, s_down) = forward_call(
            (n_seq, sib, planes), inputs[0], cotangent[0], tables, widen, widen_att,
            wq_s, gu_s, dn_s, wo_s,
        )
        block_out, input_grad, g_qkv, g_gu, g_down, g_out = backward_call(
            (n_seq, sib, planes), inputs[0], tables, widen, widen_att, lse, n_one, qkv, gh, att,
            hidden, grad_hidden, act, w_down, w_qkv, s_gu, s_down,
        )
        block_out, input_grad = block_out[None], input_grad[None]
        g_qkv = g_qkv.transpose(2, 0, 1, 3).reshape(rows, n_seq * sib * head_cols).astype(F32)
        g_gu = g_gu.reshape(n_seq, sib, rows, 2, planes, units).transpose(2, 3, 4, 1, 0, 5)
        g_gu = g_gu.reshape(rows, 2 * hidden_units).astype(F32)
        g_down = g_down.reshape(ff_rows, width).astype(F32)
        g_out = g_out.transpose(1, 0, 2).reshape(rows, width).astype(F32)
        gain_grad = jnp.stack(
            [
                jnp.sum(g_qkv * qkv_weight.astype(BF).astype(F32), axis=1),
                jnp.sum(g_gu * gate_up_weight.astype(BF).astype(F32), axis=1),
            ]
        )
        g_qkv = g_qkv * gains[0][:, None]
        g_gu = g_gu * gains[1][:, None]
        qkv_new = adamw(qkv_weight, qkv_first, qkv_second, g_qkv, RATE_QKV, WEIGHT_DECAY)
        out_new = adamw(out_weight, out_first, out_second, g_out, RATE_OUT, WEIGHT_DECAY)
        gu_new = adamw(
            gate_up_weight, gate_up_first, gate_up_second, g_gu, RATE_GATE_UP, WEIGHT_DECAY
        )
        down_new = adamw(down_weight, down_first, down_second, g_down, RATE_DOWN, WEIGHT_DECAY)
        gains_new = adamw(norm_gains, gain_first, gain_second, gain_grad, RATE_GAINS, 0.0)
        return (block_out, input_grad, *qkv_new, *out_new, *gu_new, *down_new, *gains_new)

    return on_device


def solution(mesh):
    tokens = P("fsdp", "seq", None)
    weight = P("fsdp", None)
    gain = P(None, "fsdp")
    in_specs = (tokens, tokens, weight, weight, weight, weight, gain) + (weight,) * 8 + (gain,) * 2
    out_specs = (tokens, tokens) + (weight,) * 12 + (gain,) * 3
    return jax.shard_map(
        make(mesh.shape["seq"], mesh.shape["fsdp"]),
        mesh=mesh, in_specs=in_specs, out_specs=out_specs, check_vma=False,
    )
```

```python
import functools

import jax
import jax.numpy as jnp
import ml_dtypes
import numpy as np
from jax import lax
from jax.experimental import pallas as pl
from jax.experimental.pallas import tpu as pltpu
from jax.sharding import PartitionSpec as P

HEAD_DIM = 96
KV_HEADS = 8
ADAM_STEP = 10
GROUP = 2

NORM_EPS = 1e-05
ROPE_BASE = 100000.0
BETA_ONE = 0.9
BETA_TWO = 0.95
ADAM_EPS = 1e-08
WEIGHT_DECAY = 0.1
RATE_QKV = 0.07
RATE_OUT = 0.8
RATE_GATE_UP = 0.07
RATE_DOWN = 0.045
RATE_GAINS = 0.6
BF = jnp.bfloat16
F32 = jnp.float32
VMEM_LIMIT = 62 * 1024 * 1024


MESH = pl.DeviceIdType.MESH


def rdma(src, dst, ssem, rsem, dev):
    return pltpu.make_async_remote_copy(
        src_ref=src, dst_ref=dst, send_sem=ssem, recv_sem=rsem, device_id=dev, device_id_type=MESH
    )


class Place:
    def __init__(self, n, sib, planes):
        self.n, self.sib, self.planes = n, sib, planes
        self.s = lax.axis_index("seq")
        self.f = lax.axis_index("fsdp")
        self.c = lax.rem(self.f, sib)
        self.p = lax.div(self.f, sib)
        a, b = lax.div(self.s, 2), lax.rem(self.s, 2)
        self.r = a * (1 - b) + (n - 1 - a) * b

    def seq_at(self, j):
        if j == 0:
            return self.s
        n = self.n
        q = lax.rem(self.r + (j + n), n)
        t = lax.div(q, n // 2)
        return (1 - t) * 2 * q + t * (2 * (n - 1 - q) + 1)

    def dev(self, s, c):
        return (s, self.p * self.sib + c)

    def col(self, dp, dc):
        return lax.rem(self.p + dp, self.planes) * self.sib + lax.rem(self.c + dc, self.sib)

    def barrier(self):
        sem = pltpu.get_barrier_semaphore()
        group = self.n * self.sib
        tau = self.s * self.sib + self.c
        for j in range(1, group):
            t = lax.rem(tau + j, group)
            pl.semaphore_signal(
                sem, inc=1, device_id=self.dev(lax.div(t, self.sib), lax.rem(t, self.sib)),
                device_id_type=MESH,
            )
        for dp in range(1, self.planes):
            for dc in range(self.sib):
                pl.semaphore_signal(
                    sem, inc=1, device_id=(self.s, self.col(dp, dc)), device_id_type=MESH
                )
        pl.semaphore_wait(sem, group - 1 + (self.planes - 1) * self.sib)


class Gather:
    def __init__(self, at, part, sems):
        self.at, self.part = at, part
        self.ring_s, self.ring_r = sems[:2]
        self.share = at.sib > 1 and len(sems) > 2
        if self.share:
            self.sib_s, self.sib_r = sems[2:]
        self.sent = []

    @staticmethod
    def scratch(n, share=True):
        d = pltpu.SemaphoreType.DMA
        ring = [d((2, n // 2, 2)), d((2, n // 2, 2))]
        return ring + [d((n, 2)), d((n, 2))] if share else ring

    def _send(self, copy):
        copy.start()
        self.sent.append(copy)

    def _ring(self, way, hop, half):
        at = self.at
        src = self.part(at.c, at.seq_at(-(hop - 1) if way == 0 else hop - 1), half)
        to = at.dev(at.seq_at(1 if way == 0 else -1), at.c)
        self._send(
            rdma(src, src, self.ring_s.at[way, hop - 1, half], self.ring_r.at[way, hop - 1, half], to)
        )

    def _sib(self, j, half):
        at = self.at
        if self.share:
            src = self.part(at.c, at.seq_at(j), half)
            slot = j % at.n
            self._send(
                rdma(src, src, self.sib_s.at[slot, half], self.sib_r.at[slot, half],
                     at.dev(at.s, 1 - at.c))
            )

    def start(self):
        self._ring(0, 1, 0)
        self._ring(1, 1, 1)
        self._ring(0, 1, 1)
        self._ring(1, 1, 0)
        self._sib(0, 0)
        self._sib(0, 1)

    def _arrive(self, way, hop, half):
        at = self.at
        j = -hop if way == 0 else hop
        ref = self.part(at.c, at.seq_at(j), half)
        rdma(ref, ref, self.ring_s.at[way, hop - 1, half], self.ring_r.at[way, hop - 1, half],
             at.dev(at.s, at.c)).wait_recv()
        last = at.n // 2
        if hop + 1 < last or (hop + 1 == last and half == way):
            self._ring(way, hop + 1, half)
        if hop == last:
            j = last
        self._sib(j, half)

    def hop(self, hop):
        self._arrive(0, hop, 0)
        self._arrive(1, hop, 1)
        if hop < self.at.n // 2:
            self._arrive(0, hop, 1)
            self._arrive(1, hop, 0)

    def sib_wait(self, j):
        at = self.at
        if self.share:
            for half in range(2):
                ref = self.part(1 - at.c, at.seq_at(j), half)
                slot = j % at.n
                rdma(ref, ref, self.sib_s.at[slot, half], self.sib_r.at[slot, half],
                     at.dev(at.s, at.c)).wait_recv()

    def stages(self):
        last = self.at.n // 2
        yield 0, [0]
        for h in range(1, last):
            yield h, [-h, h]
        yield last, [last]

    def wait_stage(self, h, offsets):
        if h:
            self.hop(h)
        for j in offsets:
            self.sib_wait(j)

    def drain(self):
        for copy in self.sent:
            copy.wait_send()


class Move:
    def __init__(self, at, src, dst, sems, every_core=True):
        self.at, self.src, self.dst = at, src, dst
        self.ssem, self.rsem, self.hop, self.own = sems
        self.cores = at.sib if every_core else 1
        self.relay = at.planes == 4

    @staticmethod
    def sems(planes, sib):
        d = pltpu.SemaphoreType.DMA
        return [d((planes, sib)), d((planes, sib)), d((sib,)), d((1,))]

    def _pairs(self):
        for dp in [2, 1, 3] if self.relay else range(1, self.at.planes):
            for dc in range(self.cores):
                yield dp, dc
        for dc in range(1, self.cores):
            yield 0, dc

    def _direct(self, dp, body):
        if self.relay and dp in (1, 3):
            pl.when(self.at.p != (3 if dp == 1 else 0))(body)
        else:
            body()

    def _send(self, dp, dc):
        at = self.at
        return rdma(self.src(lax.rem(at.c + dc, at.sib)), self.dst(at.f), self.ssem.at[dp, dc],
                    self.rsem.at[dp, dc], (at.s, at.col(dp, dc)))

    def _local(self):
        return pltpu.make_async_copy(self.src(self.at.c), self.dst(self.at.f), self.own.at[0])

    def start(self):
        self._local().start()
        for dp, dc in self._pairs():
            self._direct(dp, lambda: self._send(dp, dc).start())

    def wait(self):
        at = self.at
        for dp, dc in self._pairs():
            source = lax.rem(at.p - dp + at.planes, at.planes) * at.sib + lax.rem(
                at.c - dc + at.sib, at.sib
            )
            ref = self.dst(source)
            rdma(ref, ref, self.ssem.at[dp, dc], self.rsem.at[dp, dc], (at.s, at.f)).wait_recv()
            if self.relay and dp == 2:
                for here, to, slot in ((2, 3, 3), (1, 0, 1)):
                    @pl.when(at.p == here)
                    def _():
                        rdma(ref, ref, self.hop.at[dc], self.rsem.at[slot, dc],
                             (at.s, to * at.sib + at.c)).start()
        self._local().wait()

    def drain(self):
        at = self.at
        for dp, dc in self._pairs():
            self._direct(dp, lambda: self._send(dp, dc).wait_send())
            if self.relay and dp == 2:
                ref = self.dst(at.f)

                @pl.when(jnp.logical_or(at.p == 1, at.p == 2))
                def _():
                    rdma(ref, ref, self.hop.at[dc], self.rsem.at[0, dc], (at.s, at.f)).wait_send()


class Scatter:
    def __init__(self, at, bufs, sems, rows, cols):
        self.at, self.rows, self.cols = at, rows, pl.ds(0, cols)
        self.stage, self.sib_in, self.out, self.inn = bufs
        self.sib_s, self.sib_r, self.ring_s, self.ring_r = sems
        self.sent = []

    @staticmethod
    def scratch(n, shape):
        return [
            pltpu.VMEM((2, *shape), BF), pltpu.VMEM((n, *shape), BF),
            pltpu.VMEM((2, n // 2, *shape), BF), pltpu.VMEM((2, n // 2, *shape), BF),
        ]

    @staticmethod
    def sems(n):
        d = pltpu.SemaphoreType.DMA
        return [d((n,)), d((n,)), d((2, n // 2)), d((2, n // 2))]

    def offsets(self):
        last = self.at.n // 2
        order = [last]
        for h in range(last - 1, 0, -1):
            order += [h, -h]
        return order + [0]

    def to_sibling(self, produce):
        at = self.at
        if at.sib == 1:
            return
        copies = []
        for k, j in enumerate(self.offsets()):
            if k >= 2:
                copies[k - 2].wait_send()
            view = self.stage.at[k % 2, pl.ds(0, self.rows), self.cols]
            produce(1 - at.c, at.seq_at(j), view)
            copy = rdma(view, self.sib_in.at[k, pl.ds(0, self.rows), self.cols],
                        self.sib_s.at[k], self.sib_r.at[k], at.dev(at.s, 1 - at.c))
            copy.start()
            copies.append(copy)
        self.sent += copies[-2:]

    def _send(self, way, k, rows):
        at = self.at
        src = self.out.at[way, k, rows, self.cols]
        copy = rdma(src, self.inn.at[way, k, rows, self.cols], self.ring_s.at[way, k], self.ring_r.at[way, k],
                    at.dev(at.seq_at(1 if way == 0 else -1), at.c))
        copy.start()
        self.sent.append(copy)

    def _wait(self, way, k, rows):
        ref = self.inn.at[way, k, rows, self.cols]
        at = self.at
        rdma(ref, ref, self.ring_s.at[way, k], self.ring_r.at[way, k],
             at.dev(at.s, at.c)).wait_recv()

    def round(self, produce, between, finish):
        for k in range(len(self.offsets())):
            self.step(k, produce, finish)
            between(k)

    def step(self, k, produce, finish):
        at = self.at
        last = at.n // 2
        length = self.rows
        half = length // 2
        halves = (pl.ds(0, half), pl.ds(half, half))
        whole = pl.ds(0, length)
        j = self.offsets()[k]
        if at.sib > 1:
            ref = self.sib_in.at[k, pl.ds(0, length), self.cols]
            rdma(ref, ref, self.sib_s.at[k], self.sib_r.at[k], at.dev(at.s, at.c)).wait_recv()
        h = abs(j)
        if h == last:
            got = []
        else:
            ways = (0, 1) if h == 0 else ((0,) if j > 0 else (1,))
            rows_in = [halves[w] if h + 1 == last else whole for w in ways]
            got = [(w, rw) for w, rw in zip(ways, rows_in)]
        pending = [True]

        def store(cols, value, k=k, h=h, j=j, got=got, pending=pending):
            if pending[0]:
                for w, rw in got:
                    self._wait(w, h, rw)
                pending[0] = False
            if at.sib > 1:
                value = value + self.sib_in[k, pl.ds(0, length), cols].astype(F32)
            for w, rw in got:
                if h + 1 == last:
                    add = self.inn[w, h, pl.ds(w * half, half), cols].astype(F32)
                    if w == 0:
                        value = jnp.concatenate([value[:half] + add, value[half:]], axis=0)
                    else:
                        value = jnp.concatenate([value[:half], value[half:] + add], axis=0)
                else:
                    value = value + self.inn[w, h, pl.ds(0, length), cols].astype(F32)
            if h == last:
                low = value.astype(BF)
                self.out[0, h - 1, pl.ds(0, half), cols] = low[:half]
                self.out[1, h - 1, pl.ds(half, half), cols] = low[half:]
            elif h:
                self.out[0 if j > 0 else 1, h - 1, pl.ds(0, length), cols] = value.astype(BF)
            else:
                finish(cols, value)

        produce(at.c, at.seq_at(j), store)
        if h == last:
            self._send(0, h - 1, halves[0])
            self._send(1, h - 1, halves[1])
        elif h:
            self._send(0 if j > 0 else 1, h - 1, whole)

    def drain(self):
        for copy in self.sent:
            copy.wait_send()


def nt(a, b):
    return lax.dot_general(a, b, (((1,), (1,)), ((), ())), preferred_element_type=F32)


def tn(a, b):
    return lax.dot_general(a, b, (((0,), (0,)), ((), ())), preferred_element_type=F32)


def nn(a, b):
    return lax.dot_general(a, b, (((1,), (0,)), ((), ())), preferred_element_type=F32)


def rope(value, cos, front, back):
    return value * cos + pltpu.roll(value, 80, 1) * front + pltpu.roll(value, 48, 1) * back


def forward_kernel(
    dims,
    x, cot, cos, front, back, widen, widen_att, gain_cols, wq_s, gu_s, dn_s, wo_s,
    o_n1, o_qkv, o_lse, o_gh, o_att, o_hidden, o_ghid, o_act, o_dn, o_wq, o_sgu, o_sdn,
    nbuf, cbuf, qkv, wq, wqp, wo, gu, dn, act, ggu, att_out, att_in, gh_in, stg, sgu_t,
    wq_f, dn_f, wo_f, wq_b, gu_b, dn_b, wo_b,
    sc_stage, sc_in, sc_out, sc_inn,
    zw_a, zw_b, zw_c, zw_d, zo_a, zo_b, zo_c, zo_d, zd_a, zd_b, zd_c, zd_d,
    zg_a, zg_b, zg_c, zg_d, z_ss, z_sr, local, loads,
    n1_a, n1_b, n1_c, n1_d, ct_a, ct_b, ct_c, ct_d, n2_a, n2_b, n2_c, n2_d, wo_ga, wo_gb, wo_gc, wo_gd,
    rs_a, rs_b, rs_c, rs_d, at_s, at_r, gh_s, gh_r,
):
    n, sib, planes = dims
    at = Place(n, sib, planes)
    length, width = x.shape
    seq_len = n * length
    raw = len(wq_s.shape) == 2
    _, rows, head_cols = wq_b.shape
    owners = planes * sib
    chunks = GROUP * HEAD_DIM // rows
    units = dn_b.shape[0]
    local_units = planes * units
    parts = planes if units % 128 == 0 else 1
    wide = local_units // parts
    part_cols = wo_b.shape[1]
    heads_per = rows // HEAD_DIM
    half_len = length // 2
    tau = at.s * sib + at.c
    scale = HEAD_DIM ** (-0.5)
    log2e = 1.4426950408889634
    sent = []

    def token_part(ref):
        return lambda c, s, h: ref.at[c, s, pl.ds(h * half_len, half_len)]

    def owner_rows(f):
        return pl.ds(pl.multiple_of(f * rows, rows), rows)

    if raw:
        gu_f = (o_ghid, o_hidden)

        def cut(ref, k, lo, size, dst):
            return pltpu.make_async_copy(
                ref.at[:, pl.ds(pl.multiple_of(lo, 128), size)], dst, loads.at[k]
            )

        in_wq = cut(wq_s, 0, at.s * (sib * head_cols), sib * head_cols, wq_f)
        in_wo = cut(wo_s, 1, at.s * part_cols, part_cols, wo_f)
        in_dn = pltpu.make_async_copy(
            dn_s.at[pl.ds(pl.multiple_of(at.s * units, units), units)], dn_f, loads.at[2]
        )
        in_gu = []
        for c in range(sib):
            for p in range(planes):
                for g in range(2):
                    lo = (g * owners + p * sib + c) * (n * units) + at.s * units
                    k = (c * planes + p) * 2 + g
                    in_gu.append(
                        cut(gu_s, 3 + k, lo, units,
                            gu_f[c].at[pl.ds(0, rows), pl.ds((p * 2 + g) * units, units)])
                    )
        for copy in (in_wq, in_wo, in_dn, *in_gu):
            copy.start()
        wq_x, gu_x, dn_x, wo_x = wq_b, gu_b, dn_b, wo_b
    else:
        wq_x, gu_x, dn_x, wo_x = wq_s, gu_s, dn_s, wo_s

    move_wq = Move(at, lambda c: wq_x.at[c], lambda f: wq.at[owner_rows(f)], (zw_a, zw_b, zw_c, zw_d))
    move_wo = Move(
        at, lambda c: wo_x, lambda f: wo.at[lax.rem(f, sib), at.s, lax.div(f, sib)],
        (zo_a, zo_b, zo_c, zo_d), False,
    )
    move_dn = Move(
        at, lambda c: dn_x,
        lambda f: dn.at[pl.ds(pl.multiple_of(lax.div(f, sib) * units, units), units)],
        (zd_a, zd_b, zd_c, zd_d), False,
    )

    def gu_move(k):
        cols = pl.ds(k * 2 * wide, 2 * wide)
        return Move(
            at, lambda c: gu_x.at[c, :, cols], lambda f: gu.at[owner_rows(f), cols],
            (zg_a.at[k], zg_b.at[k], zg_c.at[k], zg_d.at[k]),
        )

    move_gu = [gu_move(k) for k in range(parts)]

    if raw:
        in_wq.wait()
        g_one = gain_cols[:, 0:1]
        for c in range(sib):
            wq_b[c] = (wq_f[:, c * head_cols : (c + 1) * head_cols] * g_one).astype(BF)
        in_wo.wait()
        wo_b[...] = wo_f[...].astype(BF)
    at.barrier()
    move_wq.start()
    move_wo.start()

    x_f = x[...].astype(F32)
    inv_one = lax.rsqrt(jnp.mean(x_f * x_f, axis=-1, keepdims=True) + NORM_EPS)
    nbuf[at.c, at.s] = (x_f * inv_one).astype(BF)
    cbuf[at.c, at.s] = cot[...]
    n_one = Gather(at, token_part(nbuf), (n1_a, n1_b, n1_c, n1_d))
    n_one.start()
    if raw:
        in_dn.wait()
        dn_b[...] = dn_f[...].astype(BF)
        for copy in in_gu:
            copy.wait()
        g_two = gain_cols[:, 1:2]
        for c in range(sib):
            gu_b[c] = (gu_f[c][0:rows, 0 : 2 * local_units] * g_two).astype(BF)
    move_wq.wait()
    move_dn.start()
    move_gu[0].start()

    @pl.loop(0, width // 256)
    def _(t):
        here = pl.ds(pl.multiple_of(t * 256, 256), 256)
        wqp[here] = nn(wq[here], widen[...]).astype(BF)

    save_wq = pltpu.make_async_copy(wqp, o_wq, local.at[2])
    save_wq.start()

    def project(c, s):
        y = nn(nbuf[c, s], wqp[...]).astype(BF)
        here = pl.ds(pl.multiple_of(s * length, length), length)
        cs, fr, bk = cos[here], front[here], back[here]
        for k in range(3):
            lanes = slice(128 * k, 128 * k + 128)
            qkv[c, here, lanes] = rope(y[:, lanes].astype(F32), cs, fr, bk).astype(BF)
        qkv[c, here, 384:512] = y[:, 384:512]

    for h, offsets in n_one.stages():
        n_one.wait_stage(h, offsets)
        for j in offsets:
            s_j = at.seq_at(j)

            @pl.loop(0, sib)
            def _(c):
                project(c, s_j)

    save_n1 = pltpu.make_async_copy(nbuf, o_n1, local.at[3])
    save_n1.start()
    save_qkv = pltpu.make_async_copy(qkv, o_qkv, local.at[4])
    save_qkv.start()

    tri = lax.broadcasted_iota(jnp.int32, (length, length), 0) >= lax.broadcasted_iota(
        jnp.int32, (length, length), 1
    )

    def spot(k, b, i):
        return (k * sib + b) * n + i

    def attend(i):
        @pl.loop(0, sib)
        def _(b):
            past = i * length
            here = slice(past, past + length)
            outs = []
            for h in range(GROUP):
                q = qkv[b, here, 128 * h : 128 * h + 128]
                d = jnp.where(tri, nt(q, qkv[b, here, 256:384]) * (scale * log2e), -1e30)
                m = jnp.max(d, axis=1, keepdims=True)
                if i:
                    e = nt(q, qkv[b, 0:past, 256:384]) * (scale * log2e)
                    m = jnp.maximum(m, jnp.max(e, axis=1, keepdims=True))
                d = jnp.exp2(d - m)
                total = jnp.sum(d, axis=1, keepdims=True)
                o = nn(d.astype(BF), qkv[b, here, 384:512])
                if i:
                    e = jnp.exp2(e - m)
                    total = total + jnp.sum(e, axis=1, keepdims=True)
                    o = o + nn(e.astype(BF), qkv[b, 0:past, 384:512])
                outs.append((o / total).astype(BF))
                lse = jnp.broadcast_to(m + jnp.log2(total), (length, 128))
                o_lse[b, h, i] = lse.T[0:8]
            for k in range(chunks):
                pair = jnp.concatenate(outs[k * heads_per : (k + 1) * heads_per], axis=1)
                att_out[spot(k, b, i)] = nt(pair, widen_att[...]).astype(BF)

    def send_attended(i):
        for k in range(chunks):
            for b in range(sib):
                mine = jnp.logical_and(at.s == i, at.c == b)

                @pl.when(mine)
                def _():
                    att_in[tau * chunks + k] = att_out[spot(k, b, i)]

                @pl.when(jnp.logical_not(mine))
                def _():
                    rdma(att_out.at[spot(k, b, i)], att_in.at[tau * chunks + k], at_s.at[k, b, i],
                         at_r.at[tau * chunks + k], at.dev(i, b)).start()

    wo_gather = Gather(
        at, lambda c, s, h: wo.at[c, s, pl.ds(h * (planes // 2), planes // 2)],
        (wo_ga, wo_gb, wo_gc, wo_gd),
    )
    cot_gather = Gather(at, token_part(cbuf), (ct_a, ct_b, ct_c, ct_d))
    attend(n - 1)
    save_n1.wait()
    n_one.drain()
    send_attended(n - 1)
    move_wo.wait()
    wo_gather.start()
    if parts > 1:
        move_gu[1].start()
    for i in range(n - 2, 0, -1):
        attend(i)
        send_attended(i)
    wo_hops = list(wo_gather.stages())
    for h, offsets in wo_hops[:-1]:
        wo_gather.wait_stage(h, offsets)
    attend(0)
    send_attended(0)
    cot_gather.start()
    wo_gather.wait_stage(*wo_hops[-1])
    wo_gather.drain()
    save_qkv.wait()
    save_wq.wait()

    group = n * sib
    for j in range(1, group):
        t = lax.rem(tau + j, group)
        for k in range(chunks):
            ref = att_in.at[t * chunks + k]
            rdma(ref, ref, at_s.at[0, 0, 0], at_r.at[t * chunks + k], at.dev(at.s, at.c)).wait_recv()
    for k in range(chunks):
        for i in range(n):
            for b in range(sib):
                @pl.when(jnp.logical_not(jnp.logical_and(at.s == i, at.c == b)))
                def _():
                    rdma(att_out.at[spot(k, b, i)], att_out.at[spot(k, b, i)], at_s.at[k, b, i],
                         at_r.at[0], at.dev(at.s, at.c)).wait_send()
    save_att = pltpu.make_async_copy(att_in, o_att, local.at[3])
    save_att.start()

    x_f = x[...].astype(F32)
    for s in range(n):
        cols = slice(s * part_cols, (s + 1) * part_cols)
        acc = x_f[:, cols]
        for p in range(planes):
            for c in range(sib):
                acc = acc + nn(att_in[p * sib + c], wo[c, s, p])
        o_hidden[:, cols] = acc
    hidden = o_hidden[...]
    inv_mid = lax.rsqrt(jnp.mean(hidden * hidden, axis=-1, keepdims=True) + NORM_EPS)
    nbuf[at.c, at.s] = (hidden * inv_mid).astype(BF)
    n_two = Gather(at, token_part(nbuf), (n2_a, n2_b, n2_c, n2_d))
    n_two.start()

    move_dn.wait()
    save_dn = pltpu.make_async_copy(dn, o_dn, local.at[4])
    save_dn.start()
    move_gu[0].wait()
    if parts > 2:
        move_gu[2].start()

    def feed_forward(k, n_here, cot_here, store):
        y = nn(n_here, gu[:, k * 2 * wide : (k + 1) * 2 * wide])
        gate, up = y[:, :wide], y[:, wide:]
        sig = 1.0 / (1.0 + jnp.exp(-gate))
        silu = gate * sig
        grad_act = nt(cot_here, dn[k * wide : (k + 1) * wide])
        store(act, k * wide, (silu * up).astype(BF))
        store(ggu, k * 2 * wide, (grad_act * up * sig * (1.0 + gate * (1.0 - sig))).astype(BF))
        store(ggu, k * 2 * wide + wide, (grad_act * silu).astype(BF))

    for h, offsets in n_two.stages():
        if h == n // 2 and parts > 1:
            move_gu[1].wait()
            if parts > 3:
                move_gu[3].start()
        cot_gather.wait_stage(h, offsets)
        n_two.wait_stage(h, offsets)
        for j in offsets:
            s_j = at.seq_at(j)

            @pl.loop(0, sib)
            def _(c):
                def store(ref, lo, value):
                    ref[c, s_j, :, lo : lo + wide] = value

                feed_forward(0, nbuf[c, s_j], cbuf[c, s_j], store)

    for k in range(1, parts):
        if k > 1:
            move_gu[k].wait()
            if k + 2 < parts and k + 2 > 3:
                move_gu[k + 2].start()

        @pl.loop(0, sib)
        def _(c):
            def store(ref, lo, value):
                ref[c, :, :, lo : lo + wide] = value.reshape(n, length, wide)

            feed_forward(
                k, nbuf[c].reshape(seq_len, width), cbuf[c].reshape(seq_len, width), store
            )

    save_act = pltpu.make_async_copy(act, o_act, local.at[5])
    save_act.start()

    scatter = Scatter(at, (sc_stage, sc_in, sc_out, sc_inn), (rs_a, rs_b, rs_c, rs_d), length, width)
    tile = 512

    def to_stage(c, s, ref):
        for t in range(width // tile):
            cols = slice(t * tile, (t + 1) * tile)
            ref[:, cols] = nt(ggu[c, s], gu[cols, :]).astype(BF)

    def to_ring(c, s, store):
        for t in range(width // tile):
            cols = slice(t * tile, (t + 1) * tile)
            store(cols, nt(ggu[c, s], gu[cols, :]))

    tokens = sib * seq_len
    down_copies = []

    def grad_down():
        cot_all = cbuf[...].reshape(tokens, width)
        down_rows = local_units // 2
        for t in range(2):
            rows_here = slice(t * down_rows, (t + 1) * down_rows)
            lhs = act[:, :, :, rows_here].reshape(tokens, down_rows)
            stg[rows_here] = tn(lhs, cot_all).astype(BF)
        own = pltpu.make_async_copy(
            stg.at[pl.ds(pl.multiple_of(at.p * units, units), units)], o_sdn.at[at.p], local.at[6]
        )
        own.start()
        down_copies.append(own)
        for dp in range(1, planes):
            to = lax.rem(at.p + dp, planes)
            copy = rdma(stg.at[pl.ds(pl.multiple_of(to * units, units), units)], o_sdn.at[at.p],
                        z_ss.at[dp], z_sr.at[dp], (at.s, at.col(dp, 0)))
            copy.start()
            sent.append(copy)

    gu_tile = sgu_t.shape[1]
    gu_steps = width // gu_tile

    def gu_copy(m, slot):
        return pltpu.make_async_copy(
            sgu_t.at[slot], o_sgu.at[pl.ds(m * gu_tile, gu_tile)], local.at[7 + slot]
        )

    def grad_gu(lo, hi):
        for m in range(lo, hi):
            slot = m % 2
            if m >= 2:
                gu_copy(m - 2, slot).wait()
            lhs = nbuf[:, :, :, m * gu_tile : (m + 1) * gu_tile].reshape(tokens, gu_tile)
            sgu_t[slot] = tn(lhs, ggu[...].reshape(tokens, 2 * local_units)).astype(BF)
            gu_copy(m, slot).start()

    def finish(cols, value):
        o_ghid[:, cols] = value

    n_sends = len(scatter.offsets())

    def between(k):
        if k == 0:
            grad_down()
            grad_gu(0, gu_steps // 3)
        if k == n_sends - 2:
            grad_gu(gu_steps // 3, gu_steps)

    scatter.to_sibling(to_stage)
    scatter.round(to_ring, between, finish)
    e_mid = o_ghid[...]
    hidden = o_hidden[...]
    inv_mid = lax.rsqrt(jnp.mean(hidden * hidden, axis=-1, keepdims=True) + NORM_EPS)
    norm_mid = hidden * inv_mid
    o_ghid[...] = cot[...].astype(F32) + inv_mid * (
        e_mid - norm_mid * jnp.mean(e_mid * norm_mid, axis=-1, keepdims=True)
    )
    branch = o_ghid[...].astype(BF)
    for f in range(owners):
        p, c = f // sib, f % sib
        acc = nt(branch[:, :part_cols], wo[c, 0, p])
        for s in range(1, n):
            acc = acc + nt(branch[:, s * part_cols : (s + 1) * part_cols], wo[c, s, p])
        att_out[f] = acc.astype(BF)
        t, k = f // chunks, f % chunks
        mine = tau == t

        @pl.when(mine)
        def _():
            gh_in[k, at.c, at.s] = att_out[f]

        @pl.when(jnp.logical_not(mine))
        def _():
            rdma(att_out.at[f], gh_in.at[k, at.c, at.s], gh_s.at[f], gh_r.at[k, tau],
                 at.dev(t // sib, t % sib)).start()

    for j in range(1, group):
        t = lax.rem(tau + j, group)
        for k in range(chunks):
            ref = gh_in.at[k, lax.rem(t, sib), lax.div(t, sib)]
            rdma(ref, ref, gh_s.at[0], gh_r.at[k, t], at.dev(at.s, at.c)).wait_recv()
    save_gh = pltpu.make_async_copy(gh_in, o_gh, local.at[0])
    save_gh.start()
    for f in range(owners):
        @pl.when(jnp.logical_not(tau == f // chunks))
        def _():
            rdma(att_out.at[f], att_out.at[f], gh_s.at[f], gh_r.at[0, 0],
                 at.dev(at.s, at.c)).wait_send()

    for dp in range(1, planes):
        ref = o_sdn.at[lax.rem(at.p - dp + planes, planes)]
        rdma(ref, ref, z_ss.at[dp], z_sr.at[dp], (at.s, at.f)).wait_recv()
    for copy in down_copies:
        copy.wait()
    for m in range(max(0, gu_steps - 2), gu_steps):
        gu_copy(m, m % 2).wait()
    cot_gather.drain()
    n_two.drain()
    scatter.drain()
    for move in (move_wq, move_wo, move_dn, *move_gu):
        move.drain()
    for copy in sent:
        copy.wait_send()
    save_att.wait()
    save_act.wait()
    save_dn.wait()
    save_gh.wait()


def forward_call(dims, sizes, x, cot, tables, widen, widen_att, gain_cols, wq_s, gu_s, dn_s, wo_s):
    n, sib, planes = dims
    rows, units = sizes
    length, width = x.shape
    part_cols = width // n
    head_cols = (GROUP + 2) * HEAD_DIM
    owners = planes * sib
    chunks = GROUP * HEAD_DIM // rows
    ffl = planes * units
    parts = planes if units % 128 == 0 else 1
    seq_len = n * length
    vm, hb = pl.BlockSpec(memory_space=pltpu.VMEM), pl.BlockSpec(memory_space=pl.ANY)
    blocks = (sib, n, length, width)
    sds = jax.ShapeDtypeStruct
    outs = [
        (sds(blocks, BF), hb),
        (sds((sib, seq_len, 512), BF), hb),
        (sds((sib, GROUP, n, 8, length), F32), vm),
        (sds((chunks, sib, n, length, rows), BF), hb),
        (sds((owners, length, rows), BF), hb),
        (sds((length, width), F32), vm),
        (sds((length, width), F32), vm),
        (sds((sib, n, length, ffl), BF), hb),
        (sds((ffl, width), BF), hb),
        (sds((width, 512), BF), hb),
        (sds((width, 2 * ffl), BF), hb),
        (sds((planes, units, width), BF), hb),
    ]
    dma = pltpu.SemaphoreType.DMA
    scratch = [
        pltpu.VMEM(blocks, BF), pltpu.VMEM(blocks, BF), pltpu.VMEM((sib, seq_len, 512), BF),
        pltpu.VMEM((width, head_cols), BF), pltpu.VMEM((width, 512), BF),
        pltpu.VMEM((sib, n, planes, rows, part_cols), BF),
        pltpu.VMEM((width, 2 * ffl), BF), pltpu.VMEM((ffl, width), BF),
        pltpu.VMEM((sib, n, length, ffl), BF), pltpu.VMEM((sib, n, length, 2 * ffl), BF),
        pltpu.VMEM((owners, length, rows), BF), pltpu.VMEM((owners, length, rows), BF),
        pltpu.VMEM((chunks, sib, n, length, rows), BF),
        pltpu.VMEM((ffl, width), BF), pltpu.VMEM((2, 256, 2 * ffl), BF),
        pltpu.VMEM((rows, sib * head_cols), F32), pltpu.VMEM((units, width), F32),
        pltpu.VMEM((rows, part_cols), F32),
        pltpu.VMEM((sib, rows, head_cols), BF), pltpu.VMEM((sib, rows, 2 * ffl), BF),
        pltpu.VMEM((units, width), BF), pltpu.VMEM((rows, part_cols), BF),
        *Scatter.scratch(n, (length, width)),
        *Move.sems(planes, sib), *Move.sems(planes, sib), *Move.sems(planes, sib),
        dma((parts, planes, sib)), dma((parts, planes, sib)), dma((parts, sib)), dma((parts, 1)),
        dma((planes,)), dma((planes,)), dma((9,)), dma((3 + 2 * owners,)),
        *Gather.scratch(n), *Gather.scratch(n), *Gather.scratch(n), *Gather.scratch(n),
        *Scatter.sems(n),
        dma((chunks, sib, n)), dma((owners,)), dma((owners,)), dma((chunks, n * sib)),
    ]
    return pl.pallas_call(
        functools.partial(forward_kernel, dims),
        out_shape=[o[0] for o in outs],
        out_specs=[o[1] for o in outs],
        in_specs=[vm] * 8 + [hb] * 4,
        scratch_shapes=scratch,
        compiler_params=pltpu.CompilerParams(
            collective_id=0, has_side_effects=True, vmem_limit_bytes=VMEM_LIMIT
        ),
    )(x, cot, *tables, widen, widen_att, gain_cols, wq_s, gu_s, dn_s, wo_s)


def backward_kernel(
    dims,
    x, cos, front, back, widen, widen_att, lse,
    n1, qkv_h, gh_h, att_h, hidden, ghid, act_h, dn_h, wqp_h, sgu, sdn_h,
    o_block, o_input, o_gq, o_ggu, o_gdn, o_gout,
    qkv, gh, att, act, dn, wqp, sdn, gq, gk, gv, n1_t, sq, so, branch,
    r_gu, r_qkv, r_out, g_gu, g_qkv, g_dn, g_out,
    sc_stage, sc_in, sc_out, sc_inn, e_stage_b, e_sib_b, e_out_b, e_inn_b, free,
    loads, z_gs, z_gr, z_qs, z_qr, z_os, z_or,
    d_a, d_b, d_c, d_d, e_a, e_b, e_c, e_d, s_a, s_b, s_c, s_d,
    a_dn_s, a_dn_r, a_gu_s, a_gu_r, a_qk_s, a_qk_r, a_ou_s, a_ou_r,
):
    n, sib, planes = dims
    at = Place(n, sib, planes)
    length, width = x.shape
    owners = planes * sib
    chunks, _, _, _, rows = gh.shape
    heads_per = rows // HEAD_DIM
    part_cols = r_out.shape[2]
    scale = HEAD_DIM ** (-0.5)
    log2e = 1.4426950408889634
    tokens = sib * n * length
    sent = []
    bufs = (sc_stage, sc_in, sc_out, sc_inn)

    def load(src, dst, k):
        copy = pltpu.make_async_copy(src, dst, loads.at[k])
        copy.start()
        return copy

    def owner_rows(f):
        return pl.ds(pl.multiple_of(f * rows, rows), rows)

    def z_source(dp, dc):
        return (
            lax.rem(at.p - dp + planes, planes) * sib + lax.rem(at.c - dc + sib, sib)
        )

    def z_scatter(src, dst, ssem, rsem, k):
        own = load(src.at[owner_rows(at.f)], dst.at[at.f], k)
        for dp in range(planes):
            for dc in range(sib):
                if dp or dc:
                    to = at.col(dp, dc)
                    copy = rdma(src.at[owner_rows(to)], dst.at[at.f],
                                ssem.at[dp, dc], rsem.at[dp, dc], (at.s, to))
                    copy.start()
                    sent.append(copy)
        return own

    def z_collect(dst, ssem, rsem, own):
        own.wait()
        for dp in range(planes):
            for dc in range(sib):
                if dp or dc:
                    ref = dst.at[z_source(dp, dc)]
                    rdma(ref, ref, ssem.at[dp, dc], rsem.at[dp, dc], (at.s, at.f)).wait_recv()

    def plane_total(dst, c):
        acc = dst[c].astype(F32)
        for p in range(1, planes):
            acc = acc + dst[p * sib + c].astype(F32)
        return acc.astype(BF)

    def release():
        if sib > 1:
            pl.semaphore_signal(free, inc=1, device_id=at.dev(at.s, 1 - at.c), device_id_type=MESH)
        for way in (1, -1):
            pl.semaphore_signal(
                free, inc=1, device_id=at.dev(at.seq_at(way), at.c), device_id_type=MESH
            )

    def acquire():
        pl.semaphore_wait(free, 3 if sib > 1 else 2)

    at.barrier()
    in_qkv, in_gh = load(qkv_h, qkv, 0), load(gh_h, gh, 1)
    in_act, in_dn, in_sdn = load(act_h, act, 2), load(dn_h, dn, 3), load(sdn_h, sdn, 4)
    gu_own = z_scatter(sgu, r_gu, z_gs, z_gr, 5)
    in_att, in_wqp = load(att_h, att, 6), load(wqp_h, wqp, 7)
    n1_cols = n1_t.shape[4]
    n1_steps = width // n1_cols

    def n1_load(m):
        return pltpu.make_async_copy(
            n1.at[:, :, :, pl.ds(m * n1_cols, n1_cols)], n1_t.at[m % 2], loads.at[8 + m % 2]
        )

    n1_load(0).start()
    n1_load(1).start()

    def row_half(ref):
        size = ref.shape[-2] // 2
        if len(ref.shape) == 4:
            return lambda c, s, h: ref.at[s, :, pl.ds(h * size, size)]
        return lambda c, s, h: ref.at[s, pl.ds(h * size, size)]

    in_sdn.wait()
    acc = sdn[0].astype(F32)
    for p in range(1, planes):
        acc = acc + sdn[p].astype(F32)
    g_dn[at.s] = acc.astype(BF)
    ag_dn = Gather(at, row_half(g_dn), (a_dn_s, a_dn_r))
    ag_dn.start()

    tri = lax.broadcasted_iota(jnp.int32, (length, length), 0) <= lax.broadcasted_iota(
        jnp.int32, (length, length), 1
    )

    def attend_back(b):
        gk[...] = jnp.zeros_like(gk)
        gv[...] = jnp.zeros_like(gv)
        for i in range(n):
            past = i * length
            here = slice(past, past + length)
            for h in range(GROUP):
                k, slot = h // heads_per, h % heads_per
                q = qkv[b, here, 128 * h : 128 * h + 128]
                do = nn(gh[k, b, i], widen_att[:, 128 * slot : 128 * slot + 128]).astype(BF)
                row = lse[b, h, i, 0:1]
                parts = [(here, True)] + ([(slice(0, past), False)] if i else [])
                probs, grads = [], []
                delta = 0.0
                for part, diagonal in parts:
                    sc = nt(qkv[b, part, 256:384], q) * (scale * log2e)
                    if diagonal:
                        sc = jnp.where(tri, sc, -1e30)
                    pr = jnp.exp2(sc - row)
                    dp = nt(qkv[b, part, 384:512], do)
                    delta = delta + jnp.sum(pr * dp, axis=0, keepdims=True)
                    probs.append(pr)
                    grads.append(dp)
                dq = jnp.zeros((length, 128), F32)
                for (part, _), pr, dp in zip(parts, probs, grads):
                    ds = (pr * (dp - delta) * scale).astype(BF)
                    gv[part] += nn(pr.astype(BF), do)
                    gk[part] += nn(ds, q)
                    dq = dq + tn(ds, qkv[b, part, 256:384])
                gq[b, here, 128 * h : 128 * h + 128] = rope(
                    dq, cos[here], -front[here], -back[here]
                ).astype(BF)
        for i in range(n):
            here = slice(i * length, (i + 1) * length)
            gq[b, here, 256:384] = rope(gk[here], cos[here], -front[here], -back[here]).astype(BF)
            gq[b, here, 384:512] = gv[here].astype(BF)

    tile = 512

    def tiles():
        return [slice(t * tile, (t + 1) * tile) for t in range(width // tile)]

    in_act.wait()
    in_dn.wait()
    down = Scatter(at, bufs, (d_a, d_b, d_c, d_d), length, width)

    def down_stage(c, s, ref):
        for cols in tiles():
            ref[:, cols] = nn(act[c, s], dn[:, cols]).astype(BF)

    def down_ring(c, s, store):
        for cols in tiles():
            store(cols, nn(act[c, s], dn[:, cols]))

    def down_finish(cols, value):
        o_block[:, cols] = (hidden[:, cols] + value).astype(BF)

    last = len(down.offsets()) - 1
    hops = n // 2
    down.to_sibling(down_stage)
    down.step(0, down_ring, down_finish)
    in_qkv.wait()
    in_gh.wait()
    attend_back(0)
    ag_dn.hop(1)
    for k in range(1, last):
        down.step(k, down_ring, down_finish)
    if sib > 1:
        attend_back(1)
    for h in range(2, hops + 1):
        ag_dn.hop(h)

    for m in range(n1_steps):
        n1_load(m).wait()
        part = tn(n1_t[m % 2].reshape(tokens, n1_cols), gq[...].reshape(tokens, 512)).astype(BF)
        sq[m * n1_cols : (m + 1) * n1_cols] = nt(part, widen[...]).astype(BF)
        if m + 2 < n1_steps:
            n1_load(m + 2).start()
    qkv_own = z_scatter(sq, r_qkv, z_qs, z_qr, 10)

    in_wqp.wait()
    in_att.wait()
    e_in = Scatter(
        at, (e_stage_b, e_sib_b, e_out_b, e_inn_b), (e_a, e_b, e_c, e_d), length, width
    )

    def gq_block(c, s):
        return gq[c, pl.ds(pl.multiple_of(s * length, length), length)]

    def e_stage(c, s, ref):
        for cols in tiles():
            ref[:, cols] = nt(gq_block(c, s), wqp[cols, :]).astype(BF)

    def e_ring(c, s, store):
        for cols in tiles():
            store(cols, nt(gq_block(c, s), wqp[cols, :]))

    def e_finish(cols, value):
        o_input[:, cols] = value

    e_in.to_sibling(e_stage)
    e_in.step(0, e_ring, e_finish)
    down.step(last, down_ring, down_finish)
    down.drain()
    release()
    for k in range(1, last):
        e_in.step(k, e_ring, e_finish)

    s_out = Scatter(at, bufs, (s_a, s_b, s_c, s_d), rows, planes * part_cols)
    for s in range(n):
        branch[s] = ghid[:, s * part_cols : (s + 1) * part_cols].astype(BF)

    def out_pieces(c, s):
        low = branch[s]
        for p in range(planes):
            yield slice(p * part_cols, (p + 1) * part_cols), tn(att[p * sib + c], low)

    def out_stage(c, s, ref):
        for cols, value in out_pieces(c, s):
            ref[:, cols] = value.astype(BF)

    def out_ring(c, s, store):
        for cols, value in out_pieces(c, s):
            store(cols, value)

    def out_finish(cols, value):
        so[cols.start // part_cols] = value.astype(BF)

    acquire()
    s_out.to_sibling(out_stage)
    s_out.step(0, out_ring, out_finish)
    e_in.step(last, e_ring, e_finish)
    for k in range(1, last):
        s_out.step(k, out_ring, out_finish)
    x_f = x[...].astype(F32)
    inv_one = lax.rsqrt(jnp.mean(x_f * x_f, axis=-1, keepdims=True) + NORM_EPS)
    norm_one = x_f * inv_one
    e_val = o_input[...]
    o_input[...] = ghid[...] + inv_one * (
        e_val - norm_one * jnp.mean(e_val * norm_one, axis=-1, keepdims=True)
    )
    s_out.step(last, out_ring, out_finish)
    out_own = load(so.at[at.p], r_out.at[at.p], 11)
    for dp in range(1, planes):
        to = lax.rem(at.p + dp, planes)
        copy = rdma(so.at[to], r_out.at[at.p], z_os.at[dp], z_or.at[dp], (at.s, at.col(dp, 0)))
        copy.start()
        sent.append(copy)

    z_collect(r_gu, z_gs, z_gr, gu_own)
    for c in range(sib):
        g_gu[at.s, c] = plane_total(r_gu, c)
    ag_gu = Gather(at, row_half(g_gu), (a_gu_s, a_gu_r))
    ag_gu.start()
    z_collect(r_qkv, z_qs, z_qr, qkv_own)
    for c in range(sib):
        g_qkv[at.s, c] = plane_total(r_qkv, c)
    ag_qkv = Gather(at, row_half(g_qkv), (a_qk_s, a_qk_r))
    ag_qkv.start()
    out_own.wait()
    for dp in range(1, planes):
        ref = r_out.at[lax.rem(at.p - dp + planes, planes)]
        rdma(ref, ref, z_os.at[dp], z_or.at[dp], (at.s, at.f)).wait_recv()
    acc = r_out[0].astype(F32)
    for p in range(1, planes):
        acc = acc + r_out[p].astype(F32)
    g_out[at.s] = acc.astype(BF)
    ag_out = Gather(at, row_half(g_out), (a_ou_s, a_ou_r))
    ag_out.start()
    save_dn = load(g_dn, o_gdn, 0)
    for h in range(1, hops + 1):
        for ag in (ag_gu, ag_qkv, ag_out):
            ag.hop(h)
    saves = [load(g_gu, o_ggu, 1), load(g_qkv, o_gq, 2), load(g_out, o_gout, 3), save_dn]
    e_in.drain()
    s_out.drain()
    for ag in (ag_dn, ag_gu, ag_qkv, ag_out):
        ag.drain()
    for copy in sent:
        copy.wait_send()
    for copy in saves:
        copy.wait()


def backward_call(dims, x, tables, widen, widen_att, lse, n1, qkv, gh, att, hidden, ghid, act, dn, wqp, sgu, sdn):
    n, sib, planes = dims
    length, width = x.shape
    chunks, _, _, _, rows = gh.shape
    owners = planes * sib
    units = sdn.shape[1]
    part_cols = width // n
    seq_len = n * length
    head_cols = (GROUP + 2) * HEAD_DIM
    vm, hb = pl.BlockSpec(memory_space=pltpu.VMEM), pl.BlockSpec(memory_space=pl.ANY)
    sds = jax.ShapeDtypeStruct
    g_shapes = [
        (n, sib, rows, head_cols), (n, sib, rows, sgu.shape[1]), (n, units, width),
        (n, rows, part_cols),
    ]
    outs = [(sds((length, width), BF), vm), (sds((length, width), F32), vm)] + [
        (sds(shape, BF), hb) for shape in g_shapes
    ]
    dma = pltpu.SemaphoreType.DMA
    scratch = [
        pltpu.VMEM(qkv.shape, BF), pltpu.VMEM(gh.shape, BF), pltpu.VMEM(att.shape, BF),
        pltpu.VMEM(act.shape, BF), pltpu.VMEM(dn.shape, BF), pltpu.VMEM(wqp.shape, BF),
        pltpu.VMEM(sdn.shape, BF), pltpu.VMEM(qkv.shape, BF),
        pltpu.VMEM((seq_len, 128), F32), pltpu.VMEM((seq_len, 128), F32),
        pltpu.VMEM((2, *n1.shape[:3], 384), BF), pltpu.VMEM((width, head_cols), BF),
        pltpu.VMEM((planes, rows, part_cols), BF), pltpu.VMEM((n, length, part_cols), BF),
        pltpu.VMEM((owners, rows, sgu.shape[1]), BF), pltpu.VMEM((owners, rows, head_cols), BF),
        pltpu.VMEM((planes, rows, part_cols), BF),
        pltpu.VMEM(g_shapes[1], BF), pltpu.VMEM(g_shapes[0], BF), pltpu.VMEM(g_shapes[2], BF),
        pltpu.VMEM(g_shapes[3], BF),
        *Scatter.scratch(n, (length, max(width, planes * part_cols))),
        *Scatter.scratch(n, (length, width)),
        pltpu.SemaphoreType.REGULAR,
        dma((12,)), dma((planes, sib)), dma((planes, sib)), dma((planes, sib)),
        dma((planes, sib)), dma((planes,)), dma((planes,)),
        *Scatter.sems(n), *Scatter.sems(n), *Scatter.sems(n),
        *Gather.scratch(n, False), *Gather.scratch(n, False), *Gather.scratch(n, False),
        *Gather.scratch(n, False),
    ]
    return pl.pallas_call(
        functools.partial(backward_kernel, dims),
        out_shape=[o[0] for o in outs],
        out_specs=[o[1] for o in outs],
        in_specs=[vm] * 7 + [hb] * 4 + [vm] * 2 + [hb] * 5,
        scratch_shapes=scratch,
        compiler_params=pltpu.CompilerParams(
            collective_id=1, has_side_effects=True, vmem_limit_bytes=VMEM_LIMIT
        ),
    )(x, *tables, widen, widen_att, lse, n1, qkv, gh, att, hidden, ghid, act, dn, wqp, sgu, sdn)


def adamw(weight, first, second, grad, rate, decay):
    first_new = BETA_ONE * first + (1.0 - BETA_ONE) * grad
    second_new = BETA_TWO * second + (1.0 - BETA_TWO) * grad * grad
    first_hat = first_new / (1.0 - BETA_ONE**ADAM_STEP)
    second_hat = second_new / (1.0 - BETA_TWO**ADAM_STEP)
    weight_new = weight - rate * (first_hat / (jnp.sqrt(second_hat) + ADAM_EPS) + decay * weight)
    return (weight_new, first_new, second_new)


def adam_kernel(rate, decay, scale_col, spread, *refs):
    if scale_col is None:
        w, m, v, g, w_new, m_new, v_new = refs
    else:
        w, m, v, g, gains, w_new, m_new, v_new, total = refs
    weight = w[...]
    grad = g[...].astype(F32)
    grad = grad.reshape(-1, *weight.shape[:1], spread)
    grad = jnp.concatenate([grad[i] for i in range(grad.shape[0])], axis=1)
    if scale_col is not None:
        @pl.when(pl.program_id(0) == 0)
        def _():
            total[...] = jnp.zeros_like(total)

        product = weight.astype(BF).astype(F32) * grad
        acc = product[:, :128]
        for k in range(1, product.shape[1] // 128):
            acc = acc + product[:, 128 * k : 128 * k + 128]
        total[...] += acc
        grad = grad * gains[:, scale_col : scale_col + 1]
    first, second = BETA_ONE * m[...] + (1.0 - BETA_ONE) * grad, BETA_TWO * v[...] + (
        1.0 - BETA_TWO
    ) * grad * grad
    m_new[...] = first
    v_new[...] = second
    step = (first * (1.0 / (1.0 - BETA_ONE**ADAM_STEP))) / (
        jnp.sqrt(second * (1.0 / (1.0 - BETA_TWO**ADAM_STEP))) + ADAM_EPS
    )
    w_new[...] = weight - rate * (step + decay * weight)


def adam_call(weight, first, second, grad, block, place, grad_block, grad_place, rate, spread,
              gain_cols=None, scale_col=None):
    steps = weight.size // (block[0] * block[1])
    spec = pl.BlockSpec(block, place)
    in_specs = [spec] * 3 + [pl.BlockSpec(grad_block, grad_place)]
    out_specs = [spec] * 3
    out_shape = [jax.ShapeDtypeStruct(weight.shape, F32)] * 3
    args = [weight, first, second, grad]
    if scale_col is not None:
        in_specs.append(pl.BlockSpec(gain_cols.shape, lambda i: (0, 0)))
        out_specs.append(pl.BlockSpec((block[0], 128), lambda i: (0, 0)))
        out_shape.append(jax.ShapeDtypeStruct((block[0], 128), F32))
        args.append(gain_cols)
    return pl.pallas_call(
        functools.partial(adam_kernel, rate, WEIGHT_DECAY, scale_col, spread),
        grid=(steps,), in_specs=in_specs, out_specs=out_specs, out_shape=out_shape,
        compiler_params=pltpu.CompilerParams(vmem_limit_bytes=VMEM_LIMIT),
    )(*args)


def rope_arrays(seq_len):
    half = HEAD_DIM // 2
    frequencies = (ROPE_BASE ** (-(2.0 * np.arange(half)) / HEAD_DIM)).astype(np.float32)
    angles = np.arange(seq_len, dtype=np.float32)[:, None] * frequencies[None, :]
    cos, sin = np.cos(angles), np.sin(angles)
    pad = np.zeros((seq_len, 128 - HEAD_DIM), np.float32)
    none = np.zeros_like(sin)
    return tuple(
        np.concatenate(columns, axis=1).astype(np.float32)
        for columns in ([cos, cos, pad], [-sin, none, pad], [none, sin, pad])
    )


def widening(heads):
    row = np.arange(heads * HEAD_DIM)[:, None]
    col = np.arange(heads * 128)[None, :]
    return (col == row // HEAD_DIM * 128 + row % HEAD_DIM).astype(ml_dtypes.bfloat16)


def make(n_seq, n_fsdp):
    sib = KV_HEADS // n_seq
    planes = n_fsdp // sib

    def on_device(
        inputs, cotangent, qkv_weight, out_weight, gate_up_weight, down_weight, norm_gains,
        qkv_first, qkv_second, out_first, out_second, gate_up_first, gate_up_second,
        down_first, down_second, gain_first, gain_second,
    ):
        s_idx = lax.axis_index("seq")
        _, length, width = inputs.shape
        seq_len = length * n_seq
        rows = qkv_weight.shape[0]
        head_cols = (GROUP + 2) * HEAD_DIM
        ff_rows = down_weight.shape[0]
        units = ff_rows // n_seq
        hidden_units = ff_rows * n_fsdp
        part_cols = width // n_seq
        aligned = units % 128 == 0 and part_cols % 128 == 0
        gains = norm_gains.astype(BF).astype(F32)
        gain_cols = gains.T

        if aligned:
            pieces = (qkv_weight, gate_up_weight, down_weight, out_weight)
        else:
            wq_s = lax.dynamic_slice_in_dim(
                qkv_weight, s_idx * sib * head_cols, sib * head_cols, 1
            )
            wq_s = (wq_s * gains[0][:, None]).astype(BF).reshape(rows, sib, head_cols)
            gu_s = gate_up_weight.reshape(rows, 2, planes, sib, n_seq, units)
            gu_s = lax.dynamic_index_in_dim(gu_s, s_idx, 4, keepdims=False)
            gu_s = (gu_s * gains[1][:, None, None, None, None]).astype(BF)
            gu_s = gu_s.transpose(3, 0, 1, 2, 4).reshape(sib, rows, 2 * planes * units)
            dn_s = lax.dynamic_slice_in_dim(down_weight, s_idx * units, units, 0).astype(BF)
            wo_s = lax.dynamic_slice_in_dim(out_weight, s_idx * part_cols, part_cols, 1).astype(BF)
            pieces = (wq_s.transpose(1, 0, 2), gu_s, dn_s, wo_s)
        tables = tuple(jnp.asarray(table) for table in rope_arrays(seq_len))
        widen = jnp.asarray(widening(GROUP + 2))
        widen_att = jnp.asarray(widening(rows // HEAD_DIM))

        (n_one, qkv, lse, gh, att, hidden, grad_hidden, act, w_down, w_qkv, s_gu, s_down) = forward_call(
            (n_seq, sib, planes), (rows, units), inputs[0], cotangent[0], tables, widen, widen_att,
            gain_cols, *pieces,
        )
        block_out, input_grad, g_qkv, g_gu, g_down, g_out = backward_call(
            (n_seq, sib, planes), inputs[0], tables, widen, widen_att, lse, n_one, qkv, gh, att,
            hidden, grad_hidden, act, w_down, w_qkv, s_gu, s_down,
        )
        block_out, input_grad = block_out[None], input_grad[None]
        if aligned:
            *qkv_new, qkv_total = adam_call(
                qkv_weight, qkv_first, qkv_second, g_qkv, (rows, head_cols), lambda i: (0, i),
                (1, 1, rows, head_cols), lambda i: (i // sib, i % sib, 0, 0), RATE_QKV, head_cols,
                gain_cols, 0,
            )
            out_new = adam_call(
                out_weight, out_first, out_second, g_out, (rows, part_cols), lambda i: (0, i),
                (1, rows, part_cols), lambda i: (i, 0, 0), RATE_OUT, part_cols,
            )
            *gu_new, gu_total = adam_call(
                gate_up_weight, gate_up_first, gate_up_second, g_gu, (rows, ff_rows),
                lambda i: (0, i), (n_seq, 1, rows, units),
                lambda i: (0, i % sib, 0, i // sib % planes * 2 + i // n_fsdp),
                RATE_GATE_UP, units, gain_cols, 1,
            )
            down_new = adam_call(
                down_weight, down_first, down_second, g_down, (units, width), lambda i: (i, 0),
                (1, units, width), lambda i: (i, 0, 0), RATE_DOWN, width,
            )
            gain_grad = jnp.stack([jnp.sum(qkv_total, axis=1), jnp.sum(gu_total, axis=1)])
        else:
            g_qkv = g_qkv.transpose(2, 0, 1, 3).reshape(rows, n_seq * sib * head_cols).astype(F32)
            g_gu = g_gu.reshape(n_seq, sib, rows, 2, planes, units).transpose(2, 3, 4, 1, 0, 5)
            g_gu = g_gu.reshape(rows, 2 * hidden_units).astype(F32)
            g_down = g_down.reshape(ff_rows, width).astype(F32)
            g_out = g_out.transpose(1, 0, 2).reshape(rows, width).astype(F32)
            gain_grad = jnp.stack(
                [
                    jnp.sum(g_qkv * qkv_weight.astype(BF).astype(F32), axis=1),
                    jnp.sum(g_gu * gate_up_weight.astype(BF).astype(F32), axis=1),
                ]
            )
            g_qkv = g_qkv * gains[0][:, None]
            g_gu = g_gu * gains[1][:, None]
            qkv_new = adamw(qkv_weight, qkv_first, qkv_second, g_qkv, RATE_QKV, WEIGHT_DECAY)
            out_new = adamw(out_weight, out_first, out_second, g_out, RATE_OUT, WEIGHT_DECAY)
            gu_new = adamw(
                gate_up_weight, gate_up_first, gate_up_second, g_gu, RATE_GATE_UP, WEIGHT_DECAY
            )
            down_new = adamw(
                down_weight, down_first, down_second, g_down, RATE_DOWN, WEIGHT_DECAY
            )
        gains_new = adamw(norm_gains, gain_first, gain_second, gain_grad, RATE_GAINS, 0.0)
        return (block_out, input_grad, *qkv_new, *out_new, *gu_new, *down_new, *gains_new)

    return on_device


def solution(mesh):
    tokens = P("fsdp", "seq", None)
    weight = P("fsdp", None)
    gain = P(None, "fsdp")
    in_specs = (tokens, tokens, weight, weight, weight, weight, gain) + (weight,) * 8 + (gain,) * 2
    out_specs = (tokens, tokens) + (weight,) * 12 + (gain,) * 3
    return jax.shard_map(
        make(mesh.shape["seq"], mesh.shape["fsdp"]),
        mesh=mesh, in_specs=in_specs, out_specs=out_specs, check_vma=False,
    )
```

```python
import functools

import jax
import jax.numpy as jnp
import ml_dtypes
import numpy as np
from jax import lax
from jax.experimental import pallas as pl
from jax.experimental.pallas import tpu as pltpu
from jax.sharding import PartitionSpec as P

HEAD_DIM = 96
KV_HEADS = 8
ADAM_STEP = 10
GROUP = 2

NORM_EPS = 1e-05
ROPE_BASE = 100000.0
BETA_ONE = 0.9
BETA_TWO = 0.95
ADAM_EPS = 1e-08
WEIGHT_DECAY = 0.1
RATE_QKV = 0.07
RATE_OUT = 0.8
RATE_GATE_UP = 0.07
RATE_DOWN = 0.045
RATE_GAINS = 0.6
BF = jnp.bfloat16
F32 = jnp.float32
VMEM_LIMIT = 62 * 1024 * 1024


MESH = pl.DeviceIdType.MESH


def rdma(src, dst, ssem, rsem, dev):
    return pltpu.make_async_remote_copy(
        src_ref=src, dst_ref=dst, send_sem=ssem, recv_sem=rsem, device_id=dev, device_id_type=MESH
    )


class Place:
    def __init__(self, n, sib, planes):
        self.n, self.sib, self.planes = n, sib, planes
        self.s = lax.axis_index("seq")
        self.f = lax.axis_index("fsdp")
        self.c = lax.rem(self.f, sib)
        self.p = lax.div(self.f, sib)
        a, b = lax.div(self.s, 2), lax.rem(self.s, 2)
        self.r = a * (1 - b) + (n - 1 - a) * b

    def seq_at(self, j):
        if j == 0:
            return self.s
        n = self.n
        q = lax.rem(self.r + (j + n), n)
        t = lax.div(q, n // 2)
        return (1 - t) * 2 * q + t * (2 * (n - 1 - q) + 1)

    def dev(self, s, c):
        return (s, self.p * self.sib + c)

    def col(self, dp, dc):
        return lax.rem(self.p + dp, self.planes) * self.sib + lax.rem(self.c + dc, self.sib)

    def barrier(self):
        sem = pltpu.get_barrier_semaphore()
        group = self.n * self.sib
        tau = self.s * self.sib + self.c
        for j in range(1, group):
            t = lax.rem(tau + j, group)
            pl.semaphore_signal(
                sem, inc=1, device_id=self.dev(lax.div(t, self.sib), lax.rem(t, self.sib)),
                device_id_type=MESH,
            )
        for dp in range(1, self.planes):
            for dc in range(self.sib):
                pl.semaphore_signal(
                    sem, inc=1, device_id=(self.s, self.col(dp, dc)), device_id_type=MESH
                )
        pl.semaphore_wait(sem, group - 1 + (self.planes - 1) * self.sib)


class Gather:
    def __init__(self, at, part, sems):
        self.at, self.part = at, part
        self.ring_s, self.ring_r = sems[:2]
        self.share = at.sib > 1 and len(sems) > 2
        if self.share:
            self.sib_s, self.sib_r = sems[2:]
        self.sent = []

    @staticmethod
    def scratch(n, share=True):
        d = pltpu.SemaphoreType.DMA
        ring = [d((2, n // 2, 2)), d((2, n // 2, 2))]
        return ring + [d((n, 2)), d((n, 2))] if share else ring

    def _send(self, copy):
        copy.start()
        self.sent.append(copy)

    def _ring(self, way, hop, half):
        at = self.at
        src = self.part(at.c, at.seq_at(-(hop - 1) if way == 0 else hop - 1), half)
        to = at.dev(at.seq_at(1 if way == 0 else -1), at.c)
        self._send(
            rdma(src, src, self.ring_s.at[way, hop - 1, half], self.ring_r.at[way, hop - 1, half], to)
        )

    def _sib(self, j, half):
        at = self.at
        if self.share:
            src = self.part(at.c, at.seq_at(j), half)
            slot = j % at.n
            self._send(
                rdma(src, src, self.sib_s.at[slot, half], self.sib_r.at[slot, half],
                     at.dev(at.s, 1 - at.c))
            )

    def start(self):
        self._ring(0, 1, 0)
        self._ring(1, 1, 1)
        self._ring(0, 1, 1)
        self._ring(1, 1, 0)
        self._sib(0, 0)
        self._sib(0, 1)

    def _arrive(self, way, hop, half):
        at = self.at
        j = -hop if way == 0 else hop
        ref = self.part(at.c, at.seq_at(j), half)
        rdma(ref, ref, self.ring_s.at[way, hop - 1, half], self.ring_r.at[way, hop - 1, half],
             at.dev(at.s, at.c)).wait_recv()
        last = at.n // 2
        if hop + 1 < last or (hop + 1 == last and half == way):
            self._ring(way, hop + 1, half)
        if hop == last:
            j = last
        self._sib(j, half)

    def hop(self, hop):
        self._arrive(0, hop, 0)
        self._arrive(1, hop, 1)
        if hop < self.at.n // 2:
            self._arrive(0, hop, 1)
            self._arrive(1, hop, 0)

    def sib_wait(self, j):
        at = self.at
        if self.share:
            for half in range(2):
                ref = self.part(1 - at.c, at.seq_at(j), half)
                slot = j % at.n
                rdma(ref, ref, self.sib_s.at[slot, half], self.sib_r.at[slot, half],
                     at.dev(at.s, at.c)).wait_recv()

    def stages(self):
        last = self.at.n // 2
        yield 0, [0]
        for h in range(1, last):
            yield h, [-h, h]
        yield last, [last]

    def wait_stage(self, h, offsets):
        if h:
            self.hop(h)
        for j in offsets:
            self.sib_wait(j)

    def drain(self):
        for copy in self.sent:
            copy.wait_send()


class Move:
    def __init__(self, at, src, dst, sems, every_core=True):
        self.at, self.src, self.dst = at, src, dst
        self.ssem, self.rsem, self.hop, self.own = sems
        self.cores = at.sib if every_core else 1
        self.relay = at.planes == 4

    @staticmethod
    def sems(planes, sib):
        d = pltpu.SemaphoreType.DMA
        return [d((planes, sib)), d((planes, sib)), d((sib,)), d((1,))]

    def _pairs(self):
        for dp in [2, 1, 3] if self.relay else range(1, self.at.planes):
            for dc in range(self.cores):
                yield dp, dc
        for dc in range(1, self.cores):
            yield 0, dc

    def _direct(self, dp, body):
        if self.relay and dp in (1, 3):
            pl.when(self.at.p != (3 if dp == 1 else 0))(body)
        else:
            body()

    def _send(self, dp, dc):
        at = self.at
        return rdma(self.src(lax.rem(at.c + dc, at.sib)), self.dst(at.f), self.ssem.at[dp, dc],
                    self.rsem.at[dp, dc], (at.s, at.col(dp, dc)))

    def _local(self):
        return pltpu.make_async_copy(self.src(self.at.c), self.dst(self.at.f), self.own.at[0])

    def start(self):
        self._local().start()
        for dp, dc in self._pairs():
            self._direct(dp, lambda: self._send(dp, dc).start())

    def wait(self):
        at = self.at
        for dp, dc in self._pairs():
            source = lax.rem(at.p - dp + at.planes, at.planes) * at.sib + lax.rem(
                at.c - dc + at.sib, at.sib
            )
            ref = self.dst(source)
            rdma(ref, ref, self.ssem.at[dp, dc], self.rsem.at[dp, dc], (at.s, at.f)).wait_recv()
            if self.relay and dp == 2:
                for here, to, slot in ((2, 3, 3), (1, 0, 1)):
                    @pl.when(at.p == here)
                    def _():
                        rdma(ref, ref, self.hop.at[dc], self.rsem.at[slot, dc],
                             (at.s, to * at.sib + at.c)).start()
        self._local().wait()

    def drain(self):
        at = self.at
        for dp, dc in self._pairs():
            self._direct(dp, lambda: self._send(dp, dc).wait_send())
            if self.relay and dp == 2:
                ref = self.dst(at.f)

                @pl.when(jnp.logical_or(at.p == 1, at.p == 2))
                def _():
                    rdma(ref, ref, self.hop.at[dc], self.rsem.at[0, dc], (at.s, at.f)).wait_send()


class Scatter:
    def __init__(self, at, bufs, sems, rows, cols):
        self.at, self.rows, self.cols = at, rows, pl.ds(0, cols)
        self.stage, self.sib_in, self.out, self.inn = bufs
        self.sib_s, self.sib_r, self.ring_s, self.ring_r = sems
        self.sent = []

    @staticmethod
    def scratch(n, shape):
        return [
            pltpu.VMEM((2, *shape), BF), pltpu.VMEM((n, *shape), BF),
            pltpu.VMEM((2, n // 2, *shape), BF), pltpu.VMEM((2, n // 2, *shape), BF),
        ]

    @staticmethod
    def views(stage, sib_in, out, inn):
        return (
            lambda k: stage.at[k], lambda k: sib_in.at[k],
            lambda w, k: out.at[w, k], lambda w, k: inn.at[w, k],
        )

    @staticmethod
    def sems(n):
        d = pltpu.SemaphoreType.DMA
        return [d((n,)), d((n,)), d((2, n // 2)), d((2, n // 2))]

    def offsets(self):
        last = self.at.n // 2
        order = [last]
        for h in range(last - 1, 0, -1):
            order += [h, -h]
        return order + [0]

    def to_sibling(self, produce):
        at = self.at
        if at.sib == 1:
            return
        copies = []
        for k, j in enumerate(self.offsets()):
            if k >= 2:
                copies[k - 2].wait_send()
            view = self.stage(k % 2).at[pl.ds(0, self.rows), self.cols]
            produce(1 - at.c, at.seq_at(j), view)
            copy = rdma(view, self.sib_in(k).at[pl.ds(0, self.rows), self.cols],
                        self.sib_s.at[k], self.sib_r.at[k], at.dev(at.s, 1 - at.c))
            copy.start()
            copies.append(copy)
        self.sent += copies[-2:]

    def _send(self, way, k, rows):
        at = self.at
        src = self.out(way, k).at[rows, self.cols]
        copy = rdma(src, self.inn(way, k).at[rows, self.cols], self.ring_s.at[way, k], self.ring_r.at[way, k],
                    at.dev(at.seq_at(1 if way == 0 else -1), at.c))
        copy.start()
        self.sent.append(copy)

    def _wait(self, way, k, rows):
        ref = self.inn(way, k).at[rows, self.cols]
        at = self.at
        rdma(ref, ref, self.ring_s.at[way, k], self.ring_r.at[way, k],
             at.dev(at.s, at.c)).wait_recv()

    def round(self, produce, between, finish):
        for k in range(len(self.offsets())):
            self.step(k, produce, finish)
            between(k)

    def step(self, k, produce, finish):
        at = self.at
        last = at.n // 2
        length = self.rows
        half = length // 2
        halves = (pl.ds(0, half), pl.ds(half, half))
        whole = pl.ds(0, length)
        j = self.offsets()[k]
        if at.sib > 1:
            ref = self.sib_in(k).at[pl.ds(0, length), self.cols]
            rdma(ref, ref, self.sib_s.at[k], self.sib_r.at[k], at.dev(at.s, at.c)).wait_recv()
        h = abs(j)
        if h == last:
            got = []
        else:
            ways = (0, 1) if h == 0 else ((0,) if j > 0 else (1,))
            rows_in = [halves[w] if h + 1 == last else whole for w in ways]
            got = [(w, rw) for w, rw in zip(ways, rows_in)]
        pending = [True]

        def store(cols, value, k=k, h=h, j=j, got=got, pending=pending):
            if pending[0]:
                for w, rw in got:
                    self._wait(w, h, rw)
                pending[0] = False
            if at.sib > 1:
                value = value + self.sib_in(k)[pl.ds(0, length), cols].astype(F32)
            for w, rw in got:
                if h + 1 == last:
                    add = self.inn(w, h)[pl.ds(w * half, half), cols].astype(F32)
                    if w == 0:
                        value = jnp.concatenate([value[:half] + add, value[half:]], axis=0)
                    else:
                        value = jnp.concatenate([value[:half], value[half:] + add], axis=0)
                else:
                    value = value + self.inn(w, h)[pl.ds(0, length), cols].astype(F32)
            if h == last:
                low = value.astype(BF)
                self.out(0, h - 1)[pl.ds(0, half), cols] = low[:half]
                self.out(1, h - 1)[pl.ds(half, half), cols] = low[half:]
            elif h:
                self.out(0 if j > 0 else 1, h - 1)[pl.ds(0, length), cols] = value.astype(BF)
            else:
                finish(cols, value)

        produce(at.c, at.seq_at(j), store)
        if h == last:
            self._send(0, h - 1, halves[0])
            self._send(1, h - 1, halves[1])
        elif h:
            self._send(0 if j > 0 else 1, h - 1, whole)

    def drain(self):
        for copy in self.sent:
            copy.wait_send()


class Credits:
    def __init__(self, at, sem):
        self.at, self.sem = at, sem

    def give(self):
        at = self.at
        if at.sib > 1:
            pl.semaphore_signal(
                self.sem, inc=1, device_id=at.dev(at.s, 1 - at.c), device_id_type=MESH
            )
        for way in (1, -1):
            pl.semaphore_signal(
                self.sem, inc=1, device_id=at.dev(at.seq_at(way), at.c), device_id_type=MESH
            )

    def take(self):
        pl.semaphore_wait(self.sem, 3 if self.at.sib > 1 else 2)


def nt(a, b):
    return lax.dot_general(a, b, (((1,), (1,)), ((), ())), preferred_element_type=F32)


def tn(a, b):
    return lax.dot_general(a, b, (((0,), (0,)), ((), ())), preferred_element_type=F32)


def nn(a, b):
    return lax.dot_general(a, b, (((1,), (0,)), ((), ())), preferred_element_type=F32)


def rope(value, cos, front, back):
    return value * cos + pltpu.roll(value, 80, 1) * front + pltpu.roll(value, 48, 1) * back


def forward_kernel(
    dims,
    x, cot, cos, front, back, widen, widen_att, gain_cols, wq_s, gu_s, dn_s, wo_s,
    o_n1, o_qkv, o_lse, o_gh, o_att, o_block, o_ghid, o_wq, o_sgu, o_rgu, o_sdn,
    hid,
    nbuf, cbuf, qkv, wq, wqp, wo, gu, dn, act, ggu, att_out, att_in, gh_in, stg, sgu_t,
    wo_f, wq_b, gu_b, dn_b, wo_b,
    sc_stage, sc_in, sc_out, sc_inn,
    zw_a, zw_b, zw_c, zw_d, zo_a, zo_b, zo_c, zo_d, zd_a, zd_b, zd_c, zd_d,
    zg_a, zg_b, zg_c, zg_d, z_ss, z_sr, local, loads,
    n1_a, n1_b, n1_c, n1_d, ct_a, ct_b, ct_c, ct_d, n2_a, n2_b, n2_c, n2_d, wo_ga, wo_gb, wo_gc, wo_gd,
    rs_a, rs_b, rs_c, rs_d, ds_a, ds_b, ds_c, ds_d, at_s, at_r, gh_s, gh_r, near_s, near_r, free,
):
    n, sib, planes = dims
    at = Place(n, sib, planes)
    length, width = x.shape
    seq_len = n * length
    raw = len(wq_s.shape) == 2
    _, rows, head_cols = wq_b.shape
    owners = planes * sib
    chunks = GROUP * HEAD_DIM // rows
    units = dn_b.shape[0]
    local_units = planes * units
    parts = planes if units % 128 == 0 else 1
    wide = local_units // parts
    part_cols = wo_b.shape[1]
    heads_per = rows // HEAD_DIM
    half_len = length // 2
    tau = at.s * sib + at.c
    scale = HEAD_DIM ** (-0.5)
    log2e = 1.4426950408889634
    sent = []

    def token_part(ref):
        return lambda c, s, h: ref.at[c, s, pl.ds(h * half_len, half_len)]

    def owner_rows(f):
        return pl.ds(pl.multiple_of(f * rows, rows), rows)

    if raw:
        gu_f = (o_ghid, hid)

        def cut(ref, k, lo, size, dst):
            return pltpu.make_async_copy(
                ref.at[:, pl.ds(pl.multiple_of(lo, 128), size)], dst, loads.at[k]
            )

        def wq_f(c):
            return gu_f[c].at[pl.ds(0, rows), pl.ds(2 * local_units, head_cols)]

        in_wq = [
            cut(wq_s, 3 + 2 * owners + c, (at.s * sib + c) * head_cols, head_cols, wq_f(c))
            for c in range(sib)
        ]
        in_wo = cut(wo_s, 1, at.s * part_cols, part_cols, wo_f)
        half_units = units // 2

        def dn_f(h):
            return gu_f[h].at[pl.ds(rows, half_units)]

        in_dn = [
            pltpu.make_async_copy(
                dn_s.at[pl.ds(pl.multiple_of(at.s * units + h * half_units, half_units), half_units)],
                dn_f(h), loads.at[2 * h],
            )
            for h in range(2)
        ]
        in_gu = []
        for c in range(sib):
            for p in range(planes):
                for g in range(2):
                    lo = (g * owners + p * sib + c) * (n * units) + at.s * units
                    k = (c * planes + p) * 2 + g
                    in_gu.append(
                        cut(gu_s, 3 + k, lo, units,
                            gu_f[c].at[pl.ds(0, rows), pl.ds((p * 2 + g) * units, units)])
                    )
        for copy in (*in_wq, in_wo, *in_dn, *in_gu):
            copy.start()
        wq_x, gu_x, dn_x, wo_x = wq_b, gu_b, dn_b, wo_b
    else:
        wq_x, gu_x, dn_x, wo_x = wq_s, gu_s, dn_s, wo_s

    move_wq = Move(at, lambda c: wq_x.at[c], lambda f: wq.at[owner_rows(f)], (zw_a, zw_b, zw_c, zw_d))
    move_wo = Move(
        at, lambda c: wo_x, lambda f: wo.at[lax.rem(f, sib), at.s, lax.div(f, sib)],
        (zo_a, zo_b, zo_c, zo_d), False,
    )
    move_dn = Move(
        at, lambda c: dn_x,
        lambda f: dn.at[pl.ds(pl.multiple_of(lax.div(f, sib) * units, units), units)],
        (zd_a, zd_b, zd_c, zd_d), False,
    )

    def gu_move(k):
        return Move(
            at, lambda c: gu_x.at[k, c], lambda f: gu.at[k, owner_rows(f)],
            (zg_a.at[k], zg_b.at[k], zg_c.at[k], zg_d.at[k]),
        )

    move_gu = [gu_move(k) for k in range(parts)]

    x_f = x[...].astype(F32)
    inv_one = lax.rsqrt(jnp.mean(x_f * x_f, axis=-1, keepdims=True) + NORM_EPS)
    nbuf[at.c, at.s] = (x_f * inv_one).astype(BF)
    cbuf[at.c, at.s] = cot[...]
    n_one = Gather(at, token_part(nbuf), (n1_a, n1_b, n1_c, n1_d))
    at.barrier()
    n_one.start()
    if raw:
        g_one = gain_cols[:, 0:1]
        for c in range(sib):
            in_wq[c].wait()
            wq_b[c] = (wq_f(c)[...] * g_one).astype(BF)
        in_wo.wait()
        wo_b[...] = wo_f[...].astype(BF)
    move_wq.start()
    move_wo.start()
    if raw:
        for h in range(2):
            in_dn[h].wait()
            dn_b[h * half_units : (h + 1) * half_units] = dn_f(h)[...].astype(BF)
        for copy in in_gu:
            copy.wait()
        g_two = gain_cols[:, 1:2]
        for c in range(sib):
            for k in range(parts):
                lanes = slice(k * 2 * wide, (k + 1) * 2 * wide)
                gu_b[k, c] = (gu_f[c][0:rows, lanes] * g_two).astype(BF)
    move_wq.wait()
    move_dn.start()
    move_gu[0].start()

    @pl.loop(0, width // 256)
    def _(t):
        here = pl.ds(pl.multiple_of(t * 256, 256), 256)
        wqp[here] = nn(wq[here], widen[...]).astype(BF)

    save_wq = pltpu.make_async_copy(wqp, o_wq, local.at[2])
    save_wq.start()

    def project(c, s):
        y = nn(nbuf[c, s], wqp[...]).astype(BF)
        here = pl.ds(pl.multiple_of(s * length, length), length)
        cs, fr, bk = cos[here], front[here], back[here]
        for k in range(3):
            lanes = slice(128 * k, 128 * k + 128)
            qkv[c, here, lanes] = rope(y[:, lanes].astype(F32), cs, fr, bk).astype(BF)
        qkv[c, here, 384:512] = y[:, 384:512]

    for h, offsets in n_one.stages():
        n_one.wait_stage(h, offsets)
        for j in offsets:
            s_j = at.seq_at(j)

            @pl.loop(0, sib)
            def _(c):
                project(c, s_j)

    cot_gather = Gather(at, token_part(cbuf), (ct_a, ct_b, ct_c, ct_d))
    cot_gather.start()
    save_n1 = pltpu.make_async_copy(nbuf, o_n1, local.at[3])
    save_n1.start()
    save_qkv = pltpu.make_async_copy(qkv, o_qkv, local.at[4])
    save_qkv.start()

    tri = lax.broadcasted_iota(jnp.int32, (length, length), 0) >= lax.broadcasted_iota(
        jnp.int32, (length, length), 1
    )

    def spot(k, b, i):
        return (k * sib + b) * n + i

    def attend(i):
        @pl.loop(0, sib)
        def _(b):
            past = i * length
            here = slice(past, past + length)
            outs = []
            for h in range(GROUP):
                q = qkv[b, here, 128 * h : 128 * h + 128]
                d = jnp.where(tri, nt(q, qkv[b, here, 256:384]) * (scale * log2e), -1e30)
                m = jnp.max(d, axis=1, keepdims=True)
                if i:
                    e = nt(q, qkv[b, 0:past, 256:384]) * (scale * log2e)
                    m = jnp.maximum(m, jnp.max(e, axis=1, keepdims=True))
                d = jnp.exp2(d - m)
                total = jnp.sum(d, axis=1, keepdims=True)
                o = nn(d.astype(BF), qkv[b, here, 384:512])
                if i:
                    e = jnp.exp2(e - m)
                    total = total + jnp.sum(e, axis=1, keepdims=True)
                    o = o + nn(e.astype(BF), qkv[b, 0:past, 384:512])
                outs.append((o / total).astype(BF))
                lse = jnp.broadcast_to(m + jnp.log2(total), (length, 128))
                o_lse[b, h, i] = lse.T[0:8]
            for k in range(chunks):
                pair = jnp.concatenate(outs[k * heads_per : (k + 1) * heads_per], axis=1)
                att_out[spot(k, b, i)] = nt(pair, widen_att[...]).astype(BF)

    def send_attended(i):
        for k in range(chunks):
            for b in range(sib):
                mine = jnp.logical_and(at.s == i, at.c == b)

                @pl.when(mine)
                def _():
                    att_in[tau * chunks + k] = att_out[spot(k, b, i)]

                @pl.when(jnp.logical_not(mine))
                def _():
                    rdma(att_out.at[spot(k, b, i)], att_in.at[tau * chunks + k], at_s.at[k, b, i],
                         at_r.at[tau * chunks + k], at.dev(i, b)).start()

    wo_gather = Gather(
        at, lambda c, s, h: wo.at[c, s, pl.ds(h * (planes // 2), planes // 2)],
        (wo_ga, wo_gb, wo_gc, wo_gd),
    )
    attend(n - 1)
    save_n1.wait()
    n_one.drain()
    send_attended(n - 1)
    move_wo.wait()
    wo_gather.start()
    if parts > 1:
        move_gu[1].start()
    for i in range(n - 2, 0, -1):
        attend(i)
        send_attended(i)
    wo_hops = list(wo_gather.stages())
    attend(0)
    send_attended(0)
    cot_hops = list(cot_gather.stages())
    for h in range(1, n // 2 + 1):
        cot_gather.hop(h)
        wo_gather.hop(h)
    for h, offsets in wo_hops:
        for j in offsets:
            wo_gather.sib_wait(j)
    wo_gather.drain()
    save_qkv.wait()
    save_wq.wait()

    group = n * sib
    for j in range(1, group):
        t = lax.rem(tau + j, group)
        for k in range(chunks):
            ref = att_in.at[t * chunks + k]
            rdma(ref, ref, at_s.at[0, 0, 0], at_r.at[t * chunks + k], at.dev(at.s, at.c)).wait_recv()
    for k in range(chunks):
        for i in range(n):
            for b in range(sib):
                @pl.when(jnp.logical_not(jnp.logical_and(at.s == i, at.c == b)))
                def _():
                    rdma(att_out.at[spot(k, b, i)], att_out.at[spot(k, b, i)], at_s.at[k, b, i],
                         at_r.at[0], at.dev(at.s, at.c)).wait_send()
    save_att = pltpu.make_async_copy(att_in, o_att, local.at[3])
    save_att.start()

    x_f = x[...].astype(F32)
    for s in range(n):
        cols = slice(s * part_cols, (s + 1) * part_cols)
        acc = x_f[:, cols]
        for p in range(planes):
            for c in range(sib):
                acc = acc + nn(att_in[p * sib + c], wo[c, s, p])
        hid[:, cols] = acc
    hidden = hid[...]
    inv_mid = lax.rsqrt(jnp.mean(hidden * hidden, axis=-1, keepdims=True) + NORM_EPS)
    nbuf[at.c, at.s] = (hidden * inv_mid).astype(BF)
    n_two = Gather(at, token_part(nbuf), (n2_a, n2_b, n2_c, n2_d))
    n_two.start()

    move_dn.wait()
    move_gu[0].wait()
    if parts > 2:
        move_gu[2].start()

    def feed_forward(k, n_here, cot_here, store):
        y = nn(n_here, gu[k])
        gate, up = y[:, :wide], y[:, wide:]
        sig = 1.0 / (1.0 + jnp.exp(-gate))
        silu = gate * sig
        grad_act = nt(cot_here, dn[k * wide : (k + 1) * wide])
        store(act, k * wide, (silu * up).astype(BF))
        store(ggu, k * 2 * wide, (grad_act * up * sig * (1.0 + gate * (1.0 - sig))).astype(BF))
        store(ggu, k * 2 * wide + wide, (grad_act * silu).astype(BF))

    def feed_blocks(k, offsets):
        for j in offsets:
            s_j = at.seq_at(j)

            @pl.loop(0, sib)
            def _(c):
                def store(ref, lo, value):
                    ref[c, s_j, :, lo : lo + wide] = value

                feed_forward(k, nbuf[c, s_j], cbuf[c, s_j], store)

    def feed_all(k):
        @pl.loop(0, sib)
        def _(c):
            def store(ref, lo, value):
                ref[c, :, :, lo : lo + wide] = value.reshape(n, length, wide)

            feed_forward(
                k, nbuf[c].reshape(seq_len, width), cbuf[c].reshape(seq_len, width), store
            )

    def blocks_at(h, offsets):
        n_two.wait_stage(h, offsets)
        for j in offsets:
            cot_gather.sib_wait(j)

    stages = list(n_two.stages())
    early = [j for _, offsets in stages[:-1] for j in offsets]
    blocks_at(*stages[0])
    feed_blocks(0, stages[0][1])
    if parts > 1:
        move_gu[1].wait()
        if parts > 3:
            move_gu[3].start()
        feed_blocks(1, stages[0][1])
    for h, offsets in stages[1:-1]:
        blocks_at(h, offsets)
        for k in range(min(2, parts)):
            feed_blocks(k, offsets)
    if parts > 2:
        move_gu[2].wait()
        feed_blocks(2, early)
    blocks_at(*stages[-1])
    for k in range(min(3, parts)):
        feed_blocks(k, stages[-1][1])
    for k in range(3, parts):
        move_gu[k].wait()
        feed_all(k)

    scatter = Scatter(
        at, Scatter.views(sc_stage, sc_in, sc_out, sc_inn), (rs_a, rs_b, rs_c, rs_d), length, width
    )
    tile = 512

    def column_tiles():
        return [slice(t * tile, (t + 1) * tile) for t in range(width // tile)]

    def mid_part(c, s, cols):
        acc = nt(ggu[c, s, :, 0 : 2 * wide], gu[0, cols, :])
        for k in range(1, parts):
            acc = acc + nt(ggu[c, s, :, k * 2 * wide : (k + 1) * 2 * wide], gu[k, cols, :])
        return acc

    def to_stage(c, s, ref):
        for cols in column_tiles():
            ref[:, cols] = mid_part(c, s, cols).astype(BF)

    def to_ring(c, s, store):
        for cols in column_tiles():
            store(cols, mid_part(c, s, cols))

    tokens = sib * seq_len
    down_copies = []

    def grad_down():
        cot_all = cbuf[...].reshape(tokens, width)
        down_rows = local_units // 2
        for t in range(2):
            rows_here = slice(t * down_rows, (t + 1) * down_rows)
            lhs = act[:, :, :, rows_here].reshape(tokens, down_rows)
            stg[rows_here] = tn(lhs, cot_all).astype(BF)
        own = pltpu.make_async_copy(
            stg.at[pl.ds(pl.multiple_of(at.p * units, units), units)], o_sdn.at[at.p], local.at[6]
        )
        own.start()
        down_copies.append(own)
        for dp in range(1, planes):
            to = lax.rem(at.p + dp, planes)
            copy = rdma(stg.at[pl.ds(pl.multiple_of(to * units, units), units)], o_sdn.at[at.p],
                        z_ss.at[dp], z_sr.at[dp], (at.s, at.col(dp, 0)))
            copy.start()
            sent.append(copy)

    gu_tile = sgu_t.shape[1]
    gu_steps = width // gu_tile
    near = planes == 4

    def gu_copy(m, slot):
        return pltpu.make_async_copy(
            sgu_t.at[slot], o_sgu.at[pl.ds(m * gu_tile, gu_tile)], local.at[7 + slot]
        )

    def near_send(m, dc, slot):
        c = lax.rem(at.c + dc, sib)
        return rdma(
            sgu_t.at[slot, pl.ds(pl.multiple_of(c * rows, rows), rows)], o_rgu.at[at.f],
            near_s.at[m, dc], near_r.at[at.p, dc], (at.s, m * sib + c),
        )

    def if_near(m, body):
        pl.when(jnp.logical_or(at.p == m - 1, at.p == m + 1))(body)

    def near_wait(m, slot):
        for dc in range(sib):
            if_near(m, lambda: near_send(m, dc, slot).wait_send())

    def grad_gu():
        for m in range(gu_steps):
            slot = m % 2
            if m >= 2:
                gu_copy(m - 2, slot).wait()
                if near:
                    near_wait(m - 2, slot)
            lhs = nbuf[:, :, :, m * gu_tile : (m + 1) * gu_tile].reshape(tokens, gu_tile)
            sgu_t[slot] = tn(lhs, ggu[...].reshape(tokens, 2 * local_units)).astype(BF)
            gu_copy(m, slot).start()
            if near:
                for dc in range(sib):
                    if_near(m, lambda: near_send(m, dc, slot).start())

    def finish(cols, value):
        o_ghid[:, cols] = value

    def flat(ref, base):
        return lambda w, k: ref.at[base, w * (n // 2) + k]

    down = Scatter(
        at, (lambda k: cbuf.at[0, k], lambda k: nbuf.at[0, k], flat(cbuf, sib - 1), flat(nbuf, sib - 1)),
        (ds_a, ds_b, ds_c, ds_d), length, width,
    )

    def down_stage(c, s, ref):
        for cols in column_tiles():
            ref[:, cols] = nn(act[c, s], dn[:, cols]).astype(BF)

    def down_ring(c, s, store):
        for cols in column_tiles():
            store(cols, nn(act[c, s], dn[:, cols]))

    def down_finish(cols, value):
        o_block[:, cols] = (hid[:, cols] + value).astype(BF)

    credits = Credits(at, free)
    last = len(scatter.offsets()) - 1
    scatter.to_sibling(to_stage)
    scatter.step(0, to_ring, finish)
    grad_down()
    for k in range(1, last):
        scatter.step(k, to_ring, finish)
    grad_gu()
    cot_gather.drain()
    n_two.drain()
    credits.give()
    credits.take()
    down.to_sibling(down_stage)
    down.step(0, down_ring, down_finish)
    scatter.step(last, to_ring, finish)
    e_mid = o_ghid[...]
    hidden = hid[...]
    inv_mid = lax.rsqrt(jnp.mean(hidden * hidden, axis=-1, keepdims=True) + NORM_EPS)
    norm_mid = hidden * inv_mid
    o_ghid[...] = cot[...].astype(F32) + inv_mid * (
        e_mid - norm_mid * jnp.mean(e_mid * norm_mid, axis=-1, keepdims=True)
    )
    branch = o_ghid[...].astype(BF)
    for f in range(owners):
        p, c = f // sib, f % sib
        acc = nt(branch[:, :part_cols], wo[c, 0, p])
        for s in range(1, n):
            acc = acc + nt(branch[:, s * part_cols : (s + 1) * part_cols], wo[c, s, p])
        att_out[f] = acc.astype(BF)
        t, k = f // chunks, f % chunks
        mine = tau == t

        @pl.when(mine)
        def _():
            gh_in[k, at.c, at.s] = att_out[f]

        @pl.when(jnp.logical_not(mine))
        def _():
            rdma(att_out.at[f], gh_in.at[k, at.c, at.s], gh_s.at[f], gh_r.at[k, tau],
                 at.dev(t // sib, t % sib)).start()

    for k in range(1, last):
        down.step(k, down_ring, down_finish)
    for j in range(1, group):
        t = lax.rem(tau + j, group)
        for k in range(chunks):
            ref = gh_in.at[k, lax.rem(t, sib), lax.div(t, sib)]
            rdma(ref, ref, gh_s.at[0], gh_r.at[k, t], at.dev(at.s, at.c)).wait_recv()
    save_gh = pltpu.make_async_copy(gh_in, o_gh, local.at[0])
    save_gh.start()
    for f in range(owners):
        @pl.when(jnp.logical_not(tau == f // chunks))
        def _():
            rdma(att_out.at[f], att_out.at[f], gh_s.at[f], gh_r.at[0, 0],
                 at.dev(at.s, at.c)).wait_send()

    down.step(last, down_ring, down_finish)

    for dp in range(1, planes):
        ref = o_sdn.at[lax.rem(at.p - dp + planes, planes)]
        rdma(ref, ref, z_ss.at[dp], z_sr.at[dp], (at.s, at.f)).wait_recv()
    for copy in down_copies:
        copy.wait()
    for m in range(max(0, gu_steps - 2), gu_steps):
        gu_copy(m, m % 2).wait()
        if near:
            near_wait(m, m % 2)
    if near:
        for q in range(planes):
            for dc in range(sib):
                def arrived():
                    ref = o_rgu.at[q * sib + lax.rem(at.c - dc + sib, sib)]
                    rdma(ref, ref, near_s.at[q, dc], near_r.at[q, dc], (at.s, at.f)).wait_recv()

                if_near(q, arrived)
    scatter.drain()
    down.drain()
    for move in (move_wq, move_wo, move_dn, *move_gu):
        move.drain()
    for copy in sent:
        copy.wait_send()
    save_att.wait()
    save_gh.wait()


def forward_call(dims, sizes, x, cot, tables, widen, widen_att, gain_cols, wq_s, gu_s, dn_s, wo_s):
    n, sib, planes = dims
    rows, units = sizes
    length, width = x.shape
    part_cols = width // n
    head_cols = (GROUP + 2) * HEAD_DIM
    owners = planes * sib
    chunks = GROUP * HEAD_DIM // rows
    ffl = planes * units
    parts = planes if units % 128 == 0 else 1
    seq_len = n * length
    vm, hb = pl.BlockSpec(memory_space=pltpu.VMEM), pl.BlockSpec(memory_space=pl.ANY)
    blocks = (sib, n, length, width)
    sds = jax.ShapeDtypeStruct
    outs = [
        (sds(blocks, BF), hb),
        (sds((sib, seq_len, 512), BF), hb),
        (sds((sib, GROUP, n, 8, length), F32), vm),
        (sds((chunks, sib, n, length, rows), BF), hb),
        (sds((owners, length, rows), BF), hb),
        (sds((length, width), BF), vm),
        (sds((length, width), F32), vm),
        (sds((width, 512), BF), hb),
        (sds((width, 2 * ffl), BF), hb),
        (sds((owners, rows, 2 * ffl), BF), hb),
        (sds((planes, units, width), BF), hb),
    ]
    dma = pltpu.SemaphoreType.DMA
    scratch = [
        pltpu.VMEM((length, width), F32),
        pltpu.VMEM(blocks, BF), pltpu.VMEM(blocks, BF), pltpu.VMEM((sib, seq_len, 512), BF),
        pltpu.VMEM((width, head_cols), BF), pltpu.VMEM((width, 512), BF),
        pltpu.VMEM((sib, n, planes, rows, part_cols), BF),
        pltpu.VMEM((parts, width, 2 * ffl // parts), BF), pltpu.VMEM((ffl, width), BF),
        pltpu.VMEM((sib, n, length, ffl), BF), pltpu.VMEM((sib, n, length, 2 * ffl), BF),
        pltpu.VMEM((owners, length, rows), BF), pltpu.VMEM((owners, length, rows), BF),
        pltpu.VMEM((chunks, sib, n, length, rows), BF),
        pltpu.VMEM((ffl, width), BF), pltpu.VMEM((2, 384, 2 * ffl), BF),

        pltpu.VMEM((rows, part_cols), F32),
        pltpu.VMEM((sib, rows, head_cols), BF),
        pltpu.VMEM((parts, sib, rows, 2 * ffl // parts), BF),
        pltpu.VMEM((units, width), BF), pltpu.VMEM((rows, part_cols), BF),
        *Scatter.scratch(n, (length, width)),
        *Move.sems(planes, sib), *Move.sems(planes, sib), *Move.sems(planes, sib),
        dma((parts, planes, sib)), dma((parts, planes, sib)), dma((parts, sib)), dma((parts, 1)),
        dma((planes,)), dma((planes,)), dma((9,)), dma((3 + 2 * owners + sib,)),
        *Gather.scratch(n), *Gather.scratch(n), *Gather.scratch(n), *Gather.scratch(n),
        *Scatter.sems(n), *Scatter.sems(n),
        dma((chunks, sib, n)), dma((owners,)), dma((owners,)), dma((chunks, n * sib)),
        dma((planes, sib)), dma((planes, sib)), pltpu.SemaphoreType.REGULAR,
    ]
    return pl.pallas_call(
        functools.partial(forward_kernel, dims),
        out_shape=[o[0] for o in outs],
        out_specs=[o[1] for o in outs],
        in_specs=[vm] * 8 + [hb] * 4,
        scratch_shapes=scratch,
        compiler_params=pltpu.CompilerParams(
            collective_id=0, has_side_effects=True, vmem_limit_bytes=VMEM_LIMIT
        ),
    )(x, cot, *tables, widen, widen_att, gain_cols, wq_s, gu_s, dn_s, wo_s)


def backward_kernel(
    dims,
    x, cos, front, back, widen, widen_att, lse,
    n1, qkv_h, gh_h, att_h, ghid, wqp_h, sgu, rgu_h, sdn_h,
    o_input, o_gq, o_ggu, o_gdn, o_gout,
    qkv, gh, att, wqp, sdn, gq, gk, gv, n1_t, sq, so, branch,
    r_gu, r_qkv, r_out, g_gu, g_qkv, g_dn, g_out,
    sc_stage, sc_in, sc_out, sc_inn, e_stage_b, e_sib_b, e_out_b, e_inn_b,
    loads, near_l, saves_gu, saves_qkv, saves_row, z_gs, z_gr, z_qs, z_qr, z_os, z_or,
    e_a, e_b, e_c, e_d, s_a, s_b, s_c, s_d,
    a_dn_s, a_dn_r, a_gu_s, a_gu_r, a_qk_s, a_qk_r, a_ou_s, a_ou_r,
):
    n, sib, planes = dims
    at = Place(n, sib, planes)
    length, width = x.shape
    owners = planes * sib
    chunks, _, _, _, rows = gh.shape
    heads_per = rows // HEAD_DIM
    part_cols = r_out.shape[2]
    scale = HEAD_DIM ** (-0.5)
    log2e = 1.4426950408889634
    tokens = sib * n * length
    sent = []
    near = planes == 4
    units = g_dn.shape[1]
    aligned = len(o_ggu.shape) == 2

    def load(src, dst, k):
        copy = pltpu.make_async_copy(src, dst, loads.at[k])
        copy.start()
        return copy

    def owner_rows(f):
        return pl.ds(pl.multiple_of(f * rows, rows), rows)

    def z_source(dp, dc):
        return (
            lax.rem(at.p - dp + planes, planes) * sib + lax.rem(at.c - dc + sib, sib)
        )

    def z_scatter(src, dst, ssem, rsem, k):
        own = load(src.at[owner_rows(at.f)], dst.at[at.f], k)
        for dp in range(planes):
            for dc in range(sib):
                if dp or dc:
                    to = at.col(dp, dc)
                    copy = rdma(src.at[owner_rows(to)], dst.at[at.f],
                                ssem.at[dp, dc], rsem.at[dp, dc], (at.s, to))
                    copy.start()
                    sent.append(copy)
        return own

    def z_collect(dst, ssem, rsem, own):
        own.wait()
        for dp in range(planes):
            for dc in range(sib):
                if dp or dc:
                    ref = dst.at[z_source(dp, dc)]
                    rdma(ref, ref, ssem.at[dp, dc], rsem.at[dp, dc], (at.s, at.f)).wait_recv()

    def plane_total(dst, c):
        acc = dst[c].astype(F32)
        for p in range(1, planes):
            acc = acc + dst[p * sib + c].astype(F32)
        return acc.astype(BF)

    def far(dp, body):
        if not near or dp == 0:
            body()
        elif dp == 2:
            body()
        else:
            pl.when(at.p == (3 if dp == 1 else 0))(body)

    def gu_pairs():
        for dp in [2, 1, 3, 0] if near else range(planes):
            for dc in range(sib):
                if dp or dc:
                    yield dp, dc

    def gu_send(dp, dc):
        to = at.col(dp, dc)
        return rdma(sgu.at[owner_rows(to)], r_gu.at[at.f], z_gs.at[dp, dc], z_gr.at[dp, dc],
                    (at.s, to))

    def gu_near(q, dc):
        f = q * sib + dc
        return pltpu.make_async_copy(rgu_h.at[f], r_gu.at[f], near_l.at[q, dc])

    def if_near(q, body):
        pl.when(jnp.logical_or(at.p == q - 1, at.p == q + 1))(body)

    def gu_wait(dp, dc):
        ref = r_gu.at[z_source(dp, dc)]
        rdma(ref, ref, z_gs.at[dp, dc], z_gr.at[dp, dc], (at.s, at.f)).wait_recv()

    def gu_arrived(dp, dc):
        if not near or dp in (0, 2):
            gu_wait(dp, dc)
        else:
            pl.when(at.p == (0 if dp == 1 else 3))(lambda: gu_wait(dp, dc))

    at.barrier()
    in_qkv, in_gh = load(qkv_h, qkv, 0), load(gh_h, gh, 1)
    in_sdn, in_att, in_wqp = load(sdn_h, sdn, 4), load(att_h, att, 6), load(wqp_h, wqp, 7)
    gu_own = load(sgu.at[owner_rows(at.f)], r_gu.at[at.f], 5)
    for dp, dc in gu_pairs():
        far(dp, lambda: gu_send(dp, dc).start())
    if near:
        for q in range(planes):
            for dc in range(sib):
                if_near(q, lambda: gu_near(q, dc).start())
    n1_cols = n1_t.shape[4]
    n1_steps = width // n1_cols

    def n1_load(m):
        return pltpu.make_async_copy(
            n1.at[:, :, :, pl.ds(m * n1_cols, n1_cols)], n1_t.at[m % 2], loads.at[8 + m % 2]
        )

    n1_load(0).start()
    n1_load(1).start()

    def row_half(ref):
        size = ref.shape[-2] // 2
        if len(ref.shape) == 4:
            return lambda c, s, h: ref.at[s, :, pl.ds(h * size, size)]
        return lambda c, s, h: ref.at[s, pl.ds(h * size, size)]

    in_sdn.wait()
    acc = sdn[0].astype(F32)
    for p in range(1, planes):
        acc = acc + sdn[p].astype(F32)
    g_dn[at.s] = acc.astype(BF)
    ag_dn = Gather(at, row_half(g_dn), (a_dn_s, a_dn_r))
    ag_dn.start()

    tri = lax.broadcasted_iota(jnp.int32, (length, length), 0) <= lax.broadcasted_iota(
        jnp.int32, (length, length), 1
    )

    def attend_back(b):
        gk[...] = jnp.zeros_like(gk)
        gv[...] = jnp.zeros_like(gv)
        for i in range(n):
            past = i * length
            here = slice(past, past + length)
            for h in range(GROUP):
                k, slot = h // heads_per, h % heads_per
                q = qkv[b, here, 128 * h : 128 * h + 128]
                do = nn(gh[k, b, i], widen_att[:, 128 * slot : 128 * slot + 128]).astype(BF)
                row = lse[b, h, i, 0:1]
                parts = [(here, True)] + ([(slice(0, past), False)] if i else [])
                probs, grads = [], []
                delta = 0.0
                for part, diagonal in parts:
                    sc = nt(qkv[b, part, 256:384], q) * (scale * log2e)
                    if diagonal:
                        sc = jnp.where(tri, sc, -1e30)
                    pr = jnp.exp2(sc - row)
                    dp = nt(qkv[b, part, 384:512], do)
                    delta = delta + jnp.sum(pr * dp, axis=0, keepdims=True)
                    probs.append(pr)
                    grads.append(dp)
                dq = jnp.zeros((length, 128), F32)
                for (part, _), pr, dp in zip(parts, probs, grads):
                    ds = (pr * (dp - delta) * scale).astype(BF)
                    gv[part] += nn(pr.astype(BF), do)
                    gk[part] += nn(ds, q)
                    dq = dq + tn(ds, qkv[b, part, 256:384])
                gq[b, here, 128 * h : 128 * h + 128] = rope(
                    dq, cos[here], -front[here], -back[here]
                ).astype(BF)
        for i in range(n):
            here = slice(i * length, (i + 1) * length)
            gq[b, here, 256:384] = rope(gk[here], cos[here], -front[here], -back[here]).astype(BF)
            gq[b, here, 384:512] = gv[here].astype(BF)

    tile = 512

    def tiles():
        return [slice(t * tile, (t + 1) * tile) for t in range(width // tile)]

    last = len(Scatter(at, (None,) * 4, (None,) * 4, rows, width).offsets()) - 1
    hops = n // 2

    s_out = Scatter(
        at, Scatter.views(sc_stage, sc_in, sc_out, sc_inn), (s_a, s_b, s_c, s_d),
        rows, planes * part_cols,
    )
    for s in range(n):
        branch[s] = ghid[:, s * part_cols : (s + 1) * part_cols].astype(BF)

    def out_pieces(c, s):
        low = branch[s]
        for p in range(planes):
            yield slice(p * part_cols, (p + 1) * part_cols), tn(att[p * sib + c], low)

    def out_stage(c, s, ref):
        for cols, value in out_pieces(c, s):
            ref[:, cols] = value.astype(BF)

    def out_ring(c, s, store):
        for cols, value in out_pieces(c, s):
            store(cols, value)

    def out_finish(cols, value):
        so[cols.start // part_cols] = value.astype(BF)

    in_att.wait()
    s_out.to_sibling(out_stage)
    s_out.step(0, out_ring, out_finish)
    in_qkv.wait()
    in_gh.wait()
    attend_back(0)
    ag_dn.hop(1)
    for k in range(1, last):
        s_out.step(k, out_ring, out_finish)
    if sib > 1:
        attend_back(1)
    for h in range(2, hops + 1):
        ag_dn.hop(h)
    s_out.step(last, out_ring, out_finish)
    out_own = load(so.at[at.p], r_out.at[at.p], 11)
    for dp in range(1, planes):
        to = lax.rem(at.p + dp, planes)
        copy = rdma(so.at[to], r_out.at[at.p], z_os.at[dp], z_or.at[dp], (at.s, at.col(dp, 0)))
        copy.start()
        sent.append(copy)

    for m in range(n1_steps):
        n1_load(m).wait()
        part = tn(n1_t[m % 2].reshape(tokens, n1_cols), gq[...].reshape(tokens, 512)).astype(BF)
        sq[m * n1_cols : (m + 1) * n1_cols] = nt(part, widen[...]).astype(BF)
        if m + 2 < n1_steps:
            n1_load(m + 2).start()
    qkv_own = z_scatter(sq, r_qkv, z_qs, z_qr, 10)

    in_wqp.wait()
    e_in = Scatter(
        at, Scatter.views(e_stage_b, e_sib_b, e_out_b, e_inn_b), (e_a, e_b, e_c, e_d), length, width
    )

    def gq_block(c, s):
        return gq[c, pl.ds(pl.multiple_of(s * length, length), length)]

    def e_stage(c, s, ref):
        for cols in tiles():
            ref[:, cols] = nt(gq_block(c, s), wqp[cols, :]).astype(BF)

    def e_ring(c, s, store):
        for cols in tiles():
            store(cols, nt(gq_block(c, s), wqp[cols, :]))

    def e_finish(cols, value):
        o_input[:, cols] = value

    e_in.to_sibling(e_stage)
    e_in.step(0, e_ring, e_finish)
    for k in range(1, last):
        e_in.step(k, e_ring, e_finish)

    gu_own.wait()
    if near:
        for q in range(planes):
            for dc in range(sib):
                if_near(q, lambda: gu_near(q, dc).wait())
    for dp, dc in gu_pairs():
        gu_arrived(dp, dc)
    for c in range(sib):
        g_gu[at.s, c] = plane_total(r_gu, c)
    ag_gu = Gather(at, row_half(g_gu), (a_gu_s, a_gu_r))
    ag_gu.start()

    def save_gu(j):
        s = at.seq_at(j)
        slot = j % n
        if not aligned:
            return [pltpu.make_async_copy(g_gu.at[s], o_ggu.at[s], saves_gu.at[slot, 0])]
        copies = []
        for c in range(sib):
            for p in range(planes):
                for g in range(2):
                    lo = (g * owners + p * sib + c) * (n * units) + s * units
                    copies.append(pltpu.make_async_copy(
                        g_gu.at[s, c, :, pl.ds((p * 2 + g) * units, units)],
                        o_ggu.at[:, pl.ds(pl.multiple_of(lo, 128), units)],
                        saves_gu.at[slot, (c * planes + p) * 2 + g],
                    ))
        return copies

    def save_qkv(j):
        s = at.seq_at(j)
        slot = j % n
        if not aligned:
            return [pltpu.make_async_copy(g_qkv.at[s], o_gq.at[s], saves_qkv.at[slot, 0])]
        cols = g_qkv.shape[3]
        return [
            pltpu.make_async_copy(
                g_qkv.at[s, c], o_gq.at[:, pl.ds(pl.multiple_of((s * sib + c) * cols, 128), cols)],
                saves_qkv.at[slot, c],
            )
            for c in range(sib)
        ]

    def save_out(j):
        s = at.seq_at(j)
        slot = j % n
        if not aligned:
            return [pltpu.make_async_copy(g_out.at[s], o_gout.at[s], saves_row.at[0, slot])]
        place = o_gout.at[:, pl.ds(pl.multiple_of(s * part_cols, 128), part_cols)]
        return [pltpu.make_async_copy(g_out.at[s], place, saves_row.at[0, slot])]

    def save_down(j):
        s = at.seq_at(j)
        place = o_gdn.at[pl.ds(pl.multiple_of(s * units, units), units)]
        return [pltpu.make_async_copy(g_dn.at[s], place, saves_row.at[1, j % n])]

    saves = []

    def save(copies):
        for copy in copies:
            copy.start()
        saves.extend(copies)

    ring = [0] + [j for h in range(1, hops) for j in (-h, h)] + [hops]
    for j in ring:
        save(save_down(j))
    e_in.step(last, e_ring, e_finish)
    x_f = x[...].astype(F32)
    inv_one = lax.rsqrt(jnp.mean(x_f * x_f, axis=-1, keepdims=True) + NORM_EPS)
    norm_one = x_f * inv_one
    e_val = o_input[...]
    o_input[...] = ghid[...] + inv_one * (
        e_val - norm_one * jnp.mean(e_val * norm_one, axis=-1, keepdims=True)
    )
    out_own.wait()
    for dp in range(1, planes):
        ref = r_out.at[lax.rem(at.p - dp + planes, planes)]
        rdma(ref, ref, z_os.at[dp], z_or.at[dp], (at.s, at.f)).wait_recv()
    acc = r_out[0].astype(F32)
    for p in range(1, planes):
        acc = acc + r_out[p].astype(F32)
    g_out[at.s] = acc.astype(BF)
    ag_out = Gather(at, row_half(g_out), (a_ou_s, a_ou_r))
    ag_out.start()
    save(save_out(0))
    save(save_gu(0))
    z_collect(r_qkv, z_qs, z_qr, qkv_own)
    for c in range(sib):
        g_qkv[at.s, c] = plane_total(r_qkv, c)
    ag_qkv = Gather(at, row_half(g_qkv), (a_qk_s, a_qk_r))
    ag_qkv.start()
    save(save_qkv(0))
    for h in range(1, hops + 1):
        for ag, put in ((ag_gu, save_gu), (ag_out, save_out), (ag_qkv, save_qkv)):
            ag.hop(h)
            for j in (-h, h) if h < hops else (h,):
                save(put(j))
    e_in.drain()
    s_out.drain()
    for ag in (ag_dn, ag_gu, ag_qkv, ag_out):
        ag.drain()
    for dp, dc in gu_pairs():
        far(dp, lambda: gu_send(dp, dc).wait_send())
    for copy in sent:
        copy.wait_send()
    for copy in saves:
        copy.wait()


def backward_call(dims, aligned, x, tables, widen, widen_att, lse, n1, qkv, gh, att, ghid, wqp, sgu, rgu, sdn):
    n, sib, planes = dims
    length, width = x.shape
    rows = gh.shape[4]
    owners = planes * sib
    units = sdn.shape[1]
    part_cols = width // n
    seq_len = n * length
    head_cols = (GROUP + 2) * HEAD_DIM
    vm, hb = pl.BlockSpec(memory_space=pltpu.VMEM), pl.BlockSpec(memory_space=pl.ANY)
    sds = jax.ShapeDtypeStruct
    g_shapes = [
        (n, sib, rows, head_cols), (n, sib, rows, sgu.shape[1]), (n, units, width),
        (n, rows, part_cols),
    ]
    o_shapes = g_shapes
    if aligned:
        o_shapes = [
            (rows, n * sib * head_cols), (rows, n * sib * sgu.shape[1]), None, (rows, width)
        ]
    o_shapes = [*o_shapes[:2], (n * units, width), o_shapes[3]]
    outs = [(sds((length, width), F32), vm)] + [(sds(shape, BF), hb) for shape in o_shapes]
    dma = pltpu.SemaphoreType.DMA
    scratch = [
        pltpu.VMEM(qkv.shape, BF), pltpu.VMEM(gh.shape, BF), pltpu.VMEM(att.shape, BF),
        pltpu.VMEM(wqp.shape, BF), pltpu.VMEM(sdn.shape, BF), pltpu.VMEM(qkv.shape, BF),
        pltpu.VMEM((seq_len, 128), F32), pltpu.VMEM((seq_len, 128), F32),
        pltpu.VMEM((2, *n1.shape[:3], 384), BF), pltpu.VMEM((width, head_cols), BF),
        pltpu.VMEM((planes, rows, part_cols), BF), pltpu.VMEM((n, length, part_cols), BF),
        pltpu.VMEM((owners, rows, sgu.shape[1]), BF), pltpu.VMEM((owners, rows, head_cols), BF),
        pltpu.VMEM((planes, rows, part_cols), BF),
        pltpu.VMEM(g_shapes[1], BF), pltpu.VMEM(g_shapes[0], BF), pltpu.VMEM(g_shapes[2], BF),
        pltpu.VMEM(g_shapes[3], BF),
        *Scatter.scratch(n, (length, max(width, planes * part_cols))),
        *Scatter.scratch(n, (length, width)),
        dma((12,)), dma((planes, sib)), dma((n, 2 * owners)), dma((n, sib)), dma((2, n)),
        dma((planes, sib)), dma((planes, sib)), dma((planes, sib)),
        dma((planes, sib)), dma((planes,)), dma((planes,)),
        *Scatter.sems(n), *Scatter.sems(n),
        *Gather.scratch(n, False), *Gather.scratch(n, False), *Gather.scratch(n, False),
        *Gather.scratch(n, False),
    ]
    return pl.pallas_call(
        functools.partial(backward_kernel, dims),
        out_shape=[o[0] for o in outs],
        out_specs=[o[1] for o in outs],
        in_specs=[vm] * 7 + [hb] * 4 + [vm] + [hb] * 4,
        scratch_shapes=scratch,
        compiler_params=pltpu.CompilerParams(
            collective_id=1, has_side_effects=True, vmem_limit_bytes=VMEM_LIMIT
        ),
    )(x, *tables, widen, widen_att, lse, n1, qkv, gh, att, ghid, wqp, sgu, rgu, sdn)


def adamw(weight, first, second, grad, rate, decay):
    first_new = BETA_ONE * first + (1.0 - BETA_ONE) * grad
    second_new = BETA_TWO * second + (1.0 - BETA_TWO) * grad * grad
    first_hat = first_new / (1.0 - BETA_ONE**ADAM_STEP)
    second_hat = second_new / (1.0 - BETA_TWO**ADAM_STEP)
    weight_new = weight - rate * (first_hat / (jnp.sqrt(second_hat) + ADAM_EPS) + decay * weight)
    return (weight_new, first_new, second_new)


def to_bf16(value):
    return lax.reduce_precision(value, exponent_bits=8, mantissa_bits=7)


def rope_arrays(seq_len):
    half = HEAD_DIM // 2
    frequencies = (ROPE_BASE ** (-(2.0 * np.arange(half)) / HEAD_DIM)).astype(np.float32)
    angles = np.arange(seq_len, dtype=np.float32)[:, None] * frequencies[None, :]
    cos, sin = np.cos(angles), np.sin(angles)
    pad = np.zeros((seq_len, 128 - HEAD_DIM), np.float32)
    none = np.zeros_like(sin)
    return tuple(
        np.concatenate(columns, axis=1).astype(np.float32)
        for columns in ([cos, cos, pad], [-sin, none, pad], [none, sin, pad])
    )


def widening(heads):
    row = np.arange(heads * HEAD_DIM)[:, None]
    col = np.arange(heads * 128)[None, :]
    return (col == row // HEAD_DIM * 128 + row % HEAD_DIM).astype(ml_dtypes.bfloat16)


def make(n_seq, n_fsdp):
    sib = KV_HEADS // n_seq
    planes = n_fsdp // sib

    def on_device(
        inputs, cotangent, qkv_weight, out_weight, gate_up_weight, down_weight, norm_gains,
        qkv_first, qkv_second, out_first, out_second, gate_up_first, gate_up_second,
        down_first, down_second, gain_first, gain_second,
    ):
        s_idx = lax.axis_index("seq")
        _, length, width = inputs.shape
        seq_len = length * n_seq
        rows = qkv_weight.shape[0]
        head_cols = (GROUP + 2) * HEAD_DIM
        ff_rows = down_weight.shape[0]
        units = ff_rows // n_seq
        hidden_units = ff_rows * n_fsdp
        part_cols = width // n_seq
        aligned = units % 128 == 0 and part_cols % 128 == 0 and sib == 2
        aligned = aligned and rows + units // 2 <= length
        gains = to_bf16(norm_gains)
        gain_cols = gains.T

        if aligned:
            pieces = (qkv_weight, gate_up_weight, down_weight, out_weight)
        else:
            wq_s = lax.dynamic_slice_in_dim(
                qkv_weight, s_idx * sib * head_cols, sib * head_cols, 1
            )
            wq_s = (wq_s * gains[0][:, None]).astype(BF).reshape(rows, sib, head_cols)
            gu_s = gate_up_weight.reshape(rows, 2, planes, sib, n_seq, units)
            gu_s = lax.dynamic_index_in_dim(gu_s, s_idx, 4, keepdims=False)
            gu_s = (gu_s * gains[1][:, None, None, None, None]).astype(BF)
            gu_s = gu_s.transpose(3, 0, 1, 2, 4).reshape(1, sib, rows, 2 * planes * units)
            dn_s = lax.dynamic_slice_in_dim(down_weight, s_idx * units, units, 0).astype(BF)
            wo_s = lax.dynamic_slice_in_dim(out_weight, s_idx * part_cols, part_cols, 1).astype(BF)
            pieces = (wq_s.transpose(1, 0, 2), gu_s, dn_s, wo_s)
        tables = tuple(jnp.asarray(table) for table in rope_arrays(seq_len))
        widen = jnp.asarray(widening(GROUP + 2))
        widen_att = jnp.asarray(widening(rows // HEAD_DIM))

        n_one, qkv, lse, gh, att, block_out, grad_hidden, w_qkv, s_gu, r_gu, s_down = forward_call(
            (n_seq, sib, planes), (rows, units), inputs[0], cotangent[0], tables, widen, widen_att,
            gain_cols, *pieces,
        )
        input_grad, g_qkv, g_gu, g_down, g_out = backward_call(
            (n_seq, sib, planes), aligned, inputs[0], tables, widen, widen_att, lse, n_one, qkv, gh,
            att, grad_hidden, w_qkv, s_gu, r_gu, s_down,
        )
        block_out, input_grad = block_out[None], input_grad[None]
        if not aligned:
            g_qkv = g_qkv.transpose(2, 0, 1, 3).reshape(rows, n_seq * sib * head_cols)
            g_gu = g_gu.reshape(n_seq, sib, rows, 2, planes, units).transpose(2, 3, 4, 1, 0, 5)
            g_gu = g_gu.reshape(rows, 2 * hidden_units)
            g_out = g_out.transpose(1, 0, 2).reshape(rows, width)
        g_qkv, g_gu, g_down, g_out = (g.astype(F32) for g in (g_qkv, g_gu, g_down, g_out))
        gain_grad = jnp.stack(
            [
                jnp.sum(g_qkv * to_bf16(qkv_weight), axis=1),
                jnp.sum(g_gu * to_bf16(gate_up_weight), axis=1),
            ]
        )
        g_qkv = g_qkv * gains[0][:, None]
        g_gu = g_gu * gains[1][:, None]
        qkv_new = adamw(qkv_weight, qkv_first, qkv_second, g_qkv, RATE_QKV, WEIGHT_DECAY)
        out_new = adamw(out_weight, out_first, out_second, g_out, RATE_OUT, WEIGHT_DECAY)
        gu_new = adamw(
            gate_up_weight, gate_up_first, gate_up_second, g_gu, RATE_GATE_UP, WEIGHT_DECAY
        )
        down_new = adamw(
            down_weight, down_first, down_second, g_down, RATE_DOWN, WEIGHT_DECAY
        )
        gains_new = adamw(norm_gains, gain_first, gain_second, gain_grad, RATE_GAINS, 0.0)
        return (block_out, input_grad, *qkv_new, *out_new, *gu_new, *down_new, *gains_new)

    return on_device


def solution(mesh):
    tokens = P("fsdp", "seq", None)
    weight = P("fsdp", None)
    gain = P(None, "fsdp")
    in_specs = (tokens, tokens, weight, weight, weight, weight, gain) + (weight,) * 8 + (gain,) * 2
    out_specs = (tokens, tokens) + (weight,) * 12 + (gain,) * 3
    return jax.shard_map(
        make(mesh.shape["seq"], mesh.shape["fsdp"]),
        mesh=mesh, in_specs=in_specs, out_specs=out_specs, check_vma=False,
    )
```

```python
import functools

import jax
import jax.numpy as jnp
import ml_dtypes
import numpy as np
from jax import lax
from jax.experimental import pallas as pl
from jax.experimental.pallas import tpu as pltpu
from jax.sharding import PartitionSpec as P

HEAD_DIM = 96
KV_HEADS = 8
ADAM_STEP = 10
GROUP = 2

NORM_EPS = 1e-05
ROPE_BASE = 100000.0
BETA_ONE = 0.9
BETA_TWO = 0.95
ADAM_EPS = 1e-08
WEIGHT_DECAY = 0.1
RATE_QKV = 0.07
RATE_OUT = 0.8
RATE_GATE_UP = 0.07
RATE_DOWN = 0.045
RATE_GAINS = 0.6
BF = jnp.bfloat16
F32 = jnp.float32
VMEM_LIMIT = 62 * 1024 * 1024


MESH = pl.DeviceIdType.MESH


def rdma(src, dst, ssem, rsem, dev):
    return pltpu.make_async_remote_copy(
        src_ref=src, dst_ref=dst, send_sem=ssem, recv_sem=rsem, device_id=dev, device_id_type=MESH
    )


class Place:
    def __init__(self, n, sib, planes):
        self.n, self.sib, self.planes = n, sib, planes
        self.s = lax.axis_index("seq")
        self.f = lax.axis_index("fsdp")
        self.c = lax.rem(self.f, sib)
        self.p = lax.div(self.f, sib)
        a, b = lax.div(self.s, 2), lax.rem(self.s, 2)
        self.r = a * (1 - b) + (n - 1 - a) * b

    def seq_at(self, j):
        if j == 0:
            return self.s
        n = self.n
        q = lax.rem(self.r + (j + n), n)
        t = lax.div(q, n // 2)
        return (1 - t) * 2 * q + t * (2 * (n - 1 - q) + 1)

    def dev(self, s, c):
        return (s, self.p * self.sib + c)

    def col(self, dp, dc):
        return lax.rem(self.p + dp, self.planes) * self.sib + lax.rem(self.c + dc, self.sib)

    def barrier(self):
        sem = pltpu.get_barrier_semaphore()
        group = self.n * self.sib
        tau = self.s * self.sib + self.c
        for j in range(1, group):
            t = lax.rem(tau + j, group)
            pl.semaphore_signal(
                sem, inc=1, device_id=self.dev(lax.div(t, self.sib), lax.rem(t, self.sib)),
                device_id_type=MESH,
            )
        for dp in range(1, self.planes):
            for dc in range(self.sib):
                pl.semaphore_signal(
                    sem, inc=1, device_id=(self.s, self.col(dp, dc)), device_id_type=MESH
                )
        pl.semaphore_wait(sem, group - 1 + (self.planes - 1) * self.sib)


class Gather:
    def __init__(self, at, part, sems):
        self.at, self.part = at, part
        self.ring_s, self.ring_r = sems[:2]
        self.share = at.sib > 1 and len(sems) > 2
        if self.share:
            self.sib_s, self.sib_r = sems[2:]
        self.sent = []

    @staticmethod
    def scratch(n, share=True):
        d = pltpu.SemaphoreType.DMA
        ring = [d((2, n // 2, 2)), d((2, n // 2, 2))]
        return ring + [d((n, 2)), d((n, 2))] if share else ring

    def _send(self, copy):
        copy.start()
        self.sent.append(copy)

    def _ring(self, way, hop, half):
        at = self.at
        src = self.part(at.c, at.seq_at(-(hop - 1) if way == 0 else hop - 1), half)
        to = at.dev(at.seq_at(1 if way == 0 else -1), at.c)
        self._send(
            rdma(src, src, self.ring_s.at[way, hop - 1, half], self.ring_r.at[way, hop - 1, half], to)
        )

    def _sib(self, j, half):
        at = self.at
        if self.share:
            src = self.part(at.c, at.seq_at(j), half)
            slot = j % at.n
            self._send(
                rdma(src, src, self.sib_s.at[slot, half], self.sib_r.at[slot, half],
                     at.dev(at.s, 1 - at.c))
            )

    def start(self):
        self._ring(0, 1, 0)
        self._ring(1, 1, 1)
        self._ring(0, 1, 1)
        self._ring(1, 1, 0)
        self._sib(0, 0)
        self._sib(0, 1)

    def _arrive(self, way, hop, half):
        at = self.at
        j = -hop if way == 0 else hop
        ref = self.part(at.c, at.seq_at(j), half)
        rdma(ref, ref, self.ring_s.at[way, hop - 1, half], self.ring_r.at[way, hop - 1, half],
             at.dev(at.s, at.c)).wait_recv()
        last = at.n // 2
        if hop + 1 < last or (hop + 1 == last and half == way):
            self._ring(way, hop + 1, half)
        if hop == last:
            j = last
        self._sib(j, half)

    def hop(self, hop):
        self._arrive(0, hop, 0)
        self._arrive(1, hop, 1)
        if hop < self.at.n // 2:
            self._arrive(0, hop, 1)
            self._arrive(1, hop, 0)

    def sib_wait(self, j):
        at = self.at
        if self.share:
            for half in range(2):
                ref = self.part(1 - at.c, at.seq_at(j), half)
                slot = j % at.n
                rdma(ref, ref, self.sib_s.at[slot, half], self.sib_r.at[slot, half],
                     at.dev(at.s, at.c)).wait_recv()

    def stages(self):
        last = self.at.n // 2
        yield 0, [0]
        for h in range(1, last):
            yield h, [-h, h]
        yield last, [last]

    def wait_stage(self, h, offsets):
        if h:
            self.hop(h)
        for j in offsets:
            self.sib_wait(j)

    def drain(self):
        for copy in self.sent:
            copy.wait_send()


class Move:
    def __init__(self, at, src, dst, sems, every_core=True):
        self.at, self.src, self.dst = at, src, dst
        self.ssem, self.rsem, self.hop, self.own = sems
        self.cores = at.sib if every_core else 1
        self.relay = at.planes == 4

    @staticmethod
    def sems(planes, sib):
        d = pltpu.SemaphoreType.DMA
        return [d((planes, sib)), d((planes, sib)), d((sib,)), d((1,))]

    def _pairs(self):
        for dp in [2, 1, 3] if self.relay else range(1, self.at.planes):
            for dc in range(self.cores):
                yield dp, dc
        for dc in range(1, self.cores):
            yield 0, dc

    def _direct(self, dp, body):
        if self.relay and dp in (1, 3):
            pl.when(self.at.p != (3 if dp == 1 else 0))(body)
        else:
            body()

    def _send(self, dp, dc):
        at = self.at
        return rdma(self.src(lax.rem(at.c + dc, at.sib)), self.dst(at.f), self.ssem.at[dp, dc],
                    self.rsem.at[dp, dc], (at.s, at.col(dp, dc)))

    def _local(self):
        return pltpu.make_async_copy(self.src(self.at.c), self.dst(self.at.f), self.own.at[0])

    def start(self):
        self._local().start()
        for dp, dc in self._pairs():
            self._direct(dp, lambda: self._send(dp, dc).start())

    def wait(self):
        at = self.at
        for dp, dc in self._pairs():
            source = lax.rem(at.p - dp + at.planes, at.planes) * at.sib + lax.rem(
                at.c - dc + at.sib, at.sib
            )
            ref = self.dst(source)
            rdma(ref, ref, self.ssem.at[dp, dc], self.rsem.at[dp, dc], (at.s, at.f)).wait_recv()
            if self.relay and dp == 2:
                for here, to, slot in ((2, 3, 3), (1, 0, 1)):
                    @pl.when(at.p == here)
                    def _():
                        rdma(ref, ref, self.hop.at[dc], self.rsem.at[slot, dc],
                             (at.s, to * at.sib + at.c)).start()
        self._local().wait()

    def drain(self):
        at = self.at
        for dp, dc in self._pairs():
            self._direct(dp, lambda: self._send(dp, dc).wait_send())
            if self.relay and dp == 2:
                ref = self.dst(at.f)

                @pl.when(jnp.logical_or(at.p == 1, at.p == 2))
                def _():
                    rdma(ref, ref, self.hop.at[dc], self.rsem.at[0, dc], (at.s, at.f)).wait_send()


class Scatter:
    def __init__(self, at, bufs, sems, rows, cols):
        self.at, self.rows, self.cols = at, rows, pl.ds(0, cols)
        self.stage, self.sib_in, self.out, self.inn = bufs
        self.sib_s, self.sib_r, self.ring_s, self.ring_r = sems
        self.sent, self.handed = [], []

    @staticmethod
    def scratch(n, shape):
        return [
            pltpu.VMEM((2, *shape), BF), pltpu.VMEM((n, *shape), BF),
            pltpu.VMEM((2, n // 2, *shape), BF), pltpu.VMEM((2, n // 2, *shape), BF),
        ]

    @staticmethod
    def views(stage, sib_in, out, inn):
        return (
            lambda k: stage.at[k], lambda k: sib_in.at[k],
            lambda w, k: out.at[w, k], lambda w, k: inn.at[w, k],
        )

    @staticmethod
    def sems(n):
        d = pltpu.SemaphoreType.DMA
        return [d((n,)), d((n,)), d((2, n // 2)), d((2, n // 2))]

    def offsets(self):
        last = self.at.n // 2
        order = [last]
        for h in range(last - 1, 0, -1):
            order += [h, -h]
        return order + [0]

    def to_sibling(self, k, produce):
        at = self.at
        if at.sib == 1:
            return
        if k >= 2:
            self.handed[k - 2].wait_send()
        view = self.stage(k % 2).at[pl.ds(0, self.rows), self.cols]
        produce(1 - at.c, at.seq_at(self.offsets()[k]), view)
        copy = rdma(view, self.sib_in(k).at[pl.ds(0, self.rows), self.cols],
                    self.sib_s.at[k], self.sib_r.at[k], at.dev(at.s, 1 - at.c))
        copy.start()
        self.handed.append(copy)

    def open(self, stage, ring, finish):
        self.to_sibling(0, stage)
        self.step(0, ring, finish)
        for k in range(1, len(self.offsets())):
            self.to_sibling(k, stage)

    def _send(self, way, k, rows):
        at = self.at
        src = self.out(way, k).at[rows, self.cols]
        copy = rdma(src, self.inn(way, k).at[rows, self.cols], self.ring_s.at[way, k], self.ring_r.at[way, k],
                    at.dev(at.seq_at(1 if way == 0 else -1), at.c))
        copy.start()
        self.sent.append(copy)

    def _wait(self, way, k, rows):
        ref = self.inn(way, k).at[rows, self.cols]
        at = self.at
        rdma(ref, ref, self.ring_s.at[way, k], self.ring_r.at[way, k],
             at.dev(at.s, at.c)).wait_recv()

    def step(self, k, produce, finish):
        at = self.at
        last = at.n // 2
        length = self.rows
        half = length // 2
        halves = (pl.ds(0, half), pl.ds(half, half))
        whole = pl.ds(0, length)
        j = self.offsets()[k]
        if at.sib > 1:
            ref = self.sib_in(k).at[pl.ds(0, length), self.cols]
            rdma(ref, ref, self.sib_s.at[k], self.sib_r.at[k], at.dev(at.s, at.c)).wait_recv()
        h = abs(j)
        if h == last:
            got = []
        else:
            ways = (0, 1) if h == 0 else ((0,) if j > 0 else (1,))
            rows_in = [halves[w] if h + 1 == last else whole for w in ways]
            got = [(w, rw) for w, rw in zip(ways, rows_in)]
        pending = [True]

        def store(cols, value, k=k, h=h, j=j, got=got, pending=pending):
            if pending[0]:
                for w, rw in got:
                    self._wait(w, h, rw)
                pending[0] = False
            if at.sib > 1:
                value = value + self.sib_in(k)[pl.ds(0, length), cols].astype(F32)
            for w, rw in got:
                if h + 1 == last:
                    add = self.inn(w, h)[pl.ds(w * half, half), cols].astype(F32)
                    if w == 0:
                        value = jnp.concatenate([value[:half] + add, value[half:]], axis=0)
                    else:
                        value = jnp.concatenate([value[:half], value[half:] + add], axis=0)
                else:
                    value = value + self.inn(w, h)[pl.ds(0, length), cols].astype(F32)
            if h == last:
                low = value.astype(BF)
                self.out(0, h - 1)[pl.ds(0, half), cols] = low[:half]
                self.out(1, h - 1)[pl.ds(half, half), cols] = low[half:]
            elif h:
                self.out(0 if j > 0 else 1, h - 1)[pl.ds(0, length), cols] = value.astype(BF)
            else:
                finish(cols, value)

        produce(at.c, at.seq_at(j), store)
        if h == last:
            self._send(0, h - 1, halves[0])
            self._send(1, h - 1, halves[1])
        elif h:
            self._send(0 if j > 0 else 1, h - 1, whole)

    def drain(self):
        for copy in self.sent + self.handed[-2:]:
            copy.wait_send()


class Credits:
    def __init__(self, at, sem):
        self.at, self.sem = at, sem

    def give(self):
        at = self.at
        if at.sib > 1:
            pl.semaphore_signal(
                self.sem, inc=1, device_id=at.dev(at.s, 1 - at.c), device_id_type=MESH
            )
        for way in (1, -1):
            pl.semaphore_signal(
                self.sem, inc=1, device_id=at.dev(at.seq_at(way), at.c), device_id_type=MESH
            )

    def take(self):
        pl.semaphore_wait(self.sem, 3 if self.at.sib > 1 else 2)


def nt(a, b):
    return lax.dot_general(a, b, (((1,), (1,)), ((), ())), preferred_element_type=F32)


def tn(a, b):
    return lax.dot_general(a, b, (((0,), (0,)), ((), ())), preferred_element_type=F32)


def nn(a, b):
    return lax.dot_general(a, b, (((1,), (0,)), ((), ())), preferred_element_type=F32)


def rope(value, cos, front, back):
    return value * cos + pltpu.roll(value, 80, 1) * front + pltpu.roll(value, 48, 1) * back


def forward_kernel(
    dims,
    x, cot, cos, front, back, widen, widen_att, gain_cols, wq_s, gu_s, dn_s, wo_s,
    o_n1, o_qkv, o_lse, o_gh, o_att, o_block, o_ghid, o_wq, o_sgu, o_rgu, o_sdn,
    hid,
    nbuf, cbuf, qkv, wq, wqp, wo, gu, dn, act, ggu, att_out, att_in, gh_in, stg, sgu_t,
    wo_f, wq_b, gu_b, dn_b, wo_b,
    sc_stage, sc_in, sc_out, sc_inn,
    zw_a, zw_b, zw_c, zw_d, zo_a, zo_b, zo_c, zo_d, zd_a, zd_b, zd_c, zd_d,
    zg_a, zg_b, zg_c, zg_d, z_ss, z_sr, local, loads,
    n1_a, n1_b, n1_c, n1_d, ct_a, ct_b, ct_c, ct_d, n2_a, n2_b, n2_c, n2_d, wo_ga, wo_gb, wo_gc, wo_gd,
    rs_a, rs_b, rs_c, rs_d, ds_a, ds_b, ds_c, ds_d, at_s, at_r, gh_s, gh_r, near_s, near_r, free,
):
    n, sib, planes = dims
    at = Place(n, sib, planes)
    length, width = x.shape
    seq_len = n * length
    raw = len(wq_s.shape) == 2
    _, rows, head_cols = wq_b.shape
    owners = planes * sib
    chunks = GROUP * HEAD_DIM // rows
    units = dn_b.shape[0]
    local_units = planes * units
    parts = 2 if units % 128 == 0 else 1
    wide = local_units // parts
    part_cols = wo_b.shape[1]
    heads_per = rows // HEAD_DIM
    half_len = length // 2
    tau = at.s * sib + at.c
    scale = HEAD_DIM ** (-0.5)
    log2e = 1.4426950408889634
    sent = []

    def token_part(ref):
        return lambda c, s, h: ref.at[c, s, pl.ds(h * half_len, half_len)]

    def owner_rows(f):
        return pl.ds(pl.multiple_of(f * rows, rows), rows)

    if raw:
        gu_f = (o_ghid, hid)

        def cut(ref, k, lo, size, dst):
            return pltpu.make_async_copy(
                ref.at[:, pl.ds(pl.multiple_of(lo, 128), size)], dst, loads.at[k]
            )

        def wq_f(c):
            return gu_f[c].at[pl.ds(0, rows), pl.ds(2 * local_units, head_cols)]

        in_wq = [
            cut(wq_s, 3 + 2 * owners + c, (at.s * sib + c) * head_cols, head_cols, wq_f(c))
            for c in range(sib)
        ]
        in_wo = cut(wo_s, 1, at.s * part_cols, part_cols, wo_f)
        half_units = units // 2

        def dn_f(h):
            return gu_f[h].at[pl.ds(rows, half_units)]

        in_dn = [
            pltpu.make_async_copy(
                dn_s.at[pl.ds(pl.multiple_of(at.s * units + h * half_units, half_units), half_units)],
                dn_f(h), loads.at[2 * h],
            )
            for h in range(2)
        ]
        in_gu = []

        def gu_lane(p, g):
            return p * units // wide * 2 * wide + g * wide + p * units % wide

        for c in range(sib):
            for p in range(planes):
                for g in range(2):
                    lo = (g * owners + p * sib + c) * (n * units) + at.s * units
                    k = (c * planes + p) * 2 + g
                    in_gu.append(
                        cut(gu_s, 3 + k, lo, units,
                            gu_f[c].at[pl.ds(0, rows), pl.ds(gu_lane(p, g), units)])
                    )
        for copy in (*in_wq, in_wo, *in_dn, *in_gu):
            copy.start()
        wq_x, gu_x, dn_x, wo_x = wq_b, gu_b, dn_b, wo_b
    else:
        wq_x, gu_x, dn_x, wo_x = wq_s, gu_s, dn_s, wo_s

    move_wq = Move(at, lambda c: wq_x.at[c], lambda f: wq.at[owner_rows(f)], (zw_a, zw_b, zw_c, zw_d))
    move_wo = Move(
        at, lambda c: wo_x, lambda f: wo.at[lax.rem(f, sib), at.s, lax.div(f, sib)],
        (zo_a, zo_b, zo_c, zo_d), False,
    )
    move_dn = Move(
        at, lambda c: dn_x,
        lambda f: dn.at[pl.ds(pl.multiple_of(lax.div(f, sib) * units, units), units)],
        (zd_a, zd_b, zd_c, zd_d), False,
    )

    def gu_move(k):
        return Move(
            at, lambda c: gu_x.at[k, c], lambda f: gu.at[k, owner_rows(f)],
            (zg_a.at[k], zg_b.at[k], zg_c.at[k], zg_d.at[k]),
        )

    move_gu = [gu_move(k) for k in range(parts)]

    x_f = x[...].astype(F32)
    inv_one = lax.rsqrt(jnp.mean(x_f * x_f, axis=-1, keepdims=True) + NORM_EPS)
    nbuf[at.c, at.s] = (x_f * inv_one).astype(BF)
    cbuf[at.c, at.s] = cot[...]
    n_one = Gather(at, token_part(nbuf), (n1_a, n1_b, n1_c, n1_d))
    at.barrier()
    n_one.start()
    if raw:
        g_one = gain_cols[:, 0:1]
        for c in range(sib):
            in_wq[c].wait()
            wq_b[c] = (wq_f(c)[...] * g_one).astype(BF)
        in_wo.wait()
        wo_b[...] = wo_f[...].astype(BF)
    move_wq.start()
    if raw:
        for h in range(2):
            in_dn[h].wait()
            dn_b[h * half_units : (h + 1) * half_units] = dn_f(h)[...].astype(BF)
        for copy in in_gu:
            copy.wait()
        g_two = gain_cols[:, 1:2]
        for c in range(sib):
            for k in range(parts):
                lanes = slice(k * 2 * wide, (k + 1) * 2 * wide)
                gu_b[k, c] = (gu_f[c][0:rows, lanes] * g_two).astype(BF)
    n_stages = list(n_one.stages())
    for h, _ in n_stages[1:-1]:
        n_one.hop(h)
    move_wo.start()
    move_wq.wait()

    @pl.loop(0, width // 256)
    def _(t):
        here = pl.ds(pl.multiple_of(t * 256, 256), 256)
        wqp[here] = nn(wq[here], widen[...]).astype(BF)

    save_wq = pltpu.make_async_copy(wqp, o_wq, local.at[2])
    save_wq.start()

    def project(c, s):
        y = nn(nbuf[c, s], wqp[...]).astype(BF)
        here = pl.ds(pl.multiple_of(s * length, length), length)
        cs, fr, bk = cos[here], front[here], back[here]
        for k in range(3):
            lanes = slice(128 * k, 128 * k + 128)
            qkv[c, here, lanes] = rope(y[:, lanes].astype(F32), cs, fr, bk).astype(BF)
        qkv[c, here, 384:512] = y[:, 384:512]

    for h, offsets in n_stages:
        if h == n // 2:
            n_one.hop(h)
        for j in offsets:
            n_one.sib_wait(j)
            s_j = at.seq_at(j)

            @pl.loop(0, sib)
            def _(c):
                project(c, s_j)

    cot_gather = Gather(at, token_part(cbuf), (ct_a, ct_b, ct_c, ct_d))
    cot_gather.start()
    save_n1 = pltpu.make_async_copy(nbuf, o_n1, local.at[3])
    save_n1.start()
    save_qkv = pltpu.make_async_copy(qkv, o_qkv, local.at[4])
    save_qkv.start()

    tri = lax.broadcasted_iota(jnp.int32, (length, length), 0) >= lax.broadcasted_iota(
        jnp.int32, (length, length), 1
    )

    def spot(k, b, i):
        return (k * sib + b) * n + i

    def attend(i):
        @pl.loop(0, sib)
        def _(b):
            past = i * length
            here = slice(past, past + length)
            outs = []
            for h in range(GROUP):
                q = qkv[b, here, 128 * h : 128 * h + 128]
                d = jnp.where(tri, nt(q, qkv[b, here, 256:384]) * (scale * log2e), -1e30)
                m = jnp.max(d, axis=1, keepdims=True)
                if i:
                    e = nt(q, qkv[b, 0:past, 256:384]) * (scale * log2e)
                    m = jnp.maximum(m, jnp.max(e, axis=1, keepdims=True))
                d = jnp.exp2(d - m)
                total = jnp.sum(d, axis=1, keepdims=True)
                o = nn(d.astype(BF), qkv[b, here, 384:512])
                if i:
                    e = jnp.exp2(e - m)
                    total = total + jnp.sum(e, axis=1, keepdims=True)
                    o = o + nn(e.astype(BF), qkv[b, 0:past, 384:512])
                outs.append((o / total).astype(BF))
                lse = jnp.broadcast_to(m + jnp.log2(total), (length, 128))
                o_lse[b, h, i] = lse.T[0:8]
            for k in range(chunks):
                pair = jnp.concatenate(outs[k * heads_per : (k + 1) * heads_per], axis=1)
                att_out[spot(k, b, i)] = nt(pair, widen_att[...]).astype(BF)

    def send_attended(i):
        for k in range(chunks):
            for b in range(sib):
                mine = jnp.logical_and(at.s == i, at.c == b)

                @pl.when(mine)
                def _():
                    att_in[tau * chunks + k] = att_out[spot(k, b, i)]

                @pl.when(jnp.logical_not(mine))
                def _():
                    rdma(att_out.at[spot(k, b, i)], att_in.at[tau * chunks + k], at_s.at[k, b, i],
                         at_r.at[tau * chunks + k], at.dev(i, b)).start()

    wo_gather = Gather(
        at, lambda c, s, h: wo.at[c, s, pl.ds(h * (planes // 2), planes // 2)],
        (wo_ga, wo_gb, wo_gc, wo_gd),
    )
    attend(n - 1)
    save_n1.wait()
    n_one.drain()
    send_attended(n - 1)
    move_wo.wait()
    wo_gather.start()
    move_dn.start()
    move_gu[0].start()
    for i in range(n - 2, 0, -1):
        attend(i)
        send_attended(i)
    wo_hops = list(wo_gather.stages())
    attend(0)
    send_attended(0)
    cot_hops = list(cot_gather.stages())
    for h in range(1, n // 2 + 1):
        cot_gather.hop(h)
        wo_gather.hop(h)
    for h, offsets in wo_hops:
        for j in offsets:
            wo_gather.sib_wait(j)
    wo_gather.drain()
    save_qkv.wait()
    save_wq.wait()

    group = n * sib
    for j in range(1, group):
        t = lax.rem(tau + j, group)
        for k in range(chunks):
            ref = att_in.at[t * chunks + k]
            rdma(ref, ref, at_s.at[0, 0, 0], at_r.at[t * chunks + k], at.dev(at.s, at.c)).wait_recv()
    for k in range(chunks):
        for i in range(n):
            for b in range(sib):
                @pl.when(jnp.logical_not(jnp.logical_and(at.s == i, at.c == b)))
                def _():
                    rdma(att_out.at[spot(k, b, i)], att_out.at[spot(k, b, i)], at_s.at[k, b, i],
                         at_r.at[0], at.dev(at.s, at.c)).wait_send()
    save_att = pltpu.make_async_copy(att_in, o_att, local.at[3])
    save_att.start()

    x_f = x[...].astype(F32)
    for s in range(n):
        cols = slice(s * part_cols, (s + 1) * part_cols)
        acc = x_f[:, cols]
        for p in range(planes):
            for c in range(sib):
                acc = acc + nn(att_in[p * sib + c], wo[c, s, p])
        hid[:, cols] = acc
    hidden = hid[...]
    inv_mid = lax.rsqrt(jnp.mean(hidden * hidden, axis=-1, keepdims=True) + NORM_EPS)
    nbuf[at.c, at.s] = (hidden * inv_mid).astype(BF)
    n_two = Gather(at, token_part(nbuf), (n2_a, n2_b, n2_c, n2_d))
    n_two.start()

    stages = list(n_two.stages())
    for h, _ in stages[1:-1]:
        n_two.hop(h)
    if parts > 1:
        move_gu[1].start()
    move_dn.wait()
    move_gu[0].wait()

    def feed_forward(k, n_here, cot_here, store):
        y = nn(n_here, gu[k])
        gate, up = y[:, :wide], y[:, wide:]
        sig = 1.0 / (1.0 + jnp.exp(-gate))
        silu = gate * sig
        grad_act = nt(cot_here, dn[k * wide : (k + 1) * wide])
        store(act, k * wide, (silu * up).astype(BF))
        store(ggu, k * 2 * wide, (grad_act * up * sig * (1.0 + gate * (1.0 - sig))).astype(BF))
        store(ggu, k * 2 * wide + wide, (grad_act * silu).astype(BF))

    def feed_blocks(k, offsets):
        for j in offsets:
            s_j = at.seq_at(j)

            @pl.loop(0, sib)
            def _(c):
                def store(ref, lo, value):
                    ref[c, s_j, :, lo : lo + wide] = value

                feed_forward(k, nbuf[c, s_j], cbuf[c, s_j], store)

    for h, offsets in stages:
        if h == n // 2:
            n_two.hop(h)
        for j in offsets:
            n_two.sib_wait(j)
            cot_gather.sib_wait(j)
        feed_blocks(0, offsets)
    for k in range(1, parts):
        move_gu[k].wait()

        @pl.loop(0, n)
        def _(s):
            @pl.loop(0, sib)
            def _(c):
                def store(ref, lo, value):
                    ref[c, s, :, lo : lo + wide] = value

                feed_forward(k, nbuf[c, s], cbuf[c, s], store)

    scatter = Scatter(
        at, Scatter.views(sc_stage, sc_in, sc_out, sc_inn), (rs_a, rs_b, rs_c, rs_d), length, width
    )
    tile = 512

    def column_tiles():
        return [slice(t * tile, (t + 1) * tile) for t in range(width // tile)]

    def mid_part(c, s, cols):
        acc = nt(ggu[c, s, :, 0 : 2 * wide], gu[0, cols, :])
        for k in range(1, parts):
            acc = acc + nt(ggu[c, s, :, k * 2 * wide : (k + 1) * 2 * wide], gu[k, cols, :])
        return acc

    def to_stage(c, s, ref):
        for cols in column_tiles():
            ref[:, cols] = mid_part(c, s, cols).astype(BF)

    def to_ring(c, s, store):
        for cols in column_tiles():
            store(cols, mid_part(c, s, cols))

    tokens = sib * seq_len
    down_copies = []

    def grad_down():
        cot_all = cbuf[...].reshape(tokens, width)
        down_rows = local_units // 2
        for t in range(2):
            rows_here = slice(t * down_rows, (t + 1) * down_rows)
            lhs = act[:, :, :, rows_here].reshape(tokens, down_rows)
            stg[rows_here] = tn(lhs, cot_all).astype(BF)
        own = pltpu.make_async_copy(
            stg.at[pl.ds(pl.multiple_of(at.p * units, units), units)], o_sdn.at[at.p], local.at[6]
        )
        own.start()
        down_copies.append(own)
        for dp in range(1, planes):
            to = lax.rem(at.p + dp, planes)
            copy = rdma(stg.at[pl.ds(pl.multiple_of(to * units, units), units)], o_sdn.at[at.p],
                        z_ss.at[dp], z_sr.at[dp], (at.s, at.col(dp, 0)))
            copy.start()
            sent.append(copy)

    gu_tile = sgu_t.shape[1]
    gu_steps = width // gu_tile
    near = planes == 4

    def gu_copy(m, slot):
        return pltpu.make_async_copy(
            sgu_t.at[slot], o_sgu.at[pl.ds(m * gu_tile, gu_tile)], local.at[7 + slot]
        )

    def near_send(m, dc):
        to = m * sib + lax.rem(at.c + dc, sib)
        return rdma(o_sgu.at[owner_rows(to)], o_rgu.at[at.f], near_s.at[m, dc],
                    near_r.at[at.p, dc], (at.s, to))

    def if_near(m, body):
        pl.when(jnp.logical_or(at.p == m - 1, at.p == m + 1))(body)

    def grad_gu():
        for m in range(gu_steps):
            slot = m % 2
            if m >= 2:
                gu_copy(m - 2, slot).wait()
            lhs = nbuf[:, :, :, m * gu_tile : (m + 1) * gu_tile].reshape(tokens, gu_tile)
            sgu_t[slot] = tn(lhs, ggu[...].reshape(tokens, 2 * local_units)).astype(BF)
            gu_copy(m, slot).start()
        for m in range(max(0, gu_steps - 2), gu_steps):
            gu_copy(m, m % 2).wait()
        if near:
            for m in range(planes):
                for dc in range(sib):
                    if_near(m, lambda: near_send(m, dc).start())

    def finish(cols, value):
        o_ghid[:, cols] = value

    def flat(ref, base):
        return lambda w, k: ref.at[base, w * (n // 2) + k]

    down = Scatter(
        at, (lambda k: cbuf.at[0, k], lambda k: nbuf.at[0, k], flat(cbuf, sib - 1), flat(nbuf, sib - 1)),
        (ds_a, ds_b, ds_c, ds_d), length, width,
    )

    def down_stage(c, s, ref):
        for cols in column_tiles():
            ref[:, cols] = nn(act[c, s], dn[:, cols]).astype(BF)

    def down_ring(c, s, store):
        for cols in column_tiles():
            store(cols, nn(act[c, s], dn[:, cols]))

    def down_finish(cols, value):
        o_block[:, cols] = (hid[:, cols] + value).astype(BF)

    credits = Credits(at, free)
    last = len(scatter.offsets()) - 1
    scatter.open(to_stage, to_ring, finish)
    grad_down()
    for k in range(1, last):
        scatter.step(k, to_ring, finish)
    grad_gu()
    cot_gather.drain()
    n_two.drain()
    credits.give()
    credits.take()
    down.open(down_stage, down_ring, down_finish)
    scatter.step(last, to_ring, finish)
    e_mid = o_ghid[...]
    hidden = hid[...]
    inv_mid = lax.rsqrt(jnp.mean(hidden * hidden, axis=-1, keepdims=True) + NORM_EPS)
    norm_mid = hidden * inv_mid
    o_ghid[...] = cot[...].astype(F32) + inv_mid * (
        e_mid - norm_mid * jnp.mean(e_mid * norm_mid, axis=-1, keepdims=True)
    )
    branch = o_ghid[...].astype(BF)
    for f in range(owners):
        p, c = f // sib, f % sib
        acc = nt(branch[:, :part_cols], wo[c, 0, p])
        for s in range(1, n):
            acc = acc + nt(branch[:, s * part_cols : (s + 1) * part_cols], wo[c, s, p])
        att_out[f] = acc.astype(BF)
        t, k = f // chunks, f % chunks
        mine = tau == t

        @pl.when(mine)
        def _():
            gh_in[k, at.c, at.s] = att_out[f]

        @pl.when(jnp.logical_not(mine))
        def _():
            rdma(att_out.at[f], gh_in.at[k, at.c, at.s], gh_s.at[f], gh_r.at[k, tau],
                 at.dev(t // sib, t % sib)).start()

    for k in range(1, last):
        down.step(k, down_ring, down_finish)
    for j in range(1, group):
        t = lax.rem(tau + j, group)
        for k in range(chunks):
            ref = gh_in.at[k, lax.rem(t, sib), lax.div(t, sib)]
            rdma(ref, ref, gh_s.at[0], gh_r.at[k, t], at.dev(at.s, at.c)).wait_recv()
    save_gh = pltpu.make_async_copy(gh_in, o_gh, local.at[0])
    save_gh.start()
    for f in range(owners):
        @pl.when(jnp.logical_not(tau == f // chunks))
        def _():
            rdma(att_out.at[f], att_out.at[f], gh_s.at[f], gh_r.at[0, 0],
                 at.dev(at.s, at.c)).wait_send()

    down.step(last, down_ring, down_finish)

    for dp in range(1, planes):
        ref = o_sdn.at[lax.rem(at.p - dp + planes, planes)]
        rdma(ref, ref, z_ss.at[dp], z_sr.at[dp], (at.s, at.f)).wait_recv()
    for copy in down_copies:
        copy.wait()
    if near:
        for q in range(planes):
            for dc in range(sib):
                def arrived():
                    ref = o_rgu.at[q * sib + lax.rem(at.c - dc + sib, sib)]
                    rdma(ref, ref, near_s.at[q, dc], near_r.at[q, dc], (at.s, at.f)).wait_recv()
                    near_send(q, dc).wait_send()

                if_near(q, arrived)
    scatter.drain()
    down.drain()
    for move in (move_wq, move_wo, move_dn, *move_gu):
        move.drain()
    for copy in sent:
        copy.wait_send()
    save_att.wait()
    save_gh.wait()


def forward_call(dims, sizes, x, cot, tables, widen, widen_att, gain_cols, wq_s, gu_s, dn_s, wo_s):
    n, sib, planes = dims
    rows, units = sizes
    length, width = x.shape
    part_cols = width // n
    head_cols = (GROUP + 2) * HEAD_DIM
    owners = planes * sib
    chunks = GROUP * HEAD_DIM // rows
    ffl = planes * units
    parts = 2 if units % 128 == 0 else 1
    seq_len = n * length
    vm, hb = pl.BlockSpec(memory_space=pltpu.VMEM), pl.BlockSpec(memory_space=pl.ANY)
    blocks = (sib, n, length, width)
    sds = jax.ShapeDtypeStruct
    outs = [
        (sds(blocks, BF), hb),
        (sds((sib, seq_len, 512), BF), hb),
        (sds((sib, GROUP, n, 8, length), F32), vm),
        (sds((chunks, sib, n, length, rows), BF), hb),
        (sds((owners, length, rows), BF), hb),
        (sds((length, width), BF), vm),
        (sds((length, width), F32), vm),
        (sds((width, 512), BF), hb),
        (sds((width, 2 * ffl), BF), hb),
        (sds((owners, rows, 2 * ffl), BF), hb),
        (sds((planes, units, width), BF), hb),
    ]
    dma = pltpu.SemaphoreType.DMA
    scratch = [
        pltpu.VMEM((length, width), F32),
        pltpu.VMEM(blocks, BF), pltpu.VMEM(blocks, BF), pltpu.VMEM((sib, seq_len, 512), BF),
        pltpu.VMEM((width, head_cols), BF), pltpu.VMEM((width, 512), BF),
        pltpu.VMEM((sib, n, planes, rows, part_cols), BF),
        pltpu.VMEM((parts, width, 2 * ffl // parts), BF), pltpu.VMEM((ffl, width), BF),
        pltpu.VMEM((sib, n, length, ffl), BF), pltpu.VMEM((sib, n, length, 2 * ffl), BF),
        pltpu.VMEM((owners, length, rows), BF), pltpu.VMEM((owners, length, rows), BF),
        pltpu.VMEM((chunks, sib, n, length, rows), BF),
        pltpu.VMEM((ffl, width), BF), pltpu.VMEM((2, 384, 2 * ffl), BF),

        pltpu.VMEM((rows, part_cols), F32),
        pltpu.VMEM((sib, rows, head_cols), BF),
        pltpu.VMEM((parts, sib, rows, 2 * ffl // parts), BF),
        pltpu.VMEM((units, width), BF), pltpu.VMEM((rows, part_cols), BF),
        *Scatter.scratch(n, (length, width)),
        *Move.sems(planes, sib), *Move.sems(planes, sib), *Move.sems(planes, sib),
        dma((parts, planes, sib)), dma((parts, planes, sib)), dma((parts, sib)), dma((parts, 1)),
        dma((planes,)), dma((planes,)), dma((9,)), dma((3 + 2 * owners + sib,)),
        *Gather.scratch(n), *Gather.scratch(n), *Gather.scratch(n), *Gather.scratch(n),
        *Scatter.sems(n), *Scatter.sems(n),
        dma((chunks, sib, n)), dma((owners,)), dma((owners,)), dma((chunks, n * sib)),
        dma((planes, sib)), dma((planes, sib)), pltpu.SemaphoreType.REGULAR,
    ]
    return pl.pallas_call(
        functools.partial(forward_kernel, dims),
        out_shape=[o[0] for o in outs],
        out_specs=[o[1] for o in outs],
        in_specs=[vm] * 8 + [hb] * 4,
        scratch_shapes=scratch,
        compiler_params=pltpu.CompilerParams(
            collective_id=0, has_side_effects=True, vmem_limit_bytes=VMEM_LIMIT
        ),
    )(x, cot, *tables, widen, widen_att, gain_cols, wq_s, gu_s, dn_s, wo_s)


def backward_kernel(
    dims,
    x, cos, front, back, widen, widen_att, lse,
    n1, qkv_h, gh_h, att_h, ghid, wqp_h, sgu, rgu_h, sdn_h,
    o_input, o_gq, o_ggu, o_gdn, o_gout,
    qkv, gh, att, wqp, sdn, gq, gk, gv, n1_t, sq, so, branch,
    r_gu, r_qkv, r_out, g_gu, g_qkv, g_dn, g_out,
    sc_stage, sc_in, sc_out, sc_inn, e_stage_b, e_sib_b, e_out_b, e_inn_b,
    loads, near_l, saves_gu, saves_qkv, saves_row, z_gs, z_gr, z_qs, z_qr, z_os, z_or,
    e_a, e_b, e_c, e_d, s_a, s_b, s_c, s_d,
    a_dn_s, a_dn_r, a_gu_s, a_gu_r, a_qk_s, a_qk_r, a_ou_s, a_ou_r,
):
    n, sib, planes = dims
    at = Place(n, sib, planes)
    length, width = x.shape
    owners = planes * sib
    chunks, _, _, _, rows = gh.shape
    heads_per = rows // HEAD_DIM
    part_cols = r_out.shape[2]
    scale = HEAD_DIM ** (-0.5)
    log2e = 1.4426950408889634
    tokens = sib * n * length
    sent = []
    near = planes == 4
    units = g_dn.shape[1]
    aligned = len(o_ggu.shape) == 2

    def load(src, dst, k):
        copy = pltpu.make_async_copy(src, dst, loads.at[k])
        copy.start()
        return copy

    def owner_rows(f):
        return pl.ds(pl.multiple_of(f * rows, rows), rows)

    def z_source(dp, dc):
        return (
            lax.rem(at.p - dp + planes, planes) * sib + lax.rem(at.c - dc + sib, sib)
        )

    def z_scatter(src, dst, ssem, rsem, k):
        own = load(src.at[owner_rows(at.f)], dst.at[at.f], k)
        for dp in range(planes):
            for dc in range(sib):
                if dp or dc:
                    to = at.col(dp, dc)
                    copy = rdma(src.at[owner_rows(to)], dst.at[at.f],
                                ssem.at[dp, dc], rsem.at[dp, dc], (at.s, to))
                    copy.start()
                    sent.append(copy)
        return own

    def z_collect(dst, ssem, rsem, own):
        own.wait()
        for dp in range(planes):
            for dc in range(sib):
                if dp or dc:
                    ref = dst.at[z_source(dp, dc)]
                    rdma(ref, ref, ssem.at[dp, dc], rsem.at[dp, dc], (at.s, at.f)).wait_recv()

    def plane_total(dst, c):
        acc = dst[c].astype(F32)
        for p in range(1, planes):
            acc = acc + dst[p * sib + c].astype(F32)
        return acc.astype(BF)

    def far(dp, body):
        if not near or dp == 0:
            body()
        elif dp == 2:
            body()
        else:
            pl.when(at.p == (3 if dp == 1 else 0))(body)

    def gu_pairs():
        for dp in [2, 1, 3, 0] if near else range(planes):
            for dc in range(sib):
                if dp or dc:
                    yield dp, dc

    def gu_send(dp, dc):
        to = at.col(dp, dc)
        return rdma(sgu.at[owner_rows(to)], r_gu.at[at.f], z_gs.at[dp, dc], z_gr.at[dp, dc],
                    (at.s, to))

    def gu_near(q, dc):
        f = q * sib + dc
        return pltpu.make_async_copy(rgu_h.at[f], r_gu.at[f], near_l.at[q, dc])

    def if_near(q, body):
        pl.when(jnp.logical_or(at.p == q - 1, at.p == q + 1))(body)

    def gu_wait(dp, dc):
        ref = r_gu.at[z_source(dp, dc)]
        rdma(ref, ref, z_gs.at[dp, dc], z_gr.at[dp, dc], (at.s, at.f)).wait_recv()

    def gu_arrived(dp, dc):
        if not near or dp in (0, 2):
            gu_wait(dp, dc)
        else:
            pl.when(at.p == (0 if dp == 1 else 3))(lambda: gu_wait(dp, dc))

    at.barrier()
    in_qkv, in_gh = load(qkv_h, qkv, 0), load(gh_h, gh, 1)
    in_sdn, in_att, in_wqp = load(sdn_h, sdn, 4), load(att_h, att, 6), load(wqp_h, wqp, 7)
    gu_own = load(sgu.at[owner_rows(at.f)], r_gu.at[at.f], 5)
    for dp, dc in gu_pairs():
        far(dp, lambda: gu_send(dp, dc).start())
    if near:
        for q in range(planes):
            for dc in range(sib):
                if_near(q, lambda: gu_near(q, dc).start())
    n1_cols = n1_t.shape[4]
    n1_steps = width // n1_cols

    def n1_load(m):
        return pltpu.make_async_copy(
            n1.at[:, :, :, pl.ds(m * n1_cols, n1_cols)], n1_t.at[m % 2], loads.at[8 + m % 2]
        )

    n1_load(0).start()
    n1_load(1).start()

    def row_half(ref):
        size = ref.shape[-2] // 2
        if len(ref.shape) == 4:
            return lambda c, s, h: ref.at[s, :, pl.ds(h * size, size)]
        return lambda c, s, h: ref.at[s, pl.ds(h * size, size)]

    in_sdn.wait()
    acc = sdn[0].astype(F32)
    for p in range(1, planes):
        acc = acc + sdn[p].astype(F32)
    g_dn[at.s] = acc.astype(BF)
    ag_dn = Gather(at, row_half(g_dn), (a_dn_s, a_dn_r))
    ag_dn.start()

    tri = lax.broadcasted_iota(jnp.int32, (length, length), 0) <= lax.broadcasted_iota(
        jnp.int32, (length, length), 1
    )

    def attend_back(b):
        gk[...] = jnp.zeros_like(gk)
        gv[...] = jnp.zeros_like(gv)
        for i in range(n):
            past = i * length
            here = slice(past, past + length)
            for h in range(GROUP):
                k, slot = h // heads_per, h % heads_per
                q = qkv[b, here, 128 * h : 128 * h + 128]
                do = nn(gh[k, b, i], widen_att[:, 128 * slot : 128 * slot + 128]).astype(BF)
                row = lse[b, h, i, 0:1]
                parts = [(here, True)] + ([(slice(0, past), False)] if i else [])
                probs, grads = [], []
                delta = 0.0
                for part, diagonal in parts:
                    sc = nt(qkv[b, part, 256:384], q) * (scale * log2e)
                    if diagonal:
                        sc = jnp.where(tri, sc, -1e30)
                    pr = jnp.exp2(sc - row)
                    dp = nt(qkv[b, part, 384:512], do)
                    delta = delta + jnp.sum(pr * dp, axis=0, keepdims=True)
                    probs.append(pr)
                    grads.append(dp)
                dq = jnp.zeros((length, 128), F32)
                for (part, _), pr, dp in zip(parts, probs, grads):
                    ds = (pr * (dp - delta) * scale).astype(BF)
                    gv[part] += nn(pr.astype(BF), do)
                    gk[part] += nn(ds, q)
                    dq = dq + tn(ds, qkv[b, part, 256:384])
                gq[b, here, 128 * h : 128 * h + 128] = rope(
                    dq, cos[here], -front[here], -back[here]
                ).astype(BF)
        for i in range(n):
            here = slice(i * length, (i + 1) * length)
            gq[b, here, 256:384] = rope(gk[here], cos[here], -front[here], -back[here]).astype(BF)
            gq[b, here, 384:512] = gv[here].astype(BF)

    tile = 512

    def tiles():
        return [slice(t * tile, (t + 1) * tile) for t in range(width // tile)]

    last = len(Scatter(at, (None,) * 4, (None,) * 4, rows, width).offsets()) - 1
    hops = n // 2

    s_out = Scatter(
        at, Scatter.views(sc_stage, sc_in, sc_out, sc_inn), (s_a, s_b, s_c, s_d),
        rows, planes * part_cols,
    )
    for s in range(n):
        branch[s] = ghid[:, s * part_cols : (s + 1) * part_cols].astype(BF)

    def out_pieces(c, s):
        low = branch[s]
        for p in range(planes):
            yield slice(p * part_cols, (p + 1) * part_cols), tn(att[p * sib + c], low)

    def out_stage(c, s, ref):
        for cols, value in out_pieces(c, s):
            ref[:, cols] = value.astype(BF)

    def out_ring(c, s, store):
        for cols, value in out_pieces(c, s):
            store(cols, value)

    def out_finish(cols, value):
        so[cols.start // part_cols] = value.astype(BF)

    in_att.wait()
    s_out.open(out_stage, out_ring, out_finish)
    in_qkv.wait()
    in_gh.wait()
    attend_back(0)
    ag_dn.hop(1)
    for k in range(1, last):
        s_out.step(k, out_ring, out_finish)
    if sib > 1:
        attend_back(1)
    for h in range(2, hops + 1):
        ag_dn.hop(h)
    s_out.step(last, out_ring, out_finish)
    out_own = load(so.at[at.p], r_out.at[at.p], 11)
    for dp in range(1, planes):
        to = lax.rem(at.p + dp, planes)
        copy = rdma(so.at[to], r_out.at[at.p], z_os.at[dp], z_or.at[dp], (at.s, at.col(dp, 0)))
        copy.start()
        sent.append(copy)

    for m in range(n1_steps):
        n1_load(m).wait()
        part = tn(n1_t[m % 2].reshape(tokens, n1_cols), gq[...].reshape(tokens, 512)).astype(BF)
        sq[m * n1_cols : (m + 1) * n1_cols] = nt(part, widen[...]).astype(BF)
        if m + 2 < n1_steps:
            n1_load(m + 2).start()
    qkv_own = z_scatter(sq, r_qkv, z_qs, z_qr, 10)

    in_wqp.wait()
    e_in = Scatter(
        at, Scatter.views(e_stage_b, e_sib_b, e_out_b, e_inn_b), (e_a, e_b, e_c, e_d), length, width
    )

    def gq_block(c, s):
        return gq[c, pl.ds(pl.multiple_of(s * length, length), length)]

    def e_stage(c, s, ref):
        for cols in tiles():
            ref[:, cols] = nt(gq_block(c, s), wqp[cols, :]).astype(BF)

    def e_ring(c, s, store):
        for cols in tiles():
            store(cols, nt(gq_block(c, s), wqp[cols, :]))

    def e_finish(cols, value):
        o_input[:, cols] = value

    e_in.open(e_stage, e_ring, e_finish)
    for k in range(1, last):
        e_in.step(k, e_ring, e_finish)

    gu_own.wait()
    if near:
        for q in range(planes):
            for dc in range(sib):
                if_near(q, lambda: gu_near(q, dc).wait())
    for dp, dc in gu_pairs():
        gu_arrived(dp, dc)
    for c in range(sib):
        g_gu[at.s, c] = plane_total(r_gu, c)
    ag_gu = Gather(at, row_half(g_gu), (a_gu_s, a_gu_r))
    ag_gu.start()

    wide = planes * units // 2

    def gu_lane(p, g):
        return p * units // wide * 2 * wide + g * wide + p * units % wide

    def save_gu(j):
        s = at.seq_at(j)
        slot = j % n
        if not aligned:
            return [pltpu.make_async_copy(g_gu.at[s], o_ggu.at[s], saves_gu.at[slot, 0])]
        copies = []
        for c in range(sib):
            for p in range(planes):
                for g in range(2):
                    lo = (g * owners + p * sib + c) * (n * units) + s * units
                    copies.append(pltpu.make_async_copy(
                        g_gu.at[s, c, :, pl.ds(gu_lane(p, g), units)],
                        o_ggu.at[:, pl.ds(pl.multiple_of(lo, 128), units)],
                        saves_gu.at[slot, (c * planes + p) * 2 + g],
                    ))
        return copies

    def save_qkv(j):
        s = at.seq_at(j)
        slot = j % n
        if not aligned:
            return [pltpu.make_async_copy(g_qkv.at[s], o_gq.at[s], saves_qkv.at[slot, 0])]
        cols = g_qkv.shape[3]
        return [
            pltpu.make_async_copy(
                g_qkv.at[s, c], o_gq.at[:, pl.ds(pl.multiple_of((s * sib + c) * cols, 128), cols)],
                saves_qkv.at[slot, c],
            )
            for c in range(sib)
        ]

    def save_out(j):
        s = at.seq_at(j)
        slot = j % n
        if not aligned:
            return [pltpu.make_async_copy(g_out.at[s], o_gout.at[s], saves_row.at[0, slot])]
        place = o_gout.at[:, pl.ds(pl.multiple_of(s * part_cols, 128), part_cols)]
        return [pltpu.make_async_copy(g_out.at[s], place, saves_row.at[0, slot])]

    def save_down(j):
        s = at.seq_at(j)
        place = o_gdn.at[pl.ds(pl.multiple_of(s * units, units), units)]
        return [pltpu.make_async_copy(g_dn.at[s], place, saves_row.at[1, j % n])]

    saves = []

    def save(copies):
        for copy in copies:
            copy.start()
        saves.extend(copies)

    ring = [0] + [j for h in range(1, hops) for j in (-h, h)] + [hops]
    for j in ring:
        save(save_down(j))
    e_in.step(last, e_ring, e_finish)
    x_f = x[...].astype(F32)
    inv_one = lax.rsqrt(jnp.mean(x_f * x_f, axis=-1, keepdims=True) + NORM_EPS)
    norm_one = x_f * inv_one
    e_val = o_input[...]
    o_input[...] = ghid[...] + inv_one * (
        e_val - norm_one * jnp.mean(e_val * norm_one, axis=-1, keepdims=True)
    )
    out_own.wait()
    for dp in range(1, planes):
        ref = r_out.at[lax.rem(at.p - dp + planes, planes)]
        rdma(ref, ref, z_os.at[dp], z_or.at[dp], (at.s, at.f)).wait_recv()
    acc = r_out[0].astype(F32)
    for p in range(1, planes):
        acc = acc + r_out[p].astype(F32)
    g_out[at.s] = acc.astype(BF)
    ag_out = Gather(at, row_half(g_out), (a_ou_s, a_ou_r))
    ag_out.start()
    save(save_out(0))
    save(save_gu(0))
    z_collect(r_qkv, z_qs, z_qr, qkv_own)
    for c in range(sib):
        g_qkv[at.s, c] = plane_total(r_qkv, c)
    ag_qkv = Gather(at, row_half(g_qkv), (a_qk_s, a_qk_r))
    ag_qkv.start()
    save(save_qkv(0))
    for h in range(1, hops + 1):
        for ag, put in ((ag_gu, save_gu), (ag_out, save_out), (ag_qkv, save_qkv)):
            ag.hop(h)
            for j in (-h, h) if h < hops else (h,):
                save(put(j))
    e_in.drain()
    s_out.drain()
    for ag in (ag_dn, ag_gu, ag_qkv, ag_out):
        ag.drain()
    for dp, dc in gu_pairs():
        far(dp, lambda: gu_send(dp, dc).wait_send())
    for copy in sent:
        copy.wait_send()
    for copy in saves:
        copy.wait()


def backward_call(dims, aligned, x, tables, widen, widen_att, lse, n1, qkv, gh, att, ghid, wqp, sgu, rgu, sdn):
    n, sib, planes = dims
    length, width = x.shape
    rows = gh.shape[4]
    owners = planes * sib
    units = sdn.shape[1]
    part_cols = width // n
    seq_len = n * length
    head_cols = (GROUP + 2) * HEAD_DIM
    vm, hb = pl.BlockSpec(memory_space=pltpu.VMEM), pl.BlockSpec(memory_space=pl.ANY)
    sds = jax.ShapeDtypeStruct
    g_shapes = [
        (n, sib, rows, head_cols), (n, sib, rows, sgu.shape[1]), (n, units, width),
        (n, rows, part_cols),
    ]
    o_shapes = g_shapes
    if aligned:
        o_shapes = [
            (rows, n * sib * head_cols), (rows, n * sib * sgu.shape[1]), None, (rows, width)
        ]
    o_shapes = [*o_shapes[:2], (n * units, width), o_shapes[3]]
    outs = [(sds((length, width), F32), vm)] + [(sds(shape, BF), hb) for shape in o_shapes]
    dma = pltpu.SemaphoreType.DMA
    scratch = [
        pltpu.VMEM(qkv.shape, BF), pltpu.VMEM(gh.shape, BF), pltpu.VMEM(att.shape, BF),
        pltpu.VMEM(wqp.shape, BF), pltpu.VMEM(sdn.shape, BF), pltpu.VMEM(qkv.shape, BF),
        pltpu.VMEM((seq_len, 128), F32), pltpu.VMEM((seq_len, 128), F32),
        pltpu.VMEM((2, *n1.shape[:3], 384), BF), pltpu.VMEM((width, head_cols), BF),
        pltpu.VMEM((planes, rows, part_cols), BF), pltpu.VMEM((n, length, part_cols), BF),
        pltpu.VMEM((owners, rows, sgu.shape[1]), BF), pltpu.VMEM((owners, rows, head_cols), BF),
        pltpu.VMEM((planes, rows, part_cols), BF),
        pltpu.VMEM(g_shapes[1], BF), pltpu.VMEM(g_shapes[0], BF), pltpu.VMEM(g_shapes[2], BF),
        pltpu.VMEM(g_shapes[3], BF),
        *Scatter.scratch(n, (length, max(width, planes * part_cols))),
        *Scatter.scratch(n, (length, width)),
        dma((12,)), dma((planes, sib)), dma((n, 2 * owners)), dma((n, sib)), dma((2, n)),
        dma((planes, sib)), dma((planes, sib)), dma((planes, sib)),
        dma((planes, sib)), dma((planes,)), dma((planes,)),
        *Scatter.sems(n), *Scatter.sems(n),
        *Gather.scratch(n, False), *Gather.scratch(n, False), *Gather.scratch(n, False),
        *Gather.scratch(n, False),
    ]
    return pl.pallas_call(
        functools.partial(backward_kernel, dims),
        out_shape=[o[0] for o in outs],
        out_specs=[o[1] for o in outs],
        in_specs=[vm] * 7 + [hb] * 4 + [vm] + [hb] * 4,
        scratch_shapes=scratch,
        compiler_params=pltpu.CompilerParams(
            collective_id=1, has_side_effects=True, vmem_limit_bytes=VMEM_LIMIT
        ),
    )(x, *tables, widen, widen_att, lse, n1, qkv, gh, att, ghid, wqp, sgu, rgu, sdn)


def adamw(weight, first, second, grad, rate, decay):
    first_new = BETA_ONE * first + (1.0 - BETA_ONE) * grad
    second_new = BETA_TWO * second + (1.0 - BETA_TWO) * grad * grad
    first_hat = first_new / (1.0 - BETA_ONE**ADAM_STEP)
    second_hat = second_new / (1.0 - BETA_TWO**ADAM_STEP)
    weight_new = weight - rate * (first_hat / (jnp.sqrt(second_hat) + ADAM_EPS) + decay * weight)
    return (weight_new, first_new, second_new)


def to_bf16(value):
    return lax.reduce_precision(value, exponent_bits=8, mantissa_bits=7)


def rope_arrays(seq_len):
    half = HEAD_DIM // 2
    frequencies = (ROPE_BASE ** (-(2.0 * np.arange(half)) / HEAD_DIM)).astype(np.float32)
    angles = np.arange(seq_len, dtype=np.float32)[:, None] * frequencies[None, :]
    cos, sin = np.cos(angles), np.sin(angles)
    pad = np.zeros((seq_len, 128 - HEAD_DIM), np.float32)
    none = np.zeros_like(sin)
    return tuple(
        np.concatenate(columns, axis=1).astype(np.float32)
        for columns in ([cos, cos, pad], [-sin, none, pad], [none, sin, pad])
    )


def widening(heads):
    row = np.arange(heads * HEAD_DIM)[:, None]
    col = np.arange(heads * 128)[None, :]
    return (col == row // HEAD_DIM * 128 + row % HEAD_DIM).astype(ml_dtypes.bfloat16)


def make(n_seq, n_fsdp):
    sib = KV_HEADS // n_seq
    planes = n_fsdp // sib

    def on_device(
        inputs, cotangent, qkv_weight, out_weight, gate_up_weight, down_weight, norm_gains,
        qkv_first, qkv_second, out_first, out_second, gate_up_first, gate_up_second,
        down_first, down_second, gain_first, gain_second,
    ):
        s_idx = lax.axis_index("seq")
        _, length, width = inputs.shape
        seq_len = length * n_seq
        rows = qkv_weight.shape[0]
        head_cols = (GROUP + 2) * HEAD_DIM
        ff_rows = down_weight.shape[0]
        units = ff_rows // n_seq
        hidden_units = ff_rows * n_fsdp
        part_cols = width // n_seq
        aligned = units % 128 == 0 and part_cols % 128 == 0 and sib == 2
        aligned = aligned and rows + units // 2 <= length
        gains = to_bf16(norm_gains)
        gain_cols = gains.T

        if aligned:
            pieces = (qkv_weight, gate_up_weight, down_weight, out_weight)
        else:
            wq_s = lax.dynamic_slice_in_dim(
                qkv_weight, s_idx * sib * head_cols, sib * head_cols, 1
            )
            wq_s = (wq_s * gains[0][:, None]).astype(BF).reshape(rows, sib, head_cols)
            gu_s = gate_up_weight.reshape(rows, 2, planes, sib, n_seq, units)
            gu_s = lax.dynamic_index_in_dim(gu_s, s_idx, 4, keepdims=False)
            gu_s = (gu_s * gains[1][:, None, None, None, None]).astype(BF)
            gu_s = gu_s.transpose(3, 0, 1, 2, 4).reshape(1, sib, rows, 2 * planes * units)
            dn_s = lax.dynamic_slice_in_dim(down_weight, s_idx * units, units, 0).astype(BF)
            wo_s = lax.dynamic_slice_in_dim(out_weight, s_idx * part_cols, part_cols, 1).astype(BF)
            pieces = (wq_s.transpose(1, 0, 2), gu_s, dn_s, wo_s)
        tables = tuple(jnp.asarray(table) for table in rope_arrays(seq_len))
        widen = jnp.asarray(widening(GROUP + 2))
        widen_att = jnp.asarray(widening(rows // HEAD_DIM))

        n_one, qkv, lse, gh, att, block_out, grad_hidden, w_qkv, s_gu, r_gu, s_down = forward_call(
            (n_seq, sib, planes), (rows, units), inputs[0], cotangent[0], tables, widen, widen_att,
            gain_cols, *pieces,
        )
        input_grad, g_qkv, g_gu, g_down, g_out = backward_call(
            (n_seq, sib, planes), aligned, inputs[0], tables, widen, widen_att, lse, n_one, qkv, gh,
            att, grad_hidden, w_qkv, s_gu, r_gu, s_down,
        )
        block_out, input_grad = block_out[None], input_grad[None]
        if not aligned:
            g_qkv = g_qkv.transpose(2, 0, 1, 3).reshape(rows, n_seq * sib * head_cols)
            g_gu = g_gu.reshape(n_seq, sib, rows, 2, planes, units).transpose(2, 3, 4, 1, 0, 5)
            g_gu = g_gu.reshape(rows, 2 * hidden_units)
            g_out = g_out.transpose(1, 0, 2).reshape(rows, width)
        g_qkv, g_gu, g_down, g_out = (g.astype(F32) for g in (g_qkv, g_gu, g_down, g_out))
        gain_grad = jnp.stack(
            [
                jnp.sum(g_qkv * to_bf16(qkv_weight), axis=1),
                jnp.sum(g_gu * to_bf16(gate_up_weight), axis=1),
            ]
        )
        g_qkv = g_qkv * gains[0][:, None]
        g_gu = g_gu * gains[1][:, None]
        qkv_new = adamw(qkv_weight, qkv_first, qkv_second, g_qkv, RATE_QKV, WEIGHT_DECAY)
        out_new = adamw(out_weight, out_first, out_second, g_out, RATE_OUT, WEIGHT_DECAY)
        gu_new = adamw(
            gate_up_weight, gate_up_first, gate_up_second, g_gu, RATE_GATE_UP, WEIGHT_DECAY
        )
        down_new = adamw(
            down_weight, down_first, down_second, g_down, RATE_DOWN, WEIGHT_DECAY
        )
        gains_new = adamw(norm_gains, gain_first, gain_second, gain_grad, RATE_GAINS, 0.0)
        return (block_out, input_grad, *qkv_new, *out_new, *gu_new, *down_new, *gains_new)

    return on_device


def solution(mesh):
    tokens = P("fsdp", "seq", None)
    weight = P("fsdp", None)
    gain = P(None, "fsdp")
    in_specs = (tokens, tokens, weight, weight, weight, weight, gain) + (weight,) * 8 + (gain,) * 2
    out_specs = (tokens, tokens) + (weight,) * 12 + (gain,) * 3
    return jax.shard_map(
        make(mesh.shape["seq"], mesh.shape["fsdp"]),
        mesh=mesh, in_specs=in_specs, out_specs=out_specs, check_vma=False,
    )
```

```python
import functools

import jax
import jax.numpy as jnp
import ml_dtypes
import numpy as np
from jax import lax
from jax.experimental import pallas as pl
from jax.experimental.pallas import tpu as pltpu
from jax.sharding import PartitionSpec as P

HEAD_DIM = 96
KV_HEADS = 8
ADAM_STEP = 10
GROUP = 2

NORM_EPS = 1e-05
ROPE_BASE = 100000.0
BETA_ONE = 0.9
BETA_TWO = 0.95
ADAM_EPS = 1e-08
WEIGHT_DECAY = 0.1
RATE_QKV = 0.07
RATE_OUT = 0.8
RATE_GATE_UP = 0.07
RATE_DOWN = 0.045
RATE_GAINS = 0.6
BF = jnp.bfloat16
F32 = jnp.float32
VMEM_LIMIT = 62 * 1024 * 1024


MESH = pl.DeviceIdType.MESH


def rdma(src, dst, ssem, rsem, dev):
    return pltpu.make_async_remote_copy(
        src_ref=src, dst_ref=dst, send_sem=ssem, recv_sem=rsem, device_id=dev, device_id_type=MESH
    )


class Place:
    def __init__(self, n, sib, planes):
        self.n, self.sib, self.planes = n, sib, planes
        self.s = lax.axis_index("seq")
        self.f = lax.axis_index("fsdp")
        self.c = lax.rem(self.f, sib)
        self.p = lax.div(self.f, sib)
        a, b = lax.div(self.s, 2), lax.rem(self.s, 2)
        self.r = a * (1 - b) + (n - 1 - a) * b

    def seq_at(self, j):
        if j == 0:
            return self.s
        n = self.n
        q = lax.rem(self.r + (j + n), n)
        t = lax.div(q, n // 2)
        return (1 - t) * 2 * q + t * (2 * (n - 1 - q) + 1)

    def dev(self, s, c):
        return (s, self.p * self.sib + c)

    def col(self, dp, dc):
        return lax.rem(self.p + dp, self.planes) * self.sib + lax.rem(self.c + dc, self.sib)

    def barrier(self):
        sem = pltpu.get_barrier_semaphore()
        group = self.n * self.sib
        tau = self.s * self.sib + self.c
        for j in range(1, group):
            t = lax.rem(tau + j, group)
            pl.semaphore_signal(
                sem, inc=1, device_id=self.dev(lax.div(t, self.sib), lax.rem(t, self.sib)),
                device_id_type=MESH,
            )
        for dp in range(1, self.planes):
            for dc in range(self.sib):
                pl.semaphore_signal(
                    sem, inc=1, device_id=(self.s, self.col(dp, dc)), device_id_type=MESH
                )
        pl.semaphore_wait(sem, group - 1 + (self.planes - 1) * self.sib)


class Gather:
    def __init__(self, at, part, sems):
        self.at, self.part = at, part
        self.ring_s, self.ring_r = sems[:2]
        self.share = at.sib > 1 and len(sems) > 2
        if self.share:
            self.sib_s, self.sib_r = sems[2:]
        self.sent = []

    @staticmethod
    def scratch(n, share=True):
        d = pltpu.SemaphoreType.DMA
        ring = [d((2, n // 2, 2)), d((2, n // 2, 2))]
        return ring + [d((n, 2)), d((n, 2))] if share else ring

    def _send(self, copy):
        copy.start()
        self.sent.append(copy)

    def _ring(self, way, hop, half):
        at = self.at
        src = self.part(at.c, at.seq_at(-(hop - 1) if way == 0 else hop - 1), half)
        to = at.dev(at.seq_at(1 if way == 0 else -1), at.c)
        self._send(
            rdma(src, src, self.ring_s.at[way, hop - 1, half], self.ring_r.at[way, hop - 1, half], to)
        )

    def _sib(self, j, half):
        at = self.at
        if self.share:
            src = self.part(at.c, at.seq_at(j), half)
            slot = j % at.n
            self._send(
                rdma(src, src, self.sib_s.at[slot, half], self.sib_r.at[slot, half],
                     at.dev(at.s, 1 - at.c))
            )

    def start(self):
        self._ring(0, 1, 0)
        self._ring(1, 1, 1)
        self._ring(0, 1, 1)
        self._ring(1, 1, 0)
        self._sib(0, 0)
        self._sib(0, 1)

    def _arrive(self, way, hop, half):
        at = self.at
        j = -hop if way == 0 else hop
        ref = self.part(at.c, at.seq_at(j), half)
        rdma(ref, ref, self.ring_s.at[way, hop - 1, half], self.ring_r.at[way, hop - 1, half],
             at.dev(at.s, at.c)).wait_recv()
        last = at.n // 2
        if hop + 1 < last or (hop + 1 == last and half == way):
            self._ring(way, hop + 1, half)
        if hop == last:
            j = last
        self._sib(j, half)

    def hop(self, hop):
        self.hop_first(hop)
        self.hop_second(hop)

    def hop_first(self, hop):
        self._arrive(0, hop, 0)
        self._arrive(1, hop, 1)

    def hop_second(self, hop):
        if hop < self.at.n // 2:
            self._arrive(0, hop, 1)
            self._arrive(1, hop, 0)

    def sib_wait(self, j):
        at = self.at
        if self.share:
            for half in range(2):
                ref = self.part(1 - at.c, at.seq_at(j), half)
                slot = j % at.n
                rdma(ref, ref, self.sib_s.at[slot, half], self.sib_r.at[slot, half],
                     at.dev(at.s, at.c)).wait_recv()

    def stages(self):
        last = self.at.n // 2
        yield 0, [0]
        for h in range(1, last):
            yield h, [-h, h]
        yield last, [last]

    def wait_stage(self, h, offsets):
        if h:
            self.hop(h)
        for j in offsets:
            self.sib_wait(j)

    def drain(self):
        for copy in self.sent:
            copy.wait_send()


class Move:
    def __init__(self, at, src, dst, sems, every_core=True):
        self.at, self.src, self.dst = at, src, dst
        self.ssem, self.rsem, self.hop, self.own = sems
        self.cores = at.sib if every_core else 1
        self.relay = at.planes == 4

    @staticmethod
    def sems(planes, sib):
        d = pltpu.SemaphoreType.DMA
        return [d((planes, sib)), d((planes, sib)), d((sib,)), d((1,))]

    def _pairs(self):
        for dp in [2, 1, 3] if self.relay else range(1, self.at.planes):
            for dc in range(self.cores):
                yield dp, dc
        for dc in range(1, self.cores):
            yield 0, dc

    def _direct(self, dp, body):
        if self.relay and dp in (1, 3):
            pl.when(self.at.p != (3 if dp == 1 else 0))(body)
        else:
            body()

    def _send(self, dp, dc):
        at = self.at
        return rdma(self.src(lax.rem(at.c + dc, at.sib)), self.dst(at.f), self.ssem.at[dp, dc],
                    self.rsem.at[dp, dc], (at.s, at.col(dp, dc)))

    def _local(self):
        return pltpu.make_async_copy(self.src(self.at.c), self.dst(self.at.f), self.own.at[0])

    def start(self):
        self._local().start()
        for dp, dc in self._pairs():
            self._direct(dp, lambda: self._send(dp, dc).start())

    def _got(self, dp, dc):
        at = self.at
        source = lax.rem(at.p - dp + at.planes, at.planes) * at.sib + lax.rem(
            at.c - dc + at.sib, at.sib
        )
        ref = self.dst(source)
        rdma(ref, ref, self.ssem.at[dp, dc], self.rsem.at[dp, dc], (at.s, at.f)).wait_recv()
        return ref

    def pass_on(self):
        at = self.at
        if not self.relay:
            return
        for dp, dc in self._pairs():
            if dp == 2:
                ref = self._got(dp, dc)
                for here, to, slot in ((2, 3, 3), (1, 0, 1)):
                    @pl.when(at.p == here)
                    def _():
                        rdma(ref, ref, self.hop.at[dc], self.rsem.at[slot, dc],
                             (at.s, to * at.sib + at.c)).start()

    def wait(self):
        for dp, dc in self._pairs():
            if not (self.relay and dp == 2):
                self._got(dp, dc)
        self._local().wait()

    def drain(self):
        at = self.at
        for dp, dc in self._pairs():
            self._direct(dp, lambda: self._send(dp, dc).wait_send())
            if self.relay and dp == 2:
                ref = self.dst(at.f)

                @pl.when(jnp.logical_or(at.p == 1, at.p == 2))
                def _():
                    rdma(ref, ref, self.hop.at[dc], self.rsem.at[0, dc], (at.s, at.f)).wait_send()


class Scatter:
    def __init__(self, at, bufs, sems, rows, cols):
        self.at, self.rows, self.cols = at, rows, pl.ds(0, cols)
        self.stage, self.sib_in, self.out, self.inn = bufs
        self.sib_s, self.sib_r, self.ring_s, self.ring_r = sems
        self.sent, self.handed = [], []

    @staticmethod
    def scratch(n, shape):
        return [
            pltpu.VMEM((2, *shape), BF), pltpu.VMEM((n, *shape), BF),
            pltpu.VMEM((2, n // 2, *shape), BF), pltpu.VMEM((2, n // 2, *shape), BF),
        ]

    @staticmethod
    def views(stage, sib_in, out, inn):
        return (
            lambda k: stage.at[k], lambda k: sib_in.at[k],
            lambda w, k: out.at[w, k], lambda w, k: inn.at[w, k],
        )

    @staticmethod
    def sems(n):
        d = pltpu.SemaphoreType.DMA
        return [d((n,)), d((n,)), d((2, n // 2)), d((2, n // 2))]

    def offsets(self):
        last = self.at.n // 2
        order = [last]
        for h in range(last - 1, 0, -1):
            order += [h, -h]
        return order + [0]

    def to_sibling(self, k, produce):
        at = self.at
        if at.sib == 1:
            return
        if k >= 2:
            self.handed[k - 2].wait_send()
        view = self.stage(k % 2).at[pl.ds(0, self.rows), self.cols]
        produce(1 - at.c, at.seq_at(self.offsets()[k]), view)
        copy = rdma(view, self.sib_in(k).at[pl.ds(0, self.rows), self.cols],
                    self.sib_s.at[k], self.sib_r.at[k], at.dev(at.s, 1 - at.c))
        copy.start()
        self.handed.append(copy)

    def open(self, stage, ring, finish):
        self.to_sibling(0, stage)
        self.step(0, ring, finish)
        for k in range(1, len(self.offsets())):
            self.to_sibling(k, stage)

    def _send(self, way, k, rows):
        at = self.at
        src = self.out(way, k).at[rows, self.cols]
        copy = rdma(src, self.inn(way, k).at[rows, self.cols], self.ring_s.at[way, k], self.ring_r.at[way, k],
                    at.dev(at.seq_at(1 if way == 0 else -1), at.c))
        copy.start()
        self.sent.append(copy)

    def _wait(self, way, k, rows):
        ref = self.inn(way, k).at[rows, self.cols]
        at = self.at
        rdma(ref, ref, self.ring_s.at[way, k], self.ring_r.at[way, k],
             at.dev(at.s, at.c)).wait_recv()

    def step(self, k, produce, finish):
        at = self.at
        last = at.n // 2
        length = self.rows
        half = length // 2
        halves = (pl.ds(0, half), pl.ds(half, half))
        whole = pl.ds(0, length)
        j = self.offsets()[k]
        if at.sib > 1:
            ref = self.sib_in(k).at[pl.ds(0, length), self.cols]
            rdma(ref, ref, self.sib_s.at[k], self.sib_r.at[k], at.dev(at.s, at.c)).wait_recv()
        h = abs(j)
        if h == last:
            got = []
        else:
            ways = (0, 1) if h == 0 else ((0,) if j > 0 else (1,))
            rows_in = [halves[w] if h + 1 == last else whole for w in ways]
            got = [(w, rw) for w, rw in zip(ways, rows_in)]
        pending = [True]

        def store(cols, value, k=k, h=h, j=j, got=got, pending=pending):
            if pending[0]:
                for w, rw in got:
                    self._wait(w, h, rw)
                pending[0] = False
            if at.sib > 1:
                value = value + self.sib_in(k)[pl.ds(0, length), cols].astype(F32)
            for w, rw in got:
                if h + 1 == last:
                    add = self.inn(w, h)[pl.ds(w * half, half), cols].astype(F32)
                    if w == 0:
                        value = jnp.concatenate([value[:half] + add, value[half:]], axis=0)
                    else:
                        value = jnp.concatenate([value[:half], value[half:] + add], axis=0)
                else:
                    value = value + self.inn(w, h)[pl.ds(0, length), cols].astype(F32)
            if h == last:
                low = value.astype(BF)
                self.out(0, h - 1)[pl.ds(0, half), cols] = low[:half]
                self.out(1, h - 1)[pl.ds(half, half), cols] = low[half:]
            elif h:
                self.out(0 if j > 0 else 1, h - 1)[pl.ds(0, length), cols] = value.astype(BF)
            else:
                finish(cols, value)

        produce(at.c, at.seq_at(j), store)
        if h == last:
            self._send(0, h - 1, halves[0])
            self._send(1, h - 1, halves[1])
        elif h:
            self._send(0 if j > 0 else 1, h - 1, whole)

    def drain(self):
        for copy in self.sent + self.handed[-2:]:
            copy.wait_send()


class Credits:
    def __init__(self, at, sem):
        self.at, self.sem = at, sem

    def give(self):
        at = self.at
        if at.sib > 1:
            pl.semaphore_signal(
                self.sem, inc=1, device_id=at.dev(at.s, 1 - at.c), device_id_type=MESH
            )
        for way in (1, -1):
            pl.semaphore_signal(
                self.sem, inc=1, device_id=at.dev(at.seq_at(way), at.c), device_id_type=MESH
            )

    def take(self):
        pl.semaphore_wait(self.sem, 3 if self.at.sib > 1 else 2)


def nt(a, b):
    return lax.dot_general(a, b, (((1,), (1,)), ((), ())), preferred_element_type=F32)


def tn(a, b):
    return lax.dot_general(a, b, (((0,), (0,)), ((), ())), preferred_element_type=F32)


def nn(a, b):
    return lax.dot_general(a, b, (((1,), (0,)), ((), ())), preferred_element_type=F32)


def rope(value, cos, front, back):
    return value * cos + pltpu.roll(value, 80, 1) * front + pltpu.roll(value, 48, 1) * back


def forward_kernel(
    dims,
    x, cot, cos, front, back, widen, widen_att, gain_cols, wq_s, gu_s, dn_s, wo_s,
    o_n1, o_qkv, o_lse, o_gh, o_att, o_block, o_ghid, o_wq, o_sgu, o_rgu, o_sdn,
    hid,
    nbuf, cbuf, qkv, wq, wqp, wo, gu, dn, act, ggu, att_out, att_in, gh_in, stg, sgu_t,
    wo_f, wq_b, gu_b, dn_b, wo_b,
    sc_stage, sc_in, sc_out, sc_inn,
    zw_a, zw_b, zw_c, zw_d, zo_a, zo_b, zo_c, zo_d, zd_a, zd_b, zd_c, zd_d,
    zg_a, zg_b, zg_c, zg_d, z_ss, z_sr, local, loads,
    n1_a, n1_b, n1_c, n1_d, ct_a, ct_b, ct_c, ct_d, n2_a, n2_b, n2_c, n2_d, wo_ga, wo_gb, wo_gc, wo_gd,
    rs_a, rs_b, rs_c, rs_d, ds_a, ds_b, ds_c, ds_d, at_s, at_r, gh_s, gh_r, near_s, near_r, free,
):
    n, sib, planes = dims
    at = Place(n, sib, planes)
    length, width = x.shape
    seq_len = n * length
    raw = len(wq_s.shape) == 2
    _, rows, head_cols = wq_b.shape
    owners = planes * sib
    chunks = GROUP * HEAD_DIM // rows
    units = dn_b.shape[0]
    local_units = planes * units
    parts = 2 if units % 128 == 0 else 1
    wide = local_units // parts
    part_cols = wo_b.shape[1]
    heads_per = rows // HEAD_DIM
    half_len = length // 2
    tau = at.s * sib + at.c
    scale = HEAD_DIM ** (-0.5)
    log2e = 1.4426950408889634
    sent = []

    def token_part(ref):
        return lambda c, s, h: ref.at[c, s, pl.ds(h * half_len, half_len)]

    def owner_rows(f):
        return pl.ds(pl.multiple_of(f * rows, rows), rows)

    if raw:
        gu_f = (o_ghid, hid)

        def cut(ref, k, lo, size, dst):
            return pltpu.make_async_copy(
                ref.at[:, pl.ds(pl.multiple_of(lo, 128), size)], dst, loads.at[k]
            )

        def wq_f(c):
            return gu_f[c].at[pl.ds(0, rows), pl.ds(2 * local_units, head_cols)]

        in_wq = [
            cut(wq_s, 3 + 2 * owners + c, (at.s * sib + c) * head_cols, head_cols, wq_f(c))
            for c in range(sib)
        ]
        in_wo = cut(wo_s, 1, at.s * part_cols, part_cols, wo_f)
        half_units = units // 2

        def dn_f(h):
            return gu_f[h].at[pl.ds(rows, half_units)]

        in_dn = [
            pltpu.make_async_copy(
                dn_s.at[pl.ds(pl.multiple_of(at.s * units + h * half_units, half_units), half_units)],
                dn_f(h), loads.at[2 * h],
            )
            for h in range(2)
        ]
        in_gu = []

        def gu_lane(p, g):
            return p * units // wide * 2 * wide + g * wide + p * units % wide

        for c in range(sib):
            for p in range(planes):
                for g in range(2):
                    lo = (g * owners + p * sib + c) * (n * units) + at.s * units
                    k = (c * planes + p) * 2 + g
                    in_gu.append(
                        cut(gu_s, 3 + k, lo, units,
                            gu_f[c].at[pl.ds(0, rows), pl.ds(gu_lane(p, g), units)])
                    )
        for copy in (*in_wq, in_wo, *in_dn, *in_gu):
            copy.start()
        wq_x, gu_x, dn_x, wo_x = wq_b, gu_b, dn_b, wo_b
    else:
        wq_x, gu_x, dn_x, wo_x = wq_s, gu_s, dn_s, wo_s

    move_wq = Move(at, lambda c: wq_x.at[c], lambda f: wq.at[owner_rows(f)], (zw_a, zw_b, zw_c, zw_d))
    move_wo = Move(
        at, lambda c: wo_x, lambda f: wo.at[lax.rem(f, sib), at.s, lax.div(f, sib)],
        (zo_a, zo_b, zo_c, zo_d), False,
    )
    move_dn = Move(
        at, lambda c: dn_x,
        lambda f: dn.at[pl.ds(pl.multiple_of(lax.div(f, sib) * units, units), units)],
        (zd_a, zd_b, zd_c, zd_d), False,
    )

    def gu_move(k):
        return Move(
            at, lambda c: gu_x.at[k, c], lambda f: gu.at[k, owner_rows(f)],
            (zg_a.at[k], zg_b.at[k], zg_c.at[k], zg_d.at[k]),
        )

    move_gu = [gu_move(k) for k in range(parts)]

    x_f = x[...].astype(F32)
    inv_one = lax.rsqrt(jnp.mean(x_f * x_f, axis=-1, keepdims=True) + NORM_EPS)
    nbuf[at.c, at.s] = (x_f * inv_one).astype(BF)
    cbuf[at.c, at.s] = cot[...]
    n_one = Gather(at, token_part(nbuf), (n1_a, n1_b, n1_c, n1_d))
    at.barrier()
    n_one.start()
    if raw:
        g_one = gain_cols[:, 0:1]
        for c in range(sib):
            in_wq[c].wait()
            wq_b[c] = (wq_f(c)[...] * g_one).astype(BF)
        in_wo.wait()
        wo_b[...] = wo_f[...].astype(BF)
    move_wq.start()
    if raw:
        for h in range(2):
            in_dn[h].wait()
            dn_b[h * half_units : (h + 1) * half_units] = dn_f(h)[...].astype(BF)
        for copy in in_gu:
            copy.wait()
        g_two = gain_cols[:, 1:2]
        for c in range(sib):
            for k in range(parts):
                lanes = slice(k * 2 * wide, (k + 1) * 2 * wide)
                gu_b[k, c] = (gu_f[c][0:rows, lanes] * g_two).astype(BF)
    n_stages = list(n_one.stages())
    n_one.hop_first(1)
    move_wq.pass_on()
    move_wo.start()
    n_one.hop_second(1)
    for h, _ in n_stages[2:-1]:
        n_one.hop(h)
    move_wq.wait()
    move_gu[0].start()

    @pl.loop(0, width // 256)
    def _(t):
        here = pl.ds(pl.multiple_of(t * 256, 256), 256)
        wqp[here] = nn(wq[here], widen[...]).astype(BF)

    save_wq = pltpu.make_async_copy(wqp, o_wq, local.at[2])
    save_wq.start()

    def project(c, s):
        y = nn(nbuf[c, s], wqp[...]).astype(BF)
        here = pl.ds(pl.multiple_of(s * length, length), length)
        cs, fr, bk = cos[here], front[here], back[here]
        for k in range(3):
            lanes = slice(128 * k, 128 * k + 128)
            qkv[c, here, lanes] = rope(y[:, lanes].astype(F32), cs, fr, bk).astype(BF)
        qkv[c, here, 384:512] = y[:, 384:512]

    for h, offsets in n_stages:
        if h == n // 2:
            n_one.hop(h)
        for j in offsets:
            n_one.sib_wait(j)
            s_j = at.seq_at(j)

            @pl.loop(0, sib)
            def _(c):
                project(c, s_j)

    cot_gather = Gather(at, token_part(cbuf), (ct_a, ct_b, ct_c, ct_d))
    save_n1 = pltpu.make_async_copy(nbuf, o_n1, local.at[3])
    save_n1.start()
    save_qkv = pltpu.make_async_copy(qkv, o_qkv, local.at[4])
    save_qkv.start()

    tri = lax.broadcasted_iota(jnp.int32, (length, length), 0) >= lax.broadcasted_iota(
        jnp.int32, (length, length), 1
    )

    def spot(k, b, i):
        return (k * sib + b) * n + i

    def attend(i):
        @pl.loop(0, sib)
        def _(b):
            past = i * length
            here = slice(past, past + length)
            outs = []
            for h in range(GROUP):
                q = qkv[b, here, 128 * h : 128 * h + 128]
                d = jnp.where(tri, nt(q, qkv[b, here, 256:384]) * (scale * log2e), -1e30)
                m = jnp.max(d, axis=1, keepdims=True)
                if i:
                    e = nt(q, qkv[b, 0:past, 256:384]) * (scale * log2e)
                    m = jnp.maximum(m, jnp.max(e, axis=1, keepdims=True))
                d = jnp.exp2(d - m)
                total = jnp.sum(d, axis=1, keepdims=True)
                o = nn(d.astype(BF), qkv[b, here, 384:512])
                if i:
                    e = jnp.exp2(e - m)
                    total = total + jnp.sum(e, axis=1, keepdims=True)
                    o = o + nn(e.astype(BF), qkv[b, 0:past, 384:512])
                outs.append((o / total).astype(BF))
                lse = jnp.broadcast_to(m + jnp.log2(total), (length, 128))
                o_lse[b, h, i] = lse.T[0:8]
            for k in range(chunks):
                pair = jnp.concatenate(outs[k * heads_per : (k + 1) * heads_per], axis=1)
                att_out[spot(k, b, i)] = nt(pair, widen_att[...]).astype(BF)

    def send_attended(i):
        for k in range(chunks):
            for b in range(sib):
                mine = jnp.logical_and(at.s == i, at.c == b)

                @pl.when(mine)
                def _():
                    att_in[tau * chunks + k] = att_out[spot(k, b, i)]

                @pl.when(jnp.logical_not(mine))
                def _():
                    rdma(att_out.at[spot(k, b, i)], att_in.at[tau * chunks + k], at_s.at[k, b, i],
                         at_r.at[tau * chunks + k], at.dev(i, b)).start()

    wo_gather = Gather(
        at, lambda c, s, h: wo.at[c, s, pl.ds(h * (planes // 2), planes // 2)],
        (wo_ga, wo_gb, wo_gc, wo_gd),
    )
    attend(n - 1)
    save_n1.wait()
    n_one.drain()
    send_attended(n - 1)
    move_wo.pass_on()
    move_wo.wait()
    wo_gather.start()
    for move in move_gu[1:]:
        move.start()
    for i in range(n - 2, -1, -1):
        attend(i)
        send_attended(i)
    wo_hops = list(wo_gather.stages())
    for h, _ in wo_hops[1:-1]:
        wo_gather.hop(h)
    cot_gather.start()
    wo_gather.hop(n // 2)
    for _, offsets in wo_hops:
        for j in offsets:
            wo_gather.sib_wait(j)
    wo_gather.drain()
    save_qkv.wait()
    save_wq.wait()

    group = n * sib
    for j in range(1, group):
        t = lax.rem(tau + j, group)
        for k in range(chunks):
            ref = att_in.at[t * chunks + k]
            rdma(ref, ref, at_s.at[0, 0, 0], at_r.at[t * chunks + k], at.dev(at.s, at.c)).wait_recv()
    for k in range(chunks):
        for i in range(n):
            for b in range(sib):
                @pl.when(jnp.logical_not(jnp.logical_and(at.s == i, at.c == b)))
                def _():
                    rdma(att_out.at[spot(k, b, i)], att_out.at[spot(k, b, i)], at_s.at[k, b, i],
                         at_r.at[0], at.dev(at.s, at.c)).wait_send()
    save_att = pltpu.make_async_copy(att_in, o_att, local.at[3])
    save_att.start()

    x_f = x[...].astype(F32)
    for s in range(n):
        cols = slice(s * part_cols, (s + 1) * part_cols)
        acc = x_f[:, cols]
        for p in range(planes):
            for c in range(sib):
                acc = acc + nn(att_in[p * sib + c], wo[c, s, p])
        hid[:, cols] = acc
    hidden = hid[...]
    inv_mid = lax.rsqrt(jnp.mean(hidden * hidden, axis=-1, keepdims=True) + NORM_EPS)
    nbuf[at.c, at.s] = (hidden * inv_mid).astype(BF)
    n_two = Gather(at, token_part(nbuf), (n2_a, n2_b, n2_c, n2_d))
    n_two.start()

    stages = list(n_two.stages())
    move_gu[0].pass_on()
    move_dn.start()
    for h, _ in stages[1:-1]:
        cot_gather.hop(h)
        n_two.hop(h)

    def gate_pass(k, c, s):
        y = nn(nbuf[c, s], gu[k])
        gate, up = y[:, :wide], y[:, wide:]
        act[c, s, :, k * wide : (k + 1) * wide] = (gate / (1.0 + jnp.exp(-gate)) * up).astype(BF)
        ggu[c, s, :, k * 2 * wide : (k + 1) * 2 * wide] = y.astype(BF)

    def grad_pass(c, s):
        for k in range(parts):
            lo = k * 2 * wide
            gate = ggu[c, s, :, lo : lo + wide].astype(F32)
            up = ggu[c, s, :, lo + wide : lo + 2 * wide].astype(F32)
            grad_act = nt(cbuf[c, s], dn[k * wide : (k + 1) * wide])
            sig = 1.0 / (1.0 + jnp.exp(-gate))
            ggu[c, s, :, lo : lo + wide] = (
                grad_act * up * sig * (1.0 + gate * (1.0 - sig))
            ).astype(BF)
            ggu[c, s, :, lo + wide : lo + 2 * wide] = (grad_act * (gate * sig)).astype(BF)

    def every_block(body):
        @pl.loop(0, n)
        def _(s):
            @pl.loop(0, sib)
            def _(c):
                body(c, s)

    move_gu[0].wait()
    for h, offsets in stages:
        if h == n // 2:
            for move in move_gu[1:]:
                move.pass_on()
            cot_gather.hop(h)
            n_two.hop(h)
        for j in offsets:
            n_two.sib_wait(j)
            s_j = at.seq_at(j)

            @pl.loop(0, sib)
            def _(c):
                gate_pass(0, c, s_j)

    for k in range(1, parts):
        move_gu[k].wait()
        if k == parts - 1:
            move_dn.pass_on()
        every_block(lambda c, s: gate_pass(k, c, s))
    if parts == 1:
        move_dn.pass_on()
    for _, offsets in stages:
        for j in offsets:
            cot_gather.sib_wait(j)
    move_dn.wait()
    every_block(grad_pass)

    scatter = Scatter(
        at, Scatter.views(sc_stage, sc_in, sc_out, sc_inn), (rs_a, rs_b, rs_c, rs_d), length, width
    )
    tile = 512

    def column_tiles():
        return [slice(t * tile, (t + 1) * tile) for t in range(width // tile)]

    def mid_part(c, s, cols):
        acc = nt(ggu[c, s, :, 0 : 2 * wide], gu[0, cols, :])
        for k in range(1, parts):
            acc = acc + nt(ggu[c, s, :, k * 2 * wide : (k + 1) * 2 * wide], gu[k, cols, :])
        return acc

    def to_stage(c, s, ref):
        for cols in column_tiles():
            ref[:, cols] = mid_part(c, s, cols).astype(BF)

    def to_ring(c, s, store):
        for cols in column_tiles():
            store(cols, mid_part(c, s, cols))

    tokens = sib * seq_len
    down_copies = []

    def grad_down():
        cot_all = cbuf[...].reshape(tokens, width)
        down_rows = local_units // 2
        for t in range(2):
            rows_here = slice(t * down_rows, (t + 1) * down_rows)
            lhs = act[:, :, :, rows_here].reshape(tokens, down_rows)
            stg[rows_here] = tn(lhs, cot_all).astype(BF)
        own = pltpu.make_async_copy(
            stg.at[pl.ds(pl.multiple_of(at.p * units, units), units)], o_sdn.at[at.p], local.at[6]
        )
        own.start()
        down_copies.append(own)
        for dp in range(1, planes):
            to = lax.rem(at.p + dp, planes)
            copy = rdma(stg.at[pl.ds(pl.multiple_of(to * units, units), units)], o_sdn.at[at.p],
                        z_ss.at[dp], z_sr.at[dp], (at.s, at.col(dp, 0)))
            copy.start()
            sent.append(copy)

    gu_tile = sgu_t.shape[1]
    gu_steps = width // gu_tile
    near = planes == 4

    def gu_copy(m, slot):
        return pltpu.make_async_copy(
            sgu_t.at[slot], o_sgu.at[pl.ds(m * gu_tile, gu_tile)], local.at[7 + slot]
        )

    def near_send(m, dc):
        to = m * sib + lax.rem(at.c + dc, sib)
        return rdma(o_sgu.at[owner_rows(to)], o_rgu.at[at.f], near_s.at[m, dc],
                    near_r.at[at.p, dc], (at.s, to))

    def if_near(m, body):
        pl.when(jnp.logical_or(at.p == m - 1, at.p == m + 1))(body)

    def grad_gu():
        for m in range(gu_steps):
            slot = m % 2
            if m >= 2:
                gu_copy(m - 2, slot).wait()
            lhs = nbuf[:, :, :, m * gu_tile : (m + 1) * gu_tile].reshape(tokens, gu_tile)
            sgu_t[slot] = tn(lhs, ggu[...].reshape(tokens, 2 * local_units)).astype(BF)
            gu_copy(m, slot).start()
        for m in range(max(0, gu_steps - 2), gu_steps):
            gu_copy(m, m % 2).wait()
        if near:
            for m in range(planes):
                for dc in range(sib):
                    if_near(m, lambda: near_send(m, dc).start())

    def finish(cols, value):
        o_ghid[:, cols] = value

    def flat(ref, base):
        return lambda w, k: ref.at[base, w * (n // 2) + k]

    down = Scatter(
        at, (lambda k: cbuf.at[0, k], lambda k: nbuf.at[0, k], flat(cbuf, sib - 1), flat(nbuf, sib - 1)),
        (ds_a, ds_b, ds_c, ds_d), length, width,
    )

    def down_stage(c, s, ref):
        for cols in column_tiles():
            ref[:, cols] = nn(act[c, s], dn[:, cols]).astype(BF)

    def down_ring(c, s, store):
        for cols in column_tiles():
            store(cols, nn(act[c, s], dn[:, cols]))

    def down_finish(cols, value):
        o_block[:, cols] = (hid[:, cols] + value).astype(BF)

    credits = Credits(at, free)
    last = len(scatter.offsets()) - 1
    scatter.open(to_stage, to_ring, finish)
    grad_down()
    for k in range(1, last):
        scatter.step(k, to_ring, finish)
    grad_gu()
    cot_gather.drain()
    n_two.drain()
    credits.give()
    credits.take()
    down.open(down_stage, down_ring, down_finish)
    scatter.step(last, to_ring, finish)
    e_mid = o_ghid[...]
    hidden = hid[...]
    inv_mid = lax.rsqrt(jnp.mean(hidden * hidden, axis=-1, keepdims=True) + NORM_EPS)
    norm_mid = hidden * inv_mid
    o_ghid[...] = cot[...].astype(F32) + inv_mid * (
        e_mid - norm_mid * jnp.mean(e_mid * norm_mid, axis=-1, keepdims=True)
    )
    branch = o_ghid[...].astype(BF)
    for f in range(owners):
        p, c = f // sib, f % sib
        acc = nt(branch[:, :part_cols], wo[c, 0, p])
        for s in range(1, n):
            acc = acc + nt(branch[:, s * part_cols : (s + 1) * part_cols], wo[c, s, p])
        att_out[f] = acc.astype(BF)
        t, k = f // chunks, f % chunks
        mine = tau == t

        @pl.when(mine)
        def _():
            gh_in[k, at.c, at.s] = att_out[f]

        @pl.when(jnp.logical_not(mine))
        def _():
            rdma(att_out.at[f], gh_in.at[k, at.c, at.s], gh_s.at[f], gh_r.at[k, tau],
                 at.dev(t // sib, t % sib)).start()

    for k in range(1, last):
        down.step(k, down_ring, down_finish)
    for j in range(1, group):
        t = lax.rem(tau + j, group)
        for k in range(chunks):
            ref = gh_in.at[k, lax.rem(t, sib), lax.div(t, sib)]
            rdma(ref, ref, gh_s.at[0], gh_r.at[k, t], at.dev(at.s, at.c)).wait_recv()
    save_gh = pltpu.make_async_copy(gh_in, o_gh, local.at[0])
    save_gh.start()
    for f in range(owners):
        @pl.when(jnp.logical_not(tau == f // chunks))
        def _():
            rdma(att_out.at[f], att_out.at[f], gh_s.at[f], gh_r.at[0, 0],
                 at.dev(at.s, at.c)).wait_send()

    down.step(last, down_ring, down_finish)

    for dp in range(1, planes):
        ref = o_sdn.at[lax.rem(at.p - dp + planes, planes)]
        rdma(ref, ref, z_ss.at[dp], z_sr.at[dp], (at.s, at.f)).wait_recv()
    for copy in down_copies:
        copy.wait()
    if near:
        for q in range(planes):
            for dc in range(sib):
                def arrived():
                    ref = o_rgu.at[q * sib + lax.rem(at.c - dc + sib, sib)]
                    rdma(ref, ref, near_s.at[q, dc], near_r.at[q, dc], (at.s, at.f)).wait_recv()
                    near_send(q, dc).wait_send()

                if_near(q, arrived)
    scatter.drain()
    down.drain()
    for move in (move_wq, move_wo, move_dn, *move_gu):
        move.drain()
    for copy in sent:
        copy.wait_send()
    save_att.wait()
    save_gh.wait()


def forward_call(dims, sizes, x, cot, tables, widen, widen_att, gain_cols, wq_s, gu_s, dn_s, wo_s):
    n, sib, planes = dims
    rows, units = sizes
    length, width = x.shape
    part_cols = width // n
    head_cols = (GROUP + 2) * HEAD_DIM
    owners = planes * sib
    chunks = GROUP * HEAD_DIM // rows
    ffl = planes * units
    parts = 2 if units % 128 == 0 else 1
    seq_len = n * length
    vm, hb = pl.BlockSpec(memory_space=pltpu.VMEM), pl.BlockSpec(memory_space=pl.ANY)
    blocks = (sib, n, length, width)
    sds = jax.ShapeDtypeStruct
    outs = [
        (sds(blocks, BF), hb),
        (sds((sib, seq_len, 512), BF), hb),
        (sds((sib, GROUP, n, 8, length), F32), vm),
        (sds((chunks, sib, n, length, rows), BF), hb),
        (sds((owners, length, rows), BF), hb),
        (sds((length, width), BF), vm),
        (sds((length, width), F32), vm),
        (sds((width, 512), BF), hb),
        (sds((width, 2 * ffl), BF), hb),
        (sds((owners, rows, 2 * ffl), BF), hb),
        (sds((planes, units, width), BF), hb),
    ]
    dma = pltpu.SemaphoreType.DMA
    scratch = [
        pltpu.VMEM((length, width), F32),
        pltpu.VMEM(blocks, BF), pltpu.VMEM(blocks, BF), pltpu.VMEM((sib, seq_len, 512), BF),
        pltpu.VMEM((width, head_cols), BF), pltpu.VMEM((width, 512), BF),
        pltpu.VMEM((sib, n, planes, rows, part_cols), BF),
        pltpu.VMEM((parts, width, 2 * ffl // parts), BF), pltpu.VMEM((ffl, width), BF),
        pltpu.VMEM((sib, n, length, ffl), BF), pltpu.VMEM((sib, n, length, 2 * ffl), BF),
        pltpu.VMEM((owners, length, rows), BF), pltpu.VMEM((owners, length, rows), BF),
        pltpu.VMEM((chunks, sib, n, length, rows), BF),
        pltpu.VMEM((ffl, width), BF), pltpu.VMEM((2, 384, 2 * ffl), BF),

        pltpu.VMEM((rows, part_cols), F32),
        pltpu.VMEM((sib, rows, head_cols), BF),
        pltpu.VMEM((parts, sib, rows, 2 * ffl // parts), BF),
        pltpu.VMEM((units, width), BF), pltpu.VMEM((rows, part_cols), BF),
        *Scatter.scratch(n, (length, width)),
        *Move.sems(planes, sib), *Move.sems(planes, sib), *Move.sems(planes, sib),
        dma((parts, planes, sib)), dma((parts, planes, sib)), dma((parts, sib)), dma((parts, 1)),
        dma((planes,)), dma((planes,)), dma((9,)), dma((3 + 2 * owners + sib,)),
        *Gather.scratch(n), *Gather.scratch(n), *Gather.scratch(n), *Gather.scratch(n),
        *Scatter.sems(n), *Scatter.sems(n),
        dma((chunks, sib, n)), dma((owners,)), dma((owners,)), dma((chunks, n * sib)),
        dma((planes, sib)), dma((planes, sib)), pltpu.SemaphoreType.REGULAR,
    ]
    return pl.pallas_call(
        functools.partial(forward_kernel, dims),
        out_shape=[o[0] for o in outs],
        out_specs=[o[1] for o in outs],
        in_specs=[vm] * 8 + [hb] * 4,
        scratch_shapes=scratch,
        compiler_params=pltpu.CompilerParams(
            collective_id=0, has_side_effects=True, vmem_limit_bytes=VMEM_LIMIT
        ),
    )(x, cot, *tables, widen, widen_att, gain_cols, wq_s, gu_s, dn_s, wo_s)


def backward_kernel(
    dims,
    x, cos, front, back, widen, widen_att, lse,
    n1, qkv_h, gh_h, att_h, ghid, wqp_h, sgu, rgu_h, sdn_h,
    o_input, o_gq, o_ggu, o_gdn, o_gout,
    qkv, gh, att, wqp, sdn, gq, gk, gv, n1_t, sq, so, branch,
    r_gu, r_qkv, r_out, g_gu, g_qkv, g_dn, g_out,
    sc_stage, sc_in, sc_out, sc_inn, e_stage_b, e_sib_b, e_out_b, e_inn_b,
    loads, near_l, saves_gu, saves_qkv, saves_row, z_gs, z_gr, z_qs, z_qr, z_os, z_or,
    e_a, e_b, e_c, e_d, s_a, s_b, s_c, s_d,
    a_dn_s, a_dn_r, a_gu_s, a_gu_r, a_qk_s, a_qk_r, a_ou_s, a_ou_r,
):
    n, sib, planes = dims
    at = Place(n, sib, planes)
    length, width = x.shape
    owners = planes * sib
    chunks, _, _, _, rows = gh.shape
    heads_per = rows // HEAD_DIM
    part_cols = r_out.shape[2]
    scale = HEAD_DIM ** (-0.5)
    log2e = 1.4426950408889634
    tokens = sib * n * length
    sent = []
    near = planes == 4
    units = g_dn.shape[1]
    aligned = len(o_ggu.shape) == 2

    def load(src, dst, k):
        copy = pltpu.make_async_copy(src, dst, loads.at[k])
        copy.start()
        return copy

    def owner_rows(f):
        return pl.ds(pl.multiple_of(f * rows, rows), rows)

    def z_source(dp, dc):
        return (
            lax.rem(at.p - dp + planes, planes) * sib + lax.rem(at.c - dc + sib, sib)
        )

    def z_scatter(src, dst, ssem, rsem, k):
        own = load(src.at[owner_rows(at.f)], dst.at[at.f], k)
        for dp in range(planes):
            for dc in range(sib):
                if dp or dc:
                    to = at.col(dp, dc)
                    copy = rdma(src.at[owner_rows(to)], dst.at[at.f],
                                ssem.at[dp, dc], rsem.at[dp, dc], (at.s, to))
                    copy.start()
                    sent.append(copy)
        return own

    def z_collect(dst, ssem, rsem, own):
        own.wait()
        for dp in range(planes):
            for dc in range(sib):
                if dp or dc:
                    ref = dst.at[z_source(dp, dc)]
                    rdma(ref, ref, ssem.at[dp, dc], rsem.at[dp, dc], (at.s, at.f)).wait_recv()

    def plane_total(dst, c):
        acc = dst[c].astype(F32)
        for p in range(1, planes):
            acc = acc + dst[p * sib + c].astype(F32)
        return acc.astype(BF)

    def far(dp, body):
        if not near or dp == 0:
            body()
        elif dp == 2:
            body()
        else:
            pl.when(at.p == (3 if dp == 1 else 0))(body)

    def gu_pairs():
        for dp in [2, 1, 3, 0] if near else range(planes):
            for dc in range(sib):
                if dp or dc:
                    yield dp, dc

    def gu_send(dp, dc):
        to = at.col(dp, dc)
        return rdma(sgu.at[owner_rows(to)], r_gu.at[at.f], z_gs.at[dp, dc], z_gr.at[dp, dc],
                    (at.s, to))

    def gu_near(q, dc):
        f = q * sib + dc
        return pltpu.make_async_copy(rgu_h.at[f], r_gu.at[f], near_l.at[q, dc])

    def if_near(q, body):
        pl.when(jnp.logical_or(at.p == q - 1, at.p == q + 1))(body)

    def gu_wait(dp, dc):
        ref = r_gu.at[z_source(dp, dc)]
        rdma(ref, ref, z_gs.at[dp, dc], z_gr.at[dp, dc], (at.s, at.f)).wait_recv()

    def gu_arrived(dp, dc):
        if not near or dp in (0, 2):
            gu_wait(dp, dc)
        else:
            pl.when(at.p == (0 if dp == 1 else 3))(lambda: gu_wait(dp, dc))

    at.barrier()
    in_qkv, in_gh = load(qkv_h, qkv, 0), load(gh_h, gh, 1)
    in_sdn, in_att, in_wqp = load(sdn_h, sdn, 4), load(att_h, att, 6), load(wqp_h, wqp, 7)
    gu_own = load(sgu.at[owner_rows(at.f)], r_gu.at[at.f], 5)
    for dp, dc in gu_pairs():
        far(dp, lambda: gu_send(dp, dc).start())
    if near:
        for q in range(planes):
            for dc in range(sib):
                if_near(q, lambda: gu_near(q, dc).start())
    n1_cols = n1_t.shape[4]
    n1_steps = width // n1_cols

    def n1_load(m):
        return pltpu.make_async_copy(
            n1.at[:, :, :, pl.ds(m * n1_cols, n1_cols)], n1_t.at[m % 2], loads.at[8 + m % 2]
        )

    n1_load(0).start()
    n1_load(1).start()

    def row_half(ref):
        size = ref.shape[-2] // 2
        if len(ref.shape) == 4:
            return lambda c, s, h: ref.at[s, :, pl.ds(h * size, size)]
        return lambda c, s, h: ref.at[s, pl.ds(h * size, size)]

    in_sdn.wait()
    acc = sdn[0].astype(F32)
    for p in range(1, planes):
        acc = acc + sdn[p].astype(F32)
    g_dn[at.s] = acc.astype(BF)
    ag_dn = Gather(at, row_half(g_dn), (a_dn_s, a_dn_r))
    ag_dn.start()

    tri = lax.broadcasted_iota(jnp.int32, (length, length), 0) <= lax.broadcasted_iota(
        jnp.int32, (length, length), 1
    )

    def attend_back(b):
        gk[...] = jnp.zeros_like(gk)
        gv[...] = jnp.zeros_like(gv)
        for i in range(n):
            past = i * length
            here = slice(past, past + length)
            for h in range(GROUP):
                k, slot = h // heads_per, h % heads_per
                q = qkv[b, here, 128 * h : 128 * h + 128]
                do = nn(gh[k, b, i], widen_att[:, 128 * slot : 128 * slot + 128]).astype(BF)
                row = lse[b, h, i, 0:1]
                parts = [(here, True)] + ([(slice(0, past), False)] if i else [])
                probs, grads = [], []
                delta = 0.0
                for part, diagonal in parts:
                    sc = nt(qkv[b, part, 256:384], q) * (scale * log2e)
                    if diagonal:
                        sc = jnp.where(tri, sc, -1e30)
                    pr = jnp.exp2(sc - row)
                    dp = nt(qkv[b, part, 384:512], do)
                    delta = delta + jnp.sum(pr * dp, axis=0, keepdims=True)
                    probs.append(pr)
                    grads.append(dp)
                dq = jnp.zeros((length, 128), F32)
                for (part, _), pr, dp in zip(parts, probs, grads):
                    ds = (pr * (dp - delta) * scale).astype(BF)
                    gv[part] += nn(pr.astype(BF), do)
                    gk[part] += nn(ds, q)
                    dq = dq + tn(ds, qkv[b, part, 256:384])
                gq[b, here, 128 * h : 128 * h + 128] = rope(
                    dq, cos[here], -front[here], -back[here]
                ).astype(BF)
        for i in range(n):
            here = slice(i * length, (i + 1) * length)
            gq[b, here, 256:384] = rope(gk[here], cos[here], -front[here], -back[here]).astype(BF)
            gq[b, here, 384:512] = gv[here].astype(BF)

    tile = 512

    def tiles():
        return [slice(t * tile, (t + 1) * tile) for t in range(width // tile)]

    last = len(Scatter(at, (None,) * 4, (None,) * 4, rows, width).offsets()) - 1
    hops = n // 2

    s_out = Scatter(
        at, Scatter.views(sc_stage, sc_in, sc_out, sc_inn), (s_a, s_b, s_c, s_d),
        rows, planes * part_cols,
    )
    for s in range(n):
        branch[s] = ghid[:, s * part_cols : (s + 1) * part_cols].astype(BF)

    def out_pieces(c, s):
        low = branch[s]
        for p in range(planes):
            yield slice(p * part_cols, (p + 1) * part_cols), tn(att[p * sib + c], low)

    def out_stage(c, s, ref):
        for cols, value in out_pieces(c, s):
            ref[:, cols] = value.astype(BF)

    def out_ring(c, s, store):
        for cols, value in out_pieces(c, s):
            store(cols, value)

    def out_finish(cols, value):
        so[cols.start // part_cols] = value.astype(BF)

    in_att.wait()
    s_out.open(out_stage, out_ring, out_finish)
    in_qkv.wait()
    in_gh.wait()
    attend_back(0)
    ag_dn.hop(1)
    for k in range(1, last):
        s_out.step(k, out_ring, out_finish)
    if sib > 1:
        attend_back(1)
    for h in range(2, hops + 1):
        ag_dn.hop(h)
    s_out.step(last, out_ring, out_finish)
    out_own = load(so.at[at.p], r_out.at[at.p], 11)
    for dp in range(1, planes):
        to = lax.rem(at.p + dp, planes)
        copy = rdma(so.at[to], r_out.at[at.p], z_os.at[dp], z_or.at[dp], (at.s, at.col(dp, 0)))
        copy.start()
        sent.append(copy)

    for m in range(n1_steps):
        n1_load(m).wait()
        part = tn(n1_t[m % 2].reshape(tokens, n1_cols), gq[...].reshape(tokens, 512)).astype(BF)
        sq[m * n1_cols : (m + 1) * n1_cols] = nt(part, widen[...]).astype(BF)
        if m + 2 < n1_steps:
            n1_load(m + 2).start()
    qkv_own = z_scatter(sq, r_qkv, z_qs, z_qr, 10)

    in_wqp.wait()
    e_in = Scatter(
        at, Scatter.views(e_stage_b, e_sib_b, e_out_b, e_inn_b), (e_a, e_b, e_c, e_d), length, width
    )

    def gq_block(c, s):
        return gq[c, pl.ds(pl.multiple_of(s * length, length), length)]

    def e_stage(c, s, ref):
        for cols in tiles():
            ref[:, cols] = nt(gq_block(c, s), wqp[cols, :]).astype(BF)

    def e_ring(c, s, store):
        for cols in tiles():
            store(cols, nt(gq_block(c, s), wqp[cols, :]))

    def e_finish(cols, value):
        o_input[:, cols] = value

    e_in.open(e_stage, e_ring, e_finish)
    for k in range(1, last):
        e_in.step(k, e_ring, e_finish)

    gu_own.wait()
    if near:
        for q in range(planes):
            for dc in range(sib):
                if_near(q, lambda: gu_near(q, dc).wait())
    for dp, dc in gu_pairs():
        gu_arrived(dp, dc)
    for c in range(sib):
        g_gu[at.s, c] = plane_total(r_gu, c)
    ag_gu = Gather(at, row_half(g_gu), (a_gu_s, a_gu_r))
    ag_gu.start()

    wide = planes * units // 2

    def gu_lane(p, g):
        return p * units // wide * 2 * wide + g * wide + p * units % wide

    def save_gu(j):
        s = at.seq_at(j)
        slot = j % n
        if not aligned:
            return [pltpu.make_async_copy(g_gu.at[s], o_ggu.at[s], saves_gu.at[slot, 0])]
        copies = []
        for c in range(sib):
            for p in range(planes):
                for g in range(2):
                    lo = (g * owners + p * sib + c) * (n * units) + s * units
                    copies.append(pltpu.make_async_copy(
                        g_gu.at[s, c, :, pl.ds(gu_lane(p, g), units)],
                        o_ggu.at[:, pl.ds(pl.multiple_of(lo, 128), units)],
                        saves_gu.at[slot, (c * planes + p) * 2 + g],
                    ))
        return copies

    def save_qkv(j):
        s = at.seq_at(j)
        slot = j % n
        if not aligned:
            return [pltpu.make_async_copy(g_qkv.at[s], o_gq.at[s], saves_qkv.at[slot, 0])]
        cols = g_qkv.shape[3]
        return [
            pltpu.make_async_copy(
                g_qkv.at[s, c], o_gq.at[:, pl.ds(pl.multiple_of((s * sib + c) * cols, 128), cols)],
                saves_qkv.at[slot, c],
            )
            for c in range(sib)
        ]

    def save_out(j):
        s = at.seq_at(j)
        slot = j % n
        if not aligned:
            return [pltpu.make_async_copy(g_out.at[s], o_gout.at[s], saves_row.at[0, slot])]
        place = o_gout.at[:, pl.ds(pl.multiple_of(s * part_cols, 128), part_cols)]
        return [pltpu.make_async_copy(g_out.at[s], place, saves_row.at[0, slot])]

    def save_down(j):
        s = at.seq_at(j)
        place = o_gdn.at[pl.ds(pl.multiple_of(s * units, units), units)]
        return [pltpu.make_async_copy(g_dn.at[s], place, saves_row.at[1, j % n])]

    saves = []

    def save(copies):
        for copy in copies:
            copy.start()
        saves.extend(copies)

    ring = [0] + [j for h in range(1, hops) for j in (-h, h)] + [hops]
    for j in ring:
        save(save_down(j))
    e_in.step(last, e_ring, e_finish)
    x_f = x[...].astype(F32)
    inv_one = lax.rsqrt(jnp.mean(x_f * x_f, axis=-1, keepdims=True) + NORM_EPS)
    norm_one = x_f * inv_one
    e_val = o_input[...]
    o_input[...] = ghid[...] + inv_one * (
        e_val - norm_one * jnp.mean(e_val * norm_one, axis=-1, keepdims=True)
    )
    out_own.wait()
    for dp in range(1, planes):
        ref = r_out.at[lax.rem(at.p - dp + planes, planes)]
        rdma(ref, ref, z_os.at[dp], z_or.at[dp], (at.s, at.f)).wait_recv()
    acc = r_out[0].astype(F32)
    for p in range(1, planes):
        acc = acc + r_out[p].astype(F32)
    g_out[at.s] = acc.astype(BF)
    ag_out = Gather(at, row_half(g_out), (a_ou_s, a_ou_r))
    ag_out.start()
    save(save_out(0))
    save(save_gu(0))
    z_collect(r_qkv, z_qs, z_qr, qkv_own)
    for c in range(sib):
        g_qkv[at.s, c] = plane_total(r_qkv, c)
    ag_qkv = Gather(at, row_half(g_qkv), (a_qk_s, a_qk_r))
    ag_qkv.start()
    save(save_qkv(0))
    for h in range(1, hops + 1):
        for ag, put in ((ag_gu, save_gu), (ag_out, save_out), (ag_qkv, save_qkv)):
            ag.hop(h)
            for j in (-h, h) if h < hops else (h,):
                save(put(j))
    e_in.drain()
    s_out.drain()
    for ag in (ag_dn, ag_gu, ag_qkv, ag_out):
        ag.drain()
    for dp, dc in gu_pairs():
        far(dp, lambda: gu_send(dp, dc).wait_send())
    for copy in sent:
        copy.wait_send()
    for copy in saves:
        copy.wait()


def backward_call(dims, aligned, x, tables, widen, widen_att, lse, n1, qkv, gh, att, ghid, wqp, sgu, rgu, sdn):
    n, sib, planes = dims
    length, width = x.shape
    rows = gh.shape[4]
    owners = planes * sib
    units = sdn.shape[1]
    part_cols = width // n
    seq_len = n * length
    head_cols = (GROUP + 2) * HEAD_DIM
    vm, hb = pl.BlockSpec(memory_space=pltpu.VMEM), pl.BlockSpec(memory_space=pl.ANY)
    sds = jax.ShapeDtypeStruct
    g_shapes = [
        (n, sib, rows, head_cols), (n, sib, rows, sgu.shape[1]), (n, units, width),
        (n, rows, part_cols),
    ]
    o_shapes = g_shapes
    if aligned:
        o_shapes = [
            (rows, n * sib * head_cols), (rows, n * sib * sgu.shape[1]), None, (rows, width)
        ]
    o_shapes = [*o_shapes[:2], (n * units, width), o_shapes[3]]
    outs = [(sds((length, width), F32), vm)] + [(sds(shape, BF), hb) for shape in o_shapes]
    dma = pltpu.SemaphoreType.DMA
    scratch = [
        pltpu.VMEM(qkv.shape, BF), pltpu.VMEM(gh.shape, BF), pltpu.VMEM(att.shape, BF),
        pltpu.VMEM(wqp.shape, BF), pltpu.VMEM(sdn.shape, BF), pltpu.VMEM(qkv.shape, BF),
        pltpu.VMEM((seq_len, 128), F32), pltpu.VMEM((seq_len, 128), F32),
        pltpu.VMEM((2, *n1.shape[:3], 384), BF), pltpu.VMEM((width, head_cols), BF),
        pltpu.VMEM((planes, rows, part_cols), BF), pltpu.VMEM((n, length, part_cols), BF),
        pltpu.VMEM((owners, rows, sgu.shape[1]), BF), pltpu.VMEM((owners, rows, head_cols), BF),
        pltpu.VMEM((planes, rows, part_cols), BF),
        pltpu.VMEM(g_shapes[1], BF), pltpu.VMEM(g_shapes[0], BF), pltpu.VMEM(g_shapes[2], BF),
        pltpu.VMEM(g_shapes[3], BF),
        *Scatter.scratch(n, (length, max(width, planes * part_cols))),
        *Scatter.scratch(n, (length, width)),
        dma((12,)), dma((planes, sib)), dma((n, 2 * owners)), dma((n, sib)), dma((2, n)),
        dma((planes, sib)), dma((planes, sib)), dma((planes, sib)),
        dma((planes, sib)), dma((planes,)), dma((planes,)),
        *Scatter.sems(n), *Scatter.sems(n),
        *Gather.scratch(n, False), *Gather.scratch(n, False), *Gather.scratch(n, False),
        *Gather.scratch(n, False),
    ]
    return pl.pallas_call(
        functools.partial(backward_kernel, dims),
        out_shape=[o[0] for o in outs],
        out_specs=[o[1] for o in outs],
        in_specs=[vm] * 7 + [hb] * 4 + [vm] + [hb] * 4,
        scratch_shapes=scratch,
        compiler_params=pltpu.CompilerParams(
            collective_id=1, has_side_effects=True, vmem_limit_bytes=VMEM_LIMIT
        ),
    )(x, *tables, widen, widen_att, lse, n1, qkv, gh, att, ghid, wqp, sgu, rgu, sdn)


def adamw(weight, first, second, grad, rate, decay):
    first_new = BETA_ONE * first + (1.0 - BETA_ONE) * grad
    second_new = BETA_TWO * second + (1.0 - BETA_TWO) * grad * grad
    first_hat = first_new / (1.0 - BETA_ONE**ADAM_STEP)
    second_hat = second_new / (1.0 - BETA_TWO**ADAM_STEP)
    weight_new = weight - rate * (first_hat / (jnp.sqrt(second_hat) + ADAM_EPS) + decay * weight)
    return (weight_new, first_new, second_new)


def to_bf16(value):
    return lax.reduce_precision(value, exponent_bits=8, mantissa_bits=7)


def rope_arrays(seq_len):
    half = HEAD_DIM // 2
    frequencies = (ROPE_BASE ** (-(2.0 * np.arange(half)) / HEAD_DIM)).astype(np.float32)
    angles = np.arange(seq_len, dtype=np.float32)[:, None] * frequencies[None, :]
    cos, sin = np.cos(angles), np.sin(angles)
    pad = np.zeros((seq_len, 128 - HEAD_DIM), np.float32)
    none = np.zeros_like(sin)
    return tuple(
        np.concatenate(columns, axis=1).astype(np.float32)
        for columns in ([cos, cos, pad], [-sin, none, pad], [none, sin, pad])
    )


def widening(heads):
    row = np.arange(heads * HEAD_DIM)[:, None]
    col = np.arange(heads * 128)[None, :]
    return (col == row // HEAD_DIM * 128 + row % HEAD_DIM).astype(ml_dtypes.bfloat16)


def make(n_seq, n_fsdp):
    sib = KV_HEADS // n_seq
    planes = n_fsdp // sib

    def on_device(
        inputs, cotangent, qkv_weight, out_weight, gate_up_weight, down_weight, norm_gains,
        qkv_first, qkv_second, out_first, out_second, gate_up_first, gate_up_second,
        down_first, down_second, gain_first, gain_second,
    ):
        s_idx = lax.axis_index("seq")
        _, length, width = inputs.shape
        seq_len = length * n_seq
        rows = qkv_weight.shape[0]
        head_cols = (GROUP + 2) * HEAD_DIM
        ff_rows = down_weight.shape[0]
        units = ff_rows // n_seq
        hidden_units = ff_rows * n_fsdp
        part_cols = width // n_seq
        aligned = units % 128 == 0 and part_cols % 128 == 0 and sib == 2
        aligned = aligned and rows + units // 2 <= length
        gains = to_bf16(norm_gains)
        gain_cols = gains.T

        if aligned:
            pieces = (qkv_weight, gate_up_weight, down_weight, out_weight)
        else:
            wq_s = lax.dynamic_slice_in_dim(
                qkv_weight, s_idx * sib * head_cols, sib * head_cols, 1
            )
            wq_s = (wq_s * gains[0][:, None]).astype(BF).reshape(rows, sib, head_cols)
            gu_s = gate_up_weight.reshape(rows, 2, planes, sib, n_seq, units)
            gu_s = lax.dynamic_index_in_dim(gu_s, s_idx, 4, keepdims=False)
            gu_s = (gu_s * gains[1][:, None, None, None, None]).astype(BF)
            gu_s = gu_s.transpose(3, 0, 1, 2, 4).reshape(1, sib, rows, 2 * planes * units)
            dn_s = lax.dynamic_slice_in_dim(down_weight, s_idx * units, units, 0).astype(BF)
            wo_s = lax.dynamic_slice_in_dim(out_weight, s_idx * part_cols, part_cols, 1).astype(BF)
            pieces = (wq_s.transpose(1, 0, 2), gu_s, dn_s, wo_s)
        tables = tuple(jnp.asarray(table) for table in rope_arrays(seq_len))
        widen = jnp.asarray(widening(GROUP + 2))
        widen_att = jnp.asarray(widening(rows // HEAD_DIM))

        n_one, qkv, lse, gh, att, block_out, grad_hidden, w_qkv, s_gu, r_gu, s_down = forward_call(
            (n_seq, sib, planes), (rows, units), inputs[0], cotangent[0], tables, widen, widen_att,
            gain_cols, *pieces,
        )
        input_grad, g_qkv, g_gu, g_down, g_out = backward_call(
            (n_seq, sib, planes), aligned, inputs[0], tables, widen, widen_att, lse, n_one, qkv, gh,
            att, grad_hidden, w_qkv, s_gu, r_gu, s_down,
        )
        block_out, input_grad = block_out[None], input_grad[None]
        if not aligned:
            g_qkv = g_qkv.transpose(2, 0, 1, 3).reshape(rows, n_seq * sib * head_cols)
            g_gu = g_gu.reshape(n_seq, sib, rows, 2, planes, units).transpose(2, 3, 4, 1, 0, 5)
            g_gu = g_gu.reshape(rows, 2 * hidden_units)
            g_out = g_out.transpose(1, 0, 2).reshape(rows, width)
        g_qkv, g_gu, g_down, g_out = (g.astype(F32) for g in (g_qkv, g_gu, g_down, g_out))
        gain_grad = jnp.stack(
            [
                jnp.sum(g_qkv * to_bf16(qkv_weight), axis=1),
                jnp.sum(g_gu * to_bf16(gate_up_weight), axis=1),
            ]
        )
        g_qkv = g_qkv * gains[0][:, None]
        g_gu = g_gu * gains[1][:, None]
        qkv_new = adamw(qkv_weight, qkv_first, qkv_second, g_qkv, RATE_QKV, WEIGHT_DECAY)
        out_new = adamw(out_weight, out_first, out_second, g_out, RATE_OUT, WEIGHT_DECAY)
        gu_new = adamw(
            gate_up_weight, gate_up_first, gate_up_second, g_gu, RATE_GATE_UP, WEIGHT_DECAY
        )
        down_new = adamw(
            down_weight, down_first, down_second, g_down, RATE_DOWN, WEIGHT_DECAY
        )
        gains_new = adamw(norm_gains, gain_first, gain_second, gain_grad, RATE_GAINS, 0.0)
        return (block_out, input_grad, *qkv_new, *out_new, *gu_new, *down_new, *gains_new)

    return on_device


def solution(mesh):
    tokens = P("fsdp", "seq", None)
    weight = P("fsdp", None)
    gain = P(None, "fsdp")
    in_specs = (tokens, tokens, weight, weight, weight, weight, gain) + (weight,) * 8 + (gain,) * 2
    out_specs = (tokens, tokens) + (weight,) * 12 + (gain,) * 3
    return jax.shard_map(
        make(mesh.shape["seq"], mesh.shape["fsdp"]),
        mesh=mesh, in_specs=in_specs, out_specs=out_specs, check_vma=False,
    )
```

```python
import functools

import jax
import jax.numpy as jnp
import ml_dtypes
import numpy as np
from jax import lax
from jax.experimental import pallas as pl
from jax.experimental.pallas import tpu as pltpu
from jax.sharding import PartitionSpec as P

HEAD_DIM = 96
KV_HEADS = 8
ADAM_STEP = 10
GROUP = 2

NORM_EPS = 1e-05
ROPE_BASE = 100000.0
BETA_ONE = 0.9
BETA_TWO = 0.95
ADAM_EPS = 1e-08
WEIGHT_DECAY = 0.1
RATE_QKV = 0.07
RATE_OUT = 0.8
RATE_GATE_UP = 0.07
RATE_DOWN = 0.045
RATE_GAINS = 0.6
BF = jnp.bfloat16
F32 = jnp.float32
VMEM_LIMIT = 62 * 1024 * 1024


MESH = pl.DeviceIdType.MESH


def rdma(src, dst, ssem, rsem, dev):
    return pltpu.make_async_remote_copy(
        src_ref=src, dst_ref=dst, send_sem=ssem, recv_sem=rsem, device_id=dev, device_id_type=MESH
    )


class Place:
    def __init__(self, n, sib, planes):
        self.n, self.sib, self.planes = n, sib, planes
        self.s = lax.axis_index("seq")
        self.f = lax.axis_index("fsdp")
        self.c = lax.rem(self.f, sib)
        self.p = lax.div(self.f, sib)
        a, b = lax.div(self.s, 2), lax.rem(self.s, 2)
        self.r = a * (1 - b) + (n - 1 - a) * b

    def seq_at(self, j):
        if j == 0:
            return self.s
        n = self.n
        q = lax.rem(self.r + (j + n), n)
        t = lax.div(q, n // 2)
        return (1 - t) * 2 * q + t * (2 * (n - 1 - q) + 1)

    def dev(self, s, c):
        return (s, self.p * self.sib + c)

    def col(self, dp, dc):
        return lax.rem(self.p + dp, self.planes) * self.sib + lax.rem(self.c + dc, self.sib)

    def barrier(self):
        sem = pltpu.get_barrier_semaphore()
        group = self.n * self.sib
        tau = self.s * self.sib + self.c
        for j in range(1, group):
            t = lax.rem(tau + j, group)
            pl.semaphore_signal(
                sem, inc=1, device_id=self.dev(lax.div(t, self.sib), lax.rem(t, self.sib)),
                device_id_type=MESH,
            )
        for dp in range(1, self.planes):
            for dc in range(self.sib):
                pl.semaphore_signal(
                    sem, inc=1, device_id=(self.s, self.col(dp, dc)), device_id_type=MESH
                )
        pl.semaphore_wait(sem, group - 1 + (self.planes - 1) * self.sib)


class Gather:
    def __init__(self, at, part, sems):
        self.at, self.part = at, part
        self.ring_s, self.ring_r = sems[:2]
        self.share = at.sib > 1 and len(sems) > 2
        if self.share:
            self.sib_s, self.sib_r = sems[2:]
        self.sent = []

    @staticmethod
    def scratch(n, share=True):
        d = pltpu.SemaphoreType.DMA
        ring = [d((2, n // 2, 2)), d((2, n // 2, 2))]
        return ring + [d((n, 2)), d((n, 2))] if share else ring

    def _send(self, copy):
        copy.start()
        self.sent.append(copy)

    def _ring(self, way, hop, half):
        at = self.at
        src = self.part(at.c, at.seq_at(-(hop - 1) if way == 0 else hop - 1), half)
        to = at.dev(at.seq_at(1 if way == 0 else -1), at.c)
        self._send(
            rdma(src, src, self.ring_s.at[way, hop - 1, half], self.ring_r.at[way, hop - 1, half], to)
        )

    def _sib(self, j, half):
        at = self.at
        if self.share:
            src = self.part(at.c, at.seq_at(j), half)
            slot = j % at.n
            self._send(
                rdma(src, src, self.sib_s.at[slot, half], self.sib_r.at[slot, half],
                     at.dev(at.s, 1 - at.c))
            )

    def start(self):
        self._ring(0, 1, 0)
        self._ring(1, 1, 1)
        self._ring(0, 1, 1)
        self._ring(1, 1, 0)
        self._sib(0, 0)
        self._sib(0, 1)

    def _arrive(self, way, hop, half):
        at = self.at
        j = -hop if way == 0 else hop
        ref = self.part(at.c, at.seq_at(j), half)
        rdma(ref, ref, self.ring_s.at[way, hop - 1, half], self.ring_r.at[way, hop - 1, half],
             at.dev(at.s, at.c)).wait_recv()
        last = at.n // 2
        if hop + 1 < last or (hop + 1 == last and half == way):
            self._ring(way, hop + 1, half)
        if hop == last:
            j = last
        self._sib(j, half)

    def hop(self, hop):
        self.hop_first(hop)
        self.hop_second(hop)

    def hop_first(self, hop):
        self._arrive(0, hop, 0)
        self._arrive(1, hop, 1)

    def hop_second(self, hop):
        if hop < self.at.n // 2:
            self._arrive(0, hop, 1)
            self._arrive(1, hop, 0)

    def sib_wait(self, j):
        at = self.at
        if self.share:
            for half in range(2):
                ref = self.part(1 - at.c, at.seq_at(j), half)
                slot = j % at.n
                rdma(ref, ref, self.sib_s.at[slot, half], self.sib_r.at[slot, half],
                     at.dev(at.s, at.c)).wait_recv()

    def stages(self):
        last = self.at.n // 2
        yield 0, [0]
        for h in range(1, last):
            yield h, [-h, h]
        yield last, [last]

    def wait_stage(self, h, offsets):
        if h:
            self.hop(h)
        for j in offsets:
            self.sib_wait(j)

    def drain(self):
        for copy in self.sent:
            copy.wait_send()


class Move:
    def __init__(self, at, src, dst, sems, every_core=True):
        self.at, self.src, self.dst = at, src, dst
        self.ssem, self.rsem, self.hop, self.own = sems
        self.cores = at.sib if every_core else 1
        self.relay = at.planes == 4

    @staticmethod
    def sems(planes, sib):
        d = pltpu.SemaphoreType.DMA
        return [d((planes, sib)), d((planes, sib)), d((sib,)), d((1,))]

    def _pairs(self):
        for dp in [2, 1, 3] if self.relay else range(1, self.at.planes):
            for dc in range(self.cores):
                yield dp, dc
        for dc in range(1, self.cores):
            yield 0, dc

    def _direct(self, dp, body):
        if self.relay and dp in (1, 3):
            pl.when(self.at.p != (3 if dp == 1 else 0))(body)
        else:
            body()

    def _send(self, dp, dc):
        at = self.at
        return rdma(self.src(lax.rem(at.c + dc, at.sib)), self.dst(at.f), self.ssem.at[dp, dc],
                    self.rsem.at[dp, dc], (at.s, at.col(dp, dc)))

    def _local(self):
        return pltpu.make_async_copy(self.src(self.at.c), self.dst(self.at.f), self.own.at[0])

    def start(self):
        self.start_far()
        self.start_near()

    def start_far(self):
        for dp, dc in self._pairs():
            if self.relay and dp == 2:
                self._send(dp, dc).start()

    def start_near(self):
        self._local().start()
        for dp, dc in self._pairs():
            if not (self.relay and dp == 2):
                self._direct(dp, lambda: self._send(dp, dc).start())

    def _got(self, dp, dc):
        at = self.at
        source = lax.rem(at.p - dp + at.planes, at.planes) * at.sib + lax.rem(
            at.c - dc + at.sib, at.sib
        )
        ref = self.dst(source)
        rdma(ref, ref, self.ssem.at[dp, dc], self.rsem.at[dp, dc], (at.s, at.f)).wait_recv()
        return ref

    def pass_on(self):
        at = self.at
        if not self.relay:
            return
        for dp, dc in self._pairs():
            if dp == 2:
                ref = self._got(dp, dc)
                for here, to, slot in ((2, 3, 3), (1, 0, 1)):
                    @pl.when(at.p == here)
                    def _():
                        rdma(ref, ref, self.hop.at[dc], self.rsem.at[slot, dc],
                             (at.s, to * at.sib + at.c)).start()

    def wait(self):
        for dp, dc in self._pairs():
            if not (self.relay and dp == 2):
                self._got(dp, dc)
        self._local().wait()

    def drain(self):
        at = self.at
        for dp, dc in self._pairs():
            self._direct(dp, lambda: self._send(dp, dc).wait_send())
            if self.relay and dp == 2:
                ref = self.dst(at.f)

                @pl.when(jnp.logical_or(at.p == 1, at.p == 2))
                def _():
                    rdma(ref, ref, self.hop.at[dc], self.rsem.at[0, dc], (at.s, at.f)).wait_send()


class Scatter:
    def __init__(self, at, bufs, sems, rows, cols):
        self.at, self.rows, self.cols = at, rows, pl.ds(0, cols)
        self.stage, self.sib_in, self.out, self.inn = bufs
        self.sib_s, self.sib_r, self.ring_s, self.ring_r = sems
        self.sent, self.handed = [], []

    @staticmethod
    def scratch(n, shape):
        return [
            pltpu.VMEM((2, *shape), BF), pltpu.VMEM((n, *shape), BF),
            pltpu.VMEM((2, n // 2, *shape), BF), pltpu.VMEM((2, n // 2, *shape), BF),
        ]

    @staticmethod
    def views(stage, sib_in, out, inn):
        return (
            lambda k: stage.at[k], lambda k: sib_in.at[k],
            lambda w, k: out.at[w, k], lambda w, k: inn.at[w, k],
        )

    @staticmethod
    def sems(n):
        d = pltpu.SemaphoreType.DMA
        return [d((n,)), d((n,)), d((2, n // 2)), d((2, n // 2))]

    def offsets(self):
        last = self.at.n // 2
        order = [last]
        for h in range(last - 1, 0, -1):
            order += [h, -h]
        return order + [0]

    def to_sibling(self, k, produce):
        at = self.at
        if at.sib == 1:
            return
        if k >= 2:
            self.handed[k - 2].wait_send()
        view = self.stage(k % 2).at[pl.ds(0, self.rows), self.cols]
        produce(1 - at.c, at.seq_at(self.offsets()[k]), view)
        copy = rdma(view, self.sib_in(k).at[pl.ds(0, self.rows), self.cols],
                    self.sib_s.at[k], self.sib_r.at[k], at.dev(at.s, 1 - at.c))
        copy.start()
        self.handed.append(copy)

    def open(self, stage, ring, finish):
        self.to_sibling(0, stage)
        self.step(0, ring, finish)
        for k in range(1, len(self.offsets())):
            self.to_sibling(k, stage)

    def _send(self, way, k, rows):
        at = self.at
        src = self.out(way, k).at[rows, self.cols]
        copy = rdma(src, self.inn(way, k).at[rows, self.cols], self.ring_s.at[way, k], self.ring_r.at[way, k],
                    at.dev(at.seq_at(1 if way == 0 else -1), at.c))
        copy.start()
        self.sent.append(copy)

    def _wait(self, way, k, rows):
        ref = self.inn(way, k).at[rows, self.cols]
        at = self.at
        rdma(ref, ref, self.ring_s.at[way, k], self.ring_r.at[way, k],
             at.dev(at.s, at.c)).wait_recv()

    def step(self, k, produce, finish):
        at = self.at
        last = at.n // 2
        length = self.rows
        half = length // 2
        halves = (pl.ds(0, half), pl.ds(half, half))
        whole = pl.ds(0, length)
        j = self.offsets()[k]
        if at.sib > 1:
            ref = self.sib_in(k).at[pl.ds(0, length), self.cols]
            rdma(ref, ref, self.sib_s.at[k], self.sib_r.at[k], at.dev(at.s, at.c)).wait_recv()
        h = abs(j)
        if h == last:
            got = []
        else:
            ways = (0, 1) if h == 0 else ((0,) if j > 0 else (1,))
            rows_in = [halves[w] if h + 1 == last else whole for w in ways]
            got = [(w, rw) for w, rw in zip(ways, rows_in)]
        pending = [True]

        def store(cols, value, k=k, h=h, j=j, got=got, pending=pending):
            if pending[0]:
                for w, rw in got:
                    self._wait(w, h, rw)
                pending[0] = False
            if at.sib > 1:
                value = value + self.sib_in(k)[pl.ds(0, length), cols].astype(F32)
            for w, rw in got:
                if h + 1 == last:
                    add = self.inn(w, h)[pl.ds(w * half, half), cols].astype(F32)
                    if w == 0:
                        value = jnp.concatenate([value[:half] + add, value[half:]], axis=0)
                    else:
                        value = jnp.concatenate([value[:half], value[half:] + add], axis=0)
                else:
                    value = value + self.inn(w, h)[pl.ds(0, length), cols].astype(F32)
            if h == last:
                low = value.astype(BF)
                self.out(0, h - 1)[pl.ds(0, half), cols] = low[:half]
                self.out(1, h - 1)[pl.ds(half, half), cols] = low[half:]
            elif h:
                self.out(0 if j > 0 else 1, h - 1)[pl.ds(0, length), cols] = value.astype(BF)
            else:
                finish(cols, value)

        produce(at.c, at.seq_at(j), store)
        if h == last:
            self._send(0, h - 1, halves[0])
            self._send(1, h - 1, halves[1])
        elif h:
            self._send(0 if j > 0 else 1, h - 1, whole)

    def drain(self):
        for copy in self.sent + self.handed[-2:]:
            copy.wait_send()


class Credits:
    def __init__(self, at, sem):
        self.at, self.sem = at, sem

    def give(self):
        at = self.at
        if at.sib > 1:
            pl.semaphore_signal(
                self.sem, inc=1, device_id=at.dev(at.s, 1 - at.c), device_id_type=MESH
            )
        for way in (1, -1):
            pl.semaphore_signal(
                self.sem, inc=1, device_id=at.dev(at.seq_at(way), at.c), device_id_type=MESH
            )

    def take(self):
        pl.semaphore_wait(self.sem, 3 if self.at.sib > 1 else 2)


def nt(a, b):
    return lax.dot_general(a, b, (((1,), (1,)), ((), ())), preferred_element_type=F32)


def tn(a, b):
    return lax.dot_general(a, b, (((0,), (0,)), ((), ())), preferred_element_type=F32)


def nn(a, b):
    return lax.dot_general(a, b, (((1,), (0,)), ((), ())), preferred_element_type=F32)


def rope(value, cos, front, back):
    return value * cos + pltpu.roll(value, 80, 1) * front + pltpu.roll(value, 48, 1) * back


def forward_kernel(
    dims,
    x, cot, cos, front, back, widen, widen_att, gain_cols, wq_s, gu_s, dn_s, wo_s,
    o_n1, o_qkv, o_lse, o_gh, o_att, o_block, o_ghid, o_wq, o_sgu, o_rgu, o_sdn,
    hid,
    nbuf, cbuf, qkv, wq, wqp, wo, gu, dn, act, ggu, att_out, att_in, gh_in, stg, sgu_t,
    wo_f, wq_b, gu_b, dn_b, wo_b,
    sc_stage, sc_in, sc_out, sc_inn,
    zw_a, zw_b, zw_c, zw_d, zo_a, zo_b, zo_c, zo_d, zd_a, zd_b, zd_c, zd_d,
    zg_a, zg_b, zg_c, zg_d, z_ss, z_sr, local, loads,
    n1_a, n1_b, n1_c, n1_d, ct_a, ct_b, ct_c, ct_d, n2_a, n2_b, n2_c, n2_d, wo_ga, wo_gb, wo_gc, wo_gd,
    rs_a, rs_b, rs_c, rs_d, ds_a, ds_b, ds_c, ds_d, at_s, at_r, gh_s, gh_r, near_s, near_r, free,
):
    n, sib, planes = dims
    at = Place(n, sib, planes)
    length, width = x.shape
    seq_len = n * length
    raw = len(wq_s.shape) == 2
    _, rows, head_cols = wq_b.shape
    owners = planes * sib
    chunks = GROUP * HEAD_DIM // rows
    units = dn_b.shape[0]
    local_units = planes * units
    parts = 2 if units % 128 == 0 else 1
    wide = local_units // parts
    part_cols = wo_b.shape[1]
    heads_per = rows // HEAD_DIM
    half_len = length // 2
    tau = at.s * sib + at.c
    scale = HEAD_DIM ** (-0.5)
    log2e = 1.4426950408889634
    sent = []

    def token_part(ref):
        return lambda c, s, h: ref.at[c, s, pl.ds(h * half_len, half_len)]

    def owner_rows(f):
        return pl.ds(pl.multiple_of(f * rows, rows), rows)

    if raw:
        gu_f = (o_ghid, hid)

        def cut(ref, k, lo, size, dst):
            return pltpu.make_async_copy(
                ref.at[:, pl.ds(pl.multiple_of(lo, 128), size)], dst, loads.at[k]
            )

        def wq_f(c):
            return gu_f[c].at[pl.ds(0, rows), pl.ds(2 * local_units, head_cols)]

        in_wq = [
            cut(wq_s, 3 + 2 * owners + c, (at.s * sib + c) * head_cols, head_cols, wq_f(c))
            for c in range(sib)
        ]
        in_wo = cut(wo_s, 1, at.s * part_cols, part_cols, wo_f)
        half_units = units // 2

        def dn_f(h):
            return gu_f[h].at[pl.ds(rows, half_units)]

        in_dn = [
            pltpu.make_async_copy(
                dn_s.at[pl.ds(pl.multiple_of(at.s * units + h * half_units, half_units), half_units)],
                dn_f(h), loads.at[2 * h],
            )
            for h in range(2)
        ]
        in_gu = []

        def gu_lane(p, g):
            return p * units // wide * 2 * wide + g * wide + p * units % wide

        for c in range(sib):
            for p in range(planes):
                for g in range(2):
                    lo = (g * owners + p * sib + c) * (n * units) + at.s * units
                    k = (c * planes + p) * 2 + g
                    in_gu.append(
                        cut(gu_s, 3 + k, lo, units,
                            gu_f[c].at[pl.ds(0, rows), pl.ds(gu_lane(p, g), units)])
                    )
        for copy in (*in_wq, in_wo, *in_dn, *in_gu):
            copy.start()
        wq_x, gu_x, dn_x, wo_x = wq_b, gu_b, dn_b, wo_b
    else:
        wq_x, gu_x, dn_x, wo_x = wq_s, gu_s, dn_s, wo_s

    move_wq = Move(at, lambda c: wq_x.at[c], lambda f: wq.at[owner_rows(f)], (zw_a, zw_b, zw_c, zw_d))
    move_wo = Move(
        at, lambda c: wo_x, lambda f: wo.at[lax.rem(f, sib), at.s, lax.div(f, sib)],
        (zo_a, zo_b, zo_c, zo_d), False,
    )
    move_dn = Move(
        at, lambda c: dn_x,
        lambda f: dn.at[pl.ds(pl.multiple_of(lax.div(f, sib) * units, units), units)],
        (zd_a, zd_b, zd_c, zd_d), False,
    )

    def gu_move(k):
        return Move(
            at, lambda c: gu_x.at[k, c], lambda f: gu.at[k, owner_rows(f)],
            (zg_a.at[k], zg_b.at[k], zg_c.at[k], zg_d.at[k]),
        )

    move_gu = [gu_move(k) for k in range(parts)]

    x_f = x[...].astype(F32)
    inv_one = lax.rsqrt(jnp.mean(x_f * x_f, axis=-1, keepdims=True) + NORM_EPS)
    nbuf[at.c, at.s] = (x_f * inv_one).astype(BF)
    cbuf[at.c, at.s] = cot[...]
    n_one = Gather(at, token_part(nbuf), (n1_a, n1_b, n1_c, n1_d))
    at.barrier()
    n_one.start()
    if raw:
        g_one = gain_cols[:, 0:1]
        for c in range(sib):
            in_wq[c].wait()
            wq_b[c] = (wq_f(c)[...] * g_one).astype(BF)
        in_wo.wait()
        wo_b[...] = wo_f[...].astype(BF)
    move_wq.start()
    if raw:
        for h in range(2):
            in_dn[h].wait()
            dn_b[h * half_units : (h + 1) * half_units] = dn_f(h)[...].astype(BF)
        for copy in in_gu:
            copy.wait()
        g_two = gain_cols[:, 1:2]
        for c in range(sib):
            for k in range(parts):
                lanes = slice(k * 2 * wide, (k + 1) * 2 * wide)
                gu_b[k, c] = (gu_f[c][0:rows, lanes] * g_two).astype(BF)
    n_stages = list(n_one.stages())
    n_one.hop_first(1)
    move_wq.pass_on()
    move_wo.start()
    n_one.hop_second(1)
    for h, _ in n_stages[2:-1]:
        n_one.hop(h)
    move_wq.wait()
    move_gu[0].start()

    @pl.loop(0, width // 256)
    def _(t):
        here = pl.ds(pl.multiple_of(t * 256, 256), 256)
        wqp[here] = nn(wq[here], widen[...]).astype(BF)

    save_wq = pltpu.make_async_copy(wqp, o_wq, local.at[2])
    save_wq.start()

    def project(c, s):
        y = nn(nbuf[c, s], wqp[...]).astype(BF)
        here = pl.ds(pl.multiple_of(s * length, length), length)
        cs, fr, bk = cos[here], front[here], back[here]
        for k in range(3):
            lanes = slice(128 * k, 128 * k + 128)
            qkv[c, here, lanes] = rope(y[:, lanes].astype(F32), cs, fr, bk).astype(BF)
        qkv[c, here, 384:512] = y[:, 384:512]

    for h, offsets in n_stages:
        if h == n // 2:
            n_one.hop(h)
        for j in offsets:
            n_one.sib_wait(j)
            s_j = at.seq_at(j)

            @pl.loop(0, sib)
            def _(c):
                project(c, s_j)

    cot_gather = Gather(at, token_part(cbuf), (ct_a, ct_b, ct_c, ct_d))
    save_n1 = pltpu.make_async_copy(nbuf, o_n1, local.at[3])
    save_n1.start()
    save_qkv = pltpu.make_async_copy(qkv, o_qkv, local.at[4])
    save_qkv.start()

    tri = lax.broadcasted_iota(jnp.int32, (length, length), 0) >= lax.broadcasted_iota(
        jnp.int32, (length, length), 1
    )

    def spot(k, b, i):
        return (k * sib + b) * n + i

    def attend(i):
        @pl.loop(0, sib)
        def _(b):
            past = i * length
            here = slice(past, past + length)
            outs = []
            for h in range(GROUP):
                q = qkv[b, here, 128 * h : 128 * h + 128]
                d = jnp.where(tri, nt(q, qkv[b, here, 256:384]) * (scale * log2e), -1e30)
                m = jnp.max(d, axis=1, keepdims=True)
                if i:
                    e = nt(q, qkv[b, 0:past, 256:384]) * (scale * log2e)
                    m = jnp.maximum(m, jnp.max(e, axis=1, keepdims=True))
                d = jnp.exp2(d - m)
                total = jnp.sum(d, axis=1, keepdims=True)
                o = nn(d.astype(BF), qkv[b, here, 384:512])
                if i:
                    e = jnp.exp2(e - m)
                    total = total + jnp.sum(e, axis=1, keepdims=True)
                    o = o + nn(e.astype(BF), qkv[b, 0:past, 384:512])
                outs.append((o / total).astype(BF))
                lse = jnp.broadcast_to(m + jnp.log2(total), (length, 128))
                o_lse[b, h, i] = lse.T[0:8]
            for k in range(chunks):
                pair = jnp.concatenate(outs[k * heads_per : (k + 1) * heads_per], axis=1)
                att_out[spot(k, b, i)] = nt(pair, widen_att[...]).astype(BF)

    def send_attended(i):
        for k in range(chunks):
            for b in range(sib):
                mine = jnp.logical_and(at.s == i, at.c == b)

                @pl.when(mine)
                def _():
                    att_in[tau * chunks + k] = att_out[spot(k, b, i)]

                @pl.when(jnp.logical_not(mine))
                def _():
                    rdma(att_out.at[spot(k, b, i)], att_in.at[tau * chunks + k], at_s.at[k, b, i],
                         at_r.at[tau * chunks + k], at.dev(i, b)).start()

    wo_gather = Gather(
        at, lambda c, s, h: wo.at[c, s, pl.ds(h * (planes // 2), planes // 2)],
        (wo_ga, wo_gb, wo_gc, wo_gd),
    )
    attend(n - 1)
    save_n1.wait()
    n_one.drain()
    send_attended(n - 1)
    move_wo.pass_on()
    move_wo.wait()
    wo_gather.start()
    for move in (*move_gu[1:], move_dn):
        move.start_far()
    for i in range(n - 2, -1, -1):
        attend(i)
        send_attended(i)
    wo_hops = list(wo_gather.stages())
    for h, _ in wo_hops[1:-1]:
        wo_gather.hop(h)
    cot_gather.start()
    wo_gather.hop(n // 2)
    for _, offsets in wo_hops:
        for j in offsets:
            wo_gather.sib_wait(j)
    wo_gather.drain()
    save_qkv.wait()
    save_wq.wait()

    group = n * sib
    for j in range(1, group):
        t = lax.rem(tau + j, group)
        for k in range(chunks):
            ref = att_in.at[t * chunks + k]
            rdma(ref, ref, at_s.at[0, 0, 0], at_r.at[t * chunks + k], at.dev(at.s, at.c)).wait_recv()
    for k in range(chunks):
        for i in range(n):
            for b in range(sib):
                @pl.when(jnp.logical_not(jnp.logical_and(at.s == i, at.c == b)))
                def _():
                    rdma(att_out.at[spot(k, b, i)], att_out.at[spot(k, b, i)], at_s.at[k, b, i],
                         at_r.at[0], at.dev(at.s, at.c)).wait_send()
    save_att = pltpu.make_async_copy(att_in, o_att, local.at[3])
    save_att.start()

    x_f = x[...].astype(F32)
    for s in range(n):
        cols = slice(s * part_cols, (s + 1) * part_cols)
        acc = x_f[:, cols]
        for p in range(planes):
            for c in range(sib):
                acc = acc + nn(att_in[p * sib + c], wo[c, s, p])
        hid[:, cols] = acc
    hidden = hid[...]
    inv_mid = lax.rsqrt(jnp.mean(hidden * hidden, axis=-1, keepdims=True) + NORM_EPS)
    nbuf[at.c, at.s] = (hidden * inv_mid).astype(BF)
    n_two = Gather(at, token_part(nbuf), (n2_a, n2_b, n2_c, n2_d))
    n_two.start()

    stages = list(n_two.stages())
    for move in (*move_gu[1:], move_dn):
        move.start_near()
    move_gu[0].pass_on()
    for h, _ in stages[1:-1]:
        cot_gather.hop(h)
        n_two.hop(h)
    for move in (*move_gu[1:], move_dn):
        move.pass_on()

    def gate_pass(k, c, s):
        y = nn(nbuf[c, s], gu[k])
        gate, up = y[:, :wide], y[:, wide:]
        act[c, s, :, k * wide : (k + 1) * wide] = (gate / (1.0 + jnp.exp(-gate)) * up).astype(BF)
        ggu[c, s, :, k * 2 * wide : (k + 1) * 2 * wide] = y.astype(BF)

    def grad_pass(c, s):
        for k in range(parts):
            lo = k * 2 * wide
            gate = ggu[c, s, :, lo : lo + wide].astype(F32)
            up = ggu[c, s, :, lo + wide : lo + 2 * wide].astype(F32)
            grad_act = nt(cbuf[c, s], dn[k * wide : (k + 1) * wide])
            sig = 1.0 / (1.0 + jnp.exp(-gate))
            ggu[c, s, :, lo : lo + wide] = (
                grad_act * up * sig * (1.0 + gate * (1.0 - sig))
            ).astype(BF)
            ggu[c, s, :, lo + wide : lo + 2 * wide] = (grad_act * (gate * sig)).astype(BF)

    def each_block(offsets, body):
        for j in offsets:
            s_j = at.seq_at(j)

            @pl.loop(0, sib)
            def _(c):
                body(c, s_j)

    def rows_wait(offsets):
        for j in offsets:
            n_two.sib_wait(j)
            cot_gather.sib_wait(j)

    early = [j for _, offsets in stages[:-1] for j in offsets]
    late = stages[-1][1]
    rows_wait(early)
    for k in range(parts):
        move_gu[k].wait()
        each_block(early, lambda c, s: gate_pass(k, c, s))
    move_dn.wait()
    each_block(early, grad_pass)
    n_two.hop(n // 2)
    cot_gather.hop(n // 2)
    rows_wait(late)
    for k in range(parts):
        each_block(late, lambda c, s: gate_pass(k, c, s))
    each_block(late, grad_pass)

    scatter = Scatter(
        at, Scatter.views(sc_stage, sc_in, sc_out, sc_inn), (rs_a, rs_b, rs_c, rs_d), length, width
    )
    tile = 512

    def column_tiles():
        return [slice(t * tile, (t + 1) * tile) for t in range(width // tile)]

    def mid_part(c, s, cols):
        acc = nt(ggu[c, s, :, 0 : 2 * wide], gu[0, cols, :])
        for k in range(1, parts):
            acc = acc + nt(ggu[c, s, :, k * 2 * wide : (k + 1) * 2 * wide], gu[k, cols, :])
        return acc

    def to_stage(c, s, ref):
        for cols in column_tiles():
            ref[:, cols] = mid_part(c, s, cols).astype(BF)

    def to_ring(c, s, store):
        for cols in column_tiles():
            store(cols, mid_part(c, s, cols))

    tokens = sib * seq_len
    down_copies = []

    def grad_down():
        cot_all = cbuf[...].reshape(tokens, width)
        down_rows = local_units // 2
        for t in range(2):
            rows_here = slice(t * down_rows, (t + 1) * down_rows)
            lhs = act[:, :, :, rows_here].reshape(tokens, down_rows)
            stg[rows_here] = tn(lhs, cot_all).astype(BF)
        own = pltpu.make_async_copy(
            stg.at[pl.ds(pl.multiple_of(at.p * units, units), units)], o_sdn.at[at.p], local.at[6]
        )
        own.start()
        down_copies.append(own)
        for dp in range(1, planes):
            to = lax.rem(at.p + dp, planes)
            copy = rdma(stg.at[pl.ds(pl.multiple_of(to * units, units), units)], o_sdn.at[at.p],
                        z_ss.at[dp], z_sr.at[dp], (at.s, at.col(dp, 0)))
            copy.start()
            sent.append(copy)

    gu_tile = sgu_t.shape[1]
    gu_steps = width // gu_tile
    near = planes == 4

    def gu_copy(m, slot):
        return pltpu.make_async_copy(
            sgu_t.at[slot], o_sgu.at[pl.ds(m * gu_tile, gu_tile)], local.at[7 + slot]
        )

    def near_send(m, dc):
        to = m * sib + lax.rem(at.c + dc, sib)
        return rdma(o_sgu.at[owner_rows(to)], o_rgu.at[at.f], near_s.at[m, dc],
                    near_r.at[at.p, dc], (at.s, to))

    def if_near(m, body):
        pl.when(jnp.logical_or(at.p == m - 1, at.p == m + 1))(body)

    def grad_gu():
        for m in range(gu_steps):
            slot = m % 2
            if m >= 2:
                gu_copy(m - 2, slot).wait()
            lhs = nbuf[:, :, :, m * gu_tile : (m + 1) * gu_tile].reshape(tokens, gu_tile)
            sgu_t[slot] = tn(lhs, ggu[...].reshape(tokens, 2 * local_units)).astype(BF)
            gu_copy(m, slot).start()
        for m in range(max(0, gu_steps - 2), gu_steps):
            gu_copy(m, m % 2).wait()
        if near:
            for m in range(planes):
                for dc in range(sib):
                    if_near(m, lambda: near_send(m, dc).start())

    def finish(cols, value):
        o_ghid[:, cols] = value

    def flat(ref, base):
        return lambda w, k: ref.at[base, w * (n // 2) + k]

    down = Scatter(
        at, (lambda k: cbuf.at[0, k], lambda k: nbuf.at[0, k], flat(cbuf, sib - 1), flat(nbuf, sib - 1)),
        (ds_a, ds_b, ds_c, ds_d), length, width,
    )

    def down_stage(c, s, ref):
        for cols in column_tiles():
            ref[:, cols] = nn(act[c, s], dn[:, cols]).astype(BF)

    def down_ring(c, s, store):
        for cols in column_tiles():
            store(cols, nn(act[c, s], dn[:, cols]))

    def down_finish(cols, value):
        o_block[:, cols] = (hid[:, cols] + value).astype(BF)

    credits = Credits(at, free)
    last = len(scatter.offsets()) - 1
    scatter.open(to_stage, to_ring, finish)
    grad_down()
    for k in range(1, last):
        scatter.step(k, to_ring, finish)
    grad_gu()
    cot_gather.drain()
    n_two.drain()
    credits.give()
    credits.take()
    down.open(down_stage, down_ring, down_finish)
    scatter.step(last, to_ring, finish)
    e_mid = o_ghid[...]
    hidden = hid[...]
    inv_mid = lax.rsqrt(jnp.mean(hidden * hidden, axis=-1, keepdims=True) + NORM_EPS)
    norm_mid = hidden * inv_mid
    o_ghid[...] = cot[...].astype(F32) + inv_mid * (
        e_mid - norm_mid * jnp.mean(e_mid * norm_mid, axis=-1, keepdims=True)
    )
    branch = o_ghid[...].astype(BF)
    for f in range(owners):
        p, c = f // sib, f % sib
        acc = nt(branch[:, :part_cols], wo[c, 0, p])
        for s in range(1, n):
            acc = acc + nt(branch[:, s * part_cols : (s + 1) * part_cols], wo[c, s, p])
        att_out[f] = acc.astype(BF)
        t, k = f // chunks, f % chunks
        mine = tau == t

        @pl.when(mine)
        def _():
            gh_in[k, at.c, at.s] = att_out[f]

        @pl.when(jnp.logical_not(mine))
        def _():
            rdma(att_out.at[f], gh_in.at[k, at.c, at.s], gh_s.at[f], gh_r.at[k, tau],
                 at.dev(t // sib, t % sib)).start()

    for k in range(1, last):
        down.step(k, down_ring, down_finish)
    for j in range(1, group):
        t = lax.rem(tau + j, group)
        for k in range(chunks):
            ref = gh_in.at[k, lax.rem(t, sib), lax.div(t, sib)]
            rdma(ref, ref, gh_s.at[0], gh_r.at[k, t], at.dev(at.s, at.c)).wait_recv()
    save_gh = pltpu.make_async_copy(gh_in, o_gh, local.at[0])
    save_gh.start()
    for f in range(owners):
        @pl.when(jnp.logical_not(tau == f // chunks))
        def _():
            rdma(att_out.at[f], att_out.at[f], gh_s.at[f], gh_r.at[0, 0],
                 at.dev(at.s, at.c)).wait_send()

    down.step(last, down_ring, down_finish)

    for dp in range(1, planes):
        ref = o_sdn.at[lax.rem(at.p - dp + planes, planes)]
        rdma(ref, ref, z_ss.at[dp], z_sr.at[dp], (at.s, at.f)).wait_recv()
    for copy in down_copies:
        copy.wait()
    if near:
        for q in range(planes):
            for dc in range(sib):
                def arrived():
                    ref = o_rgu.at[q * sib + lax.rem(at.c - dc + sib, sib)]
                    rdma(ref, ref, near_s.at[q, dc], near_r.at[q, dc], (at.s, at.f)).wait_recv()
                    near_send(q, dc).wait_send()

                if_near(q, arrived)
    scatter.drain()
    down.drain()
    for move in (move_wq, move_wo, move_dn, *move_gu):
        move.drain()
    for copy in sent:
        copy.wait_send()
    save_att.wait()
    save_gh.wait()


def forward_call(dims, sizes, x, cot, tables, widen, widen_att, gain_cols, wq_s, gu_s, dn_s, wo_s):
    n, sib, planes = dims
    rows, units = sizes
    length, width = x.shape
    part_cols = width // n
    head_cols = (GROUP + 2) * HEAD_DIM
    owners = planes * sib
    chunks = GROUP * HEAD_DIM // rows
    ffl = planes * units
    parts = 2 if units % 128 == 0 else 1
    seq_len = n * length
    vm, hb = pl.BlockSpec(memory_space=pltpu.VMEM), pl.BlockSpec(memory_space=pl.ANY)
    blocks = (sib, n, length, width)
    sds = jax.ShapeDtypeStruct
    outs = [
        (sds(blocks, BF), hb),
        (sds((sib, seq_len, 512), BF), hb),
        (sds((sib, GROUP, n, 8, length), F32), vm),
        (sds((chunks, sib, n, length, rows), BF), hb),
        (sds((owners, length, rows), BF), hb),
        (sds((length, width), BF), vm),
        (sds((length, width), F32), vm),
        (sds((width, 512), BF), hb),
        (sds((width, 2 * ffl), BF), hb),
        (sds((owners, rows, 2 * ffl), BF), hb),
        (sds((planes, units, width), BF), hb),
    ]
    dma = pltpu.SemaphoreType.DMA
    scratch = [
        pltpu.VMEM((length, width), F32),
        pltpu.VMEM(blocks, BF), pltpu.VMEM(blocks, BF), pltpu.VMEM((sib, seq_len, 512), BF),
        pltpu.VMEM((width, head_cols), BF), pltpu.VMEM((width, 512), BF),
        pltpu.VMEM((sib, n, planes, rows, part_cols), BF),
        pltpu.VMEM((parts, width, 2 * ffl // parts), BF), pltpu.VMEM((ffl, width), BF),
        pltpu.VMEM((sib, n, length, ffl), BF), pltpu.VMEM((sib, n, length, 2 * ffl), BF),
        pltpu.VMEM((owners, length, rows), BF), pltpu.VMEM((owners, length, rows), BF),
        pltpu.VMEM((chunks, sib, n, length, rows), BF),
        pltpu.VMEM((ffl, width), BF), pltpu.VMEM((2, 384, 2 * ffl), BF),

        pltpu.VMEM((rows, part_cols), F32),
        pltpu.VMEM((sib, rows, head_cols), BF),
        pltpu.VMEM((parts, sib, rows, 2 * ffl // parts), BF),
        pltpu.VMEM((units, width), BF), pltpu.VMEM((rows, part_cols), BF),
        *Scatter.scratch(n, (length, width)),
        *Move.sems(planes, sib), *Move.sems(planes, sib), *Move.sems(planes, sib),
        dma((parts, planes, sib)), dma((parts, planes, sib)), dma((parts, sib)), dma((parts, 1)),
        dma((planes,)), dma((planes,)), dma((9,)), dma((3 + 2 * owners + sib,)),
        *Gather.scratch(n), *Gather.scratch(n), *Gather.scratch(n), *Gather.scratch(n),
        *Scatter.sems(n), *Scatter.sems(n),
        dma((chunks, sib, n)), dma((owners,)), dma((owners,)), dma((chunks, n * sib)),
        dma((planes, sib)), dma((planes, sib)), pltpu.SemaphoreType.REGULAR,
    ]
    return pl.pallas_call(
        functools.partial(forward_kernel, dims),
        out_shape=[o[0] for o in outs],
        out_specs=[o[1] for o in outs],
        in_specs=[vm] * 8 + [hb] * 4,
        scratch_shapes=scratch,
        compiler_params=pltpu.CompilerParams(
            collective_id=0, has_side_effects=True, vmem_limit_bytes=VMEM_LIMIT
        ),
    )(x, cot, *tables, widen, widen_att, gain_cols, wq_s, gu_s, dn_s, wo_s)


def backward_kernel(
    dims,
    x, cos, front, back, widen, widen_att, lse,
    n1, qkv_h, gh_h, att_h, ghid, wqp_h, sgu, rgu_h, sdn_h,
    o_input, o_gq, o_ggu, o_gdn, o_gout,
    qkv, gh, att, wqp, sdn, gq, gk, gv, n1_t, sq, so, branch,
    r_gu, r_qkv, r_out, g_gu, g_qkv, g_dn, g_out,
    sc_stage, sc_in, sc_out, sc_inn, e_stage_b, e_sib_b, e_out_b, e_inn_b,
    loads, near_l, saves_gu, saves_qkv, saves_row, z_gs, z_gr, z_qs, z_qr, z_os, z_or,
    e_a, e_b, e_c, e_d, s_a, s_b, s_c, s_d,
    a_dn_s, a_dn_r, a_gu_s, a_gu_r, a_qk_s, a_qk_r, a_ou_s, a_ou_r,
):
    n, sib, planes = dims
    at = Place(n, sib, planes)
    length, width = x.shape
    owners = planes * sib
    chunks, _, _, _, rows = gh.shape
    heads_per = rows // HEAD_DIM
    part_cols = r_out.shape[2]
    scale = HEAD_DIM ** (-0.5)
    log2e = 1.4426950408889634
    tokens = sib * n * length
    sent = []
    near = planes == 4
    units = g_dn.shape[1]
    aligned = len(o_ggu.shape) == 2

    def load(src, dst, k):
        copy = pltpu.make_async_copy(src, dst, loads.at[k])
        copy.start()
        return copy

    def owner_rows(f):
        return pl.ds(pl.multiple_of(f * rows, rows), rows)

    def z_source(dp, dc):
        return (
            lax.rem(at.p - dp + planes, planes) * sib + lax.rem(at.c - dc + sib, sib)
        )

    def z_scatter(src, dst, ssem, rsem, k):
        own = load(src.at[owner_rows(at.f)], dst.at[at.f], k)
        for dp in range(planes):
            for dc in range(sib):
                if dp or dc:
                    to = at.col(dp, dc)
                    copy = rdma(src.at[owner_rows(to)], dst.at[at.f],
                                ssem.at[dp, dc], rsem.at[dp, dc], (at.s, to))
                    copy.start()
                    sent.append(copy)
        return own

    def z_collect(dst, ssem, rsem, own):
        own.wait()
        for dp in range(planes):
            for dc in range(sib):
                if dp or dc:
                    ref = dst.at[z_source(dp, dc)]
                    rdma(ref, ref, ssem.at[dp, dc], rsem.at[dp, dc], (at.s, at.f)).wait_recv()

    def plane_total(dst, c):
        acc = dst[c].astype(F32)
        for p in range(1, planes):
            acc = acc + dst[p * sib + c].astype(F32)
        return acc.astype(BF)

    def far(dp, body):
        if not near or dp == 0:
            body()
        elif dp == 2:
            body()
        else:
            pl.when(at.p == (3 if dp == 1 else 0))(body)

    def gu_pairs():
        for dp in [2, 1, 3, 0] if near else range(planes):
            for dc in range(sib):
                if dp or dc:
                    yield dp, dc

    def gu_send(dp, dc):
        to = at.col(dp, dc)
        return rdma(sgu.at[owner_rows(to)], r_gu.at[at.f], z_gs.at[dp, dc], z_gr.at[dp, dc],
                    (at.s, to))

    def gu_near(q, dc):
        f = q * sib + dc
        return pltpu.make_async_copy(rgu_h.at[f], r_gu.at[f], near_l.at[q, dc])

    def if_near(q, body):
        pl.when(jnp.logical_or(at.p == q - 1, at.p == q + 1))(body)

    def gu_wait(dp, dc):
        ref = r_gu.at[z_source(dp, dc)]
        rdma(ref, ref, z_gs.at[dp, dc], z_gr.at[dp, dc], (at.s, at.f)).wait_recv()

    def gu_arrived(dp, dc):
        if not near or dp in (0, 2):
            gu_wait(dp, dc)
        else:
            pl.when(at.p == (0 if dp == 1 else 3))(lambda: gu_wait(dp, dc))

    at.barrier()
    in_qkv, in_gh = load(qkv_h, qkv, 0), load(gh_h, gh, 1)
    in_sdn, in_att, in_wqp = load(sdn_h, sdn, 4), load(att_h, att, 6), load(wqp_h, wqp, 7)
    gu_own = load(sgu.at[owner_rows(at.f)], r_gu.at[at.f], 5)
    for dp, dc in gu_pairs():
        far(dp, lambda: gu_send(dp, dc).start())
    if near:
        for q in range(planes):
            for dc in range(sib):
                if_near(q, lambda: gu_near(q, dc).start())
    n1_cols = n1_t.shape[4]
    n1_steps = width // n1_cols

    def n1_load(m):
        return pltpu.make_async_copy(
            n1.at[:, :, :, pl.ds(m * n1_cols, n1_cols)], n1_t.at[m % 2], loads.at[8 + m % 2]
        )

    n1_load(0).start()
    n1_load(1).start()

    def row_half(ref):
        size = ref.shape[-2] // 2
        if len(ref.shape) == 4:
            return lambda c, s, h: ref.at[s, :, pl.ds(h * size, size)]
        return lambda c, s, h: ref.at[s, pl.ds(h * size, size)]

    in_sdn.wait()
    acc = sdn[0].astype(F32)
    for p in range(1, planes):
        acc = acc + sdn[p].astype(F32)
    g_dn[at.s] = acc.astype(BF)
    ag_dn = Gather(at, row_half(g_dn), (a_dn_s, a_dn_r))
    ag_dn.start()

    tri = lax.broadcasted_iota(jnp.int32, (length, length), 0) <= lax.broadcasted_iota(
        jnp.int32, (length, length), 1
    )

    def attend_back(b):
        gk[...] = jnp.zeros_like(gk)
        gv[...] = jnp.zeros_like(gv)
        for i in range(n):
            past = i * length
            here = slice(past, past + length)
            for h in range(GROUP):
                k, slot = h // heads_per, h % heads_per
                q = qkv[b, here, 128 * h : 128 * h + 128]
                do = nn(gh[k, b, i], widen_att[:, 128 * slot : 128 * slot + 128]).astype(BF)
                row = lse[b, h, i, 0:1]
                parts = [(here, True)] + ([(slice(0, past), False)] if i else [])
                probs, grads = [], []
                delta = 0.0
                for part, diagonal in parts:
                    sc = nt(qkv[b, part, 256:384], q) * (scale * log2e)
                    if diagonal:
                        sc = jnp.where(tri, sc, -1e30)
                    pr = jnp.exp2(sc - row)
                    dp = nt(qkv[b, part, 384:512], do)
                    delta = delta + jnp.sum(pr * dp, axis=0, keepdims=True)
                    probs.append(pr)
                    grads.append(dp)
                dq = jnp.zeros((length, 128), F32)
                for (part, _), pr, dp in zip(parts, probs, grads):
                    ds = (pr * (dp - delta) * scale).astype(BF)
                    gv[part] += nn(pr.astype(BF), do)
                    gk[part] += nn(ds, q)
                    dq = dq + tn(ds, qkv[b, part, 256:384])
                gq[b, here, 128 * h : 128 * h + 128] = rope(
                    dq, cos[here], -front[here], -back[here]
                ).astype(BF)
        for i in range(n):
            here = slice(i * length, (i + 1) * length)
            gq[b, here, 256:384] = rope(gk[here], cos[here], -front[here], -back[here]).astype(BF)
            gq[b, here, 384:512] = gv[here].astype(BF)

    tile = 512

    def tiles():
        return [slice(t * tile, (t + 1) * tile) for t in range(width // tile)]

    last = len(Scatter(at, (None,) * 4, (None,) * 4, rows, width).offsets()) - 1
    hops = n // 2

    s_out = Scatter(
        at, Scatter.views(sc_stage, sc_in, sc_out, sc_inn), (s_a, s_b, s_c, s_d),
        rows, planes * part_cols,
    )
    for s in range(n):
        branch[s] = ghid[:, s * part_cols : (s + 1) * part_cols].astype(BF)

    def out_pieces(c, s):
        low = branch[s]
        for p in range(planes):
            yield slice(p * part_cols, (p + 1) * part_cols), tn(att[p * sib + c], low)

    def out_stage(c, s, ref):
        for cols, value in out_pieces(c, s):
            ref[:, cols] = value.astype(BF)

    def out_ring(c, s, store):
        for cols, value in out_pieces(c, s):
            store(cols, value)

    def out_finish(cols, value):
        so[cols.start // part_cols] = value.astype(BF)

    in_att.wait()
    s_out.open(out_stage, out_ring, out_finish)
    in_qkv.wait()
    in_gh.wait()
    attend_back(0)
    ag_dn.hop(1)
    for k in range(1, last):
        s_out.step(k, out_ring, out_finish)
    if sib > 1:
        attend_back(1)
    for h in range(2, hops + 1):
        ag_dn.hop(h)
    s_out.step(last, out_ring, out_finish)

    for m in range(n1_steps):
        n1_load(m).wait()
        part = tn(n1_t[m % 2].reshape(tokens, n1_cols), gq[...].reshape(tokens, 512)).astype(BF)
        sq[m * n1_cols : (m + 1) * n1_cols] = nt(part, widen[...]).astype(BF)
        if m + 2 < n1_steps:
            n1_load(m + 2).start()

    in_wqp.wait()
    e_in = Scatter(
        at, Scatter.views(e_stage_b, e_sib_b, e_out_b, e_inn_b), (e_a, e_b, e_c, e_d), length, width
    )

    def gq_block(c, s):
        return gq[c, pl.ds(pl.multiple_of(s * length, length), length)]

    def e_stage(c, s, ref):
        for cols in tiles():
            ref[:, cols] = nt(gq_block(c, s), wqp[cols, :]).astype(BF)

    def e_ring(c, s, store):
        for cols in tiles():
            store(cols, nt(gq_block(c, s), wqp[cols, :]))

    def e_finish(cols, value):
        o_input[:, cols] = value

    e_in.open(e_stage, e_ring, e_finish)
    for k in range(1, last):
        e_in.step(k, e_ring, e_finish)

    gu_own.wait()
    if near:
        for q in range(planes):
            for dc in range(sib):
                if_near(q, lambda: gu_near(q, dc).wait())
    for dp, dc in gu_pairs():
        gu_arrived(dp, dc)
    qkv_own = z_scatter(sq, r_qkv, z_qs, z_qr, 10)
    out_own = load(so.at[at.p], r_out.at[at.p], 11)
    for dp in range(1, planes):
        to = lax.rem(at.p + dp, planes)
        copy = rdma(so.at[to], r_out.at[at.p], z_os.at[dp], z_or.at[dp], (at.s, at.col(dp, 0)))
        copy.start()
        sent.append(copy)
    for c in range(sib):
        g_gu[at.s, c] = plane_total(r_gu, c)
    ag_gu = Gather(at, row_half(g_gu), (a_gu_s, a_gu_r))
    ag_gu.start()

    wide = planes * units // 2

    def gu_lane(p, g):
        return p * units // wide * 2 * wide + g * wide + p * units % wide

    def save_gu(j):
        s = at.seq_at(j)
        slot = j % n
        if not aligned:
            return [pltpu.make_async_copy(g_gu.at[s], o_ggu.at[s], saves_gu.at[slot, 0])]
        copies = []
        for c in range(sib):
            for p in range(planes):
                for g in range(2):
                    lo = (g * owners + p * sib + c) * (n * units) + s * units
                    copies.append(pltpu.make_async_copy(
                        g_gu.at[s, c, :, pl.ds(gu_lane(p, g), units)],
                        o_ggu.at[:, pl.ds(pl.multiple_of(lo, 128), units)],
                        saves_gu.at[slot, (c * planes + p) * 2 + g],
                    ))
        return copies

    def save_qkv(j):
        s = at.seq_at(j)
        slot = j % n
        if not aligned:
            return [pltpu.make_async_copy(g_qkv.at[s], o_gq.at[s], saves_qkv.at[slot, 0])]
        cols = g_qkv.shape[3]
        return [
            pltpu.make_async_copy(
                g_qkv.at[s, c], o_gq.at[:, pl.ds(pl.multiple_of((s * sib + c) * cols, 128), cols)],
                saves_qkv.at[slot, c],
            )
            for c in range(sib)
        ]

    def save_out(j):
        s = at.seq_at(j)
        slot = j % n
        if not aligned:
            return [pltpu.make_async_copy(g_out.at[s], o_gout.at[s], saves_row.at[0, slot])]
        place = o_gout.at[:, pl.ds(pl.multiple_of(s * part_cols, 128), part_cols)]
        return [pltpu.make_async_copy(g_out.at[s], place, saves_row.at[0, slot])]

    def save_down(j):
        s = at.seq_at(j)
        place = o_gdn.at[pl.ds(pl.multiple_of(s * units, units), units)]
        return [pltpu.make_async_copy(g_dn.at[s], place, saves_row.at[1, j % n])]

    saves = []

    def save(copies):
        for copy in copies:
            copy.start()
        saves.extend(copies)

    ring = [0] + [j for h in range(1, hops) for j in (-h, h)] + [hops]
    for j in ring:
        save(save_down(j))
    e_in.step(last, e_ring, e_finish)
    x_f = x[...].astype(F32)
    inv_one = lax.rsqrt(jnp.mean(x_f * x_f, axis=-1, keepdims=True) + NORM_EPS)
    norm_one = x_f * inv_one
    e_val = o_input[...]
    o_input[...] = ghid[...] + inv_one * (
        e_val - norm_one * jnp.mean(e_val * norm_one, axis=-1, keepdims=True)
    )
    out_own.wait()
    for dp in range(1, planes):
        ref = r_out.at[lax.rem(at.p - dp + planes, planes)]
        rdma(ref, ref, z_os.at[dp], z_or.at[dp], (at.s, at.f)).wait_recv()
    acc = r_out[0].astype(F32)
    for p in range(1, planes):
        acc = acc + r_out[p].astype(F32)
    g_out[at.s] = acc.astype(BF)
    ag_out = Gather(at, row_half(g_out), (a_ou_s, a_ou_r))
    ag_out.start()
    save(save_out(0))
    save(save_gu(0))
    z_collect(r_qkv, z_qs, z_qr, qkv_own)
    for c in range(sib):
        g_qkv[at.s, c] = plane_total(r_qkv, c)
    ag_qkv = Gather(at, row_half(g_qkv), (a_qk_s, a_qk_r))
    ag_qkv.start()
    save(save_qkv(0))
    for h in range(1, hops + 1):
        for ag, put in ((ag_gu, save_gu), (ag_out, save_out), (ag_qkv, save_qkv)):
            ag.hop(h)
            for j in (-h, h) if h < hops else (h,):
                save(put(j))
    e_in.drain()
    s_out.drain()
    for ag in (ag_dn, ag_gu, ag_qkv, ag_out):
        ag.drain()
    for dp, dc in gu_pairs():
        far(dp, lambda: gu_send(dp, dc).wait_send())
    for copy in sent:
        copy.wait_send()
    for copy in saves:
        copy.wait()


def backward_call(dims, aligned, x, tables, widen, widen_att, lse, n1, qkv, gh, att, ghid, wqp, sgu, rgu, sdn):
    n, sib, planes = dims
    length, width = x.shape
    rows = gh.shape[4]
    owners = planes * sib
    units = sdn.shape[1]
    part_cols = width // n
    seq_len = n * length
    head_cols = (GROUP + 2) * HEAD_DIM
    vm, hb = pl.BlockSpec(memory_space=pltpu.VMEM), pl.BlockSpec(memory_space=pl.ANY)
    sds = jax.ShapeDtypeStruct
    g_shapes = [
        (n, sib, rows, head_cols), (n, sib, rows, sgu.shape[1]), (n, units, width),
        (n, rows, part_cols),
    ]
    o_shapes = g_shapes
    if aligned:
        o_shapes = [
            (rows, n * sib * head_cols), (rows, n * sib * sgu.shape[1]), None, (rows, width)
        ]
    o_shapes = [*o_shapes[:2], (n * units, width), o_shapes[3]]
    outs = [(sds((length, width), F32), vm)] + [(sds(shape, BF), hb) for shape in o_shapes]
    dma = pltpu.SemaphoreType.DMA
    scratch = [
        pltpu.VMEM(qkv.shape, BF), pltpu.VMEM(gh.shape, BF), pltpu.VMEM(att.shape, BF),
        pltpu.VMEM(wqp.shape, BF), pltpu.VMEM(sdn.shape, BF), pltpu.VMEM(qkv.shape, BF),
        pltpu.VMEM((seq_len, 128), F32), pltpu.VMEM((seq_len, 128), F32),
        pltpu.VMEM((2, *n1.shape[:3], 384), BF), pltpu.VMEM((width, head_cols), BF),
        pltpu.VMEM((planes, rows, part_cols), BF), pltpu.VMEM((n, length, part_cols), BF),
        pltpu.VMEM((owners, rows, sgu.shape[1]), BF), pltpu.VMEM((owners, rows, head_cols), BF),
        pltpu.VMEM((planes, rows, part_cols), BF),
        pltpu.VMEM(g_shapes[1], BF), pltpu.VMEM(g_shapes[0], BF), pltpu.VMEM(g_shapes[2], BF),
        pltpu.VMEM(g_shapes[3], BF),
        *Scatter.scratch(n, (length, max(width, planes * part_cols))),
        *Scatter.scratch(n, (length, width)),
        dma((12,)), dma((planes, sib)), dma((n, 2 * owners)), dma((n, sib)), dma((2, n)),
        dma((planes, sib)), dma((planes, sib)), dma((planes, sib)),
        dma((planes, sib)), dma((planes,)), dma((planes,)),
        *Scatter.sems(n), *Scatter.sems(n),
        *Gather.scratch(n, False), *Gather.scratch(n, False), *Gather.scratch(n, False),
        *Gather.scratch(n, False),
    ]
    return pl.pallas_call(
        functools.partial(backward_kernel, dims),
        out_shape=[o[0] for o in outs],
        out_specs=[o[1] for o in outs],
        in_specs=[vm] * 7 + [hb] * 4 + [vm] + [hb] * 4,
        scratch_shapes=scratch,
        compiler_params=pltpu.CompilerParams(
            collective_id=1, has_side_effects=True, vmem_limit_bytes=VMEM_LIMIT
        ),
    )(x, *tables, widen, widen_att, lse, n1, qkv, gh, att, ghid, wqp, sgu, rgu, sdn)


def adamw(weight, first, second, grad, rate, decay):
    first_new = BETA_ONE * first + (1.0 - BETA_ONE) * grad
    second_new = BETA_TWO * second + (1.0 - BETA_TWO) * grad * grad
    first_hat = first_new / (1.0 - BETA_ONE**ADAM_STEP)
    second_hat = second_new / (1.0 - BETA_TWO**ADAM_STEP)
    weight_new = weight - rate * (first_hat / (jnp.sqrt(second_hat) + ADAM_EPS) + decay * weight)
    return (weight_new, first_new, second_new)


def to_bf16(value):
    return lax.reduce_precision(value, exponent_bits=8, mantissa_bits=7)


def rope_arrays(seq_len):
    half = HEAD_DIM // 2
    frequencies = (ROPE_BASE ** (-(2.0 * np.arange(half)) / HEAD_DIM)).astype(np.float32)
    angles = np.arange(seq_len, dtype=np.float32)[:, None] * frequencies[None, :]
    cos, sin = np.cos(angles), np.sin(angles)
    pad = np.zeros((seq_len, 128 - HEAD_DIM), np.float32)
    none = np.zeros_like(sin)
    return tuple(
        np.concatenate(columns, axis=1).astype(np.float32)
        for columns in ([cos, cos, pad], [-sin, none, pad], [none, sin, pad])
    )


def widening(heads):
    row = np.arange(heads * HEAD_DIM)[:, None]
    col = np.arange(heads * 128)[None, :]
    return (col == row // HEAD_DIM * 128 + row % HEAD_DIM).astype(ml_dtypes.bfloat16)


def make(n_seq, n_fsdp):
    sib = KV_HEADS // n_seq
    planes = n_fsdp // sib

    def on_device(
        inputs, cotangent, qkv_weight, out_weight, gate_up_weight, down_weight, norm_gains,
        qkv_first, qkv_second, out_first, out_second, gate_up_first, gate_up_second,
        down_first, down_second, gain_first, gain_second,
    ):
        s_idx = lax.axis_index("seq")
        _, length, width = inputs.shape
        seq_len = length * n_seq
        rows = qkv_weight.shape[0]
        head_cols = (GROUP + 2) * HEAD_DIM
        ff_rows = down_weight.shape[0]
        units = ff_rows // n_seq
        hidden_units = ff_rows * n_fsdp
        part_cols = width // n_seq
        aligned = units % 128 == 0 and part_cols % 128 == 0 and sib == 2
        aligned = aligned and rows + units // 2 <= length
        gains = to_bf16(norm_gains)
        gain_cols = gains.T

        if aligned:
            pieces = (qkv_weight, gate_up_weight, down_weight, out_weight)
        else:
            wq_s = lax.dynamic_slice_in_dim(
                qkv_weight, s_idx * sib * head_cols, sib * head_cols, 1
            )
            wq_s = (wq_s * gains[0][:, None]).astype(BF).reshape(rows, sib, head_cols)
            gu_s = gate_up_weight.reshape(rows, 2, planes, sib, n_seq, units)
            gu_s = lax.dynamic_index_in_dim(gu_s, s_idx, 4, keepdims=False)
            gu_s = (gu_s * gains[1][:, None, None, None, None]).astype(BF)
            gu_s = gu_s.transpose(3, 0, 1, 2, 4).reshape(1, sib, rows, 2 * planes * units)
            dn_s = lax.dynamic_slice_in_dim(down_weight, s_idx * units, units, 0).astype(BF)
            wo_s = lax.dynamic_slice_in_dim(out_weight, s_idx * part_cols, part_cols, 1).astype(BF)
            pieces = (wq_s.transpose(1, 0, 2), gu_s, dn_s, wo_s)
        tables = tuple(jnp.asarray(table) for table in rope_arrays(seq_len))
        widen = jnp.asarray(widening(GROUP + 2))
        widen_att = jnp.asarray(widening(rows // HEAD_DIM))

        n_one, qkv, lse, gh, att, block_out, grad_hidden, w_qkv, s_gu, r_gu, s_down = forward_call(
            (n_seq, sib, planes), (rows, units), inputs[0], cotangent[0], tables, widen, widen_att,
            gain_cols, *pieces,
        )
        input_grad, g_qkv, g_gu, g_down, g_out = backward_call(
            (n_seq, sib, planes), aligned, inputs[0], tables, widen, widen_att, lse, n_one, qkv, gh,
            att, grad_hidden, w_qkv, s_gu, r_gu, s_down,
        )
        block_out, input_grad = block_out[None], input_grad[None]
        if not aligned:
            g_qkv = g_qkv.transpose(2, 0, 1, 3).reshape(rows, n_seq * sib * head_cols)
            g_gu = g_gu.reshape(n_seq, sib, rows, 2, planes, units).transpose(2, 3, 4, 1, 0, 5)
            g_gu = g_gu.reshape(rows, 2 * hidden_units)
            g_out = g_out.transpose(1, 0, 2).reshape(rows, width)
        g_qkv, g_gu, g_down, g_out = (g.astype(F32) for g in (g_qkv, g_gu, g_down, g_out))
        gain_grad = jnp.stack(
            [
                jnp.sum(g_qkv * to_bf16(qkv_weight), axis=1),
                jnp.sum(g_gu * to_bf16(gate_up_weight), axis=1),
            ]
        )
        g_qkv = g_qkv * gains[0][:, None]
        g_gu = g_gu * gains[1][:, None]
        qkv_new = adamw(qkv_weight, qkv_first, qkv_second, g_qkv, RATE_QKV, WEIGHT_DECAY)
        out_new = adamw(out_weight, out_first, out_second, g_out, RATE_OUT, WEIGHT_DECAY)
        gu_new = adamw(
            gate_up_weight, gate_up_first, gate_up_second, g_gu, RATE_GATE_UP, WEIGHT_DECAY
        )
        down_new = adamw(
            down_weight, down_first, down_second, g_down, RATE_DOWN, WEIGHT_DECAY
        )
        gains_new = adamw(norm_gains, gain_first, gain_second, gain_grad, RATE_GAINS, 0.0)
        return (block_out, input_grad, *qkv_new, *out_new, *gu_new, *down_new, *gains_new)

    return on_device


def solution(mesh):
    tokens = P("fsdp", "seq", None)
    weight = P("fsdp", None)
    gain = P(None, "fsdp")
    in_specs = (tokens, tokens, weight, weight, weight, weight, gain) + (weight,) * 8 + (gain,) * 2
    out_specs = (tokens, tokens) + (weight,) * 12 + (gain,) * 3
    return jax.shard_map(
        make(mesh.shape["seq"], mesh.shape["fsdp"]),
        mesh=mesh, in_specs=in_specs, out_specs=out_specs, check_vma=False,
    )
```

```python
import functools

import jax
import jax.numpy as jnp
import ml_dtypes
import numpy as np
from jax import lax
from jax.experimental import pallas as pl
from jax.experimental.pallas import tpu as pltpu
from jax.sharding import PartitionSpec as P

HEAD_DIM = 96
KV_HEADS = 8
ADAM_STEP = 10
GROUP = 2

NORM_EPS = 1e-05
ROPE_BASE = 100000.0
BETA_ONE = 0.9
BETA_TWO = 0.95
ADAM_EPS = 1e-08
WEIGHT_DECAY = 0.1
RATE_QKV = 0.07
RATE_OUT = 0.8
RATE_GATE_UP = 0.07
RATE_DOWN = 0.045
RATE_GAINS = 0.6
BF = jnp.bfloat16
F32 = jnp.float32
VMEM_LIMIT = 62 * 1024 * 1024


MESH = pl.DeviceIdType.MESH


def rdma(src, dst, ssem, rsem, dev):
    return pltpu.make_async_remote_copy(
        src_ref=src, dst_ref=dst, send_sem=ssem, recv_sem=rsem, device_id=dev, device_id_type=MESH
    )


class Place:
    def __init__(self, n, sib, planes):
        self.n, self.sib, self.planes = n, sib, planes
        self.s = lax.axis_index("seq")
        self.f = lax.axis_index("fsdp")
        self.c = lax.rem(self.f, sib)
        self.p = lax.div(self.f, sib)
        a, b = lax.div(self.s, 2), lax.rem(self.s, 2)
        self.r = a * (1 - b) + (n - 1 - a) * b

    def seq_at(self, j):
        if j == 0:
            return self.s
        n = self.n
        q = lax.rem(self.r + (j + n), n)
        t = lax.div(q, n // 2)
        return (1 - t) * 2 * q + t * (2 * (n - 1 - q) + 1)

    def dev(self, s, c):
        return (s, self.p * self.sib + c)

    def col(self, dp, dc):
        return lax.rem(self.p + dp, self.planes) * self.sib + lax.rem(self.c + dc, self.sib)

    def barrier(self):
        sem = pltpu.get_barrier_semaphore()
        group = self.n * self.sib
        tau = self.s * self.sib + self.c
        for j in range(1, group):
            t = lax.rem(tau + j, group)
            pl.semaphore_signal(
                sem, inc=1, device_id=self.dev(lax.div(t, self.sib), lax.rem(t, self.sib)),
                device_id_type=MESH,
            )
        for dp in range(1, self.planes):
            for dc in range(self.sib):
                pl.semaphore_signal(
                    sem, inc=1, device_id=(self.s, self.col(dp, dc)), device_id_type=MESH
                )
        pl.semaphore_wait(sem, group - 1 + (self.planes - 1) * self.sib)


class Gather:
    def __init__(self, at, part, sems):
        self.at, self.part = at, part
        self.ring_s, self.ring_r = sems[:2]
        self.share = at.sib > 1 and len(sems) > 2
        if self.share:
            self.sib_s, self.sib_r = sems[2:]
        self.sent = []

    @staticmethod
    def scratch(n, share=True):
        d = pltpu.SemaphoreType.DMA
        ring = [d((2, n // 2, 2)), d((2, n // 2, 2))]
        return ring + [d((n, 2)), d((n, 2))] if share else ring

    def _send(self, copy):
        copy.start()
        self.sent.append(copy)

    def _ring(self, way, hop, half):
        at = self.at
        src = self.part(at.c, at.seq_at(-(hop - 1) if way == 0 else hop - 1), half)
        to = at.dev(at.seq_at(1 if way == 0 else -1), at.c)
        self._send(
            rdma(src, src, self.ring_s.at[way, hop - 1, half], self.ring_r.at[way, hop - 1, half], to)
        )

    def _sib(self, j, half):
        at = self.at
        if self.share:
            src = self.part(at.c, at.seq_at(j), half)
            slot = j % at.n
            self._send(
                rdma(src, src, self.sib_s.at[slot, half], self.sib_r.at[slot, half],
                     at.dev(at.s, 1 - at.c))
            )

    def start(self):
        self._ring(0, 1, 0)
        self._ring(1, 1, 1)
        self._ring(0, 1, 1)
        self._ring(1, 1, 0)
        self._sib(0, 0)
        self._sib(0, 1)

    def _arrive(self, way, hop, half):
        at = self.at
        j = -hop if way == 0 else hop
        ref = self.part(at.c, at.seq_at(j), half)
        rdma(ref, ref, self.ring_s.at[way, hop - 1, half], self.ring_r.at[way, hop - 1, half],
             at.dev(at.s, at.c)).wait_recv()
        last = at.n // 2
        if hop + 1 < last or (hop + 1 == last and half == way):
            self._ring(way, hop + 1, half)
        if hop == last:
            j = last
        self._sib(j, half)

    def hop(self, hop):
        self.hop_first(hop)
        self.hop_second(hop)

    def hop_first(self, hop):
        self._arrive(0, hop, 0)
        self._arrive(1, hop, 1)

    def hop_second(self, hop):
        if hop < self.at.n // 2:
            self._arrive(0, hop, 1)
            self._arrive(1, hop, 0)

    def sib_wait(self, j):
        at = self.at
        if self.share:
            for half in range(2):
                ref = self.part(1 - at.c, at.seq_at(j), half)
                slot = j % at.n
                rdma(ref, ref, self.sib_s.at[slot, half], self.sib_r.at[slot, half],
                     at.dev(at.s, at.c)).wait_recv()

    def stages(self):
        last = self.at.n // 2
        yield 0, [0]
        for h in range(1, last):
            yield h, [-h, h]
        yield last, [last]

    def wait_stage(self, h, offsets):
        if h:
            self.hop(h)
        for j in offsets:
            self.sib_wait(j)

    def drain(self):
        for copy in self.sent:
            copy.wait_send()


class Move:
    def __init__(self, at, src, dst, sems, every_core=True):
        self.at, self.src, self.dst = at, src, dst
        self.ssem, self.rsem, self.hop, self.own = sems
        self.cores = at.sib if every_core else 1
        self.relay = at.planes == 4

    @staticmethod
    def sems(planes, sib):
        d = pltpu.SemaphoreType.DMA
        return [d((planes, sib)), d((planes, sib)), d((sib,)), d((1,))]

    def _pairs(self):
        for dp in [2, 1, 3] if self.relay else range(1, self.at.planes):
            for dc in range(self.cores):
                yield dp, dc
        for dc in range(1, self.cores):
            yield 0, dc

    def _direct(self, dp, body):
        if self.relay and dp in (1, 3):
            pl.when(self.at.p != (3 if dp == 1 else 0))(body)
        else:
            body()

    def _send(self, dp, dc):
        at = self.at
        return rdma(self.src(lax.rem(at.c + dc, at.sib)), self.dst(at.f), self.ssem.at[dp, dc],
                    self.rsem.at[dp, dc], (at.s, at.col(dp, dc)))

    def _local(self):
        return pltpu.make_async_copy(self.src(self.at.c), self.dst(self.at.f), self.own.at[0])

    def start(self):
        self.start_far()
        self.start_near()

    def start_far(self):
        for dp, dc in self._pairs():
            if self.relay and dp == 2:
                self._send(dp, dc).start()

    def start_near(self):
        self._local().start()
        for dp, dc in self._pairs():
            if not (self.relay and dp == 2):
                self._direct(dp, lambda: self._send(dp, dc).start())

    def _got(self, dp, dc):
        at = self.at
        source = lax.rem(at.p - dp + at.planes, at.planes) * at.sib + lax.rem(
            at.c - dc + at.sib, at.sib
        )
        ref = self.dst(source)
        rdma(ref, ref, self.ssem.at[dp, dc], self.rsem.at[dp, dc], (at.s, at.f)).wait_recv()
        return ref

    def pass_on(self):
        at = self.at
        if not self.relay:
            return
        for dp, dc in self._pairs():
            if dp == 2:
                ref = self._got(dp, dc)
                for here, to, slot in ((2, 3, 3), (1, 0, 1)):
                    @pl.when(at.p == here)
                    def _():
                        rdma(ref, ref, self.hop.at[dc], self.rsem.at[slot, dc],
                             (at.s, to * at.sib + at.c)).start()

    def wait(self):
        for dp, dc in self._pairs():
            if not (self.relay and dp == 2):
                self._got(dp, dc)
        self._local().wait()

    def drain(self):
        at = self.at
        for dp, dc in self._pairs():
            self._direct(dp, lambda: self._send(dp, dc).wait_send())
            if self.relay and dp == 2:
                ref = self.dst(at.f)

                @pl.when(jnp.logical_or(at.p == 1, at.p == 2))
                def _():
                    rdma(ref, ref, self.hop.at[dc], self.rsem.at[0, dc], (at.s, at.f)).wait_send()


class Scatter:
    def __init__(self, at, bufs, sems, rows, cols):
        self.at, self.rows, self.cols = at, rows, pl.ds(0, cols)
        self.stage, self.sib_in, self.out, self.inn = bufs
        self.sib_s, self.sib_r, self.ring_s, self.ring_r = sems
        self.sent, self.handed = [], []

    @staticmethod
    def scratch(n, shape):
        return [
            pltpu.VMEM((2, *shape), BF), pltpu.VMEM((n, *shape), BF),
            pltpu.VMEM((2, n // 2, *shape), BF), pltpu.VMEM((2, n // 2, *shape), BF),
        ]

    @staticmethod
    def views(stage, sib_in, out, inn):
        return (
            lambda k: stage.at[k], lambda k: sib_in.at[k],
            lambda w, k: out.at[w, k], lambda w, k: inn.at[w, k],
        )

    @staticmethod
    def sems(n):
        d = pltpu.SemaphoreType.DMA
        return [d((n,)), d((n,)), d((2, n // 2)), d((2, n // 2))]

    def offsets(self):
        last = self.at.n // 2
        order = [last]
        for h in range(last - 1, 0, -1):
            order += [h, -h]
        return order + [0]

    def to_sibling(self, k, produce):
        at = self.at
        if at.sib == 1:
            return
        if k >= 2:
            self.handed[k - 2].wait_send()
        view = self.stage(k % 2).at[pl.ds(0, self.rows), self.cols]
        produce(1 - at.c, at.seq_at(self.offsets()[k]), view)
        copy = rdma(view, self.sib_in(k).at[pl.ds(0, self.rows), self.cols],
                    self.sib_s.at[k], self.sib_r.at[k], at.dev(at.s, 1 - at.c))
        copy.start()
        self.handed.append(copy)

    def open(self, stage, ring, finish):
        self.to_sibling(0, stage)
        self.step(0, ring, finish)
        for k in range(1, len(self.offsets())):
            self.to_sibling(k, stage)

    def _send(self, way, k, rows):
        at = self.at
        src = self.out(way, k).at[rows, self.cols]
        copy = rdma(src, self.inn(way, k).at[rows, self.cols], self.ring_s.at[way, k], self.ring_r.at[way, k],
                    at.dev(at.seq_at(1 if way == 0 else -1), at.c))
        copy.start()
        self.sent.append(copy)

    def _wait(self, way, k, rows):
        ref = self.inn(way, k).at[rows, self.cols]
        at = self.at
        rdma(ref, ref, self.ring_s.at[way, k], self.ring_r.at[way, k],
             at.dev(at.s, at.c)).wait_recv()

    def step(self, k, produce, finish):
        at = self.at
        last = at.n // 2
        length = self.rows
        half = length // 2
        halves = (pl.ds(0, half), pl.ds(half, half))
        whole = pl.ds(0, length)
        j = self.offsets()[k]
        if at.sib > 1:
            ref = self.sib_in(k).at[pl.ds(0, length), self.cols]
            rdma(ref, ref, self.sib_s.at[k], self.sib_r.at[k], at.dev(at.s, at.c)).wait_recv()
        h = abs(j)
        if h == last:
            got = []
        else:
            ways = (0, 1) if h == 0 else ((0,) if j > 0 else (1,))
            rows_in = [halves[w] if h + 1 == last else whole for w in ways]
            got = [(w, rw) for w, rw in zip(ways, rows_in)]
        pending = [True]

        def store(cols, value, k=k, h=h, j=j, got=got, pending=pending):
            if pending[0]:
                for w, rw in got:
                    self._wait(w, h, rw)
                pending[0] = False
            if at.sib > 1:
                value = value + self.sib_in(k)[pl.ds(0, length), cols].astype(F32)
            for w, rw in got:
                if h + 1 == last:
                    add = self.inn(w, h)[pl.ds(w * half, half), cols].astype(F32)
                    if w == 0:
                        value = jnp.concatenate([value[:half] + add, value[half:]], axis=0)
                    else:
                        value = jnp.concatenate([value[:half], value[half:] + add], axis=0)
                else:
                    value = value + self.inn(w, h)[pl.ds(0, length), cols].astype(F32)
            if h == last:
                low = value.astype(BF)
                self.out(0, h - 1)[pl.ds(0, half), cols] = low[:half]
                self.out(1, h - 1)[pl.ds(half, half), cols] = low[half:]
            elif h:
                self.out(0 if j > 0 else 1, h - 1)[pl.ds(0, length), cols] = value.astype(BF)
            else:
                finish(cols, value)

        produce(at.c, at.seq_at(j), store)
        if h == last:
            self._send(0, h - 1, halves[0])
            self._send(1, h - 1, halves[1])
        elif h:
            self._send(0 if j > 0 else 1, h - 1, whole)

    def drain(self):
        for copy in self.sent + self.handed[-2:]:
            copy.wait_send()


class Credits:
    def __init__(self, at, sem):
        self.at, self.sem = at, sem

    def give(self):
        at = self.at
        if at.sib > 1:
            pl.semaphore_signal(
                self.sem, inc=1, device_id=at.dev(at.s, 1 - at.c), device_id_type=MESH
            )
        for way in (1, -1):
            pl.semaphore_signal(
                self.sem, inc=1, device_id=at.dev(at.seq_at(way), at.c), device_id_type=MESH
            )

    def take(self):
        pl.semaphore_wait(self.sem, 3 if self.at.sib > 1 else 2)


def nt(a, b):
    return lax.dot_general(a, b, (((1,), (1,)), ((), ())), preferred_element_type=F32)


def tn(a, b):
    return lax.dot_general(a, b, (((0,), (0,)), ((), ())), preferred_element_type=F32)


def nn(a, b):
    return lax.dot_general(a, b, (((1,), (0,)), ((), ())), preferred_element_type=F32)


def rope(value, cos, front, back):
    return value * cos + pltpu.roll(value, 80, 1) * front + pltpu.roll(value, 48, 1) * back


def forward_kernel(
    dims,
    x, cot, cos, front, back, widen, widen_att, gain_cols, wq_s, gu_s, dn_s, wo_s,
    o_n1, o_qkv, o_lse, o_gh, o_att, o_block, o_ghid, o_wq, o_sgu, o_rgu, o_sdn,
    hid,
    nbuf, cbuf, qkv, wq, wqp, wo, gu, dn, act, ggu, att_out, att_in, gh_in, stg, sgu_t,
    wo_f, wq_b, gu_b, dn_b, wo_b,
    sc_stage, sc_in, sc_out, sc_inn,
    zw_a, zw_b, zw_c, zw_d, zo_a, zo_b, zo_c, zo_d, zd_a, zd_b, zd_c, zd_d,
    zg_a, zg_b, zg_c, zg_d, z_ss, z_sr, local, loads,
    n1_a, n1_b, n1_c, n1_d, ct_a, ct_b, ct_c, ct_d, n2_a, n2_b, n2_c, n2_d, wo_ga, wo_gb, wo_gc, wo_gd,
    rs_a, rs_b, rs_c, rs_d, ds_a, ds_b, ds_c, ds_d, at_s, at_r, gh_s, gh_r, near_s, near_r, free,
):
    n, sib, planes = dims
    at = Place(n, sib, planes)
    length, width = x.shape
    seq_len = n * length
    raw = len(wq_s.shape) == 2
    _, rows, head_cols = wq_b.shape
    owners = planes * sib
    chunks = GROUP * HEAD_DIM // rows
    units = dn_b.shape[0]
    local_units = planes * units
    parts = 2 if units % 128 == 0 else 1
    wide = local_units // parts
    part_cols = wo_b.shape[1]
    heads_per = rows // HEAD_DIM
    half_len = length // 2
    tau = at.s * sib + at.c
    scale = HEAD_DIM ** (-0.5)
    log2e = 1.4426950408889634
    sent = []

    def token_part(ref):
        return lambda c, s, h: ref.at[c, s, pl.ds(h * half_len, half_len)]

    def owner_rows(f):
        return pl.ds(pl.multiple_of(f * rows, rows), rows)

    if raw:
        gu_f = (o_ghid, hid)

        def cut(ref, k, lo, size, dst):
            return pltpu.make_async_copy(
                ref.at[:, pl.ds(pl.multiple_of(lo, 128), size)], dst, loads.at[k]
            )

        def wq_f(c):
            return gu_f[c].at[pl.ds(0, rows), pl.ds(2 * local_units, head_cols)]

        in_wq = [
            cut(wq_s, 3 + 2 * owners + c, (at.s * sib + c) * head_cols, head_cols, wq_f(c))
            for c in range(sib)
        ]
        in_wo = cut(wo_s, 1, at.s * part_cols, part_cols, wo_f)
        half_units = units // 2

        def dn_f(h):
            return gu_f[h].at[pl.ds(rows, half_units)]

        in_dn = [
            pltpu.make_async_copy(
                dn_s.at[pl.ds(pl.multiple_of(at.s * units + h * half_units, half_units), half_units)],
                dn_f(h), loads.at[2 * h],
            )
            for h in range(2)
        ]
        in_gu = []

        def gu_lane(p, g):
            return p * units // wide * 2 * wide + g * wide + p * units % wide

        for c in range(sib):
            for p in range(planes):
                for g in range(2):
                    lo = (g * owners + p * sib + c) * (n * units) + at.s * units
                    k = (c * planes + p) * 2 + g
                    in_gu.append(
                        cut(gu_s, 3 + k, lo, units,
                            gu_f[c].at[pl.ds(0, rows), pl.ds(gu_lane(p, g), units)])
                    )
        for copy in (*in_wq, in_wo, *in_dn, *in_gu):
            copy.start()
        wq_x, gu_x, dn_x, wo_x = wq_b, gu_b, dn_b, wo_b
    else:
        wq_x, gu_x, dn_x, wo_x = wq_s, gu_s, dn_s, wo_s

    move_wq = Move(at, lambda c: wq_x.at[c], lambda f: wq.at[owner_rows(f)], (zw_a, zw_b, zw_c, zw_d))
    move_wo = Move(
        at, lambda c: wo_x, lambda f: wo.at[lax.rem(f, sib), at.s, lax.div(f, sib)],
        (zo_a, zo_b, zo_c, zo_d), False,
    )
    move_dn = Move(
        at, lambda c: dn_x,
        lambda f: dn.at[pl.ds(pl.multiple_of(lax.div(f, sib) * units, units), units)],
        (zd_a, zd_b, zd_c, zd_d), False,
    )

    def gu_move(k):
        return Move(
            at, lambda c: gu_x.at[k, c], lambda f: gu.at[k, owner_rows(f)],
            (zg_a.at[k], zg_b.at[k], zg_c.at[k], zg_d.at[k]),
        )

    move_gu = [gu_move(k) for k in range(parts)]

    x_f = x[...].astype(F32)
    inv_one = lax.rsqrt(jnp.mean(x_f * x_f, axis=-1, keepdims=True) + NORM_EPS)
    nbuf[at.c, at.s] = (x_f * inv_one).astype(BF)
    cbuf[at.c, at.s] = cot[...]
    n_one = Gather(at, token_part(nbuf), (n1_a, n1_b, n1_c, n1_d))
    at.barrier()
    n_one.start()
    if raw:
        g_one = gain_cols[:, 0:1]
        for c in range(sib):
            in_wq[c].wait()
            wq_b[c] = (wq_f(c)[...] * g_one).astype(BF)
        in_wo.wait()
        wo_b[...] = wo_f[...].astype(BF)
    move_wq.start()
    if raw:
        for h in range(2):
            in_dn[h].wait()
            dn_b[h * half_units : (h + 1) * half_units] = dn_f(h)[...].astype(BF)
        for copy in in_gu:
            copy.wait()
        g_two = gain_cols[:, 1:2]
        for c in range(sib):
            for k in range(parts):
                lanes = slice(k * 2 * wide, (k + 1) * 2 * wide)
                gu_b[k, c] = (gu_f[c][0:rows, lanes] * g_two).astype(BF)
    n_stages = list(n_one.stages())
    n_one.hop_first(1)
    move_wq.pass_on()
    move_wo.start()
    n_one.hop_second(1)
    for h, _ in n_stages[2:-1]:
        n_one.hop(h)
    move_wq.wait()
    move_gu[0].start()

    @pl.loop(0, width // 256)
    def _(t):
        here = pl.ds(pl.multiple_of(t * 256, 256), 256)
        wqp[here] = nn(wq[here], widen[...]).astype(BF)

    save_wq = pltpu.make_async_copy(wqp, o_wq, local.at[2])
    save_wq.start()

    def project(c, s):
        y = nn(nbuf[c, s], wqp[...]).astype(BF)
        here = pl.ds(pl.multiple_of(s * length, length), length)
        cs, fr, bk = cos[here], front[here], back[here]
        for k in range(3):
            lanes = slice(128 * k, 128 * k + 128)
            qkv[c, here, lanes] = rope(y[:, lanes].astype(F32), cs, fr, bk).astype(BF)
        qkv[c, here, 384:512] = y[:, 384:512]

    for h, offsets in n_stages:
        if h == n // 2:
            n_one.hop(h)
        for j in offsets:
            n_one.sib_wait(j)
            s_j = at.seq_at(j)

            @pl.loop(0, sib)
            def _(c):
                project(c, s_j)

    cot_gather = Gather(at, token_part(cbuf), (ct_a, ct_b, ct_c, ct_d))
    save_n1 = pltpu.make_async_copy(nbuf, o_n1, local.at[3])
    save_n1.start()
    save_qkv = pltpu.make_async_copy(qkv, o_qkv, local.at[4])
    save_qkv.start()

    tri = lax.broadcasted_iota(jnp.int32, (length, length), 0) >= lax.broadcasted_iota(
        jnp.int32, (length, length), 1
    )

    def spot(k, b, i):
        return (k * sib + b) * n + i

    def attend(i):
        @pl.loop(0, sib)
        def _(b):
            past = i * length
            here = slice(past, past + length)
            outs = []
            for h in range(GROUP):
                q = qkv[b, here, 128 * h : 128 * h + 128]
                d = jnp.where(tri, nt(q, qkv[b, here, 256:384]) * (scale * log2e), -1e30)
                m = jnp.max(d, axis=1, keepdims=True)
                if i:
                    e = nt(q, qkv[b, 0:past, 256:384]) * (scale * log2e)
                    m = jnp.maximum(m, jnp.max(e, axis=1, keepdims=True))
                d = jnp.exp2(d - m)
                total = jnp.sum(d, axis=1, keepdims=True)
                o = nn(d.astype(BF), qkv[b, here, 384:512])
                if i:
                    e = jnp.exp2(e - m)
                    total = total + jnp.sum(e, axis=1, keepdims=True)
                    o = o + nn(e.astype(BF), qkv[b, 0:past, 384:512])
                outs.append((o / total).astype(BF))
                lse = jnp.broadcast_to(m + jnp.log2(total), (length, 128))
                o_lse[b, h, i] = lse.T[0:8]
            for k in range(chunks):
                pair = jnp.concatenate(outs[k * heads_per : (k + 1) * heads_per], axis=1)
                att_out[spot(k, b, i)] = nt(pair, widen_att[...]).astype(BF)

    def send_attended(i):
        for k in range(chunks):
            for b in range(sib):
                mine = jnp.logical_and(at.s == i, at.c == b)

                @pl.when(mine)
                def _():
                    att_in[tau * chunks + k] = att_out[spot(k, b, i)]

                @pl.when(jnp.logical_not(mine))
                def _():
                    rdma(att_out.at[spot(k, b, i)], att_in.at[tau * chunks + k], at_s.at[k, b, i],
                         at_r.at[tau * chunks + k], at.dev(i, b)).start()

    wo_gather = Gather(
        at, lambda c, s, h: wo.at[c, s, pl.ds(h * (planes // 2), planes // 2)],
        (wo_ga, wo_gb, wo_gc, wo_gd),
    )
    attend(n - 1)
    save_n1.wait()
    n_one.drain()
    send_attended(n - 1)
    move_wo.pass_on()
    move_wo.wait()
    wo_gather.start()
    for move in (*move_gu[1:], move_dn):
        move.start_far()
    for i in range(n - 2, -1, -1):
        attend(i)
        send_attended(i)
    wo_hops = list(wo_gather.stages())
    for h, _ in wo_hops[1:-1]:
        wo_gather.hop(h)
    cot_gather.start()
    wo_gather.hop(n // 2)
    for _, offsets in wo_hops:
        for j in offsets:
            wo_gather.sib_wait(j)
    wo_gather.drain()
    save_qkv.wait()
    save_wq.wait()

    group = n * sib
    for j in range(1, group):
        t = lax.rem(tau + j, group)
        for k in range(chunks):
            ref = att_in.at[t * chunks + k]
            rdma(ref, ref, at_s.at[0, 0, 0], at_r.at[t * chunks + k], at.dev(at.s, at.c)).wait_recv()
    for k in range(chunks):
        for i in range(n):
            for b in range(sib):
                @pl.when(jnp.logical_not(jnp.logical_and(at.s == i, at.c == b)))
                def _():
                    rdma(att_out.at[spot(k, b, i)], att_out.at[spot(k, b, i)], at_s.at[k, b, i],
                         at_r.at[0], at.dev(at.s, at.c)).wait_send()
    save_att = pltpu.make_async_copy(att_in, o_att, local.at[3])
    save_att.start()

    x_f = x[...].astype(F32)
    for s in range(n):
        cols = slice(s * part_cols, (s + 1) * part_cols)
        acc = x_f[:, cols]
        for p in range(planes):
            for c in range(sib):
                acc = acc + nn(att_in[p * sib + c], wo[c, s, p])
        hid[:, cols] = acc
    hidden = hid[...]
    inv_mid = lax.rsqrt(jnp.mean(hidden * hidden, axis=-1, keepdims=True) + NORM_EPS)
    nbuf[at.c, at.s] = (hidden * inv_mid).astype(BF)
    n_two = Gather(at, token_part(nbuf), (n2_a, n2_b, n2_c, n2_d))
    n_two.start()

    stages = list(n_two.stages())
    for move in (*move_gu[1:], move_dn):
        move.start_near()
    move_gu[0].pass_on()
    for h, _ in stages[1:-1]:
        cot_gather.hop(h)
        n_two.hop(h)
    for move in (*move_gu[1:], move_dn):
        move.pass_on()

    def gate_pass(k, c, s):
        y = nn(nbuf[c, s], gu[k])
        gate, up = y[:, :wide], y[:, wide:]
        act[c, s, :, k * wide : (k + 1) * wide] = (gate / (1.0 + jnp.exp(-gate)) * up).astype(BF)
        ggu[c, s, :, k * 2 * wide : (k + 1) * 2 * wide] = y.astype(BF)

    def grad_pass(c, s):
        for k in range(parts):
            lo = k * 2 * wide
            gate = ggu[c, s, :, lo : lo + wide].astype(F32)
            up = ggu[c, s, :, lo + wide : lo + 2 * wide].astype(F32)
            grad_act = nt(cbuf[c, s], dn[k * wide : (k + 1) * wide])
            sig = 1.0 / (1.0 + jnp.exp(-gate))
            ggu[c, s, :, lo : lo + wide] = (
                grad_act * up * sig * (1.0 + gate * (1.0 - sig))
            ).astype(BF)
            ggu[c, s, :, lo + wide : lo + 2 * wide] = (grad_act * (gate * sig)).astype(BF)

    def each_block(offsets, body):
        for j in offsets:
            s_j = at.seq_at(j)

            @pl.loop(0, sib)
            def _(c):
                body(c, s_j)

    def rows_wait(offsets):
        for j in offsets:
            n_two.sib_wait(j)
            cot_gather.sib_wait(j)

    early = [j for _, offsets in stages[:-1] for j in offsets]
    late = stages[-1][1]
    rows_wait(early)
    for k in range(parts):
        move_gu[k].wait()
        each_block(early, lambda c, s: gate_pass(k, c, s))
    move_dn.wait()
    each_block(early, grad_pass)
    n_two.hop(n // 2)
    cot_gather.hop(n // 2)
    rows_wait(late)
    for k in range(parts):
        each_block(late, lambda c, s: gate_pass(k, c, s))
    each_block(late, grad_pass)

    scatter = Scatter(
        at, Scatter.views(sc_stage, sc_in, sc_out, sc_inn), (rs_a, rs_b, rs_c, rs_d), length, width
    )
    tile = 512

    def column_tiles():
        return [slice(t * tile, (t + 1) * tile) for t in range(width // tile)]

    def mid_part(c, s, cols):
        acc = nt(ggu[c, s, :, 0 : 2 * wide], gu[0, cols, :])
        for k in range(1, parts):
            acc = acc + nt(ggu[c, s, :, k * 2 * wide : (k + 1) * 2 * wide], gu[k, cols, :])
        return acc

    def to_stage(c, s, ref):
        for cols in column_tiles():
            ref[:, cols] = mid_part(c, s, cols).astype(BF)

    def to_ring(c, s, store):
        for cols in column_tiles():
            store(cols, mid_part(c, s, cols))

    tokens = sib * seq_len
    down_copies = []

    def grad_down():
        cot_all = cbuf[...].reshape(tokens, width)
        down_rows = local_units // 2
        for t in range(2):
            rows_here = slice(t * down_rows, (t + 1) * down_rows)
            lhs = act[:, :, :, rows_here].reshape(tokens, down_rows)
            stg[rows_here] = tn(lhs, cot_all).astype(BF)
        own = pltpu.make_async_copy(
            stg.at[pl.ds(pl.multiple_of(at.p * units, units), units)], o_sdn.at[at.p], local.at[6]
        )
        own.start()
        down_copies.append(own)
        for dp in range(1, planes):
            to = lax.rem(at.p + dp, planes)
            copy = rdma(stg.at[pl.ds(pl.multiple_of(to * units, units), units)], o_sdn.at[at.p],
                        z_ss.at[dp], z_sr.at[dp], (at.s, at.col(dp, 0)))
            copy.start()
            sent.append(copy)

    gu_tile = sgu_t.shape[1]
    gu_steps = width // gu_tile
    near = planes == 4

    def gu_copy(m, slot):
        return pltpu.make_async_copy(
            sgu_t.at[slot], o_sgu.at[pl.ds(m * gu_tile, gu_tile)], local.at[7 + slot]
        )

    def near_send(m, dc):
        to = m * sib + lax.rem(at.c + dc, sib)
        return rdma(o_sgu.at[owner_rows(to)], o_rgu.at[at.f], near_s.at[m, dc],
                    near_r.at[at.p, dc], (at.s, to))

    def if_near(m, body):
        pl.when(jnp.logical_or(at.p == m - 1, at.p == m + 1))(body)

    def leave(m):
        gu_copy(m, m % 2).wait()
        if near:
            for dc in range(sib):
                if_near(m, lambda: near_send(m, dc).start())

    def grad_gu():
        for m in range(gu_steps):
            slot = m % 2
            lhs = nbuf[:, :, :, m * gu_tile : (m + 1) * gu_tile].reshape(tokens, gu_tile)
            sgu_t[slot] = tn(lhs, ggu[...].reshape(tokens, 2 * local_units)).astype(BF)
            gu_copy(m, slot).start()
            if m:
                leave(m - 1)
        leave(gu_steps - 1)

    def finish(cols, value):
        o_ghid[:, cols] = value

    def flat(ref, base):
        return lambda w, k: ref.at[base, w * (n // 2) + k]

    down = Scatter(
        at, (lambda k: cbuf.at[0, k], lambda k: nbuf.at[0, k], flat(cbuf, sib - 1), flat(nbuf, sib - 1)),
        (ds_a, ds_b, ds_c, ds_d), length, width,
    )

    def down_stage(c, s, ref):
        for cols in column_tiles():
            ref[:, cols] = nn(act[c, s], dn[:, cols]).astype(BF)

    def down_ring(c, s, store):
        for cols in column_tiles():
            store(cols, nn(act[c, s], dn[:, cols]))

    def down_finish(cols, value):
        o_block[:, cols] = (hid[:, cols] + value).astype(BF)

    credits = Credits(at, free)
    last = len(scatter.offsets()) - 1
    scatter.open(to_stage, to_ring, finish)
    grad_down()
    for k in range(1, last):
        scatter.step(k, to_ring, finish)
    grad_gu()
    cot_gather.drain()
    n_two.drain()
    credits.give()
    credits.take()
    down.open(down_stage, down_ring, down_finish)
    scatter.step(last, to_ring, finish)
    e_mid = o_ghid[...]
    hidden = hid[...]
    inv_mid = lax.rsqrt(jnp.mean(hidden * hidden, axis=-1, keepdims=True) + NORM_EPS)
    norm_mid = hidden * inv_mid
    o_ghid[...] = cot[...].astype(F32) + inv_mid * (
        e_mid - norm_mid * jnp.mean(e_mid * norm_mid, axis=-1, keepdims=True)
    )
    branch = o_ghid[...].astype(BF)
    for f in range(owners):
        p, c = f // sib, f % sib
        acc = nt(branch[:, :part_cols], wo[c, 0, p])
        for s in range(1, n):
            acc = acc + nt(branch[:, s * part_cols : (s + 1) * part_cols], wo[c, s, p])
        att_out[f] = acc.astype(BF)
        t, k = f // chunks, f % chunks
        mine = tau == t

        @pl.when(mine)
        def _():
            gh_in[k, at.c, at.s] = att_out[f]

        @pl.when(jnp.logical_not(mine))
        def _():
            rdma(att_out.at[f], gh_in.at[k, at.c, at.s], gh_s.at[f], gh_r.at[k, tau],
                 at.dev(t // sib, t % sib)).start()

    for k in range(1, last):
        down.step(k, down_ring, down_finish)
    for j in range(1, group):
        t = lax.rem(tau + j, group)
        for k in range(chunks):
            ref = gh_in.at[k, lax.rem(t, sib), lax.div(t, sib)]
            rdma(ref, ref, gh_s.at[0], gh_r.at[k, t], at.dev(at.s, at.c)).wait_recv()
    save_gh = pltpu.make_async_copy(gh_in, o_gh, local.at[0])
    save_gh.start()
    for f in range(owners):
        @pl.when(jnp.logical_not(tau == f // chunks))
        def _():
            rdma(att_out.at[f], att_out.at[f], gh_s.at[f], gh_r.at[0, 0],
                 at.dev(at.s, at.c)).wait_send()

    down.step(last, down_ring, down_finish)

    for dp in range(1, planes):
        ref = o_sdn.at[lax.rem(at.p - dp + planes, planes)]
        rdma(ref, ref, z_ss.at[dp], z_sr.at[dp], (at.s, at.f)).wait_recv()
    for copy in down_copies:
        copy.wait()
    if near:
        for q in range(planes):
            for dc in range(sib):
                def arrived():
                    ref = o_rgu.at[q * sib + lax.rem(at.c - dc + sib, sib)]
                    rdma(ref, ref, near_s.at[q, dc], near_r.at[q, dc], (at.s, at.f)).wait_recv()
                    near_send(q, dc).wait_send()

                if_near(q, arrived)
    scatter.drain()
    down.drain()
    for move in (move_wq, move_wo, move_dn, *move_gu):
        move.drain()
    for copy in sent:
        copy.wait_send()
    save_att.wait()
    save_gh.wait()


def forward_call(dims, sizes, x, cot, tables, widen, widen_att, gain_cols, wq_s, gu_s, dn_s, wo_s):
    n, sib, planes = dims
    rows, units = sizes
    length, width = x.shape
    part_cols = width // n
    head_cols = (GROUP + 2) * HEAD_DIM
    owners = planes * sib
    chunks = GROUP * HEAD_DIM // rows
    ffl = planes * units
    parts = 2 if units % 128 == 0 else 1
    seq_len = n * length
    vm, hb = pl.BlockSpec(memory_space=pltpu.VMEM), pl.BlockSpec(memory_space=pl.ANY)
    blocks = (sib, n, length, width)
    sds = jax.ShapeDtypeStruct
    outs = [
        (sds(blocks, BF), hb),
        (sds((sib, seq_len, 512), BF), hb),
        (sds((sib, GROUP, n, 8, length), F32), vm),
        (sds((chunks, sib, n, length, rows), BF), hb),
        (sds((owners, length, rows), BF), hb),
        (sds((length, width), BF), vm),
        (sds((length, width), F32), vm),
        (sds((width, 512), BF), hb),
        (sds((width, 2 * ffl), BF), hb),
        (sds((owners, rows, 2 * ffl), BF), hb),
        (sds((planes, units, width), BF), hb),
    ]
    dma = pltpu.SemaphoreType.DMA
    scratch = [
        pltpu.VMEM((length, width), F32),
        pltpu.VMEM(blocks, BF), pltpu.VMEM(blocks, BF), pltpu.VMEM((sib, seq_len, 512), BF),
        pltpu.VMEM((width, head_cols), BF), pltpu.VMEM((width, 512), BF),
        pltpu.VMEM((sib, n, planes, rows, part_cols), BF),
        pltpu.VMEM((parts, width, 2 * ffl // parts), BF), pltpu.VMEM((ffl, width), BF),
        pltpu.VMEM((sib, n, length, ffl), BF), pltpu.VMEM((sib, n, length, 2 * ffl), BF),
        pltpu.VMEM((owners, length, rows), BF), pltpu.VMEM((owners, length, rows), BF),
        pltpu.VMEM((chunks, sib, n, length, rows), BF),
        pltpu.VMEM((ffl, width), BF), pltpu.VMEM((2, 384, 2 * ffl), BF),

        pltpu.VMEM((rows, part_cols), F32),
        pltpu.VMEM((sib, rows, head_cols), BF),
        pltpu.VMEM((parts, sib, rows, 2 * ffl // parts), BF),
        pltpu.VMEM((units, width), BF), pltpu.VMEM((rows, part_cols), BF),
        *Scatter.scratch(n, (length, width)),
        *Move.sems(planes, sib), *Move.sems(planes, sib), *Move.sems(planes, sib),
        dma((parts, planes, sib)), dma((parts, planes, sib)), dma((parts, sib)), dma((parts, 1)),
        dma((planes,)), dma((planes,)), dma((9,)), dma((3 + 2 * owners + sib,)),
        *Gather.scratch(n), *Gather.scratch(n), *Gather.scratch(n), *Gather.scratch(n),
        *Scatter.sems(n), *Scatter.sems(n),
        dma((chunks, sib, n)), dma((owners,)), dma((owners,)), dma((chunks, n * sib)),
        dma((planes, sib)), dma((planes, sib)), pltpu.SemaphoreType.REGULAR,
    ]
    return pl.pallas_call(
        functools.partial(forward_kernel, dims),
        out_shape=[o[0] for o in outs],
        out_specs=[o[1] for o in outs],
        in_specs=[vm] * 8 + [hb] * 4,
        scratch_shapes=scratch,
        compiler_params=pltpu.CompilerParams(
            collective_id=0, has_side_effects=True, vmem_limit_bytes=VMEM_LIMIT
        ),
    )(x, cot, *tables, widen, widen_att, gain_cols, wq_s, gu_s, dn_s, wo_s)


def backward_kernel(
    dims,
    x, cos, front, back, widen, widen_att, lse,
    n1, qkv_h, gh_h, att_h, ghid, wqp_h, sgu, rgu_h, sdn_h,
    o_input, o_gq, o_ggu, o_gdn, o_gout,
    qkv, gh, att, wqp, sdn, gq, gk, gv, n1_t, sq, so, branch,
    r_gu, r_qkv, r_out, g_gu, g_qkv, g_dn, g_out,
    sc_stage, sc_in, sc_out, sc_inn, e_stage_b, e_sib_b, e_out_b, e_inn_b,
    via, via_s, via_r, loads, near_l, saves_gu, saves_qkv, saves_row, z_gs, z_gr, z_qs, z_qr, z_os, z_or,
    e_a, e_b, e_c, e_d, s_a, s_b, s_c, s_d,
    a_dn_s, a_dn_r, a_gu_s, a_gu_r, a_qk_s, a_qk_r, a_ou_s, a_ou_r,
):
    n, sib, planes = dims
    at = Place(n, sib, planes)
    length, width = x.shape
    owners = planes * sib
    chunks, _, _, _, rows = gh.shape
    heads_per = rows // HEAD_DIM
    part_cols = r_out.shape[2]
    scale = HEAD_DIM ** (-0.5)
    log2e = 1.4426950408889634
    tokens = sib * n * length
    sent = []
    near = planes == 4
    units = g_dn.shape[1]
    aligned = len(o_ggu.shape) == 2

    def load(src, dst, k):
        copy = pltpu.make_async_copy(src, dst, loads.at[k])
        copy.start()
        return copy

    def owner_rows(f):
        return pl.ds(pl.multiple_of(f * rows, rows), rows)

    def z_source(dp, dc):
        return (
            lax.rem(at.p - dp + planes, planes) * sib + lax.rem(at.c - dc + sib, sib)
        )

    def z_scatter(src, dst, ssem, rsem, k):
        own = load(src.at[owner_rows(at.f)], dst.at[at.f], k)
        for dp in range(planes):
            for dc in range(sib):
                if dp or dc:
                    to = at.col(dp, dc)
                    copy = rdma(src.at[owner_rows(to)], dst.at[at.f],
                                ssem.at[dp, dc], rsem.at[dp, dc], (at.s, to))
                    copy.start()
                    sent.append(copy)
        return own

    def z_collect(dst, ssem, rsem, own):
        own.wait()
        for dp in range(planes):
            for dc in range(sib):
                if dp or dc:
                    ref = dst.at[z_source(dp, dc)]
                    rdma(ref, ref, ssem.at[dp, dc], rsem.at[dp, dc], (at.s, at.f)).wait_recv()

    def plane_total(dst, c):
        acc = dst[c].astype(F32)
        for p in range(1, planes):
            acc = acc + dst[p * sib + c].astype(F32)
        return acc.astype(BF)

    def gu_pairs():
        for dp in [2, 0] if near else range(planes):
            for dc in range(sib):
                if dp or dc:
                    yield dp, dc

    def at_ends(body):
        pl.when(jnp.logical_or(at.p == 0, at.p == planes - 1))(body)

    def at_middle(body):
        pl.when(jnp.logical_and(at.p != 0, at.p != planes - 1))(body)

    def gu_from(dp, dc):
        return at_ends if near and dp == 2 else lambda body: body()

    def gu_copy(src, dp, dc):
        to = at.col(dp, dc)
        return rdma(src, r_gu.at[at.f], z_gs.at[dp, dc], z_gr.at[dp, dc], (at.s, to))

    def gu_send(dp, dc):
        return gu_copy(sgu.at[owner_rows(at.col(dp, dc))], dp, dc)

    def plane_rows(p):
        return pl.ds(pl.multiple_of(p * (sib * rows), sib * rows), sib * rows)

    def toward_middle():
        far_plane = planes - 1 - at.p
        beside = at.p + 1 - 2 * lax.div(at.p, planes - 1)
        return rdma(sgu.at[plane_rows(far_plane)], via.at[0], via_s.at[0], via_r.at[0],
                    (at.s, beside * sib + at.c))

    def sum_load():
        return pltpu.make_async_copy(
            sgu.at[plane_rows(lax.rem(at.p + 2, planes))], via.at[1], loads.at[12]
        )

    def gu_send_sum(dc):
        c = lax.rem(at.c + dc, sib)
        return gu_copy(via.at[1, pl.ds(pl.multiple_of(c * rows, rows), rows)], 2, dc)

    def sum_on():
        def body():
            ref = via.at[0]
            rdma(ref, ref, via_s.at[0], via_r.at[0], (at.s, at.f)).wait_recv()
            sum_load().wait()
            via[1] = (via[0].astype(F32) + via[1].astype(F32)).astype(BF)
            for dc in range(sib):
                gu_send_sum(dc).start()

        at_middle(body)

    def gu_near(q, dc):
        f = q * sib + dc
        return pltpu.make_async_copy(rgu_h.at[f], r_gu.at[f], near_l.at[q, dc])

    def if_near(q, body):
        pl.when(jnp.logical_or(at.p == q - 1, at.p == q + 1))(body)

    def gu_wait(dp, dc):
        ref = r_gu.at[z_source(dp, dc)]
        rdma(ref, ref, z_gs.at[dp, dc], z_gr.at[dp, dc], (at.s, at.f)).wait_recv()

    at.barrier()
    in_qkv, in_gh = load(qkv_h, qkv, 0), load(gh_h, gh, 1)
    in_sdn, in_att, in_wqp = load(sdn_h, sdn, 4), load(att_h, att, 6), load(wqp_h, wqp, 7)
    gu_own = load(sgu.at[owner_rows(at.f)], r_gu.at[at.f], 5)
    if near:
        at_ends(lambda: toward_middle().start())
        at_middle(lambda: sum_load().start())
    for dp, dc in gu_pairs():
        gu_from(dp, dc)(lambda: gu_send(dp, dc).start())
    if near:
        for q in range(planes):
            for dc in range(sib):
                if_near(q, lambda: gu_near(q, dc).start())
    n1_cols = n1_t.shape[4]
    n1_steps = width // n1_cols

    def n1_load(m):
        return pltpu.make_async_copy(
            n1.at[:, :, :, pl.ds(m * n1_cols, n1_cols)], n1_t.at[m % 2], loads.at[8 + m % 2]
        )

    n1_load(0).start()
    n1_load(1).start()

    def row_half(ref):
        size = ref.shape[-2] // 2
        if len(ref.shape) == 4:
            return lambda c, s, h: ref.at[s, :, pl.ds(h * size, size)]
        return lambda c, s, h: ref.at[s, pl.ds(h * size, size)]

    in_sdn.wait()
    acc = sdn[0].astype(F32)
    for p in range(1, planes):
        acc = acc + sdn[p].astype(F32)
    g_dn[at.s] = acc.astype(BF)
    ag_dn = Gather(at, row_half(g_dn), (a_dn_s, a_dn_r))
    ag_dn.start()

    tri = lax.broadcasted_iota(jnp.int32, (length, length), 0) <= lax.broadcasted_iota(
        jnp.int32, (length, length), 1
    )

    def attend_back(b):
        gk[...] = jnp.zeros_like(gk)
        gv[...] = jnp.zeros_like(gv)
        for i in range(n):
            past = i * length
            here = slice(past, past + length)
            for h in range(GROUP):
                k, slot = h // heads_per, h % heads_per
                q = qkv[b, here, 128 * h : 128 * h + 128]
                do = nn(gh[k, b, i], widen_att[:, 128 * slot : 128 * slot + 128]).astype(BF)
                row = lse[b, h, i, 0:1]
                parts = [(here, True)] + ([(slice(0, past), False)] if i else [])
                probs, grads = [], []
                delta = 0.0
                for part, diagonal in parts:
                    sc = nt(qkv[b, part, 256:384], q) * (scale * log2e)
                    if diagonal:
                        sc = jnp.where(tri, sc, -1e30)
                    pr = jnp.exp2(sc - row)
                    dp = nt(qkv[b, part, 384:512], do)
                    delta = delta + jnp.sum(pr * dp, axis=0, keepdims=True)
                    probs.append(pr)
                    grads.append(dp)
                dq = jnp.zeros((length, 128), F32)
                for (part, _), pr, dp in zip(parts, probs, grads):
                    ds = (pr * (dp - delta) * scale).astype(BF)
                    gv[part] += nn(pr.astype(BF), do)
                    gk[part] += nn(ds, q)
                    dq = dq + tn(ds, qkv[b, part, 256:384])
                gq[b, here, 128 * h : 128 * h + 128] = rope(
                    dq, cos[here], -front[here], -back[here]
                ).astype(BF)
        for i in range(n):
            here = slice(i * length, (i + 1) * length)
            gq[b, here, 256:384] = rope(gk[here], cos[here], -front[here], -back[here]).astype(BF)
            gq[b, here, 384:512] = gv[here].astype(BF)

    tile = 512

    def tiles():
        return [slice(t * tile, (t + 1) * tile) for t in range(width // tile)]

    last = len(Scatter(at, (None,) * 4, (None,) * 4, rows, width).offsets()) - 1
    hops = n // 2

    s_out = Scatter(
        at, Scatter.views(sc_stage, sc_in, sc_out, sc_inn), (s_a, s_b, s_c, s_d),
        rows, planes * part_cols,
    )
    for s in range(n):
        branch[s] = ghid[:, s * part_cols : (s + 1) * part_cols].astype(BF)

    def out_pieces(c, s):
        low = branch[s]
        for p in range(planes):
            yield slice(p * part_cols, (p + 1) * part_cols), tn(att[p * sib + c], low)

    def out_stage(c, s, ref):
        for cols, value in out_pieces(c, s):
            ref[:, cols] = value.astype(BF)

    def out_ring(c, s, store):
        for cols, value in out_pieces(c, s):
            store(cols, value)

    def out_finish(cols, value):
        so[cols.start // part_cols] = value.astype(BF)

    in_att.wait()
    s_out.open(out_stage, out_ring, out_finish)
    in_qkv.wait()
    in_gh.wait()
    attend_back(0)
    ag_dn.hop(1)
    for k in range(1, last):
        s_out.step(k, out_ring, out_finish)
    if sib > 1:
        attend_back(1)
    for h in range(2, hops + 1):
        ag_dn.hop(h)
    s_out.step(last, out_ring, out_finish)

    for m in range(n1_steps):
        n1_load(m).wait()
        part = tn(n1_t[m % 2].reshape(tokens, n1_cols), gq[...].reshape(tokens, 512)).astype(BF)
        sq[m * n1_cols : (m + 1) * n1_cols] = nt(part, widen[...]).astype(BF)
        if m + 2 < n1_steps:
            n1_load(m + 2).start()

    if near:
        sum_on()

    in_wqp.wait()
    e_in = Scatter(
        at, Scatter.views(e_stage_b, e_sib_b, e_out_b, e_inn_b), (e_a, e_b, e_c, e_d), length, width
    )

    def gq_block(c, s):
        return gq[c, pl.ds(pl.multiple_of(s * length, length), length)]

    def e_stage(c, s, ref):
        for cols in tiles():
            ref[:, cols] = nt(gq_block(c, s), wqp[cols, :]).astype(BF)

    def e_ring(c, s, store):
        for cols in tiles():
            store(cols, nt(gq_block(c, s), wqp[cols, :]))

    def e_finish(cols, value):
        o_input[:, cols] = value

    e_in.open(e_stage, e_ring, e_finish)
    for k in range(1, last):
        e_in.step(k, e_ring, e_finish)

    gu_own.wait()
    if near:
        for q in range(planes):
            for dc in range(sib):
                if_near(q, lambda: gu_near(q, dc).wait())
    for dp, dc in gu_pairs():
        gu_wait(dp, dc)
    if near:
        for c in range(sib):
            @pl.when(at.p == 0)
            def _():
                r_gu[(planes - 1) * sib + c] = jnp.zeros(r_gu.shape[1:], BF)

            @pl.when(at.p == planes - 1)
            def _():
                r_gu[c] = jnp.zeros(r_gu.shape[1:], BF)
    qkv_own = z_scatter(sq, r_qkv, z_qs, z_qr, 10)
    out_own = load(so.at[at.p], r_out.at[at.p], 11)
    for dp in range(1, planes):
        to = lax.rem(at.p + dp, planes)
        copy = rdma(so.at[to], r_out.at[at.p], z_os.at[dp], z_or.at[dp], (at.s, at.col(dp, 0)))
        copy.start()
        sent.append(copy)
    for c in range(sib):
        g_gu[at.s, c] = plane_total(r_gu, c)
    ag_gu = Gather(at, row_half(g_gu), (a_gu_s, a_gu_r))
    ag_gu.start()

    wide = planes * units // 2

    def gu_lane(p, g):
        return p * units // wide * 2 * wide + g * wide + p * units % wide

    def save_gu(j):
        s = at.seq_at(j)
        slot = j % n
        if not aligned:
            return [pltpu.make_async_copy(g_gu.at[s], o_ggu.at[s], saves_gu.at[slot, 0])]
        copies = []
        for c in range(sib):
            for p in range(planes):
                for g in range(2):
                    lo = (g * owners + p * sib + c) * (n * units) + s * units
                    copies.append(pltpu.make_async_copy(
                        g_gu.at[s, c, :, pl.ds(gu_lane(p, g), units)],
                        o_ggu.at[:, pl.ds(pl.multiple_of(lo, 128), units)],
                        saves_gu.at[slot, (c * planes + p) * 2 + g],
                    ))
        return copies

    def save_qkv(j):
        s = at.seq_at(j)
        slot = j % n
        if not aligned:
            return [pltpu.make_async_copy(g_qkv.at[s], o_gq.at[s], saves_qkv.at[slot, 0])]
        cols = g_qkv.shape[3]
        return [
            pltpu.make_async_copy(
                g_qkv.at[s, c], o_gq.at[:, pl.ds(pl.multiple_of((s * sib + c) * cols, 128), cols)],
                saves_qkv.at[slot, c],
            )
            for c in range(sib)
        ]

    def save_out(j):
        s = at.seq_at(j)
        slot = j % n
        if not aligned:
            return [pltpu.make_async_copy(g_out.at[s], o_gout.at[s], saves_row.at[0, slot])]
        place = o_gout.at[:, pl.ds(pl.multiple_of(s * part_cols, 128), part_cols)]
        return [pltpu.make_async_copy(g_out.at[s], place, saves_row.at[0, slot])]

    def save_down(j):
        s = at.seq_at(j)
        place = o_gdn.at[pl.ds(pl.multiple_of(s * units, units), units)]
        return [pltpu.make_async_copy(g_dn.at[s], place, saves_row.at[1, j % n])]

    saves = []

    def save(copies):
        for copy in copies:
            copy.start()
        saves.extend(copies)

    ring = [0] + [j for h in range(1, hops) for j in (-h, h)] + [hops]
    for j in ring:
        save(save_down(j))
    e_in.step(last, e_ring, e_finish)
    x_f = x[...].astype(F32)
    inv_one = lax.rsqrt(jnp.mean(x_f * x_f, axis=-1, keepdims=True) + NORM_EPS)
    norm_one = x_f * inv_one
    e_val = o_input[...]
    o_input[...] = ghid[...] + inv_one * (
        e_val - norm_one * jnp.mean(e_val * norm_one, axis=-1, keepdims=True)
    )
    out_own.wait()
    for dp in range(1, planes):
        ref = r_out.at[lax.rem(at.p - dp + planes, planes)]
        rdma(ref, ref, z_os.at[dp], z_or.at[dp], (at.s, at.f)).wait_recv()
    acc = r_out[0].astype(F32)
    for p in range(1, planes):
        acc = acc + r_out[p].astype(F32)
    g_out[at.s] = acc.astype(BF)
    ag_out = Gather(at, row_half(g_out), (a_ou_s, a_ou_r))
    ag_out.start()
    save(save_out(0))
    save(save_gu(0))
    z_collect(r_qkv, z_qs, z_qr, qkv_own)
    for c in range(sib):
        g_qkv[at.s, c] = plane_total(r_qkv, c)
    ag_qkv = Gather(at, row_half(g_qkv), (a_qk_s, a_qk_r))
    ag_qkv.start()
    save(save_qkv(0))
    for h in range(1, hops + 1):
        for ag, put in ((ag_gu, save_gu), (ag_out, save_out), (ag_qkv, save_qkv)):
            ag.hop(h)
            for j in (-h, h) if h < hops else (h,):
                save(put(j))
    e_in.drain()
    s_out.drain()
    for ag in (ag_dn, ag_gu, ag_qkv, ag_out):
        ag.drain()
    for dp, dc in gu_pairs():
        gu_from(dp, dc)(lambda: gu_send(dp, dc).wait_send())
    if near:
        at_ends(lambda: toward_middle().wait_send())
        for dc in range(sib):
            at_middle(lambda: gu_send_sum(dc).wait_send())
    for copy in sent:
        copy.wait_send()
    for copy in saves:
        copy.wait()


def backward_call(dims, aligned, x, tables, widen, widen_att, lse, n1, qkv, gh, att, ghid, wqp, sgu, rgu, sdn):
    n, sib, planes = dims
    length, width = x.shape
    rows = gh.shape[4]
    owners = planes * sib
    units = sdn.shape[1]
    part_cols = width // n
    seq_len = n * length
    head_cols = (GROUP + 2) * HEAD_DIM
    vm, hb = pl.BlockSpec(memory_space=pltpu.VMEM), pl.BlockSpec(memory_space=pl.ANY)
    sds = jax.ShapeDtypeStruct
    g_shapes = [
        (n, sib, rows, head_cols), (n, sib, rows, sgu.shape[1]), (n, units, width),
        (n, rows, part_cols),
    ]
    o_shapes = g_shapes
    if aligned:
        o_shapes = [
            (rows, n * sib * head_cols), (rows, n * sib * sgu.shape[1]), None, (rows, width)
        ]
    o_shapes = [*o_shapes[:2], (n * units, width), o_shapes[3]]
    outs = [(sds((length, width), F32), vm)] + [(sds(shape, BF), hb) for shape in o_shapes]
    dma = pltpu.SemaphoreType.DMA
    scratch = [
        pltpu.VMEM(qkv.shape, BF), pltpu.VMEM(gh.shape, BF), pltpu.VMEM(att.shape, BF),
        pltpu.VMEM(wqp.shape, BF), pltpu.VMEM(sdn.shape, BF), pltpu.VMEM(qkv.shape, BF),
        pltpu.VMEM((seq_len, 128), F32), pltpu.VMEM((seq_len, 128), F32),
        pltpu.VMEM((2, *n1.shape[:3], 384), BF), pltpu.VMEM((width, head_cols), BF),
        pltpu.VMEM((planes, rows, part_cols), BF), pltpu.VMEM((n, length, part_cols), BF),
        pltpu.VMEM((owners, rows, sgu.shape[1]), BF), pltpu.VMEM((owners, rows, head_cols), BF),
        pltpu.VMEM((planes, rows, part_cols), BF),
        pltpu.VMEM(g_shapes[1], BF), pltpu.VMEM(g_shapes[0], BF), pltpu.VMEM(g_shapes[2], BF),
        pltpu.VMEM(g_shapes[3], BF),
        *Scatter.scratch(n, (length, max(width, planes * part_cols))),
        *Scatter.scratch(n, (length, width)),
        pltpu.VMEM((2, sib * rows, sgu.shape[1]), BF), dma((1,)), dma((1,)),
        dma((13,)), dma((planes, sib)), dma((n, 2 * owners)), dma((n, sib)), dma((2, n)),
        dma((planes, sib)), dma((planes, sib)), dma((planes, sib)),
        dma((planes, sib)), dma((planes,)), dma((planes,)),
        *Scatter.sems(n), *Scatter.sems(n),
        *Gather.scratch(n, False), *Gather.scratch(n, False), *Gather.scratch(n, False),
        *Gather.scratch(n, False),
    ]
    return pl.pallas_call(
        functools.partial(backward_kernel, dims),
        out_shape=[o[0] for o in outs],
        out_specs=[o[1] for o in outs],
        in_specs=[vm] * 7 + [hb] * 4 + [vm] + [hb] * 4,
        scratch_shapes=scratch,
        compiler_params=pltpu.CompilerParams(
            collective_id=1, has_side_effects=True, vmem_limit_bytes=VMEM_LIMIT
        ),
    )(x, *tables, widen, widen_att, lse, n1, qkv, gh, att, ghid, wqp, sgu, rgu, sdn)


def adamw(weight, first, second, grad, rate, decay):
    first_new = BETA_ONE * first + (1.0 - BETA_ONE) * grad
    second_new = BETA_TWO * second + (1.0 - BETA_TWO) * grad * grad
    first_hat = first_new / (1.0 - BETA_ONE**ADAM_STEP)
    second_hat = second_new / (1.0 - BETA_TWO**ADAM_STEP)
    weight_new = weight - rate * (first_hat / (jnp.sqrt(second_hat) + ADAM_EPS) + decay * weight)
    return (weight_new, first_new, second_new)


def to_bf16(value):
    return lax.reduce_precision(value, exponent_bits=8, mantissa_bits=7)


def rope_arrays(seq_len):
    half = HEAD_DIM // 2
    frequencies = (ROPE_BASE ** (-(2.0 * np.arange(half)) / HEAD_DIM)).astype(np.float32)
    angles = np.arange(seq_len, dtype=np.float32)[:, None] * frequencies[None, :]
    cos, sin = np.cos(angles), np.sin(angles)
    pad = np.zeros((seq_len, 128 - HEAD_DIM), np.float32)
    none = np.zeros_like(sin)
    return tuple(
        np.concatenate(columns, axis=1).astype(np.float32)
        for columns in ([cos, cos, pad], [-sin, none, pad], [none, sin, pad])
    )


def widening(heads):
    row = np.arange(heads * HEAD_DIM)[:, None]
    col = np.arange(heads * 128)[None, :]
    return (col == row // HEAD_DIM * 128 + row % HEAD_DIM).astype(ml_dtypes.bfloat16)


def make(n_seq, n_fsdp):
    sib = KV_HEADS // n_seq
    planes = n_fsdp // sib

    def on_device(
        inputs, cotangent, qkv_weight, out_weight, gate_up_weight, down_weight, norm_gains,
        qkv_first, qkv_second, out_first, out_second, gate_up_first, gate_up_second,
        down_first, down_second, gain_first, gain_second,
    ):
        s_idx = lax.axis_index("seq")
        _, length, width = inputs.shape
        seq_len = length * n_seq
        rows = qkv_weight.shape[0]
        head_cols = (GROUP + 2) * HEAD_DIM
        ff_rows = down_weight.shape[0]
        units = ff_rows // n_seq
        hidden_units = ff_rows * n_fsdp
        part_cols = width // n_seq
        aligned = units % 128 == 0 and part_cols % 128 == 0 and sib == 2
        aligned = aligned and rows + units // 2 <= length
        gains = to_bf16(norm_gains)
        gain_cols = gains.T

        if aligned:
            pieces = (qkv_weight, gate_up_weight, down_weight, out_weight)
        else:
            wq_s = lax.dynamic_slice_in_dim(
                qkv_weight, s_idx * sib * head_cols, sib * head_cols, 1
            )
            wq_s = (wq_s * gains[0][:, None]).astype(BF).reshape(rows, sib, head_cols)
            gu_s = gate_up_weight.reshape(rows, 2, planes, sib, n_seq, units)
            gu_s = lax.dynamic_index_in_dim(gu_s, s_idx, 4, keepdims=False)
            gu_s = (gu_s * gains[1][:, None, None, None, None]).astype(BF)
            gu_s = gu_s.transpose(3, 0, 1, 2, 4).reshape(1, sib, rows, 2 * planes * units)
            dn_s = lax.dynamic_slice_in_dim(down_weight, s_idx * units, units, 0).astype(BF)
            wo_s = lax.dynamic_slice_in_dim(out_weight, s_idx * part_cols, part_cols, 1).astype(BF)
            pieces = (wq_s.transpose(1, 0, 2), gu_s, dn_s, wo_s)
        tables = tuple(jnp.asarray(table) for table in rope_arrays(seq_len))
        widen = jnp.asarray(widening(GROUP + 2))
        widen_att = jnp.asarray(widening(rows // HEAD_DIM))

        n_one, qkv, lse, gh, att, block_out, grad_hidden, w_qkv, s_gu, r_gu, s_down = forward_call(
            (n_seq, sib, planes), (rows, units), inputs[0], cotangent[0], tables, widen, widen_att,
            gain_cols, *pieces,
        )
        input_grad, g_qkv, g_gu, g_down, g_out = backward_call(
            (n_seq, sib, planes), aligned, inputs[0], tables, widen, widen_att, lse, n_one, qkv, gh,
            att, grad_hidden, w_qkv, s_gu, r_gu, s_down,
        )
        block_out, input_grad = block_out[None], input_grad[None]
        if not aligned:
            g_qkv = g_qkv.transpose(2, 0, 1, 3).reshape(rows, n_seq * sib * head_cols)
            g_gu = g_gu.reshape(n_seq, sib, rows, 2, planes, units).transpose(2, 3, 4, 1, 0, 5)
            g_gu = g_gu.reshape(rows, 2 * hidden_units)
            g_out = g_out.transpose(1, 0, 2).reshape(rows, width)
        g_qkv, g_gu, g_down, g_out = (g.astype(F32) for g in (g_qkv, g_gu, g_down, g_out))
        gain_grad = jnp.stack(
            [
                jnp.sum(g_qkv * to_bf16(qkv_weight), axis=1),
                jnp.sum(g_gu * to_bf16(gate_up_weight), axis=1),
            ]
        )
        g_qkv = g_qkv * gains[0][:, None]
        g_gu = g_gu * gains[1][:, None]
        qkv_new = adamw(qkv_weight, qkv_first, qkv_second, g_qkv, RATE_QKV, WEIGHT_DECAY)
        out_new = adamw(out_weight, out_first, out_second, g_out, RATE_OUT, WEIGHT_DECAY)
        gu_new = adamw(
            gate_up_weight, gate_up_first, gate_up_second, g_gu, RATE_GATE_UP, WEIGHT_DECAY
        )
        down_new = adamw(
            down_weight, down_first, down_second, g_down, RATE_DOWN, WEIGHT_DECAY
        )
        gains_new = adamw(norm_gains, gain_first, gain_second, gain_grad, RATE_GAINS, 0.0)
        return (block_out, input_grad, *qkv_new, *out_new, *gu_new, *down_new, *gains_new)

    return on_device


def solution(mesh):
    tokens = P("fsdp", "seq", None)
    weight = P("fsdp", None)
    gain = P(None, "fsdp")
    in_specs = (tokens, tokens, weight, weight, weight, weight, gain) + (weight,) * 8 + (gain,) * 2
    out_specs = (tokens, tokens) + (weight,) * 12 + (gain,) * 3
    return jax.shard_map(
        make(mesh.shape["seq"], mesh.shape["fsdp"]),
        mesh=mesh, in_specs=in_specs, out_specs=out_specs, check_vma=False,
    )
```

```python
import functools

import jax
import jax.numpy as jnp
import ml_dtypes
import numpy as np
from jax import lax
from jax.experimental import pallas as pl
from jax.experimental.pallas import tpu as pltpu
from jax.sharding import PartitionSpec as P

HEAD_DIM = 96
KV_HEADS = 8
ADAM_STEP = 10
GROUP = 2

NORM_EPS = 1e-05
ROPE_BASE = 100000.0
BETA_ONE = 0.9
BETA_TWO = 0.95
ADAM_EPS = 1e-08
WEIGHT_DECAY = 0.1
RATE_QKV = 0.07
RATE_OUT = 0.8
RATE_GATE_UP = 0.07
RATE_DOWN = 0.045
RATE_GAINS = 0.6
BF = jnp.bfloat16
F32 = jnp.float32
VMEM_LIMIT = 62 * 1024 * 1024
BACK_LIMIT = 42 * 1024 * 1024


MESH = pl.DeviceIdType.MESH


def rdma(src, dst, ssem, rsem, dev):
    return pltpu.make_async_remote_copy(
        src_ref=src, dst_ref=dst, send_sem=ssem, recv_sem=rsem, device_id=dev, device_id_type=MESH
    )


class Place:
    def __init__(self, n, sib, planes):
        self.n, self.sib, self.planes = n, sib, planes
        self.s = lax.axis_index("seq")
        self.f = lax.axis_index("fsdp")
        self.c = lax.rem(self.f, sib)
        self.p = lax.div(self.f, sib)
        a, b = lax.div(self.s, 2), lax.rem(self.s, 2)
        self.r = a * (1 - b) + (n - 1 - a) * b

    def seq_at(self, j):
        if j == 0:
            return self.s
        n = self.n
        q = lax.rem(self.r + (j + n), n)
        t = lax.div(q, n // 2)
        return (1 - t) * 2 * q + t * (2 * (n - 1 - q) + 1)

    def dev(self, s, c):
        return (s, self.p * self.sib + c)

    def col(self, dp, dc):
        return lax.rem(self.p + dp, self.planes) * self.sib + lax.rem(self.c + dc, self.sib)

    def barrier(self):
        sem = pltpu.get_barrier_semaphore()
        group = self.n * self.sib
        tau = self.s * self.sib + self.c
        for j in range(1, group):
            t = lax.rem(tau + j, group)
            pl.semaphore_signal(
                sem, inc=1, device_id=self.dev(lax.div(t, self.sib), lax.rem(t, self.sib)),
                device_id_type=MESH,
            )
        for dp in range(1, self.planes):
            for dc in range(self.sib):
                pl.semaphore_signal(
                    sem, inc=1, device_id=(self.s, self.col(dp, dc)), device_id_type=MESH
                )
        pl.semaphore_wait(sem, group - 1 + (self.planes - 1) * self.sib)


class Gather:
    def __init__(self, at, part, sems):
        self.at, self.part = at, part
        self.ring_s, self.ring_r = sems[:2]
        self.share = at.sib > 1 and len(sems) > 2
        if self.share:
            self.sib_s, self.sib_r = sems[2:]
        self.sent = []

    @staticmethod
    def scratch(n, share=True):
        d = pltpu.SemaphoreType.DMA
        ring = [d((2, n // 2, 2)), d((2, n // 2, 2))]
        return ring + [d((n, 2)), d((n, 2))] if share else ring

    def _send(self, copy):
        copy.start()
        self.sent.append(copy)

    def _ring(self, way, hop, half):
        at = self.at
        src = self.part(at.c, at.seq_at(-(hop - 1) if way == 0 else hop - 1), half)
        to = at.dev(at.seq_at(1 if way == 0 else -1), at.c)
        self._send(
            rdma(src, src, self.ring_s.at[way, hop - 1, half], self.ring_r.at[way, hop - 1, half], to)
        )

    def _sib(self, j, half):
        at = self.at
        if self.share:
            src = self.part(at.c, at.seq_at(j), half)
            slot = j % at.n
            self._send(
                rdma(src, src, self.sib_s.at[slot, half], self.sib_r.at[slot, half],
                     at.dev(at.s, 1 - at.c))
            )

    def start(self):
        self._ring(0, 1, 0)
        self._ring(1, 1, 1)
        self._ring(0, 1, 1)
        self._ring(1, 1, 0)
        self._sib(0, 0)
        self._sib(0, 1)

    def _arrive(self, way, hop, half):
        at = self.at
        j = -hop if way == 0 else hop
        ref = self.part(at.c, at.seq_at(j), half)
        rdma(ref, ref, self.ring_s.at[way, hop - 1, half], self.ring_r.at[way, hop - 1, half],
             at.dev(at.s, at.c)).wait_recv()
        last = at.n // 2
        if hop + 1 < last or (hop + 1 == last and half == way):
            self._ring(way, hop + 1, half)
        if hop == last:
            j = last
        self._sib(j, half)

    def hop(self, hop):
        self.hop_first(hop)
        self.hop_second(hop)

    def hop_first(self, hop):
        self._arrive(0, hop, 0)
        self._arrive(1, hop, 1)

    def hop_second(self, hop):
        if hop < self.at.n // 2:
            self._arrive(0, hop, 1)
            self._arrive(1, hop, 0)

    def sib_wait(self, j):
        at = self.at
        if self.share:
            for half in range(2):
                ref = self.part(1 - at.c, at.seq_at(j), half)
                slot = j % at.n
                rdma(ref, ref, self.sib_s.at[slot, half], self.sib_r.at[slot, half],
                     at.dev(at.s, at.c)).wait_recv()

    def stages(self):
        last = self.at.n // 2
        yield 0, [0]
        for h in range(1, last):
            yield h, [-h, h]
        yield last, [last]

    def wait_stage(self, h, offsets):
        if h:
            self.hop(h)
        for j in offsets:
            self.sib_wait(j)

    def drain(self):
        for copy in self.sent:
            copy.wait_send()


class Move:
    def __init__(self, at, src, dst, sems, every_core=True):
        self.at, self.src, self.dst = at, src, dst
        self.ssem, self.rsem, self.hop, self.own = sems
        self.cores = at.sib if every_core else 1
        self.relay = at.planes == 4

    @staticmethod
    def sems(planes, sib):
        d = pltpu.SemaphoreType.DMA
        return [d((planes, sib)), d((planes, sib)), d((sib,)), d((1,))]

    def _pairs(self):
        for dp in [2, 1, 3] if self.relay else range(1, self.at.planes):
            for dc in range(self.cores):
                yield dp, dc
        for dc in range(1, self.cores):
            yield 0, dc

    def _direct(self, dp, body):
        if self.relay and dp in (1, 3):
            pl.when(self.at.p != (3 if dp == 1 else 0))(body)
        else:
            body()

    def _send(self, dp, dc):
        at = self.at
        return rdma(self.src(lax.rem(at.c + dc, at.sib)), self.dst(at.f), self.ssem.at[dp, dc],
                    self.rsem.at[dp, dc], (at.s, at.col(dp, dc)))

    def _local(self):
        return pltpu.make_async_copy(self.src(self.at.c), self.dst(self.at.f), self.own.at[0])

    def start(self):
        self.start_far()
        self.start_near()

    def start_far(self):
        for dp, dc in self._pairs():
            if self.relay and dp == 2:
                self._send(dp, dc).start()

    def start_near(self):
        self._local().start()
        for dp, dc in self._pairs():
            if not (self.relay and dp == 2):
                self._direct(dp, lambda: self._send(dp, dc).start())

    def _got(self, dp, dc):
        at = self.at
        source = lax.rem(at.p - dp + at.planes, at.planes) * at.sib + lax.rem(
            at.c - dc + at.sib, at.sib
        )
        ref = self.dst(source)
        rdma(ref, ref, self.ssem.at[dp, dc], self.rsem.at[dp, dc], (at.s, at.f)).wait_recv()
        return ref

    def pass_on(self):
        at = self.at
        if not self.relay:
            return
        for dp, dc in self._pairs():
            if dp == 2:
                ref = self._got(dp, dc)
                for here, to, slot in ((2, 3, 3), (1, 0, 1)):
                    @pl.when(at.p == here)
                    def _():
                        rdma(ref, ref, self.hop.at[dc], self.rsem.at[slot, dc],
                             (at.s, to * at.sib + at.c)).start()

    def wait(self):
        for dp, dc in self._pairs():
            if not (self.relay and dp == 2):
                self._got(dp, dc)
        self._local().wait()

    def drain(self):
        at = self.at
        for dp, dc in self._pairs():
            self._direct(dp, lambda: self._send(dp, dc).wait_send())
            if self.relay and dp == 2:
                ref = self.dst(at.f)

                @pl.when(jnp.logical_or(at.p == 1, at.p == 2))
                def _():
                    rdma(ref, ref, self.hop.at[dc], self.rsem.at[0, dc], (at.s, at.f)).wait_send()


class Scatter:
    def __init__(self, at, bufs, sems, rows, cols):
        self.at, self.rows, self.cols = at, rows, pl.ds(0, cols)
        self.stage, self.sib_in, self.out, self.inn = bufs
        self.sib_s, self.sib_r, self.ring_s, self.ring_r = sems
        self.sent, self.handed = [], []

    @staticmethod
    def scratch(n, shape):
        return [
            pltpu.VMEM((2, *shape), BF), pltpu.VMEM((n, *shape), BF),
            pltpu.VMEM((2, n // 2, *shape), BF), pltpu.VMEM((2, n // 2, *shape), BF),
        ]

    @staticmethod
    def views(stage, sib_in, out, inn):
        return (
            lambda k: stage.at[k], lambda k: sib_in.at[k],
            lambda w, k: out.at[w, k], lambda w, k: inn.at[w, k],
        )

    @staticmethod
    def sems(n):
        d = pltpu.SemaphoreType.DMA
        return [d((n,)), d((n,)), d((2, n // 2)), d((2, n // 2))]

    def offsets(self):
        last = self.at.n // 2
        order = [last]
        for h in range(last - 1, 0, -1):
            order += [h, -h]
        return order + [0]

    def to_sibling(self, k, produce):
        at = self.at
        if at.sib == 1:
            return
        if k >= 2:
            self.handed[k - 2].wait_send()
        view = self.stage(k % 2).at[pl.ds(0, self.rows), self.cols]
        produce(1 - at.c, at.seq_at(self.offsets()[k]), view)
        copy = rdma(view, self.sib_in(k).at[pl.ds(0, self.rows), self.cols],
                    self.sib_s.at[k], self.sib_r.at[k], at.dev(at.s, 1 - at.c))
        copy.start()
        self.handed.append(copy)

    def open(self, stage, ring, finish):
        self.to_sibling(0, stage)
        self.step(0, ring, finish)
        for k in range(1, len(self.offsets())):
            self.to_sibling(k, stage)

    def _send(self, way, k, rows):
        at = self.at
        src = self.out(way, k).at[rows, self.cols]
        copy = rdma(src, self.inn(way, k).at[rows, self.cols], self.ring_s.at[way, k], self.ring_r.at[way, k],
                    at.dev(at.seq_at(1 if way == 0 else -1), at.c))
        copy.start()
        self.sent.append(copy)

    def _wait(self, way, k, rows):
        ref = self.inn(way, k).at[rows, self.cols]
        at = self.at
        rdma(ref, ref, self.ring_s.at[way, k], self.ring_r.at[way, k],
             at.dev(at.s, at.c)).wait_recv()

    def step(self, k, produce, finish):
        at = self.at
        last = at.n // 2
        length = self.rows
        half = length // 2
        halves = (pl.ds(0, half), pl.ds(half, half))
        whole = pl.ds(0, length)
        j = self.offsets()[k]
        if at.sib > 1:
            ref = self.sib_in(k).at[pl.ds(0, length), self.cols]
            rdma(ref, ref, self.sib_s.at[k], self.sib_r.at[k], at.dev(at.s, at.c)).wait_recv()
        h = abs(j)
        if h == last:
            got = []
        else:
            ways = (0, 1) if h == 0 else ((0,) if j > 0 else (1,))
            rows_in = [halves[w] if h + 1 == last else whole for w in ways]
            got = [(w, rw) for w, rw in zip(ways, rows_in)]
        pending = [True]

        def store(cols, value, k=k, h=h, j=j, got=got, pending=pending):
            if pending[0]:
                for w, rw in got:
                    self._wait(w, h, rw)
                pending[0] = False
            if at.sib > 1:
                value = value + self.sib_in(k)[pl.ds(0, length), cols].astype(F32)
            for w, rw in got:
                if h + 1 == last:
                    add = self.inn(w, h)[pl.ds(w * half, half), cols].astype(F32)
                    if w == 0:
                        value = jnp.concatenate([value[:half] + add, value[half:]], axis=0)
                    else:
                        value = jnp.concatenate([value[:half], value[half:] + add], axis=0)
                else:
                    value = value + self.inn(w, h)[pl.ds(0, length), cols].astype(F32)
            if h == last:
                low = value.astype(BF)
                self.out(0, h - 1)[pl.ds(0, half), cols] = low[:half]
                self.out(1, h - 1)[pl.ds(half, half), cols] = low[half:]
            elif h:
                self.out(0 if j > 0 else 1, h - 1)[pl.ds(0, length), cols] = value.astype(BF)
            else:
                finish(cols, value)

        produce(at.c, at.seq_at(j), store)
        if h == last:
            self._send(0, h - 1, halves[0])
            self._send(1, h - 1, halves[1])
        elif h:
            self._send(0 if j > 0 else 1, h - 1, whole)

    def drain(self):
        for copy in self.sent + self.handed[-2:]:
            copy.wait_send()


class Credits:
    def __init__(self, at, sem):
        self.at, self.sem = at, sem

    def give(self):
        at = self.at
        if at.sib > 1:
            pl.semaphore_signal(
                self.sem, inc=1, device_id=at.dev(at.s, 1 - at.c), device_id_type=MESH
            )
        for way in (1, -1):
            pl.semaphore_signal(
                self.sem, inc=1, device_id=at.dev(at.seq_at(way), at.c), device_id_type=MESH
            )

    def take(self):
        pl.semaphore_wait(self.sem, 3 if self.at.sib > 1 else 2)


def nt(a, b):
    return lax.dot_general(a, b, (((1,), (1,)), ((), ())), preferred_element_type=F32)


def tn(a, b):
    return lax.dot_general(a, b, (((0,), (0,)), ((), ())), preferred_element_type=F32)


def nn(a, b):
    return lax.dot_general(a, b, (((1,), (0,)), ((), ())), preferred_element_type=F32)


def rope(value, cos, front, back):
    return value * cos + pltpu.roll(value, 80, 1) * front + pltpu.roll(value, 48, 1) * back


def forward_kernel(
    dims,
    x, cot, cos, front, back, widen, widen_att, gain_cols, wq_s, gu_s, dn_s, wo_s,
    o_n1, o_qkv, o_lse, o_gh, o_att, o_block, o_ghid, o_wq, o_sgu, o_rgu, o_sdn,
    hid,
    nbuf, cbuf, qkv, wq, wqp, wo, gu, dn, act, ggu, att_out, att_in, gh_in, stg, sgu_t,
    wo_f, wq_b, gu_b, dn_b, wo_b,
    sc_stage, sc_in, sc_out, sc_inn,
    zw_a, zw_b, zw_c, zw_d, zo_a, zo_b, zo_c, zo_d, zd_a, zd_b, zd_c, zd_d,
    zg_a, zg_b, zg_c, zg_d, z_ss, z_sr, local, loads,
    n1_a, n1_b, n1_c, n1_d, ct_a, ct_b, ct_c, ct_d, n2_a, n2_b, n2_c, n2_d, wo_ga, wo_gb, wo_gc, wo_gd,
    rs_a, rs_b, rs_c, rs_d, ds_a, ds_b, ds_c, ds_d, at_s, at_r, gh_s, gh_r, near_s, near_r, free,
):
    n, sib, planes = dims
    at = Place(n, sib, planes)
    length, width = x.shape
    seq_len = n * length
    raw = len(wq_s.shape) == 2
    _, rows, head_cols = wq_b.shape
    owners = planes * sib
    chunks = GROUP * HEAD_DIM // rows
    units = dn_b.shape[0]
    local_units = planes * units
    parts = 2 if units % 128 == 0 else 1
    wide = local_units // parts
    part_cols = wo_b.shape[1]
    heads_per = rows // HEAD_DIM
    half_len = length // 2
    tau = at.s * sib + at.c
    scale = HEAD_DIM ** (-0.5)
    log2e = 1.4426950408889634
    sent = []

    def token_part(ref):
        return lambda c, s, h: ref.at[c, s, pl.ds(h * half_len, half_len)]

    def owner_rows(f):
        return pl.ds(pl.multiple_of(f * rows, rows), rows)

    if raw:
        gu_f = (o_ghid, hid)

        def cut(ref, k, lo, size, dst):
            return pltpu.make_async_copy(
                ref.at[:, pl.ds(pl.multiple_of(lo, 128), size)], dst, loads.at[k]
            )

        def wq_f(c):
            return gu_f[c].at[pl.ds(0, rows), pl.ds(2 * local_units, head_cols)]

        in_wq = [
            cut(wq_s, 3 + 2 * owners + c, (at.s * sib + c) * head_cols, head_cols, wq_f(c))
            for c in range(sib)
        ]
        in_wo = cut(wo_s, 1, at.s * part_cols, part_cols, wo_f)
        half_units = units // 2

        def dn_f(h):
            return gu_f[h].at[pl.ds(rows, half_units)]

        in_dn = [
            pltpu.make_async_copy(
                dn_s.at[pl.ds(pl.multiple_of(at.s * units + h * half_units, half_units), half_units)],
                dn_f(h), loads.at[2 * h],
            )
            for h in range(2)
        ]
        in_gu = []

        def gu_lane(p, g):
            return p * units // wide * 2 * wide + g * wide + p * units % wide

        for c in range(sib):
            for p in range(planes):
                for g in range(2):
                    lo = (g * owners + p * sib + c) * (n * units) + at.s * units
                    k = (c * planes + p) * 2 + g
                    in_gu.append(
                        cut(gu_s, 3 + k, lo, units,
                            gu_f[c].at[pl.ds(0, rows), pl.ds(gu_lane(p, g), units)])
                    )
        for copy in (*in_wq, in_wo, *in_dn, *in_gu):
            copy.start()
        wq_x, gu_x, dn_x, wo_x = wq_b, gu_b, dn_b, wo_b
    else:
        wq_x, gu_x, dn_x, wo_x = wq_s, gu_s, dn_s, wo_s

    move_wq = Move(at, lambda c: wq_x.at[c], lambda f: wq.at[owner_rows(f)], (zw_a, zw_b, zw_c, zw_d))
    move_wo = Move(
        at, lambda c: wo_x, lambda f: wo.at[lax.rem(f, sib), at.s, lax.div(f, sib)],
        (zo_a, zo_b, zo_c, zo_d), False,
    )
    move_dn = Move(
        at, lambda c: dn_x,
        lambda f: dn.at[pl.ds(pl.multiple_of(lax.div(f, sib) * units, units), units)],
        (zd_a, zd_b, zd_c, zd_d), False,
    )

    def gu_move(k):
        return Move(
            at, lambda c: gu_x.at[k, c], lambda f: gu.at[k, owner_rows(f)],
            (zg_a.at[k], zg_b.at[k], zg_c.at[k], zg_d.at[k]),
        )

    move_gu = [gu_move(k) for k in range(parts)]

    x_f = x[...].astype(F32)
    inv_one = lax.rsqrt(jnp.mean(x_f * x_f, axis=-1, keepdims=True) + NORM_EPS)
    nbuf[at.c, at.s] = (x_f * inv_one).astype(BF)
    cbuf[at.c, at.s] = cot[...]
    n_one = Gather(at, token_part(nbuf), (n1_a, n1_b, n1_c, n1_d))
    at.barrier()
    n_one.start()
    if raw:
        g_one = gain_cols[:, 0:1]
        for c in range(sib):
            in_wq[c].wait()
            wq_b[c] = (wq_f(c)[...] * g_one).astype(BF)
        in_wo.wait()
        wo_b[...] = wo_f[...].astype(BF)
    move_wq.start()
    if raw:
        for h in range(2):
            in_dn[h].wait()
            dn_b[h * half_units : (h + 1) * half_units] = dn_f(h)[...].astype(BF)
        for copy in in_gu:
            copy.wait()
        g_two = gain_cols[:, 1:2]
        for c in range(sib):
            for k in range(parts):
                lanes = slice(k * 2 * wide, (k + 1) * 2 * wide)
                gu_b[k, c] = (gu_f[c][0:rows, lanes] * g_two).astype(BF)
    n_stages = list(n_one.stages())
    n_one.hop_first(1)
    move_wq.pass_on()
    move_wo.start()
    n_one.hop_second(1)
    for h, _ in n_stages[2:-1]:
        n_one.hop(h)
    move_wq.wait()
    move_gu[0].start_far()

    @pl.loop(0, width // 256)
    def _(t):
        here = pl.ds(pl.multiple_of(t * 256, 256), 256)
        wqp[here] = nn(wq[here], widen[...]).astype(BF)

    save_wq = pltpu.make_async_copy(wqp, o_wq, local.at[2])
    save_wq.start()

    def project(c, s):
        y = nn(nbuf[c, s], wqp[...]).astype(BF)
        here = pl.ds(pl.multiple_of(s * length, length), length)
        cs, fr, bk = cos[here], front[here], back[here]
        for k in range(3):
            lanes = slice(128 * k, 128 * k + 128)
            qkv[c, here, lanes] = rope(y[:, lanes].astype(F32), cs, fr, bk).astype(BF)
        qkv[c, here, 384:512] = y[:, 384:512]

    for h, offsets in n_stages:
        if h == n // 2:
            n_one.hop(h)
        for j in offsets:
            n_one.sib_wait(j)
            s_j = at.seq_at(j)

            @pl.loop(0, sib)
            def _(c):
                project(c, s_j)

    cot_gather = Gather(at, token_part(cbuf), (ct_a, ct_b, ct_c, ct_d))
    save_n1 = pltpu.make_async_copy(nbuf, o_n1, local.at[3])
    save_n1.start()
    save_qkv = pltpu.make_async_copy(qkv, o_qkv, local.at[4])
    save_qkv.start()

    tri = lax.broadcasted_iota(jnp.int32, (length, length), 0) >= lax.broadcasted_iota(
        jnp.int32, (length, length), 1
    )

    def spot(k, b, i):
        return (k * sib + b) * n + i

    def attend(i):
        @pl.loop(0, sib)
        def _(b):
            past = i * length
            here = slice(past, past + length)
            outs = []
            for h in range(GROUP):
                q = qkv[b, here, 128 * h : 128 * h + 128]
                d = jnp.where(tri, nt(q, qkv[b, here, 256:384]) * (scale * log2e), -1e30)
                m = jnp.max(d, axis=1, keepdims=True)
                if i:
                    e = nt(q, qkv[b, 0:past, 256:384]) * (scale * log2e)
                    m = jnp.maximum(m, jnp.max(e, axis=1, keepdims=True))
                d = jnp.exp2(d - m)
                total = jnp.sum(d, axis=1, keepdims=True)
                o = nn(d.astype(BF), qkv[b, here, 384:512])
                if i:
                    e = jnp.exp2(e - m)
                    total = total + jnp.sum(e, axis=1, keepdims=True)
                    o = o + nn(e.astype(BF), qkv[b, 0:past, 384:512])
                outs.append((o / total).astype(BF))
                lse = jnp.broadcast_to(m + jnp.log2(total), (length, 128))
                o_lse[b, h, i] = lse.T[0:8]
            for k in range(chunks):
                pair = jnp.concatenate(outs[k * heads_per : (k + 1) * heads_per], axis=1)
                att_out[spot(k, b, i)] = nt(pair, widen_att[...]).astype(BF)

    def send_attended(i):
        for k in range(chunks):
            for b in range(sib):
                mine = jnp.logical_and(at.s == i, at.c == b)

                @pl.when(mine)
                def _():
                    att_in[tau * chunks + k] = att_out[spot(k, b, i)]

                @pl.when(jnp.logical_not(mine))
                def _():
                    rdma(att_out.at[spot(k, b, i)], att_in.at[tau * chunks + k], at_s.at[k, b, i],
                         at_r.at[tau * chunks + k], at.dev(i, b)).start()

    wo_gather = Gather(
        at, lambda c, s, h: wo.at[c, s, pl.ds(h * (planes // 2), planes // 2)],
        (wo_ga, wo_gb, wo_gc, wo_gd),
    )
    attend(n - 1)
    save_n1.wait()
    n_one.drain()
    send_attended(n - 1)
    move_wo.pass_on()
    move_wo.wait()
    wo_gather.start()
    move_gu[0].start_near()
    for move in move_gu[1:]:
        move.start_far()
    for i in range(n - 2, -1, -1):
        attend(i)
        send_attended(i)
    wo_hops = list(wo_gather.stages())
    for h, _ in wo_hops[1:-1]:
        wo_gather.hop(h)
    cot_gather.start()
    wo_gather.hop(n // 2)
    for _, offsets in wo_hops:
        for j in offsets:
            wo_gather.sib_wait(j)
    wo_gather.drain()
    save_qkv.wait()
    save_wq.wait()

    group = n * sib
    for j in range(1, group):
        t = lax.rem(tau + j, group)
        for k in range(chunks):
            ref = att_in.at[t * chunks + k]
            rdma(ref, ref, at_s.at[0, 0, 0], at_r.at[t * chunks + k], at.dev(at.s, at.c)).wait_recv()
    for k in range(chunks):
        for i in range(n):
            for b in range(sib):
                @pl.when(jnp.logical_not(jnp.logical_and(at.s == i, at.c == b)))
                def _():
                    rdma(att_out.at[spot(k, b, i)], att_out.at[spot(k, b, i)], at_s.at[k, b, i],
                         at_r.at[0], at.dev(at.s, at.c)).wait_send()
    save_att = pltpu.make_async_copy(att_in, o_att, local.at[3])
    save_att.start()

    x_f = x[...].astype(F32)
    for s in range(n):
        cols = slice(s * part_cols, (s + 1) * part_cols)
        acc = x_f[:, cols]
        for p in range(planes):
            for c in range(sib):
                acc = acc + nn(att_in[p * sib + c], wo[c, s, p])
        hid[:, cols] = acc
    hidden = hid[...]
    inv_mid = lax.rsqrt(jnp.mean(hidden * hidden, axis=-1, keepdims=True) + NORM_EPS)
    nbuf[at.c, at.s] = (hidden * inv_mid).astype(BF)
    n_two = Gather(at, token_part(nbuf), (n2_a, n2_b, n2_c, n2_d))
    n_two.start()

    stages = list(n_two.stages())
    move_dn.start_far()
    for move in move_gu[1:]:
        move.start_near()
    move_gu[0].pass_on()
    for h, _ in stages[1:-1]:
        cot_gather.hop(h)
    for move in move_gu[1:]:
        move.pass_on()
    move_dn.start_near()
    for h, _ in stages[1:-1]:
        n_two.hop(h)
    move_dn.pass_on()

    def gate_pass(k, c, s):
        y = nn(nbuf[c, s], gu[k])
        gate, up = y[:, :wide], y[:, wide:]
        act[c, s, :, k * wide : (k + 1) * wide] = (gate / (1.0 + jnp.exp(-gate)) * up).astype(BF)
        ggu[c, s, :, k * 2 * wide : (k + 1) * 2 * wide] = y.astype(BF)

    def grad_pass(c, s):
        for k in range(parts):
            lo = k * 2 * wide
            gate = ggu[c, s, :, lo : lo + wide].astype(F32)
            up = ggu[c, s, :, lo + wide : lo + 2 * wide].astype(F32)
            grad_act = nt(cbuf[c, s], dn[k * wide : (k + 1) * wide])
            sig = 1.0 / (1.0 + jnp.exp(-gate))
            ggu[c, s, :, lo : lo + wide] = (
                grad_act * up * sig * (1.0 + gate * (1.0 - sig))
            ).astype(BF)
            ggu[c, s, :, lo + wide : lo + 2 * wide] = (grad_act * (gate * sig)).astype(BF)

    def each_block(offsets, body):
        for j in offsets:
            s_j = at.seq_at(j)

            @pl.loop(0, sib)
            def _(c):
                body(c, s_j)

    def rows_wait(offsets):
        for j in offsets:
            n_two.sib_wait(j)
            cot_gather.sib_wait(j)

    early = [j for _, offsets in stages[:-1] for j in offsets]
    late = stages[-1][1]
    rows_wait(early)
    for k in range(parts):
        move_gu[k].wait()
        each_block(early, lambda c, s: gate_pass(k, c, s))
    move_dn.wait()
    each_block(early, grad_pass)
    n_two.hop(n // 2)
    cot_gather.hop(n // 2)
    rows_wait(late)
    for k in range(parts):
        each_block(late, lambda c, s: gate_pass(k, c, s))
    each_block(late, grad_pass)

    scatter = Scatter(
        at, Scatter.views(sc_stage, sc_in, sc_out, sc_inn), (rs_a, rs_b, rs_c, rs_d), length, width
    )
    tile = 512

    def column_tiles():
        return [slice(t * tile, (t + 1) * tile) for t in range(width // tile)]

    def mid_part(c, s, cols):
        acc = nt(ggu[c, s, :, 0 : 2 * wide], gu[0, cols, :])
        for k in range(1, parts):
            acc = acc + nt(ggu[c, s, :, k * 2 * wide : (k + 1) * 2 * wide], gu[k, cols, :])
        return acc

    def to_stage(c, s, ref):
        for cols in column_tiles():
            ref[:, cols] = mid_part(c, s, cols).astype(BF)

    def to_ring(c, s, store):
        for cols in column_tiles():
            store(cols, mid_part(c, s, cols))

    tokens = sib * seq_len
    down_copies = []

    def grad_down():
        cot_all = cbuf[...].reshape(tokens, width)
        down_rows = local_units // 2
        for t in range(2):
            rows_here = slice(t * down_rows, (t + 1) * down_rows)
            lhs = act[:, :, :, rows_here].reshape(tokens, down_rows)
            stg[rows_here] = tn(lhs, cot_all).astype(BF)
        own = pltpu.make_async_copy(
            stg.at[pl.ds(pl.multiple_of(at.p * units, units), units)], o_sdn.at[at.p], local.at[6]
        )
        own.start()
        down_copies.append(own)
        for dp in range(1, planes):
            to = lax.rem(at.p + dp, planes)
            copy = rdma(stg.at[pl.ds(pl.multiple_of(to * units, units), units)], o_sdn.at[at.p],
                        z_ss.at[dp], z_sr.at[dp], (at.s, at.col(dp, 0)))
            copy.start()
            sent.append(copy)

    gu_tile = sgu_t.shape[1]
    gu_steps = width // gu_tile
    near = planes == 4

    def gu_copy(m, slot):
        return pltpu.make_async_copy(
            sgu_t.at[slot], o_sgu.at[pl.ds(m * gu_tile, gu_tile)], local.at[7 + slot]
        )

    def near_send(m, dc):
        to = m * sib + lax.rem(at.c + dc, sib)
        return rdma(o_sgu.at[owner_rows(to)], o_rgu.at[at.f], near_s.at[m, dc],
                    near_r.at[at.p, dc], (at.s, to))

    def if_near(m, body):
        pl.when(jnp.logical_or(at.p == m - 1, at.p == m + 1))(body)

    def leave(m):
        gu_copy(m, m % 2).wait()
        if near:
            for dc in range(sib):
                if_near(m, lambda: near_send(m, dc).start())

    def grad_gu():
        for m in range(gu_steps):
            slot = m % 2
            lhs = nbuf[:, :, :, m * gu_tile : (m + 1) * gu_tile].reshape(tokens, gu_tile)
            sgu_t[slot] = tn(lhs, ggu[...].reshape(tokens, 2 * local_units)).astype(BF)
            gu_copy(m, slot).start()
            if m:
                leave(m - 1)
        leave(gu_steps - 1)

    def finish(cols, value):
        o_ghid[:, cols] = value

    def flat(ref, base):
        return lambda w, k: ref.at[base, w * (n // 2) + k]

    down = Scatter(
        at, (lambda k: cbuf.at[0, k], lambda k: nbuf.at[0, k], flat(cbuf, sib - 1), flat(nbuf, sib - 1)),
        (ds_a, ds_b, ds_c, ds_d), length, width,
    )

    def down_stage(c, s, ref):
        for cols in column_tiles():
            ref[:, cols] = nn(act[c, s], dn[:, cols]).astype(BF)

    def down_ring(c, s, store):
        for cols in column_tiles():
            store(cols, nn(act[c, s], dn[:, cols]))

    def down_finish(cols, value):
        o_block[:, cols] = (hid[:, cols] + value).astype(BF)

    credits = Credits(at, free)
    last = len(scatter.offsets()) - 1
    scatter.open(to_stage, to_ring, finish)
    grad_down()
    for k in range(1, last):
        scatter.step(k, to_ring, finish)
    grad_gu()
    cot_gather.drain()
    n_two.drain()
    credits.give()
    credits.take()
    down.open(down_stage, down_ring, down_finish)
    scatter.step(last, to_ring, finish)
    e_mid = o_ghid[...]
    hidden = hid[...]
    inv_mid = lax.rsqrt(jnp.mean(hidden * hidden, axis=-1, keepdims=True) + NORM_EPS)
    norm_mid = hidden * inv_mid
    o_ghid[...] = cot[...].astype(F32) + inv_mid * (
        e_mid - norm_mid * jnp.mean(e_mid * norm_mid, axis=-1, keepdims=True)
    )
    branch = o_ghid[...].astype(BF)
    for f in range(owners):
        p, c = f // sib, f % sib
        acc = nt(branch[:, :part_cols], wo[c, 0, p])
        for s in range(1, n):
            acc = acc + nt(branch[:, s * part_cols : (s + 1) * part_cols], wo[c, s, p])
        att_out[f] = acc.astype(BF)
        t, k = f // chunks, f % chunks
        mine = tau == t

        @pl.when(mine)
        def _():
            gh_in[k, at.c, at.s] = att_out[f]

        @pl.when(jnp.logical_not(mine))
        def _():
            rdma(att_out.at[f], gh_in.at[k, at.c, at.s], gh_s.at[f], gh_r.at[k, tau],
                 at.dev(t // sib, t % sib)).start()

    for k in range(1, last):
        down.step(k, down_ring, down_finish)
    for j in range(1, group):
        t = lax.rem(tau + j, group)
        for k in range(chunks):
            ref = gh_in.at[k, lax.rem(t, sib), lax.div(t, sib)]
            rdma(ref, ref, gh_s.at[0], gh_r.at[k, t], at.dev(at.s, at.c)).wait_recv()
    save_gh = pltpu.make_async_copy(gh_in, o_gh, local.at[0])
    save_gh.start()
    for f in range(owners):
        @pl.when(jnp.logical_not(tau == f // chunks))
        def _():
            rdma(att_out.at[f], att_out.at[f], gh_s.at[f], gh_r.at[0, 0],
                 at.dev(at.s, at.c)).wait_send()

    down.step(last, down_ring, down_finish)

    for dp in range(1, planes):
        ref = o_sdn.at[lax.rem(at.p - dp + planes, planes)]
        rdma(ref, ref, z_ss.at[dp], z_sr.at[dp], (at.s, at.f)).wait_recv()
    for copy in down_copies:
        copy.wait()
    if near:
        for q in range(planes):
            for dc in range(sib):
                def arrived():
                    ref = o_rgu.at[q * sib + lax.rem(at.c - dc + sib, sib)]
                    rdma(ref, ref, near_s.at[q, dc], near_r.at[q, dc], (at.s, at.f)).wait_recv()
                    near_send(q, dc).wait_send()

                if_near(q, arrived)
    scatter.drain()
    down.drain()
    for move in (move_wq, move_wo, move_dn, *move_gu):
        move.drain()
    for copy in sent:
        copy.wait_send()
    save_att.wait()
    save_gh.wait()


def forward_call(dims, sizes, x, cot, tables, widen, widen_att, gain_cols, wq_s, gu_s, dn_s, wo_s):
    n, sib, planes = dims
    rows, units = sizes
    length, width = x.shape
    part_cols = width // n
    head_cols = (GROUP + 2) * HEAD_DIM
    owners = planes * sib
    chunks = GROUP * HEAD_DIM // rows
    ffl = planes * units
    parts = 2 if units % 128 == 0 else 1
    seq_len = n * length
    vm, hb = pl.BlockSpec(memory_space=pltpu.VMEM), pl.BlockSpec(memory_space=pl.ANY)
    blocks = (sib, n, length, width)
    sds = jax.ShapeDtypeStruct
    outs = [
        (sds(blocks, BF), hb),
        (sds((sib, seq_len, 512), BF), hb),
        (sds((sib, GROUP, n, 8, length), F32), vm),
        (sds((chunks, sib, n, length, rows), BF), hb),
        (sds((owners, length, rows), BF), hb),
        (sds((length, width), BF), vm),
        (sds((length, width), F32), vm),
        (sds((width, 512), BF), hb),
        (sds((width, 2 * ffl), BF), hb),
        (sds((owners, rows, 2 * ffl), BF), hb),
        (sds((planes, units, width), BF), hb),
    ]
    dma = pltpu.SemaphoreType.DMA
    scratch = [
        pltpu.VMEM((length, width), F32),
        pltpu.VMEM(blocks, BF), pltpu.VMEM(blocks, BF), pltpu.VMEM((sib, seq_len, 512), BF),
        pltpu.VMEM((width, head_cols), BF), pltpu.VMEM((width, 512), BF),
        pltpu.VMEM((sib, n, planes, rows, part_cols), BF),
        pltpu.VMEM((parts, width, 2 * ffl // parts), BF), pltpu.VMEM((ffl, width), BF),
        pltpu.VMEM((sib, n, length, ffl), BF), pltpu.VMEM((sib, n, length, 2 * ffl), BF),
        pltpu.VMEM((owners, length, rows), BF), pltpu.VMEM((owners, length, rows), BF),
        pltpu.VMEM((chunks, sib, n, length, rows), BF),
        pltpu.VMEM((ffl, width), BF), pltpu.VMEM((2, 384, 2 * ffl), BF),

        pltpu.VMEM((rows, part_cols), F32),
        pltpu.VMEM((sib, rows, head_cols), BF),
        pltpu.VMEM((parts, sib, rows, 2 * ffl // parts), BF),
        pltpu.VMEM((units, width), BF), pltpu.VMEM((rows, part_cols), BF),
        *Scatter.scratch(n, (length, width)),
        *Move.sems(planes, sib), *Move.sems(planes, sib), *Move.sems(planes, sib),
        dma((parts, planes, sib)), dma((parts, planes, sib)), dma((parts, sib)), dma((parts, 1)),
        dma((planes,)), dma((planes,)), dma((9,)), dma((3 + 2 * owners + sib,)),
        *Gather.scratch(n), *Gather.scratch(n), *Gather.scratch(n), *Gather.scratch(n),
        *Scatter.sems(n), *Scatter.sems(n),
        dma((chunks, sib, n)), dma((owners,)), dma((owners,)), dma((chunks, n * sib)),
        dma((planes, sib)), dma((planes, sib)), pltpu.SemaphoreType.REGULAR,
    ]
    return pl.pallas_call(
        functools.partial(forward_kernel, dims),
        out_shape=[o[0] for o in outs],
        out_specs=[o[1] for o in outs],
        in_specs=[vm] * 8 + [hb] * 4,
        scratch_shapes=scratch,
        compiler_params=pltpu.CompilerParams(
            collective_id=0, has_side_effects=True, vmem_limit_bytes=VMEM_LIMIT
        ),
    )(x, cot, *tables, widen, widen_att, gain_cols, wq_s, gu_s, dn_s, wo_s)


def backward_kernel(
    dims,
    x, cos, front, back, widen, widen_att, lse,
    n1, qkv_h, gh_h, att_h, ghid, wqp_h, sgu, rgu_h, sdn_h,
    o_input, o_gq, o_ggu, o_gdn, o_gout,
    qkv, gh, att, wqp, sdn, gq, gk, gv, n1_t, sq, so, branch,
    r_gu, r_qkv, r_out, g_gu, g_qkv, g_dn, g_out,
    sc_stage, sc_in, sc_out, sc_inn, free,
    via, via_s, via_r, loads, near_l, saves_gu, saves_qkv, saves_row, z_gs, z_gr, z_qs, z_qr, z_os, z_or,
    e_a, e_b, e_c, e_d, s_a, s_b, s_c, s_d,
    a_dn_s, a_dn_r, a_gu_s, a_gu_r, a_qk_s, a_qk_r, a_ou_s, a_ou_r,
):
    n, sib, planes = dims
    at = Place(n, sib, planes)
    length, width = x.shape
    owners = planes * sib
    chunks, _, _, _, rows = gh.shape
    heads_per = rows // HEAD_DIM
    part_cols = r_out.shape[2]
    scale = HEAD_DIM ** (-0.5)
    log2e = 1.4426950408889634
    tokens = sib * n * length
    sent = []
    near = planes == 4
    units = g_dn.shape[1]
    aligned = len(o_ggu.shape) == 2

    def load(src, dst, k):
        copy = pltpu.make_async_copy(src, dst, loads.at[k])
        copy.start()
        return copy

    def owner_rows(f):
        return pl.ds(pl.multiple_of(f * rows, rows), rows)

    def z_source(dp, dc):
        return (
            lax.rem(at.p - dp + planes, planes) * sib + lax.rem(at.c - dc + sib, sib)
        )

    def z_scatter(src, dst, ssem, rsem, k):
        own = load(src.at[owner_rows(at.f)], dst.at[at.f], k)
        for dp in range(planes):
            for dc in range(sib):
                if dp or dc:
                    to = at.col(dp, dc)
                    copy = rdma(src.at[owner_rows(to)], dst.at[at.f],
                                ssem.at[dp, dc], rsem.at[dp, dc], (at.s, to))
                    copy.start()
                    sent.append(copy)
        return own

    def z_collect(dst, ssem, rsem, own):
        own.wait()
        for dp in range(planes):
            for dc in range(sib):
                if dp or dc:
                    ref = dst.at[z_source(dp, dc)]
                    rdma(ref, ref, ssem.at[dp, dc], rsem.at[dp, dc], (at.s, at.f)).wait_recv()

    def plane_total(dst, c):
        acc = dst[c].astype(F32)
        for p in range(1, planes):
            acc = acc + dst[p * sib + c].astype(F32)
        return acc.astype(BF)

    def gu_pairs():
        for dp in [2, 0] if near else range(planes):
            for dc in range(sib):
                if dp or dc:
                    yield dp, dc

    def at_ends(body):
        pl.when(jnp.logical_or(at.p == 0, at.p == planes - 1))(body)

    def at_middle(body):
        pl.when(jnp.logical_and(at.p != 0, at.p != planes - 1))(body)

    def gu_from(dp, dc):
        return at_ends if near and dp == 2 else lambda body: body()

    def gu_copy(src, dp, dc):
        to = at.col(dp, dc)
        return rdma(src, r_gu.at[at.f], z_gs.at[dp, dc], z_gr.at[dp, dc], (at.s, to))

    def gu_send(dp, dc):
        return gu_copy(sgu.at[owner_rows(at.col(dp, dc))], dp, dc)

    def plane_rows(p):
        return pl.ds(pl.multiple_of(p * (sib * rows), sib * rows), sib * rows)

    def toward_middle():
        far_plane = planes - 1 - at.p
        beside = at.p + 1 - 2 * lax.div(at.p, planes - 1)
        return rdma(sgu.at[plane_rows(far_plane)], via.at[0], via_s.at[0], via_r.at[0],
                    (at.s, beside * sib + at.c))

    def sum_load():
        return pltpu.make_async_copy(
            sgu.at[plane_rows(lax.rem(at.p + 2, planes))], via.at[1], loads.at[12]
        )

    def gu_send_sum(dc):
        c = lax.rem(at.c + dc, sib)
        return gu_copy(via.at[1, pl.ds(pl.multiple_of(c * rows, rows), rows)], 2, dc)

    def sum_on():
        def body():
            ref = via.at[0]
            rdma(ref, ref, via_s.at[0], via_r.at[0], (at.s, at.f)).wait_recv()
            sum_load().wait()
            via[1] = (via[0].astype(F32) + via[1].astype(F32)).astype(BF)
            for dc in range(sib):
                gu_send_sum(dc).start()

        at_middle(body)

    def gu_near(q, dc):
        f = q * sib + dc
        return pltpu.make_async_copy(rgu_h.at[f], r_gu.at[f], near_l.at[q, dc])

    def if_near(q, body):
        pl.when(jnp.logical_or(at.p == q - 1, at.p == q + 1))(body)

    def gu_wait(dp, dc):
        ref = r_gu.at[z_source(dp, dc)]
        rdma(ref, ref, z_gs.at[dp, dc], z_gr.at[dp, dc], (at.s, at.f)).wait_recv()

    at.barrier()
    in_qkv, in_gh = load(qkv_h, qkv, 0), load(gh_h, gh, 1)
    in_sdn, in_att, in_wqp = load(sdn_h, sdn, 4), load(att_h, att, 6), load(wqp_h, wqp, 7)
    gu_own = load(sgu.at[owner_rows(at.f)], r_gu.at[at.f], 5)
    if near:
        at_ends(lambda: toward_middle().start())
        at_middle(lambda: sum_load().start())
    for dp, dc in gu_pairs():
        gu_from(dp, dc)(lambda: gu_send(dp, dc).start())
    if near:
        for q in range(planes):
            for dc in range(sib):
                if_near(q, lambda: gu_near(q, dc).start())
    n1_cols = n1_t.shape[4]
    n1_steps = width // n1_cols

    def n1_load(m):
        return pltpu.make_async_copy(
            n1.at[:, :, :, pl.ds(m * n1_cols, n1_cols)], n1_t.at[m % 2], loads.at[8 + m % 2]
        )

    n1_load(0).start()
    n1_load(1).start()

    def row_half(ref):
        size = ref.shape[-2] // 2
        if len(ref.shape) == 4:
            return lambda c, s, h: ref.at[s, :, pl.ds(h * size, size)]
        return lambda c, s, h: ref.at[s, pl.ds(h * size, size)]

    in_sdn.wait()
    acc = sdn[0].astype(F32)
    for p in range(1, planes):
        acc = acc + sdn[p].astype(F32)
    g_dn[at.s] = acc.astype(BF)
    ag_dn = Gather(at, row_half(g_dn), (a_dn_s, a_dn_r))
    ag_dn.start()

    tri = lax.broadcasted_iota(jnp.int32, (length, length), 0) <= lax.broadcasted_iota(
        jnp.int32, (length, length), 1
    )

    def attend_back(b):
        gk[...] = jnp.zeros_like(gk)
        gv[...] = jnp.zeros_like(gv)
        for i in range(n):
            past = i * length
            here = slice(past, past + length)
            for h in range(GROUP):
                k, slot = h // heads_per, h % heads_per
                q = qkv[b, here, 128 * h : 128 * h + 128]
                do = nn(gh[k, b, i], widen_att[:, 128 * slot : 128 * slot + 128]).astype(BF)
                row = lse[b, h, i, 0:1]
                parts = [(here, True)] + ([(slice(0, past), False)] if i else [])
                probs, grads = [], []
                delta = 0.0
                for part, diagonal in parts:
                    sc = nt(qkv[b, part, 256:384], q) * (scale * log2e)
                    if diagonal:
                        sc = jnp.where(tri, sc, -1e30)
                    pr = jnp.exp2(sc - row)
                    dp = nt(qkv[b, part, 384:512], do)
                    delta = delta + jnp.sum(pr * dp, axis=0, keepdims=True)
                    probs.append(pr)
                    grads.append(dp)
                dq = jnp.zeros((length, 128), F32)
                for (part, _), pr, dp in zip(parts, probs, grads):
                    ds = (pr * (dp - delta) * scale).astype(BF)
                    gv[part] += nn(pr.astype(BF), do)
                    gk[part] += nn(ds, q)
                    dq = dq + tn(ds, qkv[b, part, 256:384])
                gq[b, here, 128 * h : 128 * h + 128] = rope(
                    dq, cos[here], -front[here], -back[here]
                ).astype(BF)
        for i in range(n):
            here = slice(i * length, (i + 1) * length)
            gq[b, here, 256:384] = rope(gk[here], cos[here], -front[here], -back[here]).astype(BF)
            gq[b, here, 384:512] = gv[here].astype(BF)

    tile = 512

    def tiles():
        return [slice(t * tile, (t + 1) * tile) for t in range(width // tile)]

    last = len(Scatter(at, (None,) * 4, (None,) * 4, rows, width).offsets()) - 1
    hops = n // 2

    s_out = Scatter(
        at, Scatter.views(sc_stage, sc_in, sc_out, sc_inn), (s_a, s_b, s_c, s_d),
        rows, planes * part_cols,
    )
    for s in range(n):
        branch[s] = ghid[:, s * part_cols : (s + 1) * part_cols].astype(BF)

    def out_pieces(c, s):
        low = branch[s]
        for p in range(planes):
            yield slice(p * part_cols, (p + 1) * part_cols), tn(att[p * sib + c], low)

    def out_stage(c, s, ref):
        for cols, value in out_pieces(c, s):
            ref[:, cols] = value.astype(BF)

    def out_ring(c, s, store):
        for cols, value in out_pieces(c, s):
            store(cols, value)

    def out_finish(cols, value):
        so[cols.start // part_cols] = value.astype(BF)

    in_att.wait()
    s_out.open(out_stage, out_ring, out_finish)
    in_qkv.wait()
    in_gh.wait()
    attend_back(0)
    ag_dn.hop(1)
    for k in range(1, last):
        s_out.step(k, out_ring, out_finish)
    if sib > 1:
        attend_back(1)
    for h in range(2, hops + 1):
        ag_dn.hop(h)
    s_out.step(last, out_ring, out_finish)
    s_out.drain()
    credits = Credits(at, free)
    credits.give()

    for m in range(n1_steps):
        n1_load(m).wait()
        part = tn(n1_t[m % 2].reshape(tokens, n1_cols), gq[...].reshape(tokens, 512)).astype(BF)
        sq[m * n1_cols : (m + 1) * n1_cols] = nt(part, widen[...]).astype(BF)
        if m + 2 < n1_steps:
            n1_load(m + 2).start()

    if near:
        sum_on()

    in_wqp.wait()
    e_in = Scatter(
        at, Scatter.views(sc_stage, sc_in, sc_out, sc_inn), (e_a, e_b, e_c, e_d), length, width
    )

    def gq_block(c, s):
        return gq[c, pl.ds(pl.multiple_of(s * length, length), length)]

    def e_stage(c, s, ref):
        for cols in tiles():
            ref[:, cols] = nt(gq_block(c, s), wqp[cols, :]).astype(BF)

    def e_ring(c, s, store):
        for cols in tiles():
            store(cols, nt(gq_block(c, s), wqp[cols, :]))

    def e_finish(cols, value):
        o_input[:, cols] = value

    credits.take()
    e_in.open(e_stage, e_ring, e_finish)
    for k in range(1, last):
        e_in.step(k, e_ring, e_finish)

    gu_own.wait()
    if near:
        for q in range(planes):
            for dc in range(sib):
                if_near(q, lambda: gu_near(q, dc).wait())
    for dp, dc in gu_pairs():
        gu_wait(dp, dc)
    if near:
        for c in range(sib):
            @pl.when(at.p == 0)
            def _():
                r_gu[(planes - 1) * sib + c] = jnp.zeros(r_gu.shape[1:], BF)

            @pl.when(at.p == planes - 1)
            def _():
                r_gu[c] = jnp.zeros(r_gu.shape[1:], BF)
    qkv_own = z_scatter(sq, r_qkv, z_qs, z_qr, 10)
    out_own = load(so.at[at.p], r_out.at[at.p], 11)
    for dp in range(1, planes):
        to = lax.rem(at.p + dp, planes)
        copy = rdma(so.at[to], r_out.at[at.p], z_os.at[dp], z_or.at[dp], (at.s, at.col(dp, 0)))
        copy.start()
        sent.append(copy)
    for c in range(sib):
        g_gu[at.s, c] = plane_total(r_gu, c)
    ag_gu = Gather(at, row_half(g_gu), (a_gu_s, a_gu_r))
    ag_gu.start()

    wide = planes * units // 2

    def gu_lane(p, g):
        return p * units // wide * 2 * wide + g * wide + p * units % wide

    def save_gu(j):
        s = at.seq_at(j)
        slot = j % n
        if not aligned:
            return [pltpu.make_async_copy(g_gu.at[s], o_ggu.at[s], saves_gu.at[slot, 0])]
        copies = []
        for c in range(sib):
            for p in range(planes):
                for g in range(2):
                    lo = (g * owners + p * sib + c) * (n * units) + s * units
                    copies.append(pltpu.make_async_copy(
                        g_gu.at[s, c, :, pl.ds(gu_lane(p, g), units)],
                        o_ggu.at[:, pl.ds(pl.multiple_of(lo, 128), units)],
                        saves_gu.at[slot, (c * planes + p) * 2 + g],
                    ))
        return copies

    def save_qkv(j):
        s = at.seq_at(j)
        slot = j % n
        if not aligned:
            return [pltpu.make_async_copy(g_qkv.at[s], o_gq.at[s], saves_qkv.at[slot, 0])]
        cols = g_qkv.shape[3]
        return [
            pltpu.make_async_copy(
                g_qkv.at[s, c], o_gq.at[:, pl.ds(pl.multiple_of((s * sib + c) * cols, 128), cols)],
                saves_qkv.at[slot, c],
            )
            for c in range(sib)
        ]

    def save_out(j):
        s = at.seq_at(j)
        slot = j % n
        if not aligned:
            return [pltpu.make_async_copy(g_out.at[s], o_gout.at[s], saves_row.at[0, slot])]
        place = o_gout.at[:, pl.ds(pl.multiple_of(s * part_cols, 128), part_cols)]
        return [pltpu.make_async_copy(g_out.at[s], place, saves_row.at[0, slot])]

    def save_down(j):
        s = at.seq_at(j)
        place = o_gdn.at[pl.ds(pl.multiple_of(s * units, units), units)]
        return [pltpu.make_async_copy(g_dn.at[s], place, saves_row.at[1, j % n])]

    saves = []

    def save(copies):
        for copy in copies:
            copy.start()
        saves.extend(copies)

    ring = [0] + [j for h in range(1, hops) for j in (-h, h)] + [hops]
    for j in ring:
        save(save_down(j))
    e_in.step(last, e_ring, e_finish)
    x_f = x[...].astype(F32)
    inv_one = lax.rsqrt(jnp.mean(x_f * x_f, axis=-1, keepdims=True) + NORM_EPS)
    norm_one = x_f * inv_one
    e_val = o_input[...]
    o_input[...] = ghid[...] + inv_one * (
        e_val - norm_one * jnp.mean(e_val * norm_one, axis=-1, keepdims=True)
    )
    out_own.wait()
    for dp in range(1, planes):
        ref = r_out.at[lax.rem(at.p - dp + planes, planes)]
        rdma(ref, ref, z_os.at[dp], z_or.at[dp], (at.s, at.f)).wait_recv()
    acc = r_out[0].astype(F32)
    for p in range(1, planes):
        acc = acc + r_out[p].astype(F32)
    g_out[at.s] = acc.astype(BF)
    ag_out = Gather(at, row_half(g_out), (a_ou_s, a_ou_r))
    ag_out.start()
    save(save_out(0))
    save(save_gu(0))
    z_collect(r_qkv, z_qs, z_qr, qkv_own)
    for c in range(sib):
        g_qkv[at.s, c] = plane_total(r_qkv, c)
    ag_qkv = Gather(at, row_half(g_qkv), (a_qk_s, a_qk_r))
    ag_qkv.start()
    save(save_qkv(0))
    for h in range(1, hops + 1):
        for ag, put in ((ag_gu, save_gu), (ag_out, save_out), (ag_qkv, save_qkv)):
            ag.hop(h)
            for j in (-h, h) if h < hops else (h,):
                save(put(j))
    e_in.drain()
    for ag in (ag_dn, ag_gu, ag_qkv, ag_out):
        ag.drain()
    for dp, dc in gu_pairs():
        gu_from(dp, dc)(lambda: gu_send(dp, dc).wait_send())
    if near:
        at_ends(lambda: toward_middle().wait_send())
        for dc in range(sib):
            at_middle(lambda: gu_send_sum(dc).wait_send())
    for copy in sent:
        copy.wait_send()
    for copy in saves:
        copy.wait()


def backward_call(dims, aligned, x, tables, widen, widen_att, lse, n1, qkv, gh, att, ghid, wqp, sgu, rgu, sdn):
    n, sib, planes = dims
    length, width = x.shape
    rows = gh.shape[4]
    owners = planes * sib
    units = sdn.shape[1]
    part_cols = width // n
    seq_len = n * length
    head_cols = (GROUP + 2) * HEAD_DIM
    vm, hb = pl.BlockSpec(memory_space=pltpu.VMEM), pl.BlockSpec(memory_space=pl.ANY)
    sds = jax.ShapeDtypeStruct
    g_shapes = [
        (n, sib, rows, head_cols), (n, sib, rows, sgu.shape[1]), (n, units, width),
        (n, rows, part_cols),
    ]
    o_shapes = g_shapes
    if aligned:
        o_shapes = [
            (rows, n * sib * head_cols), (rows, n * sib * sgu.shape[1]), None, (rows, width)
        ]
    o_shapes = [*o_shapes[:2], (n * units, width), o_shapes[3]]
    outs = [(sds((length, width), F32), vm)] + [(sds(shape, BF), hb) for shape in o_shapes]
    dma = pltpu.SemaphoreType.DMA
    scratch = [
        pltpu.VMEM(qkv.shape, BF), pltpu.VMEM(gh.shape, BF), pltpu.VMEM(att.shape, BF),
        pltpu.VMEM(wqp.shape, BF), pltpu.VMEM(sdn.shape, BF), pltpu.VMEM(qkv.shape, BF),
        pltpu.VMEM((seq_len, 128), F32), pltpu.VMEM((seq_len, 128), F32),
        pltpu.VMEM((2, *n1.shape[:3], 384), BF), pltpu.VMEM((width, head_cols), BF),
        pltpu.VMEM((planes, rows, part_cols), BF), pltpu.VMEM((n, length, part_cols), BF),
        pltpu.VMEM((owners, rows, sgu.shape[1]), BF), pltpu.VMEM((owners, rows, head_cols), BF),
        pltpu.VMEM((planes, rows, part_cols), BF),
        pltpu.VMEM(g_shapes[1], BF), pltpu.VMEM(g_shapes[0], BF), pltpu.VMEM(g_shapes[2], BF),
        pltpu.VMEM(g_shapes[3], BF),
        *Scatter.scratch(n, (length, max(width, planes * part_cols))),
        pltpu.SemaphoreType.REGULAR,
        pltpu.VMEM((2, sib * rows, sgu.shape[1]), BF), dma((1,)), dma((1,)),
        dma((13,)), dma((planes, sib)), dma((n, 2 * owners)), dma((n, sib)), dma((2, n)),
        dma((planes, sib)), dma((planes, sib)), dma((planes, sib)),
        dma((planes, sib)), dma((planes,)), dma((planes,)),
        *Scatter.sems(n), *Scatter.sems(n),
        *Gather.scratch(n, False), *Gather.scratch(n, False), *Gather.scratch(n, False),
        *Gather.scratch(n, False),
    ]
    return pl.pallas_call(
        functools.partial(backward_kernel, dims),
        out_shape=[o[0] for o in outs],
        out_specs=[o[1] for o in outs],
        in_specs=[vm] * 7 + [hb] * 4 + [vm] + [hb] * 4,
        scratch_shapes=scratch,
        compiler_params=pltpu.CompilerParams(
            collective_id=1, has_side_effects=True, vmem_limit_bytes=BACK_LIMIT
        ),
    )(x, *tables, widen, widen_att, lse, n1, qkv, gh, att, ghid, wqp, sgu, rgu, sdn)


def adamw(weight, first, second, grad, rate, decay):
    first_new = BETA_ONE * first + (1.0 - BETA_ONE) * grad
    second_new = BETA_TWO * second + (1.0 - BETA_TWO) * grad * grad
    first_hat = first_new / (1.0 - BETA_ONE**ADAM_STEP)
    second_hat = second_new / (1.0 - BETA_TWO**ADAM_STEP)
    weight_new = weight - rate * (first_hat / (jnp.sqrt(second_hat) + ADAM_EPS) + decay * weight)
    return (weight_new, first_new, second_new)


def to_bf16(value):
    return lax.reduce_precision(value, exponent_bits=8, mantissa_bits=7)


def rope_arrays(seq_len):
    half = HEAD_DIM // 2
    frequencies = (ROPE_BASE ** (-(2.0 * np.arange(half)) / HEAD_DIM)).astype(np.float32)
    angles = np.arange(seq_len, dtype=np.float32)[:, None] * frequencies[None, :]
    cos, sin = np.cos(angles), np.sin(angles)
    pad = np.zeros((seq_len, 128 - HEAD_DIM), np.float32)
    none = np.zeros_like(sin)
    return tuple(
        np.concatenate(columns, axis=1).astype(np.float32)
        for columns in ([cos, cos, pad], [-sin, none, pad], [none, sin, pad])
    )


def widening(heads):
    row = np.arange(heads * HEAD_DIM)[:, None]
    col = np.arange(heads * 128)[None, :]
    return (col == row // HEAD_DIM * 128 + row % HEAD_DIM).astype(ml_dtypes.bfloat16)


def make(n_seq, n_fsdp):
    sib = KV_HEADS // n_seq
    planes = n_fsdp // sib

    def on_device(
        inputs, cotangent, qkv_weight, out_weight, gate_up_weight, down_weight, norm_gains,
        qkv_first, qkv_second, out_first, out_second, gate_up_first, gate_up_second,
        down_first, down_second, gain_first, gain_second,
    ):
        s_idx = lax.axis_index("seq")
        _, length, width = inputs.shape
        seq_len = length * n_seq
        rows = qkv_weight.shape[0]
        head_cols = (GROUP + 2) * HEAD_DIM
        ff_rows = down_weight.shape[0]
        units = ff_rows // n_seq
        hidden_units = ff_rows * n_fsdp
        part_cols = width // n_seq
        aligned = units % 128 == 0 and part_cols % 128 == 0 and sib == 2
        aligned = aligned and rows + units // 2 <= length
        gains = to_bf16(norm_gains)
        gain_cols = gains.T

        if aligned:
            pieces = (qkv_weight, gate_up_weight, down_weight, out_weight)
        else:
            wq_s = lax.dynamic_slice_in_dim(
                qkv_weight, s_idx * sib * head_cols, sib * head_cols, 1
            )
            wq_s = (wq_s * gains[0][:, None]).astype(BF).reshape(rows, sib, head_cols)
            gu_s = gate_up_weight.reshape(rows, 2, planes, sib, n_seq, units)
            gu_s = lax.dynamic_index_in_dim(gu_s, s_idx, 4, keepdims=False)
            gu_s = (gu_s * gains[1][:, None, None, None, None]).astype(BF)
            gu_s = gu_s.transpose(3, 0, 1, 2, 4).reshape(1, sib, rows, 2 * planes * units)
            dn_s = lax.dynamic_slice_in_dim(down_weight, s_idx * units, units, 0).astype(BF)
            wo_s = lax.dynamic_slice_in_dim(out_weight, s_idx * part_cols, part_cols, 1).astype(BF)
            pieces = (wq_s.transpose(1, 0, 2), gu_s, dn_s, wo_s)
        tables = tuple(jnp.asarray(table) for table in rope_arrays(seq_len))
        widen = jnp.asarray(widening(GROUP + 2))
        widen_att = jnp.asarray(widening(rows // HEAD_DIM))

        n_one, qkv, lse, gh, att, block_out, grad_hidden, w_qkv, s_gu, r_gu, s_down = forward_call(
            (n_seq, sib, planes), (rows, units), inputs[0], cotangent[0], tables, widen, widen_att,
            gain_cols, *pieces,
        )
        input_grad, g_qkv, g_gu, g_down, g_out = backward_call(
            (n_seq, sib, planes), aligned, inputs[0], tables, widen, widen_att, lse, n_one, qkv, gh,
            att, grad_hidden, w_qkv, s_gu, r_gu, s_down,
        )
        block_out, input_grad = block_out[None], input_grad[None]
        if not aligned:
            g_qkv = g_qkv.transpose(2, 0, 1, 3).reshape(rows, n_seq * sib * head_cols)
            g_gu = g_gu.reshape(n_seq, sib, rows, 2, planes, units).transpose(2, 3, 4, 1, 0, 5)
            g_gu = g_gu.reshape(rows, 2 * hidden_units)
            g_out = g_out.transpose(1, 0, 2).reshape(rows, width)
        g_qkv, g_gu, g_down, g_out = (g.astype(F32) for g in (g_qkv, g_gu, g_down, g_out))
        gain_grad = jnp.stack(
            [
                jnp.sum(g_qkv * to_bf16(qkv_weight), axis=1),
                jnp.sum(g_gu * to_bf16(gate_up_weight), axis=1),
            ]
        )
        g_qkv = g_qkv * gains[0][:, None]
        g_gu = g_gu * gains[1][:, None]
        qkv_new = adamw(qkv_weight, qkv_first, qkv_second, g_qkv, RATE_QKV, WEIGHT_DECAY)
        out_new = adamw(out_weight, out_first, out_second, g_out, RATE_OUT, WEIGHT_DECAY)
        gu_new = adamw(
            gate_up_weight, gate_up_first, gate_up_second, g_gu, RATE_GATE_UP, WEIGHT_DECAY
        )
        down_new = adamw(
            down_weight, down_first, down_second, g_down, RATE_DOWN, WEIGHT_DECAY
        )
        gains_new = adamw(norm_gains, gain_first, gain_second, gain_grad, RATE_GAINS, 0.0)
        return (block_out, input_grad, *qkv_new, *out_new, *gu_new, *down_new, *gains_new)

    return on_device


def solution(mesh):
    tokens = P("fsdp", "seq", None)
    weight = P("fsdp", None)
    gain = P(None, "fsdp")
    in_specs = (tokens, tokens, weight, weight, weight, weight, gain) + (weight,) * 8 + (gain,) * 2
    out_specs = (tokens, tokens) + (weight,) * 12 + (gain,) * 3
    return jax.shard_map(
        make(mesh.shape["seq"], mesh.shape["fsdp"]),
        mesh=mesh, in_specs=in_specs, out_specs=out_specs, check_vma=False,
    )
```

```python
import functools

import jax
import jax.numpy as jnp
import ml_dtypes
import numpy as np
from jax import lax
from jax.experimental import pallas as pl
from jax.experimental.pallas import tpu as pltpu
from jax.sharding import PartitionSpec as P

HEAD_DIM = 96
KV_HEADS = 8
ADAM_STEP = 10
GROUP = 2

NORM_EPS = 1e-05
ROPE_BASE = 100000.0
BETA_ONE = 0.9
BETA_TWO = 0.95
ADAM_EPS = 1e-08
WEIGHT_DECAY = 0.1
RATE_QKV = 0.07
RATE_OUT = 0.8
RATE_GATE_UP = 0.07
RATE_DOWN = 0.045
RATE_GAINS = 0.6
BF = jnp.bfloat16
F32 = jnp.float32
VMEM_LIMIT = 62 * 1024 * 1024
BACK_LIMIT = 42 * 1024 * 1024


MESH = pl.DeviceIdType.MESH


def rdma(src, dst, ssem, rsem, dev):
    return pltpu.make_async_remote_copy(
        src_ref=src, dst_ref=dst, send_sem=ssem, recv_sem=rsem, device_id=dev, device_id_type=MESH
    )


class Place:
    def __init__(self, n, sib, planes):
        self.n, self.sib, self.planes = n, sib, planes
        self.s = lax.axis_index("seq")
        self.f = lax.axis_index("fsdp")
        self.c = lax.rem(self.f, sib)
        self.p = lax.div(self.f, sib)
        a, b = lax.div(self.s, 2), lax.rem(self.s, 2)
        self.r = a * (1 - b) + (n - 1 - a) * b

    def seq_at(self, j):
        if j == 0:
            return self.s
        n = self.n
        q = lax.rem(self.r + (j + n), n)
        t = lax.div(q, n // 2)
        return (1 - t) * 2 * q + t * (2 * (n - 1 - q) + 1)

    def dev(self, s, c):
        return (s, self.p * self.sib + c)

    def col(self, dp, dc):
        return lax.rem(self.p + dp, self.planes) * self.sib + lax.rem(self.c + dc, self.sib)

    def barrier(self):
        sem = pltpu.get_barrier_semaphore()
        group = self.n * self.sib
        tau = self.s * self.sib + self.c
        for j in range(1, group):
            t = lax.rem(tau + j, group)
            pl.semaphore_signal(
                sem, inc=1, device_id=self.dev(lax.div(t, self.sib), lax.rem(t, self.sib)),
                device_id_type=MESH,
            )
        for dp in range(1, self.planes):
            for dc in range(self.sib):
                pl.semaphore_signal(
                    sem, inc=1, device_id=(self.s, self.col(dp, dc)), device_id_type=MESH
                )
        pl.semaphore_wait(sem, group - 1 + (self.planes - 1) * self.sib)


class Gather:
    def __init__(self, at, part, sems):
        self.at, self.part = at, part
        self.ring_s, self.ring_r = sems[:2]
        self.share = at.sib > 1 and len(sems) > 2
        if self.share:
            self.sib_s, self.sib_r = sems[2:]
        self.sent = []

    @staticmethod
    def scratch(n, share=True):
        d = pltpu.SemaphoreType.DMA
        ring = [d((2, n // 2, 2)), d((2, n // 2, 2))]
        return ring + [d((n, 2)), d((n, 2))] if share else ring

    def _send(self, copy):
        copy.start()
        self.sent.append(copy)

    def _ring(self, way, hop, half):
        at = self.at
        src = self.part(at.c, at.seq_at(-(hop - 1) if way == 0 else hop - 1), half)
        to = at.dev(at.seq_at(1 if way == 0 else -1), at.c)
        self._send(
            rdma(src, src, self.ring_s.at[way, hop - 1, half], self.ring_r.at[way, hop - 1, half], to)
        )

    def _sib(self, j, half):
        at = self.at
        if self.share:
            src = self.part(at.c, at.seq_at(j), half)
            slot = j % at.n
            self._send(
                rdma(src, src, self.sib_s.at[slot, half], self.sib_r.at[slot, half],
                     at.dev(at.s, 1 - at.c))
            )

    def start(self):
        self._ring(0, 1, 0)
        self._ring(1, 1, 1)
        self._ring(0, 1, 1)
        self._ring(1, 1, 0)
        self._sib(0, 0)
        self._sib(0, 1)

    def _arrive(self, way, hop, half):
        at = self.at
        j = -hop if way == 0 else hop
        ref = self.part(at.c, at.seq_at(j), half)
        rdma(ref, ref, self.ring_s.at[way, hop - 1, half], self.ring_r.at[way, hop - 1, half],
             at.dev(at.s, at.c)).wait_recv()
        last = at.n // 2
        if hop + 1 < last or (hop + 1 == last and half == way):
            self._ring(way, hop + 1, half)
        if hop == last:
            j = last
        self._sib(j, half)

    def hop(self, hop):
        self.hop_first(hop)
        self.hop_second(hop)

    def hop_first(self, hop):
        self._arrive(0, hop, 0)
        self._arrive(1, hop, 1)

    def hop_second(self, hop):
        if hop < self.at.n // 2:
            self._arrive(0, hop, 1)
            self._arrive(1, hop, 0)

    def sib_wait(self, j):
        at = self.at
        if self.share:
            for half in range(2):
                ref = self.part(1 - at.c, at.seq_at(j), half)
                slot = j % at.n
                rdma(ref, ref, self.sib_s.at[slot, half], self.sib_r.at[slot, half],
                     at.dev(at.s, at.c)).wait_recv()

    def stages(self):
        last = self.at.n // 2
        yield 0, [0]
        for h in range(1, last):
            yield h, [-h, h]
        yield last, [last]

    def wait_stage(self, h, offsets):
        if h:
            self.hop(h)
        for j in offsets:
            self.sib_wait(j)

    def drain(self):
        for copy in self.sent:
            copy.wait_send()


class Move:
    def __init__(self, at, src, dst, sems, every_core=True):
        self.at, self.src, self.dst = at, src, dst
        self.ssem, self.rsem, self.hop, self.own = sems
        self.cores = at.sib if every_core else 1
        self.relay = at.planes == 4

    @staticmethod
    def sems(planes, sib):
        d = pltpu.SemaphoreType.DMA
        return [d((planes, sib)), d((planes, sib)), d((sib,)), d((1,))]

    def _pairs(self):
        for dp in [2, 1, 3] if self.relay else range(1, self.at.planes):
            for dc in range(self.cores):
                yield dp, dc
        for dc in range(1, self.cores):
            yield 0, dc

    def _direct(self, dp, body):
        if self.relay and dp in (1, 3):
            pl.when(self.at.p != (3 if dp == 1 else 0))(body)
        else:
            body()

    def _send(self, dp, dc):
        at = self.at
        return rdma(self.src(lax.rem(at.c + dc, at.sib)), self.dst(at.f), self.ssem.at[dp, dc],
                    self.rsem.at[dp, dc], (at.s, at.col(dp, dc)))

    def _local(self):
        return pltpu.make_async_copy(self.src(self.at.c), self.dst(self.at.f), self.own.at[0])

    def start(self):
        self.start_far()
        self.start_near()

    def start_far(self):
        for dp, dc in self._pairs():
            if self.relay and dp == 2:
                self._send(dp, dc).start()

    def start_near(self):
        self._local().start()
        for dp, dc in self._pairs():
            if not (self.relay and dp == 2):
                self._direct(dp, lambda: self._send(dp, dc).start())

    def _got(self, dp, dc):
        at = self.at
        source = lax.rem(at.p - dp + at.planes, at.planes) * at.sib + lax.rem(
            at.c - dc + at.sib, at.sib
        )
        ref = self.dst(source)
        rdma(ref, ref, self.ssem.at[dp, dc], self.rsem.at[dp, dc], (at.s, at.f)).wait_recv()
        return ref

    def pass_on(self):
        at = self.at
        if not self.relay:
            return
        for dp, dc in self._pairs():
            if dp == 2:
                ref = self._got(dp, dc)
                for here, to, slot in ((2, 3, 3), (1, 0, 1)):
                    @pl.when(at.p == here)
                    def _():
                        rdma(ref, ref, self.hop.at[dc], self.rsem.at[slot, dc],
                             (at.s, to * at.sib + at.c)).start()

    def wait(self):
        for dp, dc in self._pairs():
            if not (self.relay and dp == 2):
                self._got(dp, dc)
        self._local().wait()

    def drain(self):
        at = self.at
        for dp, dc in self._pairs():
            self._direct(dp, lambda: self._send(dp, dc).wait_send())
            if self.relay and dp == 2:
                ref = self.dst(at.f)

                @pl.when(jnp.logical_or(at.p == 1, at.p == 2))
                def _():
                    rdma(ref, ref, self.hop.at[dc], self.rsem.at[0, dc], (at.s, at.f)).wait_send()


class Scatter:
    def __init__(self, at, bufs, sems, rows, cols):
        self.at, self.rows, self.cols = at, rows, pl.ds(0, cols)
        self.stage, self.sib_in, self.out, self.inn = bufs
        self.sib_s, self.sib_r, self.ring_s, self.ring_r = sems
        self.sent, self.handed = [], []

    @staticmethod
    def scratch(n, shape):
        return [
            pltpu.VMEM((2, *shape), BF), pltpu.VMEM((n, *shape), BF),
            pltpu.VMEM((2, n // 2, *shape), BF), pltpu.VMEM((2, n // 2, *shape), BF),
        ]

    @staticmethod
    def views(stage, sib_in, out, inn):
        return (
            lambda k: stage.at[k], lambda k: sib_in.at[k],
            lambda w, k: out.at[w, k], lambda w, k: inn.at[w, k],
        )

    @staticmethod
    def sems(n):
        d = pltpu.SemaphoreType.DMA
        return [d((n,)), d((n,)), d((2, n // 2)), d((2, n // 2))]

    def offsets(self):
        last = self.at.n // 2
        order = [last]
        for h in range(last - 1, 0, -1):
            order += [h, -h]
        return order + [0]

    def to_sibling(self, k, produce):
        at = self.at
        if at.sib == 1:
            return
        if k >= 2:
            self.handed[k - 2].wait_send()
        view = self.stage(k % 2).at[pl.ds(0, self.rows), self.cols]
        produce(1 - at.c, at.seq_at(self.offsets()[k]), view)
        copy = rdma(view, self.sib_in(k).at[pl.ds(0, self.rows), self.cols],
                    self.sib_s.at[k], self.sib_r.at[k], at.dev(at.s, 1 - at.c))
        copy.start()
        self.handed.append(copy)

    def open(self, stage, ring, finish):
        self.to_sibling(0, stage)
        self.step(0, ring, finish)
        for k in range(1, len(self.offsets())):
            self.to_sibling(k, stage)

    def _send(self, way, k, rows):
        at = self.at
        src = self.out(way, k).at[rows, self.cols]
        copy = rdma(src, self.inn(way, k).at[rows, self.cols], self.ring_s.at[way, k], self.ring_r.at[way, k],
                    at.dev(at.seq_at(1 if way == 0 else -1), at.c))
        copy.start()
        self.sent.append(copy)

    def _wait(self, way, k, rows):
        ref = self.inn(way, k).at[rows, self.cols]
        at = self.at
        rdma(ref, ref, self.ring_s.at[way, k], self.ring_r.at[way, k],
             at.dev(at.s, at.c)).wait_recv()

    def step(self, k, produce, finish):
        at = self.at
        last = at.n // 2
        length = self.rows
        half = length // 2
        halves = (pl.ds(0, half), pl.ds(half, half))
        whole = pl.ds(0, length)
        j = self.offsets()[k]
        if at.sib > 1:
            ref = self.sib_in(k).at[pl.ds(0, length), self.cols]
            rdma(ref, ref, self.sib_s.at[k], self.sib_r.at[k], at.dev(at.s, at.c)).wait_recv()
        h = abs(j)
        if h == last:
            got = []
        else:
            ways = (0, 1) if h == 0 else ((0,) if j > 0 else (1,))
            rows_in = [halves[w] if h + 1 == last else whole for w in ways]
            got = [(w, rw) for w, rw in zip(ways, rows_in)]
        pending = [True]

        def store(cols, value, k=k, h=h, j=j, got=got, pending=pending):
            if pending[0]:
                for w, rw in got:
                    self._wait(w, h, rw)
                pending[0] = False
            if at.sib > 1:
                value = value + self.sib_in(k)[pl.ds(0, length), cols].astype(F32)
            for w, rw in got:
                if h + 1 == last:
                    add = self.inn(w, h)[pl.ds(w * half, half), cols].astype(F32)
                    if w == 0:
                        value = jnp.concatenate([value[:half] + add, value[half:]], axis=0)
                    else:
                        value = jnp.concatenate([value[:half], value[half:] + add], axis=0)
                else:
                    value = value + self.inn(w, h)[pl.ds(0, length), cols].astype(F32)
            if h == last:
                low = value.astype(BF)
                self.out(0, h - 1)[pl.ds(0, half), cols] = low[:half]
                self.out(1, h - 1)[pl.ds(half, half), cols] = low[half:]
            elif h:
                self.out(0 if j > 0 else 1, h - 1)[pl.ds(0, length), cols] = value.astype(BF)
            else:
                finish(cols, value)

        produce(at.c, at.seq_at(j), store)
        if h == last:
            self._send(0, h - 1, halves[0])
            self._send(1, h - 1, halves[1])
        elif h:
            self._send(0 if j > 0 else 1, h - 1, whole)

    def drain(self):
        for copy in self.sent + self.handed[-2:]:
            copy.wait_send()


class Credits:
    def __init__(self, at, sem):
        self.at, self.sem = at, sem

    def give(self):
        at = self.at
        if at.sib > 1:
            pl.semaphore_signal(
                self.sem, inc=1, device_id=at.dev(at.s, 1 - at.c), device_id_type=MESH
            )
        for way in (1, -1):
            pl.semaphore_signal(
                self.sem, inc=1, device_id=at.dev(at.seq_at(way), at.c), device_id_type=MESH
            )

    def take(self):
        pl.semaphore_wait(self.sem, 3 if self.at.sib > 1 else 2)


def nt(a, b):
    return lax.dot_general(a, b, (((1,), (1,)), ((), ())), preferred_element_type=F32)


def tn(a, b):
    return lax.dot_general(a, b, (((0,), (0,)), ((), ())), preferred_element_type=F32)


def nn(a, b):
    return lax.dot_general(a, b, (((1,), (0,)), ((), ())), preferred_element_type=F32)


def rope(value, cos, front, back):
    return value * cos + pltpu.roll(value, 80, 1) * front + pltpu.roll(value, 48, 1) * back


def forward_kernel(
    dims,
    x, cot, cos, front, back, widen, widen_att, gain_cols, wq_s, gu_s, dn_s, wo_s,
    o_n1, o_qkv, o_lse, o_gh, o_att, o_block, o_ghid, o_wq, o_sgu, o_rgu, o_sdn,
    hid,
    nbuf, cbuf, qkv, wq, wqp, wo, gu, dn, act, ggu, att_out, att_in, gh_in, stg, sgu_t,
    wo_f, wq_b, gu_b, dn_b, wo_b,
    sc_stage, sc_in, sc_out, sc_inn,
    zw_a, zw_b, zw_c, zw_d, zo_a, zo_b, zo_c, zo_d, zd_a, zd_b, zd_c, zd_d,
    zg_a, zg_b, zg_c, zg_d, z_ss, z_sr, local, loads,
    n1_a, n1_b, n1_c, n1_d, ct_a, ct_b, ct_c, ct_d, n2_a, n2_b, n2_c, n2_d, wo_ga, wo_gb, wo_gc, wo_gd,
    rs_a, rs_b, rs_c, rs_d, ds_a, ds_b, ds_c, ds_d, at_s, at_r, gh_s, gh_r, near_s, near_r, free,
):
    n, sib, planes = dims
    at = Place(n, sib, planes)
    length, width = x.shape
    seq_len = n * length
    raw = len(wq_s.shape) == 2
    _, rows, head_cols = wq_b.shape
    owners = planes * sib
    chunks = GROUP * HEAD_DIM // rows
    units = dn_b.shape[0]
    local_units = planes * units
    parts = 2 if units % 128 == 0 else 1
    wide = local_units // parts
    part_cols = wo_b.shape[1]
    heads_per = rows // HEAD_DIM
    half_len = length // 2
    tau = at.s * sib + at.c
    scale = HEAD_DIM ** (-0.5)
    log2e = 1.4426950408889634
    sent = []

    def token_part(ref):
        return lambda c, s, h: ref.at[c, s, pl.ds(h * half_len, half_len)]

    def owner_rows(f):
        return pl.ds(pl.multiple_of(f * rows, rows), rows)

    if raw:
        gu_f = (o_ghid, hid)

        def cut(ref, k, lo, size, dst):
            return pltpu.make_async_copy(
                ref.at[:, pl.ds(pl.multiple_of(lo, 128), size)], dst, loads.at[k]
            )

        def wq_f(c):
            return gu_f[c].at[pl.ds(0, rows), pl.ds(2 * local_units, head_cols)]

        in_wq = [
            cut(wq_s, 3 + 2 * owners + c, (at.s * sib + c) * head_cols, head_cols, wq_f(c))
            for c in range(sib)
        ]
        in_wo = cut(wo_s, 1, at.s * part_cols, part_cols, wo_f)
        half_units = units // 2

        def dn_f(h):
            return gu_f[h].at[pl.ds(rows, half_units)]

        in_dn = [
            pltpu.make_async_copy(
                dn_s.at[pl.ds(pl.multiple_of(at.s * units + h * half_units, half_units), half_units)],
                dn_f(h), loads.at[2 * h],
            )
            for h in range(2)
        ]
        in_gu = []

        def gu_lane(p, g):
            return p * units // wide * 2 * wide + g * wide + p * units % wide

        for c in range(sib):
            for p in range(planes):
                for g in range(2):
                    lo = (g * owners + p * sib + c) * (n * units) + at.s * units
                    k = (c * planes + p) * 2 + g
                    in_gu.append(
                        cut(gu_s, 3 + k, lo, units,
                            gu_f[c].at[pl.ds(0, rows), pl.ds(gu_lane(p, g), units)])
                    )
        for copy in (*in_wq, in_wo, *in_dn, *in_gu):
            copy.start()
        wq_x, gu_x, dn_x, wo_x = wq_b, gu_b, dn_b, wo_b
    else:
        wq_x, gu_x, dn_x, wo_x = wq_s, gu_s, dn_s, wo_s

    move_wq = Move(at, lambda c: wq_x.at[c], lambda f: wq.at[owner_rows(f)], (zw_a, zw_b, zw_c, zw_d))
    move_wo = Move(
        at, lambda c: wo_x, lambda f: wo.at[lax.rem(f, sib), at.s, lax.div(f, sib)],
        (zo_a, zo_b, zo_c, zo_d), False,
    )
    move_dn = Move(
        at, lambda c: dn_x,
        lambda f: dn.at[pl.ds(pl.multiple_of(lax.div(f, sib) * units, units), units)],
        (zd_a, zd_b, zd_c, zd_d), False,
    )

    def gu_move(k):
        return Move(
            at, lambda c: gu_x.at[k, c], lambda f: gu.at[k, owner_rows(f)],
            (zg_a.at[k], zg_b.at[k], zg_c.at[k], zg_d.at[k]),
        )

    move_gu = [gu_move(k) for k in range(parts)]

    x_f = x[...].astype(F32)
    inv_one = lax.rsqrt(jnp.mean(x_f * x_f, axis=-1, keepdims=True) + NORM_EPS)
    nbuf[at.c, at.s] = (x_f * inv_one).astype(BF)
    cbuf[at.c, at.s] = cot[...]
    n_one = Gather(at, token_part(nbuf), (n1_a, n1_b, n1_c, n1_d))
    at.barrier()
    n_one.start()
    if raw:
        g_one = gain_cols[:, 0:1]
        for c in range(sib):
            in_wq[c].wait()
            wq_b[c] = (wq_f(c)[...] * g_one).astype(BF)
        in_wo.wait()
        wo_b[...] = wo_f[...].astype(BF)
    move_wq.start()
    if raw:
        for h in range(2):
            in_dn[h].wait()
            dn_b[h * half_units : (h + 1) * half_units] = dn_f(h)[...].astype(BF)
        for copy in in_gu:
            copy.wait()
        g_two = gain_cols[:, 1:2]
        for c in range(sib):
            for k in range(parts):
                lanes = slice(k * 2 * wide, (k + 1) * 2 * wide)
                gu_b[k, c] = (gu_f[c][0:rows, lanes] * g_two).astype(BF)
    n_stages = list(n_one.stages())
    n_one.hop_first(1)
    move_wq.pass_on()
    move_wo.start()
    n_one.hop_second(1)
    for h, _ in n_stages[2:-1]:
        n_one.hop(h)
    move_wq.wait()
    move_gu[0].start_far()

    @pl.loop(0, width // 256)
    def _(t):
        here = pl.ds(pl.multiple_of(t * 256, 256), 256)
        wqp[here] = nn(wq[here], widen[...]).astype(BF)

    save_wq = pltpu.make_async_copy(wqp, o_wq, local.at[2])
    save_wq.start()

    def project(c, s):
        y = nn(nbuf[c, s], wqp[...]).astype(BF)
        here = pl.ds(pl.multiple_of(s * length, length), length)
        cs, fr, bk = cos[here], front[here], back[here]
        for k in range(3):
            lanes = slice(128 * k, 128 * k + 128)
            qkv[c, here, lanes] = rope(y[:, lanes].astype(F32), cs, fr, bk).astype(BF)
        qkv[c, here, 384:512] = y[:, 384:512]

    for h, offsets in n_stages:
        if h == n // 2:
            n_one.hop(h)
        for j in offsets:
            n_one.sib_wait(j)
            s_j = at.seq_at(j)

            @pl.loop(0, sib)
            def _(c):
                project(c, s_j)

    cot_gather = Gather(at, token_part(cbuf), (ct_a, ct_b, ct_c, ct_d))
    save_n1 = pltpu.make_async_copy(nbuf, o_n1, local.at[3])
    save_n1.start()
    save_qkv = pltpu.make_async_copy(qkv, o_qkv, local.at[4])
    save_qkv.start()

    tri = lax.broadcasted_iota(jnp.int32, (length, length), 0) >= lax.broadcasted_iota(
        jnp.int32, (length, length), 1
    )

    def spot(k, b, i):
        return (k * sib + b) * n + i

    def attend(i):
        @pl.loop(0, sib)
        def _(b):
            past = i * length
            here = slice(past, past + length)
            outs = []
            for h in range(GROUP):
                q = qkv[b, here, 128 * h : 128 * h + 128]
                d = jnp.where(tri, nt(q, qkv[b, here, 256:384]) * (scale * log2e), -1e30)
                m = jnp.max(d, axis=1, keepdims=True)
                if i:
                    e = nt(q, qkv[b, 0:past, 256:384]) * (scale * log2e)
                    m = jnp.maximum(m, jnp.max(e, axis=1, keepdims=True))
                d = jnp.exp2(d - m)
                total = jnp.sum(d, axis=1, keepdims=True)
                o = nn(d.astype(BF), qkv[b, here, 384:512])
                if i:
                    e = jnp.exp2(e - m)
                    total = total + jnp.sum(e, axis=1, keepdims=True)
                    o = o + nn(e.astype(BF), qkv[b, 0:past, 384:512])
                outs.append((o / total).astype(BF))
                lse = jnp.broadcast_to(m + jnp.log2(total), (length, 128))
                o_lse[b, h, i] = lse.T[0:8]
            for k in range(chunks):
                pair = jnp.concatenate(outs[k * heads_per : (k + 1) * heads_per], axis=1)
                att_out[spot(k, b, i)] = nt(pair, widen_att[...]).astype(BF)

    def send_attended(i):
        for k in range(chunks):
            for b in range(sib):
                mine = jnp.logical_and(at.s == i, at.c == b)

                @pl.when(mine)
                def _():
                    att_in[tau * chunks + k] = att_out[spot(k, b, i)]

                @pl.when(jnp.logical_not(mine))
                def _():
                    rdma(att_out.at[spot(k, b, i)], att_in.at[tau * chunks + k], at_s.at[k, b, i],
                         at_r.at[tau * chunks + k], at.dev(i, b)).start()

    wo_gather = Gather(
        at, lambda c, s, h: wo.at[c, s, pl.ds(h * (planes // 2), planes // 2)],
        (wo_ga, wo_gb, wo_gc, wo_gd),
    )
    attend(n - 1)
    save_n1.wait()
    n_one.drain()
    send_attended(n - 1)
    move_wo.pass_on()
    move_wo.wait()
    wo_gather.start()
    move_gu[0].start_near()
    for move in move_gu[1:]:
        move.start_far()
    for i in range(n - 2, -1, -1):
        attend(i)
        send_attended(i)
    wo_hops = list(wo_gather.stages())
    for h, _ in wo_hops[1:-1]:
        wo_gather.hop(h)
    cot_gather.start()
    wo_gather.hop(n // 2)
    for _, offsets in wo_hops:
        for j in offsets:
            wo_gather.sib_wait(j)
    wo_gather.drain()
    save_qkv.wait()
    save_wq.wait()

    group = n * sib
    for j in range(1, group):
        t = lax.rem(tau + j, group)
        for k in range(chunks):
            ref = att_in.at[t * chunks + k]
            rdma(ref, ref, at_s.at[0, 0, 0], at_r.at[t * chunks + k], at.dev(at.s, at.c)).wait_recv()
    for k in range(chunks):
        for i in range(n):
            for b in range(sib):
                @pl.when(jnp.logical_not(jnp.logical_and(at.s == i, at.c == b)))
                def _():
                    rdma(att_out.at[spot(k, b, i)], att_out.at[spot(k, b, i)], at_s.at[k, b, i],
                         at_r.at[0], at.dev(at.s, at.c)).wait_send()
    save_att = pltpu.make_async_copy(att_in, o_att, local.at[3])
    save_att.start()

    x_f = x[...].astype(F32)
    for s in range(n):
        cols = slice(s * part_cols, (s + 1) * part_cols)
        acc = x_f[:, cols]
        for p in range(planes):
            for c in range(sib):
                acc = acc + nn(att_in[p * sib + c], wo[c, s, p])
        hid[:, cols] = acc
    hidden = hid[...]
    inv_mid = lax.rsqrt(jnp.mean(hidden * hidden, axis=-1, keepdims=True) + NORM_EPS)
    nbuf[at.c, at.s] = (hidden * inv_mid).astype(BF)
    n_two = Gather(at, token_part(nbuf), (n2_a, n2_b, n2_c, n2_d))
    n_two.start()

    stages = list(n_two.stages())
    move_dn.start_far()
    for move in move_gu[1:]:
        move.start_near()
    move_gu[0].pass_on()
    for h, _ in stages[1:-1]:
        cot_gather.hop(h)
    for move in move_gu[1:]:
        move.pass_on()
    move_dn.start_near()
    for h, _ in stages[1:-1]:
        n_two.hop(h)
    move_dn.pass_on()

    def gate_pass(k, c, s):
        y = nn(nbuf[c, s], gu[k])
        gate, up = y[:, :wide], y[:, wide:]
        act[c, s, :, k * wide : (k + 1) * wide] = (gate / (1.0 + jnp.exp(-gate)) * up).astype(BF)
        ggu[c, s, :, k * 2 * wide : (k + 1) * 2 * wide] = y.astype(BF)

    def grad_pass(c, s):
        for k in range(parts):
            lo = k * 2 * wide
            gate = ggu[c, s, :, lo : lo + wide].astype(F32)
            up = ggu[c, s, :, lo + wide : lo + 2 * wide].astype(F32)
            grad_act = nt(cbuf[c, s], dn[k * wide : (k + 1) * wide])
            sig = 1.0 / (1.0 + jnp.exp(-gate))
            ggu[c, s, :, lo : lo + wide] = (
                grad_act * up * sig * (1.0 + gate * (1.0 - sig))
            ).astype(BF)
            ggu[c, s, :, lo + wide : lo + 2 * wide] = (grad_act * (gate * sig)).astype(BF)

    def each_block(offsets, body):
        for j in offsets:
            s_j = at.seq_at(j)

            @pl.loop(0, sib)
            def _(c):
                body(c, s_j)

    def rows_wait(offsets):
        for j in offsets:
            n_two.sib_wait(j)
            cot_gather.sib_wait(j)

    early = [j for _, offsets in stages[:-1] for j in offsets]
    late = stages[-1][1]
    rows_wait(early)
    for k in range(parts):
        move_gu[k].wait()
        each_block(early, lambda c, s: gate_pass(k, c, s))
    move_dn.wait()
    each_block(early, grad_pass)
    n_two.hop(n // 2)
    cot_gather.hop(n // 2)
    rows_wait(late)
    for k in range(parts):
        each_block(late, lambda c, s: gate_pass(k, c, s))
    each_block(late, grad_pass)

    scatter = Scatter(
        at, Scatter.views(sc_stage, sc_in, sc_out, sc_inn), (rs_a, rs_b, rs_c, rs_d), length, width
    )
    tile = 512

    def column_tiles():
        return [slice(t * tile, (t + 1) * tile) for t in range(width // tile)]

    def mid_part(c, s, cols):
        acc = nt(ggu[c, s, :, 0 : 2 * wide], gu[0, cols, :])
        for k in range(1, parts):
            acc = acc + nt(ggu[c, s, :, k * 2 * wide : (k + 1) * 2 * wide], gu[k, cols, :])
        return acc

    def to_stage(c, s, ref):
        for cols in column_tiles():
            ref[:, cols] = mid_part(c, s, cols).astype(BF)

    def to_ring(c, s, store):
        for cols in column_tiles():
            store(cols, mid_part(c, s, cols))

    tokens = sib * seq_len
    down_copies = []

    def grad_down():
        cot_all = cbuf[...].reshape(tokens, width)
        down_rows = local_units // 2
        for t in range(2):
            rows_here = slice(t * down_rows, (t + 1) * down_rows)
            lhs = act[:, :, :, rows_here].reshape(tokens, down_rows)
            stg[rows_here] = tn(lhs, cot_all).astype(BF)
        own = pltpu.make_async_copy(
            stg.at[pl.ds(pl.multiple_of(at.p * units, units), units)], o_sdn.at[at.p], local.at[6]
        )
        own.start()
        down_copies.append(own)
        for dp in range(1, planes):
            to = lax.rem(at.p + dp, planes)
            copy = rdma(stg.at[pl.ds(pl.multiple_of(to * units, units), units)], o_sdn.at[at.p],
                        z_ss.at[dp], z_sr.at[dp], (at.s, at.col(dp, 0)))
            copy.start()
            sent.append(copy)

    gu_tile = sgu_t.shape[1]
    gu_steps = width // gu_tile
    near = planes == 4

    def gu_copy(m, slot):
        return pltpu.make_async_copy(
            sgu_t.at[slot], o_sgu.at[pl.ds(m * gu_tile, gu_tile)], local.at[7 + slot]
        )

    def near_send(m, dc):
        to = m * sib + lax.rem(at.c + dc, sib)
        return rdma(o_sgu.at[owner_rows(to)], o_rgu.at[at.f], near_s.at[m, dc],
                    near_r.at[at.p, dc], (at.s, to))

    def if_near(m, body):
        pl.when(jnp.logical_or(at.p == m - 1, at.p == m + 1))(body)

    def leave(m):
        gu_copy(m, m % 2).wait()
        if near:
            for dc in range(sib):
                if_near(m, lambda: near_send(m, dc).start())

    def grad_gu():
        for m in range(gu_steps):
            slot = m % 2
            lhs = nbuf[:, :, :, m * gu_tile : (m + 1) * gu_tile].reshape(tokens, gu_tile)
            sgu_t[slot] = tn(lhs, ggu[...].reshape(tokens, 2 * local_units)).astype(BF)
            gu_copy(m, slot).start()
            if m:
                leave(m - 1)
        leave(gu_steps - 1)

    def finish(cols, value):
        o_ghid[:, cols] = value

    def flat(ref, base):
        return lambda w, k: ref.at[base, w * (n // 2) + k]

    down = Scatter(
        at, (lambda k: cbuf.at[0, k], lambda k: nbuf.at[0, k], flat(cbuf, sib - 1), flat(nbuf, sib - 1)),
        (ds_a, ds_b, ds_c, ds_d), length, width,
    )

    def down_stage(c, s, ref):
        for cols in column_tiles():
            ref[:, cols] = nn(act[c, s], dn[:, cols]).astype(BF)

    def down_ring(c, s, store):
        for cols in column_tiles():
            store(cols, nn(act[c, s], dn[:, cols]))

    def down_finish(cols, value):
        o_block[:, cols] = (hid[:, cols] + value).astype(BF)

    credits = Credits(at, free)
    last = len(scatter.offsets()) - 1
    scatter.open(to_stage, to_ring, finish)
    grad_down()
    for k in range(1, last):
        scatter.step(k, to_ring, finish)
    grad_gu()
    cot_gather.drain()
    n_two.drain()
    credits.give()
    credits.take()
    down.open(down_stage, down_ring, down_finish)
    scatter.step(last, to_ring, finish)
    e_mid = o_ghid[...]
    hidden = hid[...]
    inv_mid = lax.rsqrt(jnp.mean(hidden * hidden, axis=-1, keepdims=True) + NORM_EPS)
    norm_mid = hidden * inv_mid
    o_ghid[...] = cot[...].astype(F32) + inv_mid * (
        e_mid - norm_mid * jnp.mean(e_mid * norm_mid, axis=-1, keepdims=True)
    )
    branch = o_ghid[...].astype(BF)
    for f in range(owners):
        p, c = f // sib, f % sib
        acc = nt(branch[:, :part_cols], wo[c, 0, p])
        for s in range(1, n):
            acc = acc + nt(branch[:, s * part_cols : (s + 1) * part_cols], wo[c, s, p])
        att_out[f] = acc.astype(BF)
        t, k = f // chunks, f % chunks
        mine = tau == t

        @pl.when(mine)
        def _():
            gh_in[k, at.c, at.s] = att_out[f]

        @pl.when(jnp.logical_not(mine))
        def _():
            rdma(att_out.at[f], gh_in.at[k, at.c, at.s], gh_s.at[f], gh_r.at[k, tau],
                 at.dev(t // sib, t % sib)).start()

    for k in range(1, last):
        down.step(k, down_ring, down_finish)
    for j in range(1, group):
        t = lax.rem(tau + j, group)
        for k in range(chunks):
            ref = gh_in.at[k, lax.rem(t, sib), lax.div(t, sib)]
            rdma(ref, ref, gh_s.at[0], gh_r.at[k, t], at.dev(at.s, at.c)).wait_recv()
    save_gh = pltpu.make_async_copy(gh_in, o_gh, local.at[0])
    save_gh.start()
    for f in range(owners):
        @pl.when(jnp.logical_not(tau == f // chunks))
        def _():
            rdma(att_out.at[f], att_out.at[f], gh_s.at[f], gh_r.at[0, 0],
                 at.dev(at.s, at.c)).wait_send()

    down.step(last, down_ring, down_finish)

    for dp in range(1, planes):
        ref = o_sdn.at[lax.rem(at.p - dp + planes, planes)]
        rdma(ref, ref, z_ss.at[dp], z_sr.at[dp], (at.s, at.f)).wait_recv()
    for copy in down_copies:
        copy.wait()
    if near:
        for q in range(planes):
            for dc in range(sib):
                def arrived():
                    ref = o_rgu.at[q * sib + lax.rem(at.c - dc + sib, sib)]
                    rdma(ref, ref, near_s.at[q, dc], near_r.at[q, dc], (at.s, at.f)).wait_recv()
                    near_send(q, dc).wait_send()

                if_near(q, arrived)
    scatter.drain()
    down.drain()
    for move in (move_wq, move_wo, move_dn, *move_gu):
        move.drain()
    for copy in sent:
        copy.wait_send()
    save_att.wait()
    save_gh.wait()


def forward_call(dims, sizes, x, cot, tables, widen, widen_att, gain_cols, wq_s, gu_s, dn_s, wo_s):
    n, sib, planes = dims
    rows, units = sizes
    length, width = x.shape
    part_cols = width // n
    head_cols = (GROUP + 2) * HEAD_DIM
    owners = planes * sib
    chunks = GROUP * HEAD_DIM // rows
    ffl = planes * units
    parts = 2 if units % 128 == 0 else 1
    seq_len = n * length
    vm, hb = pl.BlockSpec(memory_space=pltpu.VMEM), pl.BlockSpec(memory_space=pl.ANY)
    blocks = (sib, n, length, width)
    sds = jax.ShapeDtypeStruct
    outs = [
        (sds(blocks, BF), hb),
        (sds((sib, seq_len, 512), BF), hb),
        (sds((sib, GROUP, n, 8, length), F32), vm),
        (sds((chunks, sib, n, length, rows), BF), hb),
        (sds((owners, length, rows), BF), hb),
        (sds((length, width), BF), vm),
        (sds((length, width), F32), vm),
        (sds((width, 512), BF), hb),
        (sds((width, 2 * ffl), BF), hb),
        (sds((owners, rows, 2 * ffl), BF), hb),
        (sds((planes, units, width), BF), hb),
    ]
    dma = pltpu.SemaphoreType.DMA
    scratch = [
        pltpu.VMEM((length, width), F32),
        pltpu.VMEM(blocks, BF), pltpu.VMEM(blocks, BF), pltpu.VMEM((sib, seq_len, 512), BF),
        pltpu.VMEM((width, head_cols), BF), pltpu.VMEM((width, 512), BF),
        pltpu.VMEM((sib, n, planes, rows, part_cols), BF),
        pltpu.VMEM((parts, width, 2 * ffl // parts), BF), pltpu.VMEM((ffl, width), BF),
        pltpu.VMEM((sib, n, length, ffl), BF), pltpu.VMEM((sib, n, length, 2 * ffl), BF),
        pltpu.VMEM((owners, length, rows), BF), pltpu.VMEM((owners, length, rows), BF),
        pltpu.VMEM((chunks, sib, n, length, rows), BF),
        pltpu.VMEM((ffl, width), BF), pltpu.VMEM((2, 384, 2 * ffl), BF),

        pltpu.VMEM((rows, part_cols), F32),
        pltpu.VMEM((sib, rows, head_cols), BF),
        pltpu.VMEM((parts, sib, rows, 2 * ffl // parts), BF),
        pltpu.VMEM((units, width), BF), pltpu.VMEM((rows, part_cols), BF),
        *Scatter.scratch(n, (length, width)),
        *Move.sems(planes, sib), *Move.sems(planes, sib), *Move.sems(planes, sib),
        dma((parts, planes, sib)), dma((parts, planes, sib)), dma((parts, sib)), dma((parts, 1)),
        dma((planes,)), dma((planes,)), dma((9,)), dma((3 + 2 * owners + sib,)),
        *Gather.scratch(n), *Gather.scratch(n), *Gather.scratch(n), *Gather.scratch(n),
        *Scatter.sems(n), *Scatter.sems(n),
        dma((chunks, sib, n)), dma((owners,)), dma((owners,)), dma((chunks, n * sib)),
        dma((planes, sib)), dma((planes, sib)), pltpu.SemaphoreType.REGULAR,
    ]
    return pl.pallas_call(
        functools.partial(forward_kernel, dims),
        out_shape=[o[0] for o in outs],
        out_specs=[o[1] for o in outs],
        in_specs=[vm] * 8 + [hb] * 4,
        scratch_shapes=scratch,
        compiler_params=pltpu.CompilerParams(
            collective_id=0, has_side_effects=True, vmem_limit_bytes=VMEM_LIMIT
        ),
    )(x, cot, *tables, widen, widen_att, gain_cols, wq_s, gu_s, dn_s, wo_s)


def backward_kernel(
    dims,
    x, cos, front, back, widen, widen_att, lse,
    n1, qkv_h, gh_h, att_h, ghid, wqp_h, sgu, rgu_h, sdn_h,
    o_input, o_gq, o_ggu, o_gdn, o_gout,
    qkv, gh, att, wqp, sdn, gq, gk, gv, n1_t, sq, so, branch,
    r_gu, r_qkv, r_out, g_gu, g_qkv, g_dn, g_out,
    sc_stage, sc_in, sc_out, sc_inn, free,
    via, via_s, via_r, loads, near_l, saves_gu, saves_qkv, saves_row, z_gs, z_gr, z_qs, z_qr, z_os, z_or,
    e_a, e_b, e_c, e_d, s_a, s_b, s_c, s_d,
    a_dn_s, a_dn_r, a_gu_s, a_gu_r, a_qk_s, a_qk_r, a_ou_s, a_ou_r,
):
    n, sib, planes = dims
    at = Place(n, sib, planes)
    length, width = x.shape
    owners = planes * sib
    chunks, _, _, _, rows = gh.shape
    heads_per = rows // HEAD_DIM
    part_cols = r_out.shape[2]
    scale = HEAD_DIM ** (-0.5)
    log2e = 1.4426950408889634
    tokens = sib * n * length
    sent = []
    near = planes == 4
    units = g_dn.shape[1]
    aligned = len(o_ggu.shape) == 2

    def load(src, dst, k):
        copy = pltpu.make_async_copy(src, dst, loads.at[k])
        copy.start()
        return copy

    def owner_rows(f):
        return pl.ds(pl.multiple_of(f * rows, rows), rows)

    def z_source(dp, dc):
        return (
            lax.rem(at.p - dp + planes, planes) * sib + lax.rem(at.c - dc + sib, sib)
        )

    def z_scatter(src, dst, ssem, rsem, k):
        own = load(src.at[owner_rows(at.f)], dst.at[at.f], k)
        for dp in range(planes):
            for dc in range(sib):
                if dp or dc:
                    to = at.col(dp, dc)
                    copy = rdma(src.at[owner_rows(to)], dst.at[at.f],
                                ssem.at[dp, dc], rsem.at[dp, dc], (at.s, to))
                    copy.start()
                    sent.append(copy)
        return own

    def z_collect(dst, ssem, rsem, own):
        own.wait()
        for dp in range(planes):
            for dc in range(sib):
                if dp or dc:
                    ref = dst.at[z_source(dp, dc)]
                    rdma(ref, ref, ssem.at[dp, dc], rsem.at[dp, dc], (at.s, at.f)).wait_recv()

    def plane_total(dst, c):
        acc = dst[c].astype(F32)
        for p in range(1, planes):
            acc = acc + dst[p * sib + c].astype(F32)
        return acc.astype(BF)

    def gu_pairs():
        for dp in [2, 0] if near else range(planes):
            for dc in range(sib):
                if dp or dc:
                    yield dp, dc

    def at_ends(body):
        pl.when(jnp.logical_or(at.p == 0, at.p == planes - 1))(body)

    def at_middle(body):
        pl.when(jnp.logical_and(at.p != 0, at.p != planes - 1))(body)

    def gu_from(dp, dc):
        return at_ends if near and dp == 2 else lambda body: body()

    def gu_copy(src, dp, dc):
        to = at.col(dp, dc)
        return rdma(src, r_gu.at[at.f], z_gs.at[dp, dc], z_gr.at[dp, dc], (at.s, to))

    def gu_send(dp, dc):
        return gu_copy(sgu.at[owner_rows(at.col(dp, dc))], dp, dc)

    def plane_rows(p):
        return pl.ds(pl.multiple_of(p * (sib * rows), sib * rows), sib * rows)

    def toward_middle():
        far_plane = planes - 1 - at.p
        beside = at.p + 1 - 2 * lax.div(at.p, planes - 1)
        return rdma(sgu.at[plane_rows(far_plane)], via.at[0], via_s.at[0], via_r.at[0],
                    (at.s, beside * sib + at.c))

    def sum_load():
        return pltpu.make_async_copy(
            sgu.at[plane_rows(lax.rem(at.p + 2, planes))], via.at[1], loads.at[12]
        )

    def gu_send_sum(dc):
        c = lax.rem(at.c + dc, sib)
        return gu_copy(via.at[1, pl.ds(pl.multiple_of(c * rows, rows), rows)], 2, dc)

    def sum_on():
        def body():
            ref = via.at[0]
            rdma(ref, ref, via_s.at[0], via_r.at[0], (at.s, at.f)).wait_recv()
            sum_load().wait()
            via[1] = (via[0].astype(F32) + via[1].astype(F32)).astype(BF)
            for dc in range(sib):
                gu_send_sum(dc).start()

        at_middle(body)

    def gu_near(q, dc):
        f = q * sib + dc
        return pltpu.make_async_copy(rgu_h.at[f], r_gu.at[f], near_l.at[q, dc])

    def if_near(q, body):
        pl.when(jnp.logical_or(at.p == q - 1, at.p == q + 1))(body)

    def gu_wait(dp, dc):
        ref = r_gu.at[z_source(dp, dc)]
        rdma(ref, ref, z_gs.at[dp, dc], z_gr.at[dp, dc], (at.s, at.f)).wait_recv()

    at.barrier()
    in_qkv, in_gh = load(qkv_h, qkv, 0), load(gh_h, gh, 1)
    in_sdn, in_att, in_wqp = load(sdn_h, sdn, 4), load(att_h, att, 6), load(wqp_h, wqp, 7)
    gu_own = load(sgu.at[owner_rows(at.f)], r_gu.at[at.f], 5)
    if near:
        at_ends(lambda: toward_middle().start())
        at_middle(lambda: sum_load().start())
    for dp, dc in gu_pairs():
        gu_from(dp, dc)(lambda: gu_send(dp, dc).start())
    if near:
        for q in range(planes):
            for dc in range(sib):
                if_near(q, lambda: gu_near(q, dc).start())
    n1_cols = n1_t.shape[4]
    n1_steps = width // n1_cols

    def n1_load(m):
        return pltpu.make_async_copy(
            n1.at[:, :, :, pl.ds(m * n1_cols, n1_cols)], n1_t.at[m % 2], loads.at[8 + m % 2]
        )

    n1_load(0).start()
    n1_load(1).start()

    def row_half(ref):
        size = ref.shape[-2] // 2
        if len(ref.shape) == 4:
            return lambda c, s, h: ref.at[s, :, pl.ds(h * size, size)]
        return lambda c, s, h: ref.at[s, pl.ds(h * size, size)]

    in_sdn.wait()
    acc = sdn[0].astype(F32)
    for p in range(1, planes):
        acc = acc + sdn[p].astype(F32)
    g_dn[at.s] = acc.astype(BF)
    ag_dn = Gather(at, row_half(g_dn), (a_dn_s, a_dn_r))
    ag_dn.start()

    tri = lax.broadcasted_iota(jnp.int32, (length, length), 0) <= lax.broadcasted_iota(
        jnp.int32, (length, length), 1
    )

    def attend_back(b):
        gk[...] = jnp.zeros_like(gk)
        gv[...] = jnp.zeros_like(gv)
        for i in range(n):
            past = i * length
            here = slice(past, past + length)
            for h in range(GROUP):
                k, slot = h // heads_per, h % heads_per
                q = qkv[b, here, 128 * h : 128 * h + 128]
                do = nn(gh[k, b, i], widen_att[:, 128 * slot : 128 * slot + 128]).astype(BF)
                row = lse[b, h, i, 0:1]
                parts = [(here, True)] + ([(slice(0, past), False)] if i else [])
                probs, grads = [], []
                delta = 0.0
                for part, diagonal in parts:
                    sc = nt(qkv[b, part, 256:384], q) * (scale * log2e)
                    if diagonal:
                        sc = jnp.where(tri, sc, -1e30)
                    pr = jnp.exp2(sc - row)
                    dp = nt(qkv[b, part, 384:512], do)
                    delta = delta + jnp.sum(pr * dp, axis=0, keepdims=True)
                    probs.append(pr)
                    grads.append(dp)
                dq = jnp.zeros((length, 128), F32)
                for (part, _), pr, dp in zip(parts, probs, grads):
                    ds = (pr * (dp - delta) * scale).astype(BF)
                    gv[part] += nn(pr.astype(BF), do)
                    gk[part] += nn(ds, q)
                    dq = dq + tn(ds, qkv[b, part, 256:384])
                gq[b, here, 128 * h : 128 * h + 128] = rope(
                    dq, cos[here], -front[here], -back[here]
                ).astype(BF)
        for i in range(n):
            here = slice(i * length, (i + 1) * length)
            gq[b, here, 256:384] = rope(gk[here], cos[here], -front[here], -back[here]).astype(BF)
            gq[b, here, 384:512] = gv[here].astype(BF)

    tile = 512

    def tiles():
        return [slice(t * tile, (t + 1) * tile) for t in range(width // tile)]

    last = len(Scatter(at, (None,) * 4, (None,) * 4, rows, width).offsets()) - 1
    hops = n // 2

    s_out = Scatter(
        at, Scatter.views(sc_stage, sc_in, sc_out, sc_inn), (s_a, s_b, s_c, s_d),
        rows, planes * part_cols,
    )
    for s in range(n):
        branch[s] = ghid[:, s * part_cols : (s + 1) * part_cols].astype(BF)

    def out_pieces(c, s):
        low = branch[s]
        for p in range(planes):
            yield slice(p * part_cols, (p + 1) * part_cols), tn(att[p * sib + c], low)

    def out_stage(c, s, ref):
        for cols, value in out_pieces(c, s):
            ref[:, cols] = value.astype(BF)

    def out_ring(c, s, store):
        for cols, value in out_pieces(c, s):
            store(cols, value)

    def out_finish(cols, value):
        so[cols.start // part_cols] = value.astype(BF)

    in_att.wait()
    s_out.open(out_stage, out_ring, out_finish)
    in_qkv.wait()
    in_gh.wait()
    attend_back(0)
    ag_dn.hop(1)
    for k in range(1, last):
        s_out.step(k, out_ring, out_finish)
    if sib > 1:
        attend_back(1)
    for h in range(2, hops + 1):
        ag_dn.hop(h)
    s_out.step(last, out_ring, out_finish)
    s_out.drain()
    credits = Credits(at, free)
    credits.give()

    for m in range(n1_steps):
        n1_load(m).wait()
        part = tn(n1_t[m % 2].reshape(tokens, n1_cols), gq[...].reshape(tokens, 512)).astype(BF)
        sq[m * n1_cols : (m + 1) * n1_cols] = nt(part, widen[...]).astype(BF)
        if m + 2 < n1_steps:
            n1_load(m + 2).start()

    if near:
        sum_on()

    in_wqp.wait()
    e_in = Scatter(
        at, Scatter.views(sc_stage, sc_in, sc_out, sc_inn), (e_a, e_b, e_c, e_d), length, width
    )

    def gq_block(c, s):
        return gq[c, pl.ds(pl.multiple_of(s * length, length), length)]

    def e_stage(c, s, ref):
        for cols in tiles():
            ref[:, cols] = nt(gq_block(c, s), wqp[cols, :]).astype(BF)

    def e_ring(c, s, store):
        for cols in tiles():
            store(cols, nt(gq_block(c, s), wqp[cols, :]))

    def e_finish(cols, value):
        o_input[:, cols] = value

    credits.take()
    e_in.open(e_stage, e_ring, e_finish)
    for k in range(1, last):
        e_in.step(k, e_ring, e_finish)

    gu_own.wait()
    if near:
        for q in range(planes):
            for dc in range(sib):
                if_near(q, lambda: gu_near(q, dc).wait())
    for dp, dc in gu_pairs():
        gu_wait(dp, dc)
    if near:
        for c in range(sib):
            @pl.when(at.p == 0)
            def _():
                r_gu[(planes - 1) * sib + c] = jnp.zeros(r_gu.shape[1:], BF)

            @pl.when(at.p == planes - 1)
            def _():
                r_gu[c] = jnp.zeros(r_gu.shape[1:], BF)
    qkv_own = z_scatter(sq, r_qkv, z_qs, z_qr, 10)
    out_own = load(so.at[at.p], r_out.at[at.p], 11)
    for dp in range(1, planes):
        to = lax.rem(at.p + dp, planes)
        copy = rdma(so.at[to], r_out.at[at.p], z_os.at[dp], z_or.at[dp], (at.s, at.col(dp, 0)))
        copy.start()
        sent.append(copy)
    for c in range(sib):
        g_gu[at.s, c] = plane_total(r_gu, c)
    ag_gu = Gather(at, row_half(g_gu), (a_gu_s, a_gu_r))
    ag_gu.start()

    wide = planes * units // 2

    def gu_lane(p, g):
        return p * units // wide * 2 * wide + g * wide + p * units % wide

    def save_gu(j):
        s = at.seq_at(j)
        slot = j % n
        if not aligned:
            return [pltpu.make_async_copy(g_gu.at[s], o_ggu.at[s], saves_gu.at[slot, 0])]
        copies = []
        for c in range(sib):
            for p in range(planes):
                for g in range(2):
                    lo = (g * owners + p * sib + c) * (n * units) + s * units
                    copies.append(pltpu.make_async_copy(
                        g_gu.at[s, c, :, pl.ds(gu_lane(p, g), units)],
                        o_ggu.at[:, pl.ds(pl.multiple_of(lo, 128), units)],
                        saves_gu.at[slot, (c * planes + p) * 2 + g],
                    ))
        return copies

    def save_qkv(j):
        s = at.seq_at(j)
        slot = j % n
        if not aligned:
            return [pltpu.make_async_copy(g_qkv.at[s], o_gq.at[s], saves_qkv.at[slot, 0])]
        cols = g_qkv.shape[3]
        return [
            pltpu.make_async_copy(
                g_qkv.at[s, c], o_gq.at[:, pl.ds(pl.multiple_of((s * sib + c) * cols, 128), cols)],
                saves_qkv.at[slot, c],
            )
            for c in range(sib)
        ]

    def save_out(j):
        s = at.seq_at(j)
        slot = j % n
        if not aligned:
            return [pltpu.make_async_copy(g_out.at[s], o_gout.at[s], saves_row.at[0, slot])]
        place = o_gout.at[:, pl.ds(pl.multiple_of(s * part_cols, 128), part_cols)]
        return [pltpu.make_async_copy(g_out.at[s], place, saves_row.at[0, slot])]

    def save_down(j):
        s = at.seq_at(j)
        place = o_gdn.at[pl.ds(pl.multiple_of(s * units, units), units)]
        return [pltpu.make_async_copy(g_dn.at[s], place, saves_row.at[1, j % n])]

    saves = []

    def save(copies):
        for copy in copies:
            copy.start()
        saves.extend(copies)

    ring = [0] + [j for h in range(1, hops) for j in (-h, h)] + [hops]
    for j in ring:
        save(save_down(j))
    e_in.step(last, e_ring, e_finish)
    x_f = x[...].astype(F32)
    inv_one = lax.rsqrt(jnp.mean(x_f * x_f, axis=-1, keepdims=True) + NORM_EPS)
    norm_one = x_f * inv_one
    e_val = o_input[...]
    o_input[...] = ghid[...] + inv_one * (
        e_val - norm_one * jnp.mean(e_val * norm_one, axis=-1, keepdims=True)
    )
    out_own.wait()
    for dp in range(1, planes):
        ref = r_out.at[lax.rem(at.p - dp + planes, planes)]
        rdma(ref, ref, z_os.at[dp], z_or.at[dp], (at.s, at.f)).wait_recv()
    acc = r_out[0].astype(F32)
    for p in range(1, planes):
        acc = acc + r_out[p].astype(F32)
    g_out[at.s] = acc.astype(BF)
    ag_out = Gather(at, row_half(g_out), (a_ou_s, a_ou_r))
    ag_out.start()
    save(save_out(0))
    save(save_gu(0))
    z_collect(r_qkv, z_qs, z_qr, qkv_own)
    for c in range(sib):
        g_qkv[at.s, c] = plane_total(r_qkv, c)
    ag_qkv = Gather(at, row_half(g_qkv), (a_qk_s, a_qk_r))
    ag_qkv.start()
    save(save_qkv(0))
    for h in range(1, hops + 1):
        for ag, put in ((ag_gu, save_gu), (ag_out, save_out), (ag_qkv, save_qkv)):
            ag.hop(h)
            for j in (-h, h) if h < hops else (h,):
                save(put(j))
    e_in.drain()
    for ag in (ag_dn, ag_gu, ag_qkv, ag_out):
        ag.drain()
    for dp, dc in gu_pairs():
        gu_from(dp, dc)(lambda: gu_send(dp, dc).wait_send())
    if near:
        at_ends(lambda: toward_middle().wait_send())
        for dc in range(sib):
            at_middle(lambda: gu_send_sum(dc).wait_send())
    for copy in sent:
        copy.wait_send()
    for copy in saves:
        copy.wait()


def backward_call(dims, aligned, x, tables, widen, widen_att, lse, n1, qkv, gh, att, ghid, wqp, sgu, rgu, sdn):
    n, sib, planes = dims
    length, width = x.shape
    rows = gh.shape[4]
    owners = planes * sib
    units = sdn.shape[1]
    part_cols = width // n
    seq_len = n * length
    head_cols = (GROUP + 2) * HEAD_DIM
    vm, hb = pl.BlockSpec(memory_space=pltpu.VMEM), pl.BlockSpec(memory_space=pl.ANY)
    far = pl.BlockSpec(memory_space=pltpu.HBM)
    sds = jax.ShapeDtypeStruct
    g_shapes = [
        (n, sib, rows, head_cols), (n, sib, rows, sgu.shape[1]), (n, units, width),
        (n, rows, part_cols),
    ]
    o_shapes = g_shapes
    if aligned:
        o_shapes = [
            (rows, n * sib * head_cols), (rows, n * sib * sgu.shape[1]), None, (rows, width)
        ]
    o_shapes = [*o_shapes[:2], (n * units, width), o_shapes[3]]
    outs = [(sds((length, width), F32), vm)] + [(sds(shape, BF), hb) for shape in o_shapes]
    dma = pltpu.SemaphoreType.DMA
    scratch = [
        pltpu.VMEM(qkv.shape, BF), pltpu.VMEM(gh.shape, BF), pltpu.VMEM(att.shape, BF),
        pltpu.VMEM(wqp.shape, BF), pltpu.VMEM(sdn.shape, BF), pltpu.VMEM(qkv.shape, BF),
        pltpu.VMEM((seq_len, 128), F32), pltpu.VMEM((seq_len, 128), F32),
        pltpu.VMEM((2, *n1.shape[:3], 384), BF), pltpu.VMEM((width, head_cols), BF),
        pltpu.VMEM((planes, rows, part_cols), BF), pltpu.VMEM((n, length, part_cols), BF),
        pltpu.VMEM((owners, rows, sgu.shape[1]), BF), pltpu.VMEM((owners, rows, head_cols), BF),
        pltpu.VMEM((planes, rows, part_cols), BF),
        pltpu.VMEM(g_shapes[1], BF), pltpu.VMEM(g_shapes[0], BF), pltpu.VMEM(g_shapes[2], BF),
        pltpu.VMEM(g_shapes[3], BF),
        *Scatter.scratch(n, (length, max(width, planes * part_cols))),
        pltpu.SemaphoreType.REGULAR,
        pltpu.VMEM((2, sib * rows, sgu.shape[1]), BF), dma((1,)), dma((1,)),
        dma((13,)), dma((planes, sib)), dma((n, 2 * owners)), dma((n, sib)), dma((2, n)),
        dma((planes, sib)), dma((planes, sib)), dma((planes, sib)),
        dma((planes, sib)), dma((planes,)), dma((planes,)),
        *Scatter.sems(n), *Scatter.sems(n),
        *Gather.scratch(n, False), *Gather.scratch(n, False), *Gather.scratch(n, False),
        *Gather.scratch(n, False),
    ]
    return pl.pallas_call(
        functools.partial(backward_kernel, dims),
        out_shape=[o[0] for o in outs],
        out_specs=[o[1] for o in outs],
        in_specs=[vm] * 7 + [far] * 4 + [vm] + [far] * 4,
        scratch_shapes=scratch,
        compiler_params=pltpu.CompilerParams(
            collective_id=1, has_side_effects=True, vmem_limit_bytes=BACK_LIMIT
        ),
    )(x, *tables, widen, widen_att, lse, n1, qkv, gh, att, ghid, wqp, sgu, rgu, sdn)


def adamw(weight, first, second, grad, rate, decay):
    first_new = BETA_ONE * first + (1.0 - BETA_ONE) * grad
    second_new = BETA_TWO * second + (1.0 - BETA_TWO) * grad * grad
    first_hat = first_new / (1.0 - BETA_ONE**ADAM_STEP)
    second_hat = second_new / (1.0 - BETA_TWO**ADAM_STEP)
    weight_new = weight - rate * (first_hat / (jnp.sqrt(second_hat) + ADAM_EPS) + decay * weight)
    return (weight_new, first_new, second_new)


def to_bf16(value):
    return lax.reduce_precision(value, exponent_bits=8, mantissa_bits=7)


def rope_arrays(seq_len):
    half = HEAD_DIM // 2
    frequencies = (ROPE_BASE ** (-(2.0 * np.arange(half)) / HEAD_DIM)).astype(np.float32)
    angles = np.arange(seq_len, dtype=np.float32)[:, None] * frequencies[None, :]
    cos, sin = np.cos(angles), np.sin(angles)
    pad = np.zeros((seq_len, 128 - HEAD_DIM), np.float32)
    none = np.zeros_like(sin)
    return tuple(
        np.concatenate(columns, axis=1).astype(np.float32)
        for columns in ([cos, cos, pad], [-sin, none, pad], [none, sin, pad])
    )


def widening(heads):
    row = np.arange(heads * HEAD_DIM)[:, None]
    col = np.arange(heads * 128)[None, :]
    return (col == row // HEAD_DIM * 128 + row % HEAD_DIM).astype(ml_dtypes.bfloat16)


def make(n_seq, n_fsdp):
    sib = KV_HEADS // n_seq
    planes = n_fsdp // sib

    def on_device(
        inputs, cotangent, qkv_weight, out_weight, gate_up_weight, down_weight, norm_gains,
        qkv_first, qkv_second, out_first, out_second, gate_up_first, gate_up_second,
        down_first, down_second, gain_first, gain_second,
    ):
        s_idx = lax.axis_index("seq")
        _, length, width = inputs.shape
        seq_len = length * n_seq
        rows = qkv_weight.shape[0]
        head_cols = (GROUP + 2) * HEAD_DIM
        ff_rows = down_weight.shape[0]
        units = ff_rows // n_seq
        hidden_units = ff_rows * n_fsdp
        part_cols = width // n_seq
        aligned = units % 128 == 0 and part_cols % 128 == 0 and sib == 2
        aligned = aligned and rows + units // 2 <= length
        gains = to_bf16(norm_gains)
        gain_cols = gains.T

        if aligned:
            pieces = (qkv_weight, gate_up_weight, down_weight, out_weight)
        else:
            wq_s = lax.dynamic_slice_in_dim(
                qkv_weight, s_idx * sib * head_cols, sib * head_cols, 1
            )
            wq_s = (wq_s * gains[0][:, None]).astype(BF).reshape(rows, sib, head_cols)
            gu_s = gate_up_weight.reshape(rows, 2, planes, sib, n_seq, units)
            gu_s = lax.dynamic_index_in_dim(gu_s, s_idx, 4, keepdims=False)
            gu_s = (gu_s * gains[1][:, None, None, None, None]).astype(BF)
            gu_s = gu_s.transpose(3, 0, 1, 2, 4).reshape(1, sib, rows, 2 * planes * units)
            dn_s = lax.dynamic_slice_in_dim(down_weight, s_idx * units, units, 0).astype(BF)
            wo_s = lax.dynamic_slice_in_dim(out_weight, s_idx * part_cols, part_cols, 1).astype(BF)
            pieces = (wq_s.transpose(1, 0, 2), gu_s, dn_s, wo_s)
        tables = tuple(jnp.asarray(table) for table in rope_arrays(seq_len))
        widen = jnp.asarray(widening(GROUP + 2))
        widen_att = jnp.asarray(widening(rows // HEAD_DIM))

        n_one, qkv, lse, gh, att, block_out, grad_hidden, w_qkv, s_gu, r_gu, s_down = forward_call(
            (n_seq, sib, planes), (rows, units), inputs[0], cotangent[0], tables, widen, widen_att,
            gain_cols, *pieces,
        )
        input_grad, g_qkv, g_gu, g_down, g_out = backward_call(
            (n_seq, sib, planes), aligned, inputs[0], tables, widen, widen_att, lse, n_one, qkv, gh,
            att, grad_hidden, w_qkv, s_gu, r_gu, s_down,
        )
        block_out, input_grad = block_out[None], input_grad[None]
        if not aligned:
            g_qkv = g_qkv.transpose(2, 0, 1, 3).reshape(rows, n_seq * sib * head_cols)
            g_gu = g_gu.reshape(n_seq, sib, rows, 2, planes, units).transpose(2, 3, 4, 1, 0, 5)
            g_gu = g_gu.reshape(rows, 2 * hidden_units)
            g_out = g_out.transpose(1, 0, 2).reshape(rows, width)
        g_qkv, g_gu, g_down, g_out = (g.astype(F32) for g in (g_qkv, g_gu, g_down, g_out))
        gain_grad = jnp.stack(
            [
                jnp.sum(g_qkv * to_bf16(qkv_weight), axis=1),
                jnp.sum(g_gu * to_bf16(gate_up_weight), axis=1),
            ]
        )
        g_qkv = g_qkv * gains[0][:, None]
        g_gu = g_gu * gains[1][:, None]
        qkv_new = adamw(qkv_weight, qkv_first, qkv_second, g_qkv, RATE_QKV, WEIGHT_DECAY)
        out_new = adamw(out_weight, out_first, out_second, g_out, RATE_OUT, WEIGHT_DECAY)
        gu_new = adamw(
            gate_up_weight, gate_up_first, gate_up_second, g_gu, RATE_GATE_UP, WEIGHT_DECAY
        )
        down_new = adamw(
            down_weight, down_first, down_second, g_down, RATE_DOWN, WEIGHT_DECAY
        )
        gains_new = adamw(norm_gains, gain_first, gain_second, gain_grad, RATE_GAINS, 0.0)
        return (block_out, input_grad, *qkv_new, *out_new, *gu_new, *down_new, *gains_new)

    return on_device


def solution(mesh):
    tokens = P("fsdp", "seq", None)
    weight = P("fsdp", None)
    gain = P(None, "fsdp")
    in_specs = (tokens, tokens, weight, weight, weight, weight, gain) + (weight,) * 8 + (gain,) * 2
    out_specs = (tokens, tokens) + (weight,) * 12 + (gain,) * 3
    return jax.shard_map(
        make(mesh.shape["seq"], mesh.shape["fsdp"]),
        mesh=mesh, in_specs=in_specs, out_specs=out_specs, check_vma=False,
    )
```
